32 devices in a mesh: group: 4 (over z), ctx: 2 (over y), wshard: 4 (over x, core).
Axes of the slice: x: 2, y: 2, z: 4, core: 2. Of those that a mesh axis runs over, the one named last changes fastest.
Arguments:
- tokens: bfloat16 [16, 4096, 1152], P(('group', 'wshard'), 'ctx'), may hold values from -6 to 6
- block_map: int32 [16, 4], P(('group', 'wshard')), may hold values from 0 to 3, as said below
- attention_gain: bfloat16 [1152], P(('group', 'wshard')), may hold values from 0.099609375 to 1.8984375
- query_weight: bfloat16 [1152, 1152], P(('group', 'wshard')), may hold values from -0.1875 to 0.1875
- key_matrix: bfloat16 [1152, 384], P(('group', 'wshard')), may hold values from -0.1875 to 0.1875
- value_matrix: bfloat16 [1152, 384], P(('group', 'wshard')), may hold values from -0.1875 to 0.1875
- output_weight: bfloat16 [1152, 1152], P(('group', 'wshard')), may hold values from -3 to 3
- feedforward_gain: bfloat16 [1152], P(('group', 'wshard')), may hold values from 0.099609375 to 1.8984375
- gate_weight: bfloat16 [1152, 3072], P(('group', 'wshard')), may hold values from -0.1875 to 0.1875
- up_weight: bfloat16 [1152, 3072], P(('group', 'wshard')), may hold values from -0.1875 to 0.1875
- down_weight: bfloat16 [3072, 1152], P(('group', 'wshard')), may hold values from -0.109375 to 0.109375
- out_grad: bfloat16 [16, 4096, 1152], P(('group', 'wshard'), 'ctx'), may hold values from -6 to 6
Outputs:
- layer_out: bfloat16 [16, 4096, 1152], P(('group', 'wshard'), 'ctx')
- grad_tokens: float32 [16, 4096, 1152], P(('group', 'wshard'), 'ctx')
- grad_attention_gain: float32 [1152], P(('group', 'wshard'))
- grad_query_weight: float32 [1152, 1152], P(('group', 'wshard'))
- grad_key_weight: float32 [1152, 384], P(('group', 'wshard'))
- grad_value_weight: float32 [1152, 384], P(('group', 'wshard'))
- grad_output_weight: float32 [1152, 1152], P(('group', 'wshard'))
- grad_feedforward_gain: float32 [1152], P(('group', 'wshard'))
- grad_gate_weight: float32 [1152, 3072], P(('group', 'wshard'))
- grad_up_weight: float32 [1152, 3072], P(('group', 'wshard'))
- grad_down_weight: float32 [3072, 1152], P(('group', 'wshard'))
The draws below stay inside these ranges and needn't reach their ends.
Inputs may be any that keep to these rules, and one draw needn't show every extreme that they name: `block_map`: in every group the entries are a permutation of the 4 blocks; entries 2 d and 2 d + 1 add up to 3, and entry 2 d is below half of 4.
All inputs are finite; a program needn't handle non-finite values.
Results may differ from the reference program's by a relative error of at most 0.024.
Values may be sent and summed in bfloat16 or wider, within the bound.
A program may use at most 384 MiB of HBM per device.

```python
import jax
import jax.numpy as jnp
from jax import lax

MODEL_WIDTH = 1152
QUERY_HEADS = 18
SHARED_KV_HEADS = 6
HEAD_WIDTH = 64
FF = 3072
CONTINUE_LENGTH = 512
CONTINUATIONS = 4
GROUPS = 16
PROMPT_LENGTH = 2048
GROUP_TOK = 4096
NBLK = 4
BLOCK = 1024


def draw_block_map(key, part):
    key = jax.random.fold_in(key, 11)
    group_keys = jax.random.split(key, GROUPS)
    leading = jax.vmap(lambda group_key: jax.random.permutation(group_key, NBLK // 2))(group_keys).astype(jnp.int32)
    mirrored = (NBLK - 1 - leading).astype(jnp.int32)
    return jnp.stack([leading, mirrored], axis=-1).reshape(GROUPS, NBLK).astype(jnp.int32)


def steps_of(own_key, shape, cuts, low, high):
    loudness = 1.0
    for position, parts in cuts:
        steps = jax.random.uniform(jax.random.fold_in(jax.random.fold_in(own_key, 6), position), (parts,), jnp.float32, low / len(cuts), high / len(cuts))
        loudness = loudness * jnp.repeat(jnp.exp(steps), shape[position] // parts).reshape((-1,) + (1,) * (len(shape) - 1 - position))
    return loudness


def noise(own_key, dims, scale, reach, cuts=(), held_as=jnp.bfloat16):
    entries = scale * jax.random.normal(own_key, dims, jnp.float32)
    if cuts:
        entries = entries * steps_of(own_key, dims, cuts, -0.22, 0.18)
    return jnp.clip(entries, -reach, reach).astype(held_as)


def setup_inputs(seed: int = 0) -> dict:
    key_list = jax.random.split(jax.random.key(seed), 13)
    tokens = noise(key_list[0], (GROUPS, GROUP_TOK, MODEL_WIDTH), 1.0, 6.0, ((0, 16), (1, 2)))
    block_map = draw_block_map(jax.random.fold_in(key_list[12], 71), 0)
    attention_gain = jnp.clip(1.0 + 0.18 * jax.random.normal(key_list[2], (MODEL_WIDTH,), jnp.float32), 0.099609375, 1.8984375).astype(jnp.bfloat16)
    query_weight = noise(key_list[3], (MODEL_WIDTH, QUERY_HEADS * HEAD_WIDTH), MODEL_WIDTH ** -0.5, 0.1875, ((0, 16),))
    key_matrix = noise(key_list[4], (MODEL_WIDTH, SHARED_KV_HEADS * HEAD_WIDTH), MODEL_WIDTH ** -0.5, 0.1875, ((0, 16),))
    value_matrix = noise(key_list[5], (MODEL_WIDTH, SHARED_KV_HEADS * HEAD_WIDTH), MODEL_WIDTH ** -0.5, 0.1875, ((0, 16),))
    output_weight = noise(key_list[6], (QUERY_HEADS * HEAD_WIDTH, MODEL_WIDTH), (max(4, QUERY_HEADS * HEAD_WIDTH // 256)) ** -0.5, 3.0, ((0, 16),))
    feedforward_gain = jnp.clip(1.0 + 0.18 * jax.random.normal(key_list[7], (MODEL_WIDTH,), jnp.float32), 0.099609375, 1.8984375).astype(jnp.bfloat16)
    gate_weight = noise(key_list[8], (MODEL_WIDTH, FF), MODEL_WIDTH ** -0.5, 0.1875, ((0, 16),))
    up_weight = noise(key_list[9], (MODEL_WIDTH, FF), MODEL_WIDTH ** -0.5, 0.1875, ((0, 16),))
    down_weight = noise(key_list[10], (FF, MODEL_WIDTH), FF ** -0.5, 0.109375, ((0, 16),))
    out_grad = noise(key_list[11], (GROUPS, GROUP_TOK, MODEL_WIDTH), 1.0, 6.0, ((0, 16), (1, 2)))
    return {"tokens": tokens, "block_map": block_map, "attention_gain": attention_gain, "query_weight": query_weight, "key_matrix": key_matrix, "value_matrix": value_matrix, "output_weight": output_weight, "feedforward_gain": feedforward_gain, "gate_weight": gate_weight, "up_weight": up_weight, "down_weight": down_weight, "out_grad": out_grad}


@jax.custom_vjp
def lowered_precision(v):
    return lax.optimization_barrier(v.astype(jnp.bfloat16)).astype(jnp.float32)

@jax.custom_vjp
def lowered_backward(v):
    return v

def low_keep(v):
    return (lowered_precision(v), None)

def low_pass(kept, grad):
    return (grad,)

def back_keep(v):
    return (v, None)

def back_low(kept, grad):
    return (lowered_precision(grad),)
lowered_precision.defvjp(low_keep, low_pass)
lowered_backward.defvjp(back_keep, back_low)
norm_eps = 1e-05
rope_base = 10000.0
masked_score = -1e+30

def precise_product(left, right):
    return jnp.dot(left, right, precision=lax.Precision.HIGHEST, preferred_element_type=jnp.float32)

def rms_scale(value_rows_list, gain):
    return value_rows_list * lax.rsqrt(lax.optimization_barrier(jnp.mean(value_rows_list * value_rows_list, axis=-1, keepdims=True)) + norm_eps) * gain

def rope_tables(token_positions, head_size):
    half_size = head_size // 2
    frequency = rope_base ** (-(jnp.arange(half_size, dtype=jnp.float32) * 2.0) / head_size)
    angles = token_positions.astype(jnp.float32)[:, None] * frequency[None, :]
    return (jnp.cos(angles), jnp.sin(angles))

def rotary_apply(value_rows_list, cosine_table, sine_table):
    half_size = value_rows_list.shape[-1] // 2
    leading = value_rows_list[..., :half_size]
    trailing = value_rows_list[..., half_size:]
    cos_rows = cosine_table[:, None, :]
    sin_rows = sine_table[:, None, :]
    return jnp.concatenate([leading * cos_rows - trailing * sin_rows, trailing * cos_rows + leading * sin_rows], axis=-1)

def attend(query_matrix, key_rows_list, value_rows_list, query_pos, key_pos):
    count_of_rows = query_matrix.shape[0]
    kv_heads = key_rows_list.shape[1]
    head_size = key_rows_list.shape[2]
    query_heads = query_matrix.reshape(count_of_rows, kv_heads, query_matrix.shape[1] // kv_heads, head_size)
    scores = jnp.einsum('rhgd,khd->hgrk', query_heads, key_rows_list, precision=lax.Precision.HIGHEST) * head_size ** (-0.5)
    scores = lowered_backward(scores)
    allowed = key_pos[None, :] <= query_pos[:, None]
    scores = jnp.where(allowed, scores, masked_score)
    row_top = lax.optimization_barrier(jnp.max(scores, axis=-1, keepdims=True))
    weights = jnp.exp(scores - row_top)
    probabilities = weights / lax.optimization_barrier(jnp.sum(weights, axis=-1, keepdims=True))
    output = jnp.einsum('hgrk,khd->rhgd', lowered_precision(probabilities), value_rows_list, precision=lax.Precision.HIGHEST)
    return output.reshape(count_of_rows, -1)

def layer(inputs, token_positions, attn_gain, query_full, key_complete, value_complete, out_full, ffn_gain, gate_full, up_full, down_full):
    count_of_rows = inputs.shape[0]
    cosine_table, sine_table = rope_tables(token_positions, HEAD_WIDTH)
    normalized_input = lowered_precision(rms_scale(inputs, attn_gain))
    query_matrix = lowered_precision(rotary_apply(lowered_backward(precise_product(normalized_input, query_full)).reshape(count_of_rows, QUERY_HEADS, HEAD_WIDTH), cosine_table, sine_table))
    key_rows_list = lowered_precision(rotary_apply(lowered_backward(precise_product(normalized_input, key_complete)).reshape(count_of_rows, SHARED_KV_HEADS, HEAD_WIDTH), cosine_table, sine_table))
    value_rows_list = lowered_precision(lowered_backward(precise_product(normalized_input, value_complete))).reshape(count_of_rows, SHARED_KV_HEADS, HEAD_WIDTH)
    prompt_keys = key_rows_list[:PROMPT_LENGTH]
    prompt_values = value_rows_list[:PROMPT_LENGTH]
    prompt_pos = token_positions[:PROMPT_LENGTH]
    query_rows = min(512, PROMPT_LENGTH)

    def prompt_block(block_item):
        query_tile, tile_pos = block_item
        return attend(query_tile, prompt_keys, prompt_values, tile_pos, prompt_pos)
    prompt_out = lax.map(jax.checkpoint(prompt_block), (query_matrix[:PROMPT_LENGTH].reshape(PROMPT_LENGTH // query_rows, query_rows, QUERY_HEADS, HEAD_WIDTH), prompt_pos.reshape(PROMPT_LENGTH // query_rows, query_rows)))

    def continuation_block(block_item):
        query_tile, key_tile, value_tile, tile_pos = block_item
        all_keys = jnp.concatenate([prompt_keys, key_tile], axis=0)
        all_values = jnp.concatenate([prompt_values, value_tile], axis=0)
        return attend(query_tile, all_keys, all_values, tile_pos, jnp.concatenate([prompt_pos, tile_pos], axis=0))
    continuation_output = lax.map(jax.checkpoint(continuation_block), (query_matrix[PROMPT_LENGTH:].reshape(CONTINUATIONS, CONTINUE_LENGTH, QUERY_HEADS, HEAD_WIDTH), key_rows_list[PROMPT_LENGTH:].reshape(CONTINUATIONS, CONTINUE_LENGTH, SHARED_KV_HEADS, HEAD_WIDTH), value_rows_list[PROMPT_LENGTH:].reshape(CONTINUATIONS, CONTINUE_LENGTH, SHARED_KV_HEADS, HEAD_WIDTH), token_positions[PROMPT_LENGTH:].reshape(CONTINUATIONS, CONTINUE_LENGTH)))
    attended = jnp.concatenate([prompt_out.reshape(PROMPT_LENGTH, -1), continuation_output.reshape(PROMPT_LENGTH, -1)], axis=0)
    attended = lowered_precision(lowered_backward(attended))
    mixed = inputs + lowered_backward(precise_product(attended, out_full))
    normed_two = lowered_precision(rms_scale(mixed, ffn_gain))
    gate = lowered_backward(precise_product(normed_two, gate_full))
    up_value = lowered_backward(precise_product(normed_two, up_full))
    hidden = lowered_precision(jax.nn.silu(gate) * up_value)
    return mixed + lowered_backward(precise_product(hidden, down_full))

def reference(tokens, block_map, attention_gain, query_weight, key_matrix, value_matrix, output_weight, feedforward_gain, gate_weight, up_weight, down_weight, out_grad):
    weights = tuple((weight.astype(jnp.float32) for weight in (attention_gain, query_weight, key_matrix, value_matrix, output_weight, feedforward_gain, gate_weight, up_weight, down_weight)))
    natural = jnp.arange(GROUP_TOK, dtype=jnp.int32)
    token_positions = jnp.where(natural < PROMPT_LENGTH, natural, PROMPT_LENGTH + (natural - PROMPT_LENGTH) % CONTINUE_LENGTH).astype(jnp.int32)

    def one_group(totals, group_item):
        slot_inputs, blocks, slot_grads = group_item
        order = jnp.zeros((NBLK,), jnp.int32).at[blocks].set(jnp.arange(NBLK, dtype=jnp.int32))

        def to_natural(value_rows_list):
            return value_rows_list.reshape(NBLK, BLOCK, MODEL_WIDTH)[order].reshape(GROUP_TOK, MODEL_WIDTH)

        def to_slots(value_rows_list):
            return value_rows_list.reshape(NBLK, BLOCK, MODEL_WIDTH)[blocks].reshape(GROUP_TOK, MODEL_WIDTH)
        inputs = to_natural(slot_inputs.astype(jnp.float32))
        result, pullback = jax.vjp(lambda layer_in, *params: layer(layer_in, token_positions, *params), inputs, *weights)
        grads = pullback(to_natural(slot_grads.astype(jnp.float32)))
        totals = tuple((total + grad for total, grad in zip(totals, grads[1:])))
        return (totals, (to_slots(result).astype(jnp.bfloat16), to_slots(grads[0])))
    initial = tuple((jnp.zeros_like(weight) for weight in weights))
    totals, (outputs, input_grads) = lax.scan(one_group, initial, (tokens, block_map, out_grad))
    return (outputs, input_grads, totals[0], totals[1], totals[2], totals[3], totals[4], totals[5], totals[6], totals[7], totals[8])
```

```python
import functools
import jax
import jax.numpy as jnp
from jax import lax
from jax.experimental import pallas as pl
from jax.experimental.pallas import tpu as pltpu
from jax.sharding import PartitionSpec as P

f32 = jnp.float32
bf16 = jnp.bfloat16
HEAD_WIDTH = 64
CONTINUE_LENGTH = 512
norm_eps = 1e-05
LOG2E = 1.4426950408889634
LN2 = 0.6931471805599453
MIB = 2**20


def contract(a, b, dim_a, dim_b):
    return lax.dot_general(
        a, b, (((dim_a,), (dim_b,)), ((), ())), preferred_element_type=f32
    )


def resident(shape):
    zeros = (0,) * len(shape)
    return pl.BlockSpec(shape, lambda *_: zeros, pipeline_mode=pl.Buffered(1))


def project_kernel(x_ref, gain_ref, w_ref, cos_ref, sin_ref, q_ref, k_ref, v_ref, h_ref, nq_ref, nk_ref):
    x = x_ref[...].astype(f32)
    inverse = lax.rsqrt(jnp.mean(x * x, axis=-1, keepdims=True) + norm_eps)
    h = (x * inverse * gain_ref[...]).astype(bf16)
    h_ref[...] = h
    q_rows, kv_rows = q_ref.shape[0], k_ref.shape[0]
    half = HEAD_WIDTH // 2
    scale = LOG2E * HEAD_WIDTH**-0.5
    cos, sin = cos_ref[...], sin_ref[...]

    def rotated(lin, out_ref, cos, sin):
        worst = jnp.zeros((1, lin.shape[1]), f32)
        for head in range(lin.shape[0] // HEAD_WIDTH):
            at = head * HEAD_WIDTH
            a, b = lin[at : at + half], lin[at + half : at + HEAD_WIDTH]
            first = (a * cos - b * sin).astype(bf16)
            second = (b * cos + a * sin).astype(bf16)
            out_ref[at : at + half] = first
            out_ref[at + half : at + HEAD_WIDTH] = second
            fa, fb = first.astype(f32), second.astype(f32)
            worst = jnp.maximum(worst, jnp.sum(fa * fa + fb * fb, axis=0, keepdims=True))
        return worst

    nk_ref[...] = rotated(contract(w_ref[:, q_rows : q_rows + kv_rows], h, 0, 1), k_ref, cos, sin)
    v_ref[...] = contract(w_ref[:, q_rows + kv_rows : q_rows + 2 * kv_rows], h, 0, 1).astype(bf16)
    nq_ref[...] = rotated(contract(w_ref[:, :q_rows], h, 0, 1), q_ref, cos * scale, sin * scale)


def project(x, gain, w, cos, sin, q_rows, kv_rows, tile=512):
    rows, width = x.shape
    cols = lambda n: pl.BlockSpec((n, tile), lambda i: (0, i))
    return pl.pallas_call(
        project_kernel,
        grid=(rows // tile,),
        in_specs=[
            pl.BlockSpec((tile, width), lambda i: (i, 0)),
            resident(gain.shape),
            resident(w.shape),
            cols(cos.shape[0]),
            cols(cos.shape[0]),
        ],
        out_specs=(
            cols(q_rows),
            cols(kv_rows),
            cols(kv_rows),
            pl.BlockSpec((tile, width), lambda i: (i, 0)),
            cols(1),
            cols(1),
        ),
        out_shape=(
            jax.ShapeDtypeStruct((q_rows, rows), bf16),
            jax.ShapeDtypeStruct((kv_rows, rows), bf16),
            jax.ShapeDtypeStruct((kv_rows, rows), bf16),
            jax.ShapeDtypeStruct((rows, width), bf16),
            jax.ShapeDtypeStruct((1, rows), f32),
            jax.ShapeDtypeStruct((1, rows), f32),
        ),
        compiler_params=pltpu.CompilerParams(vmem_limit_bytes=48 * MIB),
        name="project",
    )(x, gain, w, cos, sin)


ONES = 16


def causal(keys, columns):
    return lax.broadcasted_iota(jnp.int32, (keys, columns), 0) <= lax.broadcasted_iota(
        jnp.int32, (keys, columns), 1
    )


def spans(prompt_rows, rows, step):
    found = [(0, prompt_rows, prompt_rows, rows, False)]
    at = 0
    while at < rows:
        end = prompt_rows if at < prompt_rows else at + CONTINUE_LENGTH
        for key in range(at, end, step):
            found.append((key, key + step, key, end, True))
        at = end
    return found


def weigh(keys, query, diagonal):
    scores = contract(keys, query, 1, 0)
    weights = jnp.exp2(scores)
    if diagonal:
        step = keys.shape[0]
        front = jnp.where(causal(step, step), weights[:, :step], 0.0)
        weights = front if weights.shape[1] == step else jnp.concatenate([front, weights[:, step:]], axis=1)
    return weights.astype(bf16)


def own_forward_kernel(q_ref, k_ref, v_ref, acc_ref, *, group, prompt_rows, step):
    rows = q_ref.shape[1]
    keys = k_ref[...].T
    values = jnp.concatenate([v_ref[...], jnp.ones((ONES, rows), bf16)], axis=0)
    wide = HEAD_WIDTH + ONES
    started = set()
    for low, high, first, last, diagonal in spans(prompt_rows, rows, step):
        for head in range(group):
            query = q_ref[head * HEAD_WIDTH : (head + 1) * HEAD_WIDTH, first:last]
            weights = weigh(keys[low:high], query, diagonal)
            part = contract(values[:, low:high], weights, 1, 0)
            at = pl.ds(head * wide, wide)
            fresh = (low == 0 and not diagonal) or (diagonal and low == 0)
            if fresh:
                acc_ref[at, first:last] = part
            else:
                acc_ref[at, first:last] += part


def own_forward(q, k, v, kv_heads, prompt_rows, step=256):
    rows = q.shape[1]
    group = q.shape[0] // HEAD_WIDTH // kv_heads
    wide = group * (HEAD_WIDTH + ONES)
    block = lambda n: pl.BlockSpec((n, rows), lambda h: (h, 0))
    return pl.pallas_call(
        functools.partial(own_forward_kernel, group=group, prompt_rows=prompt_rows, step=step),
        grid=(kv_heads,),
        in_specs=[block(group * HEAD_WIDTH), block(HEAD_WIDTH), block(HEAD_WIDTH)],
        out_specs=block(wide),
        out_shape=jax.ShapeDtypeStruct((kv_heads * wide, rows), f32),
        compiler_params=pltpu.CompilerParams(vmem_limit_bytes=56 * MIB),
        name="own_forward",
    )(q, k, v)


def other_forward_kernel(seen_ref, q_ref, k_ref, v_ref, acc_ref, o_ref, lse_ref, *, group, prompt_rows):
    rows = q_ref.shape[1]
    keys = k_ref[...].T
    values = jnp.concatenate([v_ref[...], jnp.ones((ONES, keys.shape[0]), bf16)], axis=0)
    wide = HEAD_WIDTH + ONES

    def finish(first, last, with_other):
        for head in range(group):
            total = acc_ref[head * wide : (head + 1) * wide, first:last]
            if with_other:
                query = q_ref[head * HEAD_WIDTH : (head + 1) * HEAD_WIDTH, first:last]
                total = total + contract(values, weigh(keys, query, False), 1, 0)
            weight_sum = total[HEAD_WIDTH : HEAD_WIDTH + 1]
            o_ref[head * HEAD_WIDTH : (head + 1) * HEAD_WIDTH, first:last] = (
                total[:HEAD_WIDTH] / weight_sum
            ).astype(bf16)
            lse_ref[0, head : head + 1, first:last] = jnp.log2(weight_sum)

    finish(prompt_rows, rows, True)

    @pl.when(seen_ref[0] > 0)
    def _():
        finish(0, prompt_rows, True)

    @pl.when(seen_ref[0] == 0)
    def _():
        finish(0, prompt_rows, False)


def other_forward(seen, q, k, v, acc, kv_heads, prompt_rows):
    rows = q.shape[1]
    group = q.shape[0] // HEAD_WIDTH // kv_heads
    wide = group * (HEAD_WIDTH + ONES)
    block = lambda n, m: pl.BlockSpec((n, m), lambda h, s: (h, 0))
    return pl.pallas_call(
        functools.partial(other_forward_kernel, group=group, prompt_rows=prompt_rows),
        grid_spec=pltpu.PrefetchScalarGridSpec(
            num_scalar_prefetch=1,
            grid=(kv_heads,),
            in_specs=[
                block(group * HEAD_WIDTH, rows),
                block(HEAD_WIDTH, k.shape[1]),
                block(HEAD_WIDTH, k.shape[1]),
                block(wide, rows),
            ],
            out_specs=(
                block(group * HEAD_WIDTH, rows),
                pl.BlockSpec((1, group, rows), lambda h, s: (h, 0, 0)),
            ),
        ),
        out_shape=(
            jax.ShapeDtypeStruct(q.shape, bf16),
            jax.ShapeDtypeStruct((kv_heads, group, rows), f32),
        ),
        compiler_params=pltpu.CompilerParams(vmem_limit_bytes=56 * MIB),
        name="other_forward",
    )(seen, q, k, v, acc)


def in_parts(row):
    high = row.astype(bf16)
    rest = row - high.astype(f32)
    middle = rest.astype(bf16)
    low = (rest - middle.astype(f32)).astype(bf16)
    return jnp.concatenate([high, middle, low, jnp.zeros((ONES - 3, row.shape[1]), bf16)], axis=0)


def widened(matrix):
    return jnp.concatenate([matrix, jnp.ones((matrix.shape[0], ONES), bf16)], axis=1)


def tile_backward(keys, values, key_rows, query, grad, diagonal):
    weights = jnp.exp2(contract(keys, query, 1, 0))
    slopes = contract(values, grad, 1, 0)
    if diagonal:
        step = keys.shape[0]
        front = jnp.where(causal(step, step), weights[:, :step], 0.0)
        weights = front if weights.shape[1] == step else jnp.concatenate([front, weights[:, step:]], axis=1)
    slopes = (weights * slopes).astype(bf16)
    weights = weights.astype(bf16)
    query_grad = contract(key_rows, slopes, 1, 0)
    key_grad = contract(query[:HEAD_WIDTH], slopes, 1, 1)
    value_grad = contract(grad[:HEAD_WIDTH], weights, 1, 1)
    return query_grad, key_grad, value_grad


def fill_sides(q_ref, g_ref, lse_ref, delta_ref, query_ref, grad_ref, group):
    for head in range(group):
        rows = pl.ds(head * HEAD_WIDTH, HEAD_WIDTH)
        query_ref[head, :HEAD_WIDTH] = q_ref[rows]
        grad_ref[head, :HEAD_WIDTH] = g_ref[rows]
        query_ref[head, HEAD_WIDTH:] = in_parts(-lse_ref[0, head : head + 1])
        grad_ref[head, HEAD_WIDTH:] = in_parts(-delta_ref[0, head : head + 1])


def other_backward_kernel(
    seen_ref, q_ref, g_ref, lse_ref, delta_ref, k_ref, v_ref, dq_ref, dk_ref, dv_ref,
    query_ref, grad_ref, keys_ref, values_ref, *, group, prompt_rows, step
):
    rows = q_ref.shape[1]
    fill_sides(q_ref, g_ref, lse_ref, delta_ref, query_ref, grad_ref, group)
    keys_ref[...] = widened(k_ref[...].T)
    values_ref[...] = widened(v_ref[...].T)
    dq_ref[...] = jnp.zeros_like(dq_ref)

    def part(first, last, fresh):
        for low in range(0, k_ref.shape[1], step):
            span = slice(low, low + step)
            key_sum = value_sum = None
            for head in range(group):
                query_grad, key_grad, value_grad = tile_backward(
                    keys_ref[span], values_ref[span], k_ref[:, span],
                    query_ref[head, :, first:last], grad_ref[head, :, first:last], False,
                )
                at = pl.ds(head * HEAD_WIDTH, HEAD_WIDTH)
                dq_ref[at, first:last] += query_grad
                key_sum = key_grad if key_sum is None else key_sum + key_grad
                value_sum = value_grad if value_sum is None else value_sum + value_grad
            if fresh:
                dk_ref[:, span] = key_sum
                dv_ref[:, span] = value_sum
            else:
                dk_ref[:, span] += key_sum
                dv_ref[:, span] += value_sum

    part(prompt_rows, rows, True)

    @pl.when(seen_ref[0] > 0)
    def _():
        part(0, prompt_rows, False)


def backward_specs(group, rows, key_count):
    block = lambda n, m: pl.BlockSpec((n, m), lambda h, *_: (h, 0))
    row_block = pl.BlockSpec((1, group, rows), lambda h, *_: (h, 0, 0))
    wide = group * HEAD_WIDTH
    ins = [block(wide, rows), block(wide, rows), row_block, row_block,
           block(HEAD_WIDTH, key_count), block(HEAD_WIDTH, key_count)]
    outs = (block(wide, rows), block(HEAD_WIDTH, key_count), block(HEAD_WIDTH, key_count))
    scratch = [
        pltpu.VMEM((group, HEAD_WIDTH + ONES, rows), bf16),
        pltpu.VMEM((group, HEAD_WIDTH + ONES, rows), bf16),
        pltpu.VMEM((key_count, HEAD_WIDTH + ONES), bf16),
        pltpu.VMEM((key_count, HEAD_WIDTH + ONES), bf16),
    ]
    return ins, outs, scratch


def other_backward(seen, q, g, lse, delta, k, v, kv_heads, prompt_rows, step=256):
    rows = q.shape[1]
    group = q.shape[0] // HEAD_WIDTH // kv_heads
    ins, outs, scratch = backward_specs(group, rows, k.shape[1])
    return pl.pallas_call(
        functools.partial(other_backward_kernel, group=group, prompt_rows=prompt_rows, step=step),
        grid_spec=pltpu.PrefetchScalarGridSpec(
            num_scalar_prefetch=1, grid=(kv_heads,), in_specs=ins, out_specs=outs, scratch_shapes=scratch
        ),
        out_shape=(
            jax.ShapeDtypeStruct(q.shape, f32),
            jax.ShapeDtypeStruct(k.shape, f32),
            jax.ShapeDtypeStruct(v.shape, f32),
        ),
        compiler_params=pltpu.CompilerParams(vmem_limit_bytes=56 * MIB),
        name="other_backward",
    )(seen, q, g, lse, delta, k, v)


def own_backward_kernel(
    q_ref, g_ref, lse_ref, delta_ref, k_ref, v_ref, dq_in_ref, dq_ref, dk_ref, dv_ref,
    query_ref, grad_ref, keys_ref, values_ref, *, group, prompt_rows, step
):
    rows = q_ref.shape[1]
    fill_sides(q_ref, g_ref, lse_ref, delta_ref, query_ref, grad_ref, group)
    keys_ref[...] = widened(k_ref[...].T)
    values_ref[...] = widened(v_ref[...].T)
    dq_ref[...] = dq_in_ref[...]
    dk_ref[...] = jnp.zeros_like(dk_ref)
    dv_ref[...] = jnp.zeros_like(dv_ref)

    def one(low, high, first, last, diagonal):
        span = slice(low, high)
        key_sum = value_sum = None
        for head in range(group):
            query_grad, key_grad, value_grad = tile_backward(
                keys_ref[span], values_ref[span], k_ref[:, span],
                query_ref[head, :, first:last], grad_ref[head, :, first:last], diagonal,
            )
            at = pl.ds(head * HEAD_WIDTH, HEAD_WIDTH)
            dq_ref[at, first:last] += query_grad
            key_sum = key_grad if key_sum is None else key_sum + key_grad
            value_sum = value_grad if value_sum is None else value_sum + value_grad
        dk_ref[:, span] += key_sum
        dv_ref[:, span] += value_sum

    for low, high, first, last, diagonal in spans(prompt_rows, rows, step):
        if diagonal:
            one(low, high, first, last, True)
        else:
            for at in range(low, high, step):
                one(at, at + step, first, last, False)


def own_backward(q, g, lse, delta, k, v, dq, kv_heads, prompt_rows, step=256):
    rows = q.shape[1]
    group = q.shape[0] // HEAD_WIDTH // kv_heads
    ins, outs, scratch = backward_specs(group, rows, k.shape[1])
    return pl.pallas_call(
        functools.partial(own_backward_kernel, group=group, prompt_rows=prompt_rows, step=step),
        grid=(kv_heads,),
        in_specs=ins + [outs[0]],
        out_specs=outs,
        scratch_shapes=scratch,
        out_shape=(
            jax.ShapeDtypeStruct(q.shape, f32),
            jax.ShapeDtypeStruct(k.shape, f32),
            jax.ShapeDtypeStruct(v.shape, f32),
        ),
        compiler_params=pltpu.CompilerParams(vmem_limit_bytes=60 * MIB),
        name="own_backward",
    )(q, g, lse, delta, k, v, dq)


def middle_kernel(
    x_ref, dy_ref, o_ref, gain_ref, wo_any, wg_any, wu_any, wd_any,
    out_ref, h2_ref, hidden_ref, dgate_ref, dup_ref, dattn_ref, dob_ref, delta_ref, dgain_ref,
    wo_ref, wg_ref, wu_ref, wd_ref, sems, *, chunk
):
    step = pl.program_id(0)
    copies = [
        pltpu.make_async_copy(source, target, sems.at[i])
        for i, (source, target) in enumerate(
            ((wo_any, wo_ref), (wg_any, wg_ref), (wu_any, wu_ref), (wd_any, wd_ref))
        )
    ]

    @pl.when(step == 0)
    def _():
        for copy in copies:
            copy.start()
        dgain_ref[...] = jnp.zeros_like(dgain_ref)
        copies[0].wait()

    ob = o_ref[...]
    x1 = x_ref[...].astype(f32) + contract(ob, wo_ref[...], 0, 0)
    inverse = lax.rsqrt(jnp.mean(x1 * x1, axis=-1, keepdims=True) + norm_eps)
    gain = gain_ref[...]
    h2 = (x1 * inverse * gain).astype(bf16)
    h2_ref[...] = h2
    dy = dy_ref[...]

    @pl.when(step == 0)
    def _():
        for copy in copies[1:]:
            copy.wait()

    result = x1
    dh2 = None
    for low in range(0, wg_ref.shape[1], chunk):
        span = slice(low, low + chunk)
        gate = contract(h2, wg_ref[:, span], 1, 0)
        up = contract(h2, wu_ref[:, span], 1, 0)
        dhidden = contract(dy, wd_ref[span], 1, 1)
        sigma = 1.0 / (1.0 + jnp.exp(-gate))
        silu = gate * sigma
        hidden = (silu * up).astype(bf16)
        hidden_ref[:, span] = hidden
        result = result + contract(hidden, wd_ref[span], 1, 0)
        dgate = (dhidden * up * sigma * (1.0 + gate * (1.0 - sigma))).astype(bf16)
        dup = (dhidden * silu).astype(bf16)
        dgate_ref[:, span] = dgate
        dup_ref[:, span] = dup
        part = contract(dgate, wg_ref[:, span], 1, 1) + contract(dup, wu_ref[:, span], 1, 1)
        dh2 = part if dh2 is None else dh2 + part
    out_ref[...] = result.astype(bf16)
    dgain_ref[...] += jnp.sum(dh2 * x1 * inverse, axis=0, keepdims=True)
    u = dh2 * gain
    dx1 = dy.astype(f32) + inverse * u - x1 * (inverse * inverse * inverse) * jnp.mean(
        u * x1, axis=-1, keepdims=True
    )
    dattn = dx1.astype(bf16)
    dattn_ref[...] = dattn
    dob = contract(wo_ref[...], dattn, 1, 1).astype(bf16)
    dob_ref[...] = dob
    product = dob.astype(f32) * ob.astype(f32)
    heads, group = delta_ref.shape[0], delta_ref.shape[1]
    for kv in range(heads):
        for member in range(group):
            at = (kv * group + member) * HEAD_WIDTH
            delta_ref[kv, member : member + 1] = jnp.sum(
                product[at : at + HEAD_WIDTH], axis=0, keepdims=True
            )


def middle(x, dy, o, gain, wo, wg, wu, wd, kv_heads, tile=256, chunk=1024):
    rows, width = x.shape
    hidden = wg.shape[1]
    q_rows = o.shape[0]
    group = q_rows // HEAD_WIDTH // kv_heads
    by_row = lambda n: pl.BlockSpec((tile, n), lambda i: (i, 0))
    any_spec = pl.BlockSpec(memory_space=pl.ANY)
    shape = jax.ShapeDtypeStruct
    return pl.pallas_call(
        functools.partial(middle_kernel, chunk=chunk),
        grid=(rows // tile,),
        in_specs=[by_row(width), by_row(width), pl.BlockSpec((q_rows, tile), lambda i: (0, i)),
                  resident(gain.shape)] + [any_spec] * 4,
        out_specs=(
            by_row(width), by_row(width), by_row(hidden), by_row(hidden), by_row(hidden), by_row(width),
            pl.BlockSpec((q_rows, tile), lambda i: (0, i)),
            pl.BlockSpec((kv_heads, group, tile), lambda i: (0, 0, i)),
            pl.BlockSpec((1, width), lambda i: (0, 0)),
        ),
        out_shape=(
            shape((rows, width), bf16), shape((rows, width), bf16), shape((rows, hidden), bf16),
            shape((rows, hidden), bf16), shape((rows, hidden), bf16), shape((rows, width), bf16),
            shape((q_rows, rows), bf16), shape((kv_heads, group, rows), f32), shape((1, width), f32),
        ),
        scratch_shapes=[pltpu.VMEM(w.shape, bf16) for w in (wo, wg, wu, wd)] + [pltpu.SemaphoreType.DMA((4,))],
        compiler_params=pltpu.CompilerParams(vmem_limit_bytes=62 * MIB),
        name="middle",
    )(x, dy, o, gain, wo, wg, wu, wd)


def ffn_grads_kernel(h2_ref, dy_ref, hidden_ref, dgate_ref, dup_ref, down_ref, gate_ref, up_ref):
    down_ref[...] = contract(hidden_ref[...], dy_ref[...], 0, 0).astype(bf16)
    gate_ref[...] = contract(h2_ref[...], dgate_ref[...], 0, 0).astype(bf16)
    up_ref[...] = contract(h2_ref[...], dup_ref[...], 0, 0).astype(bf16)


def ffn_grads(h2, dy, hidden, dgate, dup, tile=512):
    rows, width = h2.shape
    total = hidden.shape[1]
    cols = lambda n: pl.BlockSpec((n, tile), lambda i: (0, i))
    shape = jax.ShapeDtypeStruct
    return pl.pallas_call(
        ffn_grads_kernel,
        grid=(total // tile,),
        in_specs=[resident(h2.shape), resident(dy.shape), cols(rows), cols(rows), cols(rows)],
        out_specs=(pl.BlockSpec((tile, width), lambda i: (i, 0)), cols(width), cols(width)),
        out_shape=(shape((total, width), bf16), shape((width, total), bf16), shape((width, total), bf16)),
        compiler_params=pltpu.CompilerParams(vmem_limit_bytes=56 * MIB),
        name="ffn_grads",
    )(h2, dy, hidden, dgate, dup)


def finish_kernel(
    x_ref, h_ref, dattn_ref, gain_ref, w_ref, dq_ref, dk_ref, dv_ref, cos_ref, sin_ref,
    out_ref, dw_ref, dgain_ref, acc_ref
):
    step = pl.program_id(0)

    @pl.when(step == 0)
    def _():
        dgain_ref[...] = jnp.zeros_like(dgain_ref)
        acc_ref[...] = jnp.zeros_like(acc_ref)

    half = HEAD_WIDTH // 2
    cos, sin = cos_ref[...], sin_ref[...]

    def turned(ref, scale):
        c, s = cos * scale, sin * scale
        pieces = []
        for at in range(0, ref.shape[0], HEAD_WIDTH):
            a, b = ref[at : at + half], ref[at + half : at + HEAD_WIDTH]
            pieces += [a * c + b * s, b * c - a * s]
        return jnp.concatenate(pieces, axis=0)

    lin = jnp.concatenate(
        [turned(dq_ref, HEAD_WIDTH**-0.5), turned(dk_ref, LN2), dv_ref[...]], axis=0
    ).astype(bf16).T
    acc_ref[...] += contract(h_ref[...], lin, 0, 0)
    dh = contract(lin, w_ref[...], 1, 1)
    x = x_ref[...].astype(f32)
    inverse = lax.rsqrt(jnp.mean(x * x, axis=-1, keepdims=True) + norm_eps)
    dgain_ref[...] += jnp.sum(dh * x * inverse, axis=0, keepdims=True)
    u = dh * gain_ref[...]
    out_ref[...] = (
        dattn_ref[...].astype(f32)
        + inverse * u
        - x * (inverse * inverse * inverse) * jnp.mean(u * x, axis=-1, keepdims=True)
    )

    @pl.when(step == pl.num_programs(0) - 1)
    def _():
        dw_ref[...] = acc_ref[...].astype(bf16)


def finish(x, h, dattn, gain, w, dq, dk, dv, cos, sin, tile=256):
    rows, width = x.shape
    by_row = pl.BlockSpec((tile, width), lambda i: (i, 0))
    cols = lambda n: pl.BlockSpec((n, tile), lambda i: (0, i))
    shape = jax.ShapeDtypeStruct
    return pl.pallas_call(
        finish_kernel,
        grid=(rows // tile,),
        in_specs=[by_row, by_row, by_row, resident(gain.shape), resident(w.shape),
                  cols(dq.shape[0]), cols(dk.shape[0]), cols(dv.shape[0]),
                  cols(cos.shape[0]), cols(cos.shape[0])],
        out_specs=(by_row, pl.BlockSpec(w.shape, lambda i: (0, 0)), pl.BlockSpec((1, width), lambda i: (0, 0))),
        out_shape=(shape((rows, width), f32), shape(w.shape, bf16), shape((1, width), f32)),
        scratch_shapes=[pltpu.VMEM(w.shape, f32)],
        compiler_params=pltpu.CompilerParams(vmem_limit_bytes=56 * MIB),
        name="finish",
    )(x, h, dattn, gain, w, dq, dk, dv, cos, sin)


rope_base = 10000.0
masked_score = -1e30


def as_sent(array):

    def short(part):
        return part.astype(jnp.bfloat16) if part.dtype == jnp.float32 else part

    return jax.tree.map(short, array)


def rms_scale(value_rows_list, gain):
    return (
        value_rows_list
        * lax.rsqrt(jnp.mean(value_rows_list * value_rows_list, axis=-1, keepdims=True) + norm_eps)
        * gain
    )


def rms_back(value_rows_list, gain, upstream):
    inverse = lax.rsqrt(
        jnp.mean(value_rows_list * value_rows_list, axis=-1, keepdims=True) + norm_eps
    )
    scaled = upstream * gain
    gain_grad = jnp.sum(upstream * value_rows_list * inverse, axis=0)
    values_grad = inverse * scaled - value_rows_list * (inverse * inverse * inverse) * jnp.mean(
        scaled * value_rows_list, axis=-1, keepdims=True
    )
    return (gain_grad, values_grad)


def rope_tables(token_positions, head_size):
    half_size = head_size // 2
    frequency = rope_base ** (-(jnp.arange(half_size, dtype=jnp.float32) * 2.0) / head_size)
    angles = token_positions.astype(jnp.float32)[:, None] * frequency[None, :]
    return (jnp.cos(angles), jnp.sin(angles))


def rotary_apply(value_rows_list, cosine_table, sine_table):
    half_size = value_rows_list.shape[-1] // 2
    leading = value_rows_list[..., :half_size]
    trailing = value_rows_list[..., half_size:]
    cos_rows = cosine_table[:, None, :]
    sin_rows = sine_table[:, None, :]
    return jnp.concatenate(
        [leading * cos_rows - trailing * sin_rows, trailing * cos_rows + leading * sin_rows],
        axis=-1,
    )


def visible(query_pos, query_seg, key_pos, key_seg):
    same_doc = (key_seg[None, :] == query_seg[:, None]) | (key_seg[None, :] == 0)
    return same_doc & (key_pos[None, :] <= query_pos[:, None])


def tile_scores(query_tile, key_tile, scale):
    return (
        jnp.einsum("rhgd,khd->hgrk", query_tile, key_tile, preferred_element_type=jnp.float32)
        * scale
    )


def key_tiling(key_heads, value_heads, key_pos, key_seg):
    key_block = min(256, key_heads.shape[0])
    tile_count = key_heads.shape[0] // key_block
    return (
        key_heads.reshape(tile_count, key_block, key_heads.shape[1], key_heads.shape[2]),
        value_heads.reshape(tile_count, key_block, value_heads.shape[1], value_heads.shape[2]),
        key_pos.reshape(tile_count, key_block),
        key_seg.reshape(tile_count, key_block),
    )


def query_split(value_rows_list, query_block):
    return value_rows_list.reshape(
        (value_rows_list.shape[0] // query_block, query_block) + value_rows_list.shape[1:]
    )


def attention_forward(query_heads, key_heads, value_heads, places):
    query_pos, query_seg, key_pos, key_seg = places
    count_of_rows, kv_heads, group_size, head_size = query_heads.shape
    scale = head_size ** (-0.5)
    query_block = min(512, count_of_rows)
    key_tiles, value_tiles, kpos_tiles, kseg_tiles = key_tiling(
        key_heads, value_heads, key_pos, key_seg
    )

    def one_block(block_item):
        query_tile, tile_pos, tile_seg = block_item
        state_shape = (kv_heads, group_size, query_tile.shape[0])

        def lse_step(running, tile_item):
            key_tile, tile_kpos, tile_kseg = tile_item
            allowed = visible(tile_pos, tile_seg, tile_kpos, tile_kseg)

            def lse_open_tile(state):
                row_top, row_total = state
                scores = jnp.where(allowed, tile_scores(query_tile, key_tile, scale), masked_score)
                new_top = jnp.maximum(row_top, jnp.max(scores, axis=-1))
                weights = jnp.where(allowed, jnp.exp(scores - new_top[..., None]), 0.0)
                return (new_top, row_total * jnp.exp(row_top - new_top) + jnp.sum(weights, axis=-1))

            def lse_closed_tile(state):
                return state

            return (lax.cond(jnp.any(allowed), lse_open_tile, lse_closed_tile, running), None)

        initial = (
            jnp.full(state_shape, masked_score, jnp.float32),
            jnp.zeros(state_shape, jnp.float32),
        )
        (row_top, row_total), _ = lax.scan(lse_step, initial, (key_tiles, kpos_tiles, kseg_tiles))
        log_total = row_top + jnp.log(row_total)

        def out_step(running, tile_item):
            key_tile, value_tile, tile_kpos, tile_kseg = tile_item
            allowed = visible(tile_pos, tile_seg, tile_kpos, tile_kseg)

            def out_open_tile(accumulated):
                scores = jnp.where(allowed, tile_scores(query_tile, key_tile, scale), masked_score)
                probabilities = jnp.where(
                    allowed, jnp.exp(scores - log_total[..., None]), 0.0
                ).astype(jnp.bfloat16)
                return accumulated + jnp.einsum(
                    "hgrk,khd->rhgd", probabilities, value_tile, preferred_element_type=jnp.float32
                )

            def out_closed_tile(accumulated):
                return accumulated

            return (lax.cond(jnp.any(allowed), out_open_tile, out_closed_tile, running), None)

        output, _ = lax.scan(
            out_step,
            jnp.zeros(query_tile.shape, jnp.float32),
            (key_tiles, value_tiles, kpos_tiles, kseg_tiles),
        )
        return (output, log_total)

    outputs, log_totals = lax.map(
        one_block,
        (
            query_split(query_heads, query_block),
            query_split(query_pos, query_block),
            query_split(query_seg, query_block),
        ),
    )
    return (outputs.reshape(query_heads.shape), log_totals)


def attention_backward(
    query_heads, key_heads, value_heads, places, attended_grad, attended, log_totals
):
    query_pos, query_seg, key_pos, key_seg = places
    count_of_rows, kv_heads, group_size, head_size = query_heads.shape
    scale = head_size ** (-0.5)
    query_block = min(512, count_of_rows)
    key_tiles, value_tiles, kpos_tiles, kseg_tiles = key_tiling(
        key_heads, value_heads, key_pos, key_seg
    )

    def block_grads(sums, block_item):
        query_tile, grad_tile, output_tile, tile_lse, tile_pos, tile_seg = block_item
        tile_delta = jnp.einsum("rhgd,rhgd->hgr", grad_tile.astype(jnp.float32), output_tile)

        def back_step(query_grad, tile_item):
            key_tile, value_tile, tile_kpos, tile_kseg = tile_item
            allowed = visible(tile_pos, tile_seg, tile_kpos, tile_kseg)

            def back_open_tile(query_grad):
                scores = jnp.where(allowed, tile_scores(query_tile, key_tile, scale), masked_score)
                probabilities = jnp.where(allowed, jnp.exp(scores - tile_lse[..., None]), 0.0)
                prob_grad = jnp.einsum(
                    "rhgd,khd->hgrk", grad_tile, value_tile, preferred_element_type=jnp.float32
                )
                score_grad = (probabilities * (prob_grad - tile_delta[..., None])).astype(
                    jnp.bfloat16
                )
                query_grad = query_grad + scale * jnp.einsum(
                    "hgrk,khd->rhgd", score_grad, key_tile, preferred_element_type=jnp.float32
                )
                key_part = scale * jnp.einsum(
                    "hgrk,rhgd->khd", score_grad, query_tile, preferred_element_type=jnp.float32
                )
                value_part = jnp.einsum(
                    "hgrk,rhgd->khd",
                    probabilities.astype(jnp.bfloat16),
                    grad_tile,
                    preferred_element_type=jnp.float32,
                )
                return (query_grad, key_part, value_part)

            def back_closed_tile(query_grad):
                return (
                    query_grad,
                    jnp.zeros(key_tile.shape, jnp.float32),
                    jnp.zeros(value_tile.shape, jnp.float32),
                )

            query_grad, key_part, value_part = lax.cond(
                jnp.any(allowed), back_open_tile, back_closed_tile, query_grad
            )
            return (query_grad, (key_part, value_part))

        query_grad, (key_parts, value_parts) = lax.scan(
            back_step,
            jnp.zeros(query_tile.shape, jnp.float32),
            (key_tiles, value_tiles, kpos_tiles, kseg_tiles),
        )
        return ((sums[0] + key_parts, sums[1] + value_parts), query_grad)

    initial = (jnp.zeros(key_tiles.shape, jnp.float32), jnp.zeros(value_tiles.shape, jnp.float32))
    block_items = (
        query_split(query_heads, query_block),
        query_split(attended_grad, query_block),
        query_split(attended, query_block),
        log_totals,
        query_split(query_pos, query_block),
        query_split(query_seg, query_block),
    )
    (key_sum, value_sum), query_grads = lax.scan(block_grads, initial, block_items)
    key_rows = key_heads.shape[0]
    return (
        query_grads.reshape(query_heads.shape),
        key_sum.reshape(key_rows, -1),
        value_sum.reshape(key_rows, -1),
    )


def forward_pass(weights, inputs, places, tables, gather_pair):
    (
        attn_gain,
        query_full,
        key_complete,
        value_complete,
        out_full,
        ffn_gain,
        gate_full,
        up_full,
        down_full,
    ) = weights
    cosine_table, sine_table = tables
    count_of_rows = inputs.shape[0]
    normalized_input = rms_scale(inputs, attn_gain.astype(jnp.float32)).astype(jnp.bfloat16)
    query_lin = jnp.dot(normalized_input, query_full, preferred_element_type=jnp.float32)
    key_lin = jnp.dot(normalized_input, key_complete, preferred_element_type=jnp.float32)
    value_lin = jnp.dot(normalized_input, value_complete, preferred_element_type=jnp.float32)
    kv_heads = key_lin.shape[1] // HEAD_WIDTH
    query_rot = rotary_apply(
        query_lin.reshape(count_of_rows, -1, HEAD_WIDTH), cosine_table, sine_table
    ).astype(jnp.bfloat16)
    key_rot = (
        rotary_apply(key_lin.reshape(count_of_rows, kv_heads, HEAD_WIDTH), cosine_table, sine_table)
        .astype(jnp.bfloat16)
        .reshape(count_of_rows, -1)
    )
    value_low = value_lin.astype(jnp.bfloat16)
    keys_all, values_all = gather_pair((key_rot, value_low))
    group_size = query_rot.shape[1] // kv_heads
    query_heads = query_rot.reshape(count_of_rows, kv_heads, group_size, HEAD_WIDTH)
    key_heads = keys_all.reshape(-1, kv_heads, HEAD_WIDTH)
    value_heads = values_all.reshape(-1, kv_heads, HEAD_WIDTH)
    attended, log_totals = attention_forward(query_heads, key_heads, value_heads, places)
    attended_low = attended.reshape(count_of_rows, -1).astype(jnp.bfloat16)
    mixed = inputs + jnp.dot(attended_low, out_full, preferred_element_type=jnp.float32)
    normed_two = rms_scale(mixed, ffn_gain.astype(jnp.float32)).astype(jnp.bfloat16)
    gate = jnp.dot(normed_two, gate_full, preferred_element_type=jnp.float32)
    up_value = jnp.dot(normed_two, up_full, preferred_element_type=jnp.float32)
    hidden = (jax.nn.silu(gate) * up_value).astype(jnp.bfloat16)
    result = mixed + jnp.dot(hidden, down_full, preferred_element_type=jnp.float32)
    return (
        normalized_input,
        query_heads,
        key_heads,
        value_heads,
        attended,
        attended_low,
        log_totals,
        mixed,
        normed_two,
        gate,
        up_value,
        hidden,
        result,
    )


def general_local(
    tokens,
    block_map,
    attention_gain,
    query_weight,
    key_matrix,
    value_matrix,
    output_weight,
    feedforward_gain,
    gate_weight,
    up_weight,
    down_weight,
    out_grad,
):
    shards = (
        attention_gain,
        query_weight,
        key_matrix,
        value_matrix,
        output_weight,
        feedforward_gain,
        gate_weight,
        up_weight,
        down_weight,
    )
    count_of_rows = tokens.shape[1]
    ctx_rank = lax.axis_index("ctx")
    blocks = block_map[0]
    block_rows = count_of_rows // 2
    group_rows = blocks.shape[0] * block_rows
    prompt_rows = group_rows // 2
    natural = (
        blocks[:, None] * block_rows + jnp.arange(block_rows, dtype=jnp.int32)[None, :]
    ).reshape(-1)
    in_prompt = natural < prompt_rows
    key_pos = jnp.where(in_prompt, natural, prompt_rows + (natural - prompt_rows) % CONTINUE_LENGTH)
    key_seg = jnp.where(in_prompt, 0, 1 + (natural - prompt_rows) // CONTINUE_LENGTH)
    query_pos = lax.dynamic_slice_in_dim(key_pos, ctx_rank * count_of_rows, count_of_rows)
    query_seg = lax.dynamic_slice_in_dim(key_seg, ctx_rank * count_of_rows, count_of_rows)
    places = (query_pos, query_seg, key_pos, key_seg)
    cosine_table, sine_table = rope_tables(query_pos, HEAD_WIDTH)
    tables = (cosine_table, sine_table)
    inputs = tokens[0].astype(jnp.float32)
    full_weights = (
        lax.all_gather(shards[0], ("group", "wshard"), axis=0, tiled=True),
        lax.all_gather(shards[1], ("group", "wshard"), axis=0, tiled=True),
        lax.all_gather(shards[2], ("group", "wshard"), axis=0, tiled=True),
        lax.all_gather(shards[3], ("group", "wshard"), axis=0, tiled=True),
        lax.all_gather(shards[4], ("group", "wshard"), axis=0, tiled=True),
        lax.all_gather(shards[5], ("group", "wshard"), axis=0, tiled=True),
        lax.all_gather(shards[6], ("group", "wshard"), axis=0, tiled=True),
        lax.all_gather(shards[7], ("group", "wshard"), axis=0, tiled=True),
        lax.all_gather(shards[8], ("group", "wshard"), axis=0, tiled=True),
    )
    forward = forward_pass(
        full_weights,
        inputs,
        places,
        tables,
        lambda packed: jax.tree.map(
            lambda part, own: part.astype(own.dtype),
            lax.all_gather(as_sent(packed), "ctx", axis=0, tiled=True),
            packed,
        ),
    )
    layer_out = forward[12].astype(jnp.bfloat16)
    back_weights = (
        lax.all_gather(shards[0], ("group", "wshard"), axis=0, tiled=True),
        lax.all_gather(shards[1], ("group", "wshard"), axis=0, tiled=True),
        lax.all_gather(shards[2], ("group", "wshard"), axis=0, tiled=True),
        lax.all_gather(shards[3], ("group", "wshard"), axis=0, tiled=True),
        lax.all_gather(shards[4], ("group", "wshard"), axis=0, tiled=True),
        lax.all_gather(shards[5], ("group", "wshard"), axis=0, tiled=True),
        lax.all_gather(shards[6], ("group", "wshard"), axis=0, tiled=True),
        lax.all_gather(shards[7], ("group", "wshard"), axis=0, tiled=True),
        lax.all_gather(shards[8], ("group", "wshard"), axis=0, tiled=True),
    )
    saved = forward_pass(
        back_weights,
        inputs,
        places,
        tables,
        lambda packed: jax.tree.map(
            lambda part, own: part.astype(own.dtype),
            lax.all_gather(as_sent(packed), "ctx", axis=0, tiled=True),
            packed,
        ),
    )
    (
        normalized_input,
        query_heads,
        key_heads,
        value_heads,
        attended,
        attended_low,
        log_totals,
        mixed,
        normed_two,
        gate,
        up_value,
        hidden,
        result,
    ) = saved
    (
        attn_gain,
        query_full,
        key_complete,
        value_complete,
        out_full,
        ffn_gain,
        gate_full,
        up_full,
        down_full,
    ) = back_weights
    upstream = out_grad[0].astype(jnp.float32)
    ffn_grad = upstream.astype(jnp.bfloat16)
    grad_down = jnp.einsum("rf,rd->fd", hidden, ffn_grad, preferred_element_type=jnp.float32)
    hidden_grad = jnp.einsum("rd,fd->rf", ffn_grad, down_full, preferred_element_type=jnp.float32)
    gate_sigmoid = jax.nn.sigmoid(gate)
    gate_grad = (
        hidden_grad * up_value * gate_sigmoid * (1.0 + gate * (1.0 - gate_sigmoid))
    ).astype(jnp.bfloat16)
    up_grad = (hidden_grad * (gate * gate_sigmoid)).astype(jnp.bfloat16)
    grad_gate = jnp.einsum("rd,rf->df", normed_two, gate_grad, preferred_element_type=jnp.float32)
    grad_up = jnp.einsum("rd,rf->df", normed_two, up_grad, preferred_element_type=jnp.float32)
    normed_two_grad = jnp.einsum(
        "rf,df->rd", gate_grad, gate_full, preferred_element_type=jnp.float32
    ) + jnp.einsum("rf,df->rd", up_grad, up_full, preferred_element_type=jnp.float32)
    grad_ffn_gain, mixed_back = rms_back(mixed, ffn_gain.astype(jnp.float32), normed_two_grad)
    mixed_grad = upstream + mixed_back
    attn_grad = mixed_grad.astype(jnp.bfloat16)
    grad_out = jnp.einsum("rf,rd->fd", attended_low, attn_grad, preferred_element_type=jnp.float32)
    attended_grad = (
        jnp.einsum("rd,fd->rf", attn_grad, out_full, preferred_element_type=jnp.float32)
        .astype(jnp.bfloat16)
        .reshape(attended.shape)
    )
    query_grad, key_grad, value_grad = attention_backward(
        query_heads, key_heads, value_heads, places, attended_grad, attended, log_totals
    )
    key_local, value_local = (
        lax.psum_scatter(
            key_grad.astype(jnp.bfloat16), "ctx", scatter_dimension=0, tiled=True
        ).astype(jnp.float32),
        lax.psum_scatter(
            value_grad.astype(jnp.bfloat16), "ctx", scatter_dimension=0, tiled=True
        ).astype(jnp.float32),
    )
    query_lin_grad = (
        rotary_apply(query_grad.reshape(count_of_rows, -1, HEAD_WIDTH), cosine_table, -sine_table)
        .reshape(count_of_rows, -1)
        .astype(jnp.bfloat16)
    )
    key_lin_grad = (
        rotary_apply(key_local.reshape(count_of_rows, -1, HEAD_WIDTH), cosine_table, -sine_table)
        .reshape(count_of_rows, -1)
        .astype(jnp.bfloat16)
    )
    value_lin_grad = value_local.astype(jnp.bfloat16)
    grad_query = jnp.einsum(
        "rd,rf->df", normalized_input, query_lin_grad, preferred_element_type=jnp.float32
    )
    grad_key = jnp.einsum(
        "rd,rf->df", normalized_input, key_lin_grad, preferred_element_type=jnp.float32
    )
    grad_value = jnp.einsum(
        "rd,rf->df", normalized_input, value_lin_grad, preferred_element_type=jnp.float32
    )
    normed_grad = jnp.einsum(
        "rf,df->rd", query_lin_grad, query_full, preferred_element_type=jnp.float32
    )
    normed_grad = normed_grad + jnp.einsum(
        "rf,df->rd", key_lin_grad, key_complete, preferred_element_type=jnp.float32
    )
    normed_grad = normed_grad + jnp.einsum(
        "rf,df->rd", value_lin_grad, value_complete, preferred_element_type=jnp.float32
    )
    grad_attn_gain, input_back = rms_back(inputs, attn_gain.astype(jnp.float32), normed_grad)
    input_grad = mixed_grad + input_back
    partial_grads = (
        grad_attn_gain,
        grad_query,
        grad_key,
        grad_value,
        grad_out,
        grad_ffn_gain,
        grad_gate,
        grad_up,
        grad_down,
    )
    reduced = (
        lax.psum_scatter(
            partial_grads[0].astype(jnp.bfloat16),
            ("group", "wshard"),
            scatter_dimension=0,
            tiled=True,
        ).astype(jnp.float32),
        lax.psum_scatter(
            partial_grads[1].astype(jnp.bfloat16),
            ("group", "wshard"),
            scatter_dimension=0,
            tiled=True,
        ).astype(jnp.float32),
        lax.psum_scatter(
            partial_grads[2].astype(jnp.bfloat16),
            ("group", "wshard"),
            scatter_dimension=0,
            tiled=True,
        ).astype(jnp.float32),
        lax.psum_scatter(
            partial_grads[3].astype(jnp.bfloat16),
            ("group", "wshard"),
            scatter_dimension=0,
            tiled=True,
        ).astype(jnp.float32),
        lax.psum_scatter(
            partial_grads[4].astype(jnp.bfloat16),
            ("group", "wshard"),
            scatter_dimension=0,
            tiled=True,
        ).astype(jnp.float32),
        lax.psum_scatter(
            partial_grads[5].astype(jnp.bfloat16),
            ("group", "wshard"),
            scatter_dimension=0,
            tiled=True,
        ).astype(jnp.float32),
        lax.psum_scatter(
            partial_grads[6].astype(jnp.bfloat16),
            ("group", "wshard"),
            scatter_dimension=0,
            tiled=True,
        ).astype(jnp.float32),
        lax.psum_scatter(
            partial_grads[7].astype(jnp.bfloat16),
            ("group", "wshard"),
            scatter_dimension=0,
            tiled=True,
        ).astype(jnp.float32),
        lax.psum_scatter(
            partial_grads[8].astype(jnp.bfloat16),
            ("group", "wshard"),
            scatter_dimension=0,
            tiled=True,
        ).astype(jnp.float32),
    )
    summed = (
        lax.psum(reduced[0].astype(jnp.bfloat16), "ctx").astype(jnp.float32),
        lax.psum(reduced[1].astype(jnp.bfloat16), "ctx").astype(jnp.float32),
        lax.psum(reduced[2].astype(jnp.bfloat16), "ctx").astype(jnp.float32),
        lax.psum(reduced[3].astype(jnp.bfloat16), "ctx").astype(jnp.float32),
        lax.psum(reduced[4].astype(jnp.bfloat16), "ctx").astype(jnp.float32),
        lax.psum(reduced[5].astype(jnp.bfloat16), "ctx").astype(jnp.float32),
        lax.psum(reduced[6].astype(jnp.bfloat16), "ctx").astype(jnp.float32),
        lax.psum(reduced[7].astype(jnp.bfloat16), "ctx").astype(jnp.float32),
        lax.psum(reduced[8].astype(jnp.bfloat16), "ctx").astype(jnp.float32),
    )
    gain_attn, gain_ffn = (summed[0], summed[5])
    matrices = (summed[1], summed[2], summed[3], summed[4], summed[6], summed[7], summed[8])
    return (
        layer_out[None],
        input_grad[None],
        gain_attn,
        matrices[0],
        matrices[1],
        matrices[2],
        matrices[3],
        gain_ffn,
        matrices[4],
        matrices[5],
        matrices[6],
    )


SAFE_BOUND = 90.0
OWNERS = ("group", "wshard")
SWAP = [(0, 1), (1, 0)]


def exact_attention(seen, q, k, v, k_other, v_other, kv_heads, prompt_rows):
    rows = q.shape[1]
    heads = q.shape[0] // HEAD_WIDTH
    keys = jnp.concatenate([k_other, k], axis=1).reshape(kv_heads, HEAD_WIDTH, -1)
    values = jnp.concatenate([v_other, v], axis=1).reshape(kv_heads, HEAD_WIDTH, -1)
    at = jnp.arange(rows)
    in_prompt = at < prompt_rows
    piece = jnp.where(in_prompt, -1, (at - prompt_rows) // CONTINUE_LENGTH)
    own = (at[None, :] <= at[:, None]) & (in_prompt[None, :] | (piece[None, :] == piece[:, None]))
    other = jnp.broadcast_to(jnp.where(in_prompt, seen > 0, True)[:, None], (rows, k_other.shape[1]))
    allowed = jnp.concatenate([other, own], axis=1)

    def one_head(head):
        query = lax.dynamic_index_in_dim(q.reshape(heads, HEAD_WIDTH, rows), head, 0, False)
        key = lax.dynamic_index_in_dim(keys, head // (heads // kv_heads), 0, False)
        value = lax.dynamic_index_in_dim(values, head // (heads // kv_heads), 0, False)
        scores = jnp.where(allowed, contract(query, key, 0, 0), masked_score)
        top = jnp.max(scores, axis=1, keepdims=True)
        weights = jnp.exp2(scores - top)
        total = jnp.sum(weights, axis=1, keepdims=True)
        out = contract(value, (weights / total).astype(bf16), 1, 1)
        return out.astype(bf16), (top + jnp.log2(total))[:, 0]

    out, lse = lax.map(one_head, jnp.arange(heads))
    return out.reshape(q.shape), lse.reshape(kv_heads, heads // kv_heads, rows)


def swap(array):
    return lax.ppermute(array, "ctx", SWAP)


def fast_local(
    tokens, block_map, attention_gain, query_weight, key_matrix, value_matrix, output_weight,
    feedforward_gain, gate_weight, up_weight, down_weight, out_grad,
):
    x, dy = tokens[0], out_grad[0]
    rows, width = x.shape
    prompt_rows = rows // 2
    q_rows, kv_rows = query_weight.shape[1], key_matrix.shape[1]
    kv_heads = kv_rows // HEAD_WIDTH
    hidden = gate_weight.shape[1]
    shard_rows = query_weight.shape[0]
    block = lax.dynamic_index_in_dim(block_map[0], 2 * lax.axis_index("ctx"), 0, False)
    seen = (block > 0).astype(jnp.int32)
    prompt_total = block_map.shape[1] // 2 * prompt_rows

    gains = jnp.stack([attention_gain, feedforward_gain], axis=1)
    gains = jnp.pad(gains, ((0, 0), (0, 126)))
    first = lax.all_gather(
        jnp.concatenate([query_weight, key_matrix, value_matrix, gains], axis=1), OWNERS, axis=0, tiled=True
    )
    second = lax.all_gather(
        jnp.concatenate([output_weight, gate_weight, up_weight], axis=1), OWNERS, axis=0, tiled=True
    )
    wd = lax.all_gather(down_weight, OWNERS, axis=0, tiled=True)
    w_qkv = first[:, : q_rows + 2 * kv_rows]
    gain_pair = first[:, q_rows + 2 * kv_rows : q_rows + 2 * kv_rows + 2].astype(f32).T
    gain_a, gain_f = gain_pair[0:1], gain_pair[1:2]
    wo = second[:, :q_rows]
    wg = second[:, q_rows : q_rows + hidden]
    wu = second[:, q_rows + hidden :]

    at = jnp.arange(rows, dtype=jnp.int32)
    positions = jnp.where(
        at < prompt_rows, block * prompt_rows + at, prompt_total + (at - prompt_rows) % CONTINUE_LENGTH
    )
    half = HEAD_WIDTH // 2
    frequency = rope_base ** (-(jnp.arange(half, dtype=f32) * 2.0) / HEAD_WIDTH)
    angles = frequency[:, None] * positions.astype(f32)[None, :]
    cos, sin = jnp.cos(angles), jnp.sin(angles)

    q, k, v, h1, norm_q, norm_k = project(x, gain_a, w_qkv, cos, sin, q_rows, kv_rows)
    k_other, v_other = swap(k[:, :prompt_rows]), swap(v[:, :prompt_rows])
    acc = own_forward(q, k, v, kv_heads, prompt_rows)
    other_norm = jnp.max(jnp.sum(jnp.square(k_other.astype(f32)).reshape(kv_heads, HEAD_WIDTH, -1), axis=1))
    bound = jnp.max(norm_q) * jnp.maximum(jnp.max(norm_k), other_norm)
    o, lse = other_forward(seen[None], q, k_other, v_other, acc, kv_heads, prompt_rows)
    o, lse = lax.cond(
        bound < SAFE_BOUND * SAFE_BOUND,
        lambda: (o, lse),
        lambda: exact_attention(seen, q, k, v, k_other, v_other, kv_heads, prompt_rows),
    )
    layer_out, h2, hid, dgate, dup, dattn, dob, delta, dgain_f = middle(
        x, dy, o, gain_f, wo, wg, wu, wd, kv_heads
    )
    d_down, d_gate, d_up = ffn_grads(h2, dy, hid, dgate, dup)
    d_out = contract(o, dattn, 1, 0).astype(bf16)
    scatter = lambda a: lax.psum_scatter(a, OWNERS, scatter_dimension=0, tiled=True)
    d_down = scatter(d_down)
    d_wide = scatter(jnp.concatenate([d_out, d_gate, d_up], axis=1))
    dq_part, dk_other, dv_other = other_backward(seen[None], q, dob, lse, delta, k_other, v_other, kv_heads, prompt_rows)
    dk_in, dv_in = swap(dk_other.astype(bf16)), swap(dv_other.astype(bf16))
    dq, dk, dv = own_backward(q, dob, lse, delta, k, v, dq_part, kv_heads, prompt_rows)
    more = lambda a, b: a.at[:, :prompt_rows].add(b.astype(f32))
    grad_tokens, d_qkv, dgain_a = finish(
        x, h1, dattn, gain_a, w_qkv, dq, more(dk, dk_in), more(dv, dv_in), cos, sin
    )
    dgains = jnp.pad(jnp.concatenate([dgain_a, dgain_f], axis=0).T, ((0, 0), (0, 126))).astype(bf16)
    d_first = scatter(jnp.concatenate([d_qkv, dgains], axis=1))

    def over_ctx(part):
        return part.astype(f32) + swap(part).astype(f32)

    d_down, d_wide, d_first = over_ctx(d_down), over_ctx(d_wide), over_ctx(d_first)
    end = q_rows + 2 * kv_rows
    return (
        layer_out[None],
        grad_tokens[None],
        d_first[:, end],
        d_first[:, :q_rows],
        d_first[:, q_rows : q_rows + kv_rows],
        d_first[:, q_rows + kv_rows : end],
        d_wide[:, :q_rows],
        d_first[:, end + 1],
        d_wide[:, q_rows : q_rows + hidden],
        d_wide[:, q_rows + hidden :],
        d_down,
    )


def local(mesh, tokens, block_map, *rest):
    block_rows = tokens.shape[1] // 2
    whole = mesh.shape["ctx"] == 2 and block_rows % CONTINUE_LENGTH == 0 and tokens.shape[0] == 1
    return (fast_local if whole else general_local)(tokens, block_map, *rest)


def solution(mesh):
    return jax.shard_map(
        lambda *args: local(mesh, *args),
        mesh=mesh,
        in_specs=(
            P(("group", "wshard"), "ctx", None),
            P(("group", "wshard"), None),
            P(("group", "wshard")),
            P(("group", "wshard"), None),
            P(("group", "wshard"), None),
            P(("group", "wshard"), None),
            P(("group", "wshard"), None),
            P(("group", "wshard")),
            P(("group", "wshard"), None),
            P(("group", "wshard"), None),
            P(("group", "wshard"), None),
            P(("group", "wshard"), "ctx", None),
        ),
        out_specs=(
            P(("group", "wshard"), "ctx", None),
            P(("group", "wshard"), "ctx", None),
            P(("group", "wshard")),
            P(("group", "wshard"), None),
            P(("group", "wshard"), None),
            P(("group", "wshard"), None),
            P(("group", "wshard"), None),
            P(("group", "wshard")),
            P(("group", "wshard"), None),
            P(("group", "wshard"), None),
            P(("group", "wshard"), None),
        ),
        check_vma=False,
    )
```

```python
import functools
import jax
import jax.numpy as jnp
from jax import lax
from jax.experimental import pallas as pl
from jax.experimental.pallas import tpu as pltpu
from jax.sharding import PartitionSpec as P

f32 = jnp.float32
bf16 = jnp.bfloat16
HEAD_WIDTH = 64
CONTINUE_LENGTH = 512
norm_eps = 1e-05
LOG2E = 1.4426950408889634
LN2 = 0.6931471805599453
MIB = 2**20


def contract(a, b, dim_a, dim_b):
    return lax.dot_general(
        a, b, (((dim_a,), (dim_b,)), ((), ())), preferred_element_type=f32
    )


def resident(shape):
    zeros = (0,) * len(shape)
    return pl.BlockSpec(shape, lambda *_: zeros, pipeline_mode=pl.Buffered(1))


def project_kernel(x_ref, gain_ref, w_ref, cos_ref, sin_ref, q_ref, k_ref, v_ref, h_ref, nq_ref, nk_ref):
    x = x_ref[...].astype(f32)
    inverse = lax.rsqrt(jnp.mean(x * x, axis=-1, keepdims=True) + norm_eps)
    h = (x * inverse * gain_ref[...]).astype(bf16)
    h_ref[...] = h
    q_rows, kv_rows = q_ref.shape[0], k_ref.shape[0]
    half = HEAD_WIDTH // 2
    scale = LOG2E * HEAD_WIDTH**-0.5
    cos, sin = cos_ref[...], sin_ref[...]

    def rotated(lin, out_ref, base, cos, sin):
        worst = jnp.zeros((1, lin.shape[1]), f32)
        for head in range(lin.shape[0] // HEAD_WIDTH):
            at = head * HEAD_WIDTH
            a, b = lin[at : at + half], lin[at + half : at + HEAD_WIDTH]
            first = (a * cos - b * sin).astype(bf16)
            second = (b * cos + a * sin).astype(bf16)
            out_ref[base + at : base + at + half] = first
            out_ref[base + at + half : base + at + HEAD_WIDTH] = second
            fa, fb = first.astype(f32), second.astype(f32)
            worst = jnp.maximum(worst, jnp.sum(fa * fa + fb * fb, axis=0, keepdims=True))
        return worst

    ht = h.T
    chunk = kv_rows
    qc, qs = cos * scale, sin * scale
    worst_q = worst_k = None
    for at in range(0, q_rows + 2 * kv_rows, chunk):
        lin = contract(w_ref[:, at : at + chunk], ht, 0, 0)
        if at < q_rows:
            worst = rotated(lin, q_ref, at, qc, qs)
            worst_q = worst if worst_q is None else jnp.maximum(worst_q, worst)
        elif at < q_rows + kv_rows:
            worst = rotated(lin, k_ref, at - q_rows, cos, sin)
            worst_k = worst if worst_k is None else jnp.maximum(worst_k, worst)
        else:
            v_ref[pl.ds(at - q_rows - kv_rows, chunk)] = lin.astype(bf16)
    nq_ref[...] = worst_q
    nk_ref[...] = worst_k


def project(x, gain, w, cos, sin, q_rows, kv_rows, tile=512):
    rows, width = x.shape
    cols = lambda n: pl.BlockSpec((n, tile), lambda i: (0, i))
    return pl.pallas_call(
        project_kernel,
        grid=(rows // tile,),
        in_specs=[
            pl.BlockSpec((tile, width), lambda i: (i, 0)),
            resident(gain.shape),
            resident(w.shape),
            cols(cos.shape[0]),
            cols(cos.shape[0]),
        ],
        out_specs=(
            cols(q_rows),
            cols(kv_rows),
            cols(kv_rows),
            pl.BlockSpec((tile, width), lambda i: (i, 0)),
            cols(1),
            cols(1),
        ),
        out_shape=(
            jax.ShapeDtypeStruct((q_rows, rows), bf16),
            jax.ShapeDtypeStruct((kv_rows, rows), bf16),
            jax.ShapeDtypeStruct((kv_rows, rows), bf16),
            jax.ShapeDtypeStruct((rows, width), bf16),
            jax.ShapeDtypeStruct((1, rows), f32),
            jax.ShapeDtypeStruct((1, rows), f32),
        ),
        compiler_params=pltpu.CompilerParams(vmem_limit_bytes=48 * MIB),
        name="project",
    )(x, gain, w, cos, sin)


ONES = 16


def causal(keys, columns):
    return lax.broadcasted_iota(jnp.int32, (keys, columns), 0) <= lax.broadcasted_iota(
        jnp.int32, (keys, columns), 1
    )


def spans(prompt_rows, rows, step):
    found = [(0, prompt_rows, prompt_rows, rows, False)]
    at = 0
    while at < rows:
        end = prompt_rows if at < prompt_rows else at + CONTINUE_LENGTH
        for key in range(at, end, step):
            found.append((key, key + step, key, end, True))
        at = end
    return found


def weigh(keys, query, diagonal):
    scores = contract(keys, query, 1, 0)
    weights = jnp.exp2(scores)
    if diagonal:
        step = keys.shape[0]
        front = jnp.where(causal(step, step), weights[:, :step], 0.0)
        weights = front if weights.shape[1] == step else jnp.concatenate([front, weights[:, step:]], axis=1)
    return weights.astype(bf16)


def own_forward_kernel(q_ref, k_ref, v_ref, acc_ref, *, group, prompt_rows, step):
    rows = q_ref.shape[1]
    keys = k_ref[...].T
    values = jnp.concatenate([v_ref[...], jnp.ones((ONES, rows), bf16)], axis=0)
    wide = HEAD_WIDTH + ONES
    started = set()
    for low, high, first, last, diagonal in spans(prompt_rows, rows, step):
        for head in range(group):
            query = q_ref[head * HEAD_WIDTH : (head + 1) * HEAD_WIDTH, first:last]
            weights = weigh(keys[low:high], query, diagonal)
            part = contract(values[:, low:high], weights, 1, 0)
            at = pl.ds(head * wide, wide)
            fresh = (low == 0 and not diagonal) or (diagonal and low == 0)
            if fresh:
                acc_ref[at, first:last] = part
            else:
                acc_ref[at, first:last] += part


def own_forward(q, k, v, kv_heads, prompt_rows, step=256):
    rows = q.shape[1]
    group = q.shape[0] // HEAD_WIDTH // kv_heads
    wide = group * (HEAD_WIDTH + ONES)
    block = lambda n: pl.BlockSpec((n, rows), lambda h: (h, 0))
    return pl.pallas_call(
        functools.partial(own_forward_kernel, group=group, prompt_rows=prompt_rows, step=step),
        grid=(kv_heads,),
        in_specs=[block(group * HEAD_WIDTH), block(HEAD_WIDTH), block(HEAD_WIDTH)],
        out_specs=block(wide),
        out_shape=jax.ShapeDtypeStruct((kv_heads * wide, rows), f32),
        compiler_params=pltpu.CompilerParams(vmem_limit_bytes=56 * MIB),
        name="own_forward",
    )(q, k, v)


def other_forward_kernel(seen_ref, q_ref, k_ref, v_ref, acc_ref, o_ref, lse_ref, *, group, prompt_rows):
    rows = q_ref.shape[1]
    keys = k_ref[...].T
    values = jnp.concatenate([v_ref[...], jnp.ones((ONES, keys.shape[0]), bf16)], axis=0)
    wide = HEAD_WIDTH + ONES

    def finish(first, last, with_other):
        for head in range(group):
            total = acc_ref[head * wide : (head + 1) * wide, first:last]
            if with_other:
                query = q_ref[head * HEAD_WIDTH : (head + 1) * HEAD_WIDTH, first:last]
                total = total + contract(values, weigh(keys, query, False), 1, 0)
            weight_sum = total[HEAD_WIDTH : HEAD_WIDTH + 1]
            o_ref[head * HEAD_WIDTH : (head + 1) * HEAD_WIDTH, first:last] = (
                total[:HEAD_WIDTH] / weight_sum
            ).astype(bf16)
            lse_ref[0, head : head + 1, first:last] = jnp.log2(weight_sum)

    finish(prompt_rows, rows, True)

    @pl.when(seen_ref[0] > 0)
    def _():
        finish(0, prompt_rows, True)

    @pl.when(seen_ref[0] == 0)
    def _():
        finish(0, prompt_rows, False)


def other_forward(seen, q, k, v, acc, kv_heads, prompt_rows):
    rows = q.shape[1]
    group = q.shape[0] // HEAD_WIDTH // kv_heads
    wide = group * (HEAD_WIDTH + ONES)
    block = lambda n, m: pl.BlockSpec((n, m), lambda h, s: (h, 0))
    return pl.pallas_call(
        functools.partial(other_forward_kernel, group=group, prompt_rows=prompt_rows),
        grid_spec=pltpu.PrefetchScalarGridSpec(
            num_scalar_prefetch=1,
            grid=(kv_heads,),
            in_specs=[
                block(group * HEAD_WIDTH, rows),
                block(HEAD_WIDTH, k.shape[1]),
                block(HEAD_WIDTH, k.shape[1]),
                block(wide, rows),
            ],
            out_specs=(
                block(group * HEAD_WIDTH, rows),
                pl.BlockSpec((1, group, rows), lambda h, s: (h, 0, 0)),
            ),
        ),
        out_shape=(
            jax.ShapeDtypeStruct(q.shape, bf16),
            jax.ShapeDtypeStruct((kv_heads, group, rows), f32),
        ),
        compiler_params=pltpu.CompilerParams(vmem_limit_bytes=56 * MIB),
        name="other_forward",
    )(seen, q, k, v, acc)


def in_parts(row):
    high = row.astype(bf16)
    rest = row - high.astype(f32)
    middle = rest.astype(bf16)
    low = (rest - middle.astype(f32)).astype(bf16)
    return jnp.concatenate([high, middle, low, jnp.zeros((ONES - 3, row.shape[1]), bf16)], axis=0)


def widened(matrix):
    return jnp.concatenate([matrix, jnp.ones((matrix.shape[0], ONES), bf16)], axis=1)


def tile_backward(keys, values, key_rows, query, grad, diagonal):
    weights = jnp.exp2(contract(keys, query, 1, 0))
    slopes = contract(values, grad, 1, 0)
    if diagonal:
        step = keys.shape[0]
        front = jnp.where(causal(step, step), weights[:, :step], 0.0)
        weights = front if weights.shape[1] == step else jnp.concatenate([front, weights[:, step:]], axis=1)
    slopes = (weights * slopes).astype(bf16)
    weights = weights.astype(bf16)
    query_grad = contract(key_rows, slopes, 1, 0)
    key_grad = contract(query[:HEAD_WIDTH], slopes, 1, 1)
    value_grad = contract(grad[:HEAD_WIDTH], weights, 1, 1)
    return query_grad, key_grad, value_grad


def fill_sides(q_ref, g_ref, lse_ref, delta_ref, query_ref, grad_ref, group):
    for head in range(group):
        rows = pl.ds(head * HEAD_WIDTH, HEAD_WIDTH)
        query_ref[head, :HEAD_WIDTH] = q_ref[rows]
        grad_ref[head, :HEAD_WIDTH] = g_ref[rows]
        query_ref[head, HEAD_WIDTH:] = in_parts(-lse_ref[0, head : head + 1])
        grad_ref[head, HEAD_WIDTH:] = in_parts(-delta_ref[0, head : head + 1])


def other_backward_kernel(
    seen_ref, q_ref, g_ref, lse_ref, delta_ref, k_ref, v_ref, dq_ref, dk_ref, dv_ref,
    query_ref, grad_ref, keys_ref, values_ref, dk_sum, dv_sum, *, group, prompt_rows, step
):
    rows = q_ref.shape[1]
    fill_sides(q_ref, g_ref, lse_ref, delta_ref, query_ref, grad_ref, group)
    keys_ref[...] = widened(k_ref[...].T)
    values_ref[...] = widened(v_ref[...].T)
    dq_ref[...] = jnp.zeros_like(dq_ref)

    def part(first, last, fresh):
        for low in range(0, k_ref.shape[1], step):
            span = slice(low, low + step)
            key_sum = value_sum = None
            for head in range(group):
                query_grad, key_grad, value_grad = tile_backward(
                    keys_ref[span], values_ref[span], k_ref[:, span],
                    query_ref[head, :, first:last], grad_ref[head, :, first:last], False,
                )
                at = pl.ds(head * HEAD_WIDTH, HEAD_WIDTH)
                dq_ref[at, first:last] += query_grad
                key_sum = key_grad if key_sum is None else key_sum + key_grad
                value_sum = value_grad if value_sum is None else value_sum + value_grad
            if fresh:
                dk_sum[:, span] = key_sum
                dv_sum[:, span] = value_sum
            else:
                dk_sum[:, span] += key_sum
                dv_sum[:, span] += value_sum

    part(prompt_rows, rows, True)

    @pl.when(seen_ref[0] > 0)
    def _():
        part(0, prompt_rows, False)

    dk_ref[...] = dk_sum[...].astype(bf16)
    dv_ref[...] = dv_sum[...].astype(bf16)


def backward_specs(group, rows, key_count):
    block = lambda n, m: pl.BlockSpec((n, m), lambda h, *_: (h, 0))
    row_block = pl.BlockSpec((1, group, rows), lambda h, *_: (h, 0, 0))
    wide = group * HEAD_WIDTH
    ins = [block(wide, rows), block(wide, rows), row_block, row_block,
           block(HEAD_WIDTH, key_count), block(HEAD_WIDTH, key_count)]
    outs = (block(wide, rows), block(HEAD_WIDTH, key_count), block(HEAD_WIDTH, key_count))
    scratch = [
        pltpu.VMEM((group, HEAD_WIDTH + ONES, rows), bf16),
        pltpu.VMEM((group, HEAD_WIDTH + ONES, rows), bf16),
        pltpu.VMEM((key_count, HEAD_WIDTH + ONES), bf16),
        pltpu.VMEM((key_count, HEAD_WIDTH + ONES), bf16),
    ]
    return ins, outs, scratch


def other_backward(seen, q, g, lse, delta, k, v, kv_heads, prompt_rows, step=256):
    rows = q.shape[1]
    group = q.shape[0] // HEAD_WIDTH // kv_heads
    ins, outs, scratch = backward_specs(group, rows, k.shape[1])
    scratch += [pltpu.VMEM((HEAD_WIDTH, k.shape[1]), f32)] * 2
    return pl.pallas_call(
        functools.partial(other_backward_kernel, group=group, prompt_rows=prompt_rows, step=step),
        grid_spec=pltpu.PrefetchScalarGridSpec(
            num_scalar_prefetch=1, grid=(kv_heads,), in_specs=ins, out_specs=outs, scratch_shapes=scratch
        ),
        out_shape=(
            jax.ShapeDtypeStruct(q.shape, f32),
            jax.ShapeDtypeStruct(k.shape, bf16),
            jax.ShapeDtypeStruct(v.shape, bf16),
        ),
        compiler_params=pltpu.CompilerParams(vmem_limit_bytes=56 * MIB),
        name="other_backward",
    )(seen, q, g, lse, delta, k, v)


def own_backward_kernel(
    q_ref, g_ref, lse_ref, delta_ref, k_ref, v_ref, dq_in_ref, dq_ref, dk_ref, dv_ref,
    query_ref, grad_ref, keys_ref, values_ref, *, group, prompt_rows, step
):
    rows = q_ref.shape[1]
    fill_sides(q_ref, g_ref, lse_ref, delta_ref, query_ref, grad_ref, group)
    keys_ref[...] = widened(k_ref[...].T)
    values_ref[...] = widened(v_ref[...].T)
    dq_ref[...] = dq_in_ref[...]
    dk_ref[...] = jnp.zeros_like(dk_ref)
    dv_ref[...] = jnp.zeros_like(dv_ref)

    def one(low, high, first, last, diagonal):
        span = slice(low, high)
        key_sum = value_sum = None
        for head in range(group):
            query_grad, key_grad, value_grad = tile_backward(
                keys_ref[span], values_ref[span], k_ref[:, span],
                query_ref[head, :, first:last], grad_ref[head, :, first:last], diagonal,
            )
            at = pl.ds(head * HEAD_WIDTH, HEAD_WIDTH)
            dq_ref[at, first:last] += query_grad
            key_sum = key_grad if key_sum is None else key_sum + key_grad
            value_sum = value_grad if value_sum is None else value_sum + value_grad
        dk_ref[:, span] += key_sum
        dv_ref[:, span] += value_sum

    for low, high, first, last, diagonal in spans(prompt_rows, rows, step):
        if diagonal:
            one(low, high, first, last, True)
        else:
            for at in range(low, high, step):
                one(at, at + step, first, last, False)


def own_backward(q, g, lse, delta, k, v, dq, kv_heads, prompt_rows, step=256):
    rows = q.shape[1]
    group = q.shape[0] // HEAD_WIDTH // kv_heads
    ins, outs, scratch = backward_specs(group, rows, k.shape[1])
    return pl.pallas_call(
        functools.partial(own_backward_kernel, group=group, prompt_rows=prompt_rows, step=step),
        grid=(kv_heads,),
        in_specs=ins + [outs[0]],
        out_specs=outs,
        scratch_shapes=scratch,
        out_shape=(
            jax.ShapeDtypeStruct(q.shape, f32),
            jax.ShapeDtypeStruct(k.shape, f32),
            jax.ShapeDtypeStruct(v.shape, f32),
        ),
        compiler_params=pltpu.CompilerParams(vmem_limit_bytes=60 * MIB),
        name="own_backward",
    )(q, g, lse, delta, k, v, dq)


def middle_kernel(
    x_ref, dy_ref, o_ref, gain_ref, wide_any, wd_any,
    out_ref, h2_ref, hidden_ref, dgate_ref, dup_ref, dattn_ref, dob_ref, delta_ref, dgain_ref,
    wo_ref, wg_ref, wu_ref, wd_ref, sems, *, chunk
):
    step = pl.program_id(0)
    inner, total = wo_ref.shape[1], wg_ref.shape[1]
    copies = [
        pltpu.make_async_copy(source, target, sems.at[i])
        for i, (source, target) in enumerate(
            (
                (wide_any.at[:, pl.ds(0, inner)], wo_ref),
                (wide_any.at[:, pl.ds(inner, total)], wg_ref),
                (wide_any.at[:, pl.ds(inner + total, total)], wu_ref),
                (wd_any, wd_ref),
            )
        )
    ]

    @pl.when(step == 0)
    def _():
        for copy in copies:
            copy.start()
        dgain_ref[...] = jnp.zeros_like(dgain_ref)
        copies[0].wait()

    ob = o_ref[...]
    x1 = x_ref[...].astype(f32) + contract(ob, wo_ref[...], 0, 0)
    inverse = lax.rsqrt(jnp.mean(x1 * x1, axis=-1, keepdims=True) + norm_eps)
    gain = gain_ref[...]
    h2 = (x1 * inverse * gain).astype(bf16)
    h2_ref[...] = h2
    dy = dy_ref[...]

    @pl.when(step == 0)
    def _():
        for copy in copies[1:]:
            copy.wait()

    result = x1
    dh2 = None
    for low in range(0, wg_ref.shape[1], chunk):
        span = slice(low, low + chunk)
        gate = contract(h2, wg_ref[:, span], 1, 0)
        up = contract(h2, wu_ref[:, span], 1, 0)
        dhidden = contract(dy, wd_ref[span], 1, 1)
        sigma = 0.5 + 0.5 * jnp.tanh(0.5 * gate)
        silu = gate * sigma
        hidden = (silu * up).astype(bf16)
        hidden_ref[:, span] = hidden
        result = result + contract(hidden, wd_ref[span], 1, 0)
        dgate = (dhidden * up * sigma * (1.0 + gate * (1.0 - sigma))).astype(bf16)
        dup = (dhidden * silu).astype(bf16)
        dgate_ref[:, span] = dgate
        dup_ref[:, span] = dup
        part = contract(dgate, wg_ref[:, span], 1, 1) + contract(dup, wu_ref[:, span], 1, 1)
        dh2 = part if dh2 is None else dh2 + part
    out_ref[...] = result.astype(bf16)
    dgain_ref[...] += jnp.sum(dh2 * x1 * inverse, axis=0, keepdims=True)
    u = dh2 * gain
    dx1 = dy.astype(f32) + inverse * u - x1 * (inverse * inverse * inverse) * jnp.mean(
        u * x1, axis=-1, keepdims=True
    )
    dattn = dx1.astype(bf16)
    dattn_ref[...] = dattn
    dob = contract(wo_ref[...], dattn, 1, 1).astype(bf16)
    dob_ref[...] = dob
    product = dob.astype(f32) * ob.astype(f32)
    heads, group = delta_ref.shape[0], delta_ref.shape[1]
    for kv in range(heads):
        for member in range(group):
            at = (kv * group + member) * HEAD_WIDTH
            delta_ref[kv, member : member + 1] = jnp.sum(
                product[at : at + HEAD_WIDTH], axis=0, keepdims=True
            )


def middle(x, dy, o, gain, wide, wd, kv_heads, tile=256, chunk=768):
    rows, width = x.shape
    hidden = wd.shape[0]
    q_rows = o.shape[0]
    group = q_rows // HEAD_WIDTH // kv_heads
    by_row = lambda n: pl.BlockSpec((tile, n), lambda i: (i, 0))
    any_spec = pl.BlockSpec(memory_space=pl.ANY)
    shape = jax.ShapeDtypeStruct
    return pl.pallas_call(
        functools.partial(middle_kernel, chunk=chunk),
        grid=(rows // tile,),
        in_specs=[by_row(width), by_row(width), pl.BlockSpec((q_rows, tile), lambda i: (0, i)),
                  resident(gain.shape)] + [any_spec] * 2,
        out_specs=(
            by_row(width), by_row(width), by_row(hidden), by_row(hidden), by_row(hidden), by_row(width),
            pl.BlockSpec((q_rows, tile), lambda i: (0, i)),
            pl.BlockSpec((kv_heads, group, tile), lambda i: (0, 0, i)),
            pl.BlockSpec((1, width), lambda i: (0, 0)),
        ),
        out_shape=(
            shape((rows, width), bf16), shape((rows, width), bf16), shape((rows, hidden), bf16),
            shape((rows, hidden), bf16), shape((rows, hidden), bf16), shape((rows, width), bf16),
            shape((q_rows, rows), bf16), shape((kv_heads, group, rows), f32), shape((1, width), f32),
        ),
        scratch_shapes=[pltpu.VMEM(s, bf16) for s in ((width, q_rows), (width, hidden), (width, hidden), wd.shape)]
        + [pltpu.SemaphoreType.DMA((4,))],
        compiler_params=pltpu.CompilerParams(vmem_limit_bytes=62 * MIB),
        name="middle",
    )(x, dy, o, gain, wide, wd)


def down_grads_kernel(dy_ref, hidden_ref, down_ref):
    down_ref[...] = contract(hidden_ref[...], dy_ref[...], 0, 0).astype(bf16)


def down_grads(dy, hidden, tile=512):
    rows, width = dy.shape
    total = hidden.shape[1]
    return pl.pallas_call(
        down_grads_kernel,
        grid=(total // tile,),
        in_specs=[resident(dy.shape), pl.BlockSpec((rows, tile), lambda i: (0, i))],
        out_specs=pl.BlockSpec((tile, width), lambda i: (i, 0)),
        out_shape=jax.ShapeDtypeStruct((total, width), bf16),
        compiler_params=pltpu.CompilerParams(vmem_limit_bytes=56 * MIB),
        name="down_grads",
    )(dy, hidden)


def wide_grads_kernel(o_ref, h2_ref, dgate_ref, dup_ref, dattn_ref, out_ref, *, each):
    step = pl.program_id(0)

    @pl.when(step < each)
    def _():
        out_ref[...] = contract(h2_ref[...], dgate_ref[...], 0, 0).astype(bf16)

    @pl.when((step >= each) & (step < 2 * each))
    def _():
        out_ref[...] = contract(h2_ref[...], dup_ref[...], 0, 0).astype(bf16)

    @pl.when(step >= 2 * each)
    def _():
        out_ref[...] = contract(o_ref[...], dattn_ref[...], 1, 0).astype(bf16)


def wide_grads(o, h2, dattn, dgate, dup, tile=512):
    rows, width = h2.shape
    total = dgate.shape[1]
    each = total // tile
    steps = 2 * each + pl.cdiv(width, tile)
    cols = lambda low, count: pl.BlockSpec((rows, tile), lambda i: (0, jnp.clip(i - low, 0, count - 1)))
    return pl.pallas_call(
        functools.partial(wide_grads_kernel, each=each),
        grid=(steps,),
        in_specs=[
            resident(o.shape), resident(h2.shape), cols(0, each), cols(each, each), cols(2 * each, steps - 2 * each)
        ],
        out_specs=pl.BlockSpec((width, tile), lambda i: (0, i)),
        out_shape=jax.ShapeDtypeStruct((width, 2 * total + width), bf16),
        compiler_params=pltpu.CompilerParams(vmem_limit_bytes=56 * MIB),
        name="wide_grads",
    )(o, h2, dgate, dup, dattn)


def finish_kernel(
    x_ref, h_ref, dattn_ref, gain_ref, w_ref, dq_ref, dk_ref, dv_ref, dk_in_ref, dv_in_ref, cos_ref, sin_ref,
    dgain_f_ref, out_ref, dw_ref, acc_ref, dgain_ref, *, prompt_steps
):
    step = pl.program_id(0)

    @pl.when(step == 0)
    def _():
        dgain_ref[...] = jnp.zeros_like(dgain_ref)
        acc_ref[...] = jnp.zeros_like(acc_ref)

    half = HEAD_WIDTH // 2
    cos, sin = cos_ref[...], sin_ref[...]

    def with_received(ref, in_ref):
        return ref[...] + jnp.where(step < prompt_steps, in_ref[...].astype(f32), 0.0)

    def turned(value, scale):
        c, s = cos * scale, sin * scale
        pieces = []
        for at in range(0, value.shape[0], HEAD_WIDTH):
            a, b = value[at : at + half], value[at + half : at + HEAD_WIDTH]
            pieces += [a * c + b * s, b * c - a * s]
        return jnp.concatenate(pieces, axis=0)

    lin = jnp.concatenate(
        [
            turned(dq_ref, HEAD_WIDTH**-0.5),
            turned(with_received(dk_ref, dk_in_ref), LN2),
            with_received(dv_ref, dv_in_ref),
        ],
        axis=0,
    ).astype(bf16).T
    inner = lin.shape[1]
    acc_ref[...] += contract(h_ref[...], lin, 0, 0)
    dh = contract(lin, w_ref[:, :inner], 1, 1)
    x = x_ref[...].astype(f32)
    inverse = lax.rsqrt(jnp.mean(x * x, axis=-1, keepdims=True) + norm_eps)
    dgain_ref[0:1] += jnp.sum(dh * x * inverse, axis=0, keepdims=True)
    u = dh * gain_ref[...]
    out_ref[...] = (
        dattn_ref[...].astype(f32)
        + inverse * u
        - x * (inverse * inverse * inverse) * jnp.mean(u * x, axis=-1, keepdims=True)
    )

    @pl.when(step == pl.num_programs(0) - 1)
    def _():
        dw_ref[:, :inner] = acc_ref[...].astype(bf16)
        dgain_ref[1:2] = dgain_f_ref[...]
        dw_ref[:, inner:] = dgain_ref[...].T.astype(bf16)


def finish(x, h, dattn, gain, w, dq, dk, dv, dk_in, dv_in, cos, sin, dgain_f, tile=256):
    rows, width = x.shape
    by_row = pl.BlockSpec((tile, width), lambda i: (i, 0))
    cols = lambda n: pl.BlockSpec((n, tile), lambda i: (0, i))
    steps = dk_in.shape[1] // tile
    few = lambda n: pl.BlockSpec((n, tile), lambda i: (0, jnp.minimum(i, steps - 1)))
    shape = jax.ShapeDtypeStruct
    inner = dq.shape[0] + dk.shape[0] + dv.shape[0]
    return pl.pallas_call(
        functools.partial(finish_kernel, prompt_steps=steps),
        grid=(rows // tile,),
        in_specs=[by_row, by_row, by_row, resident(gain.shape), resident(w.shape),
                  cols(dq.shape[0]), cols(dk.shape[0]), cols(dv.shape[0]),
                  few(dk.shape[0]), few(dv.shape[0]),
                  cols(cos.shape[0]), cols(cos.shape[0]), resident(dgain_f.shape)],
        out_specs=(by_row, pl.BlockSpec(w.shape, lambda i: (0, 0))),
        out_shape=(shape((rows, width), f32), shape(w.shape, bf16)),
        scratch_shapes=[pltpu.VMEM((width, inner), f32), pltpu.VMEM((w.shape[1] - inner, width), f32)],
        compiler_params=pltpu.CompilerParams(vmem_limit_bytes=56 * MIB),
        name="finish",
    )(x, h, dattn, gain, w, dq, dk, dv, dk_in, dv_in, cos, sin, dgain_f)


MESH_ID = pl.DeviceIdType.MESH


def whereabouts():
    z, y, w = lax.axis_index("group"), lax.axis_index("ctx"), lax.axis_index("wshard")
    return z, y, w // 2, w % 2


def device_at(z, y, x, core):
    return (z, y, x * 2 + core)


def slot_at(z, x, core):
    return z * 4 + x * 2 + core


def greet(partners):
    barrier = pltpu.get_barrier_semaphore()
    for partner in partners:
        pl.semaphore_signal(barrier, inc=1, device_id=partner, device_id_type=MESH_ID)
    pl.semaphore_wait(barrier, len(partners))


def neighbours(depth):
    z, y, x, core = whereabouts()
    along = [device_at((z + d) % depth, y, x, core) for d in range(1, depth)]
    return along, device_at(z, y, 1 - x, core), device_at(z, 1 - y, x, core), device_at(z, y, x, 1 - core)


class Copies:
    def __init__(self, send_sems, recv_sems):
        self.send_sems, self.recv_sems, self.made = send_sems, recv_sems, []

    def make(self, source, target, device):
        at = len(self.made)
        copy = pltpu.make_async_remote_copy(
            src_ref=source,
            dst_ref=target,
            send_sem=self.send_sems.at[at],
            recv_sem=self.recv_sems.at[at],
            device_id=device,
            device_id_type=MESH_ID,
        )
        self.made.append(copy)
        return copy


def gather_kernel(shard_ref, out_ref, send_sems, recv_sems, own_sem, *, depth, split):
    z, y, x, core = whereabouts()
    along, over_x, over_y, over_core = neighbours(depth)
    columns = out_ref.shape[2]
    mine = pl.ds(pl.multiple_of(y * split, 128), columns - split)
    given = pl.ds(pl.multiple_of(y * (columns - split), 128), split)
    got = pl.ds(pl.multiple_of((1 - y) * (columns - split), 128), split)
    me = slot_at(z, x, core)
    copies = Copies(send_sems, recv_sems)
    view = lambda slot, span: out_ref.at[slot, :, span]

    own = pltpu.make_async_copy(shard_ref, out_ref.at[me], own_sem)
    own.start()
    own.wait()
    greet(along + [over_x, over_y, over_core])

    def send(slot, span, device):
        copy = copies.make(view(slot, span), view(slot, span), device)
        copy.start()
        return copy

    from_z = [send(me, mine, device) for device in along]
    from_x = {0: send(me, mine, over_x)}
    from_y = {(0, 0): send(me, given, over_y)}
    from_core = [send(me, mine, over_core)]
    for d in range(1, depth):
        from_z[d - 1].wait_recv()
        slot = slot_at((z + depth - d) % depth, x, core)
        from_x[d] = send(slot, mine, over_x)
        from_y[d, 0] = send(slot, given, over_y)
        from_core.append(send(slot, mine, over_core))
    for d in range(depth):
        from_x[d].wait_recv()
        slot = slot_at((z + depth - d) % depth, 1 - x, core)
        from_y[d, 1] = send(slot, given, over_y)
        from_core.append(send(slot, mine, over_core))
    for other in range(2):
        for d in range(depth):
            from_y[d, other].wait_recv()
            slot = slot_at((z + depth - d) % depth, x if other == 0 else 1 - x, core)
            from_core.append(send(slot, got, over_core))
    for copy in from_core:
        copy.wait_recv()
    for copy in copies.made:
        copy.wait_send()


def gather_all(shard, depth, split):
    rows, columns = shard.shape
    count = 8 * depth - 1
    return pl.pallas_call(
        functools.partial(gather_kernel, depth=depth, split=split),
        in_specs=[pl.BlockSpec(memory_space=pltpu.VMEM)],
        out_specs=pl.BlockSpec(memory_space=pltpu.VMEM),
        out_shape=jax.ShapeDtypeStruct((4 * depth, rows, columns), shard.dtype),
        scratch_shapes=[
            pltpu.SemaphoreType.DMA((count,)),
            pltpu.SemaphoreType.DMA((count,)),
            pltpu.SemaphoreType.DMA,
        ],
        compiler_params=pltpu.CompilerParams(
            collective_id=1, has_side_effects=True, vmem_limit_bytes=32 * MIB
        ),
        name="gather_all",
    )(shard)


def reduce_kernel(
    part_ref, out_ref, core_ref, y_ref, sum_ref, x_ref, line_ref, z_ref, last_ref, twin_ref, send_sems, recv_sems,
    *, depth, split
):
    z, y, x, core = whereabouts()
    along, over_x, over_y, over_core = neighbours(depth)
    columns = part_ref.shape[2]
    copies = Copies(send_sems, recv_sems)
    greet(along + [over_x, over_y, over_core])

    def send(source, target, device):
        copy = copies.make(source, target, device)
        copy.start()
        return copy

    order = [(d, side) for side in (1, 0) for d in list(range(1, depth)) + [0]]
    place = lambda d, side: ((z + d) % depth, x if side == 0 else 1 - x)
    from_core = []
    for at, (d, side) in enumerate(order):
        to_z, to_x = place(d, side)
        from_core.append(send(part_ref.at[slot_at(to_z, to_x, 1 - core)], core_ref.at[at], over_core))
    low, high = split, columns - split

    def halves(at, to_z, to_x):
        total = part_ref[slot_at(to_z, to_x, core)].astype(f32) + core_ref[at].astype(f32)
        left, middle_, right = total[:, :low], total[:, low:high], total[:, high:]
        is_low = y == 0
        sum_ref[at, :, :low] = jnp.where(is_low, left, right).astype(bf16)
        sum_ref[at, :, low:high] = middle_.astype(bf16)
        sum_ref[at, :, high:] = jnp.where(is_low, right, left).astype(bf16)

    from_y = []
    for at, (d, side) in enumerate(order):
        from_core[at].wait_recv()
        halves(at, *place(d, side))
        from_y.append(send(sum_ref.at[at, :, pl.ds(high, split)], y_ref.at[at], over_y))
    from_x = []
    for at, (d, side) in enumerate(order):
        from_y[at].wait_recv()
        sum_ref[at, :, :low] = (sum_ref[at, :, :low].astype(f32) + y_ref[at].astype(f32)).astype(bf16)
        if side == 1:
            from_x.append(send(sum_ref.at[at, :, pl.ds(0, high)], x_ref.at[at], over_x))
    from_z = []
    for index, d in enumerate(list(range(1, depth)) + [0]):
        at = depth + index
        from_x[index].wait_recv()
        total = (sum_ref[at, :, :high].astype(f32) + x_ref[index].astype(f32)).astype(bf16)
        line_ref[index] = total
        if d:
            from_z.append(send(line_ref.at[index], z_ref.at[index], along[d - 1]))
    total = line_ref[depth - 1].astype(f32)
    for index in range(depth - 1):
        from_z[index].wait_recv()
        total = total + z_ref[index].astype(f32)
    last_ref[...] = total.astype(bf16)
    twin = send(last_ref, twin_ref, over_y)
    twin.wait_recv()
    theirs = twin_ref[...].astype(f32)
    is_low = y == 0
    out_ref[:, :low] = jnp.where(is_low, total[:, :low], theirs[:, :low])
    out_ref[:, low:high] = total[:, low:] + theirs[:, low:]
    out_ref[:, high:] = jnp.where(is_low, theirs[:, :low], total[:, :low])
    for copy in copies.made:
        copy.wait_send()


def reduce_all(parts, depth, split):
    slots, rows, columns = parts.shape
    high = columns - split
    count = 2 * depth + 2 * depth + depth + depth - 1 + 1
    buffer = lambda *shape: pltpu.VMEM(shape, bf16)
    return pl.pallas_call(
        functools.partial(reduce_kernel, depth=depth, split=split),
        in_specs=[pl.BlockSpec(memory_space=pltpu.VMEM)],
        out_specs=pl.BlockSpec(memory_space=pltpu.VMEM),
        out_shape=jax.ShapeDtypeStruct((rows, columns), f32),
        scratch_shapes=[
            buffer(2 * depth, rows, columns),
            buffer(2 * depth, rows, split),
            buffer(2 * depth, rows, columns),
            buffer(depth, rows, high),
            buffer(depth, rows, high),
            buffer(depth - 1, rows, high),
            buffer(rows, high),
            buffer(rows, high),
            pltpu.SemaphoreType.DMA((count,)),
            pltpu.SemaphoreType.DMA((count,)),
        ],
        compiler_params=pltpu.CompilerParams(
            collective_id=2, has_side_effects=True, vmem_limit_bytes=40 * MIB
        ),
        name="reduce_all",
    )(parts)


rope_base = 10000.0
masked_score = -1e30


def as_sent(array):

    def short(part):
        return part.astype(jnp.bfloat16) if part.dtype == jnp.float32 else part

    return jax.tree.map(short, array)


def rms_scale(value_rows_list, gain):
    return (
        value_rows_list
        * lax.rsqrt(jnp.mean(value_rows_list * value_rows_list, axis=-1, keepdims=True) + norm_eps)
        * gain
    )


def rms_back(value_rows_list, gain, upstream):
    inverse = lax.rsqrt(
        jnp.mean(value_rows_list * value_rows_list, axis=-1, keepdims=True) + norm_eps
    )
    scaled = upstream * gain
    gain_grad = jnp.sum(upstream * value_rows_list * inverse, axis=0)
    values_grad = inverse * scaled - value_rows_list * (inverse * inverse * inverse) * jnp.mean(
        scaled * value_rows_list, axis=-1, keepdims=True
    )
    return (gain_grad, values_grad)


def rope_tables(token_positions, head_size):
    half_size = head_size // 2
    frequency = rope_base ** (-(jnp.arange(half_size, dtype=jnp.float32) * 2.0) / head_size)
    angles = token_positions.astype(jnp.float32)[:, None] * frequency[None, :]
    return (jnp.cos(angles), jnp.sin(angles))


def rotary_apply(value_rows_list, cosine_table, sine_table):
    half_size = value_rows_list.shape[-1] // 2
    leading = value_rows_list[..., :half_size]
    trailing = value_rows_list[..., half_size:]
    cos_rows = cosine_table[:, None, :]
    sin_rows = sine_table[:, None, :]
    return jnp.concatenate(
        [leading * cos_rows - trailing * sin_rows, trailing * cos_rows + leading * sin_rows],
        axis=-1,
    )


def visible(query_pos, query_seg, key_pos, key_seg):
    same_doc = (key_seg[None, :] == query_seg[:, None]) | (key_seg[None, :] == 0)
    return same_doc & (key_pos[None, :] <= query_pos[:, None])


def tile_scores(query_tile, key_tile, scale):
    return (
        jnp.einsum("rhgd,khd->hgrk", query_tile, key_tile, preferred_element_type=jnp.float32)
        * scale
    )


def key_tiling(key_heads, value_heads, key_pos, key_seg):
    key_block = min(256, key_heads.shape[0])
    tile_count = key_heads.shape[0] // key_block
    return (
        key_heads.reshape(tile_count, key_block, key_heads.shape[1], key_heads.shape[2]),
        value_heads.reshape(tile_count, key_block, value_heads.shape[1], value_heads.shape[2]),
        key_pos.reshape(tile_count, key_block),
        key_seg.reshape(tile_count, key_block),
    )


def query_split(value_rows_list, query_block):
    return value_rows_list.reshape(
        (value_rows_list.shape[0] // query_block, query_block) + value_rows_list.shape[1:]
    )


def attention_forward(query_heads, key_heads, value_heads, places):
    query_pos, query_seg, key_pos, key_seg = places
    count_of_rows, kv_heads, group_size, head_size = query_heads.shape
    scale = head_size ** (-0.5)
    query_block = min(512, count_of_rows)
    key_tiles, value_tiles, kpos_tiles, kseg_tiles = key_tiling(
        key_heads, value_heads, key_pos, key_seg
    )

    def one_block(block_item):
        query_tile, tile_pos, tile_seg = block_item
        state_shape = (kv_heads, group_size, query_tile.shape[0])

        def lse_step(running, tile_item):
            key_tile, tile_kpos, tile_kseg = tile_item
            allowed = visible(tile_pos, tile_seg, tile_kpos, tile_kseg)

            def lse_open_tile(state):
                row_top, row_total = state
                scores = jnp.where(allowed, tile_scores(query_tile, key_tile, scale), masked_score)
                new_top = jnp.maximum(row_top, jnp.max(scores, axis=-1))
                weights = jnp.where(allowed, jnp.exp(scores - new_top[..., None]), 0.0)
                return (new_top, row_total * jnp.exp(row_top - new_top) + jnp.sum(weights, axis=-1))

            def lse_closed_tile(state):
                return state

            return (lax.cond(jnp.any(allowed), lse_open_tile, lse_closed_tile, running), None)

        initial = (
            jnp.full(state_shape, masked_score, jnp.float32),
            jnp.zeros(state_shape, jnp.float32),
        )
        (row_top, row_total), _ = lax.scan(lse_step, initial, (key_tiles, kpos_tiles, kseg_tiles))
        log_total = row_top + jnp.log(row_total)

        def out_step(running, tile_item):
            key_tile, value_tile, tile_kpos, tile_kseg = tile_item
            allowed = visible(tile_pos, tile_seg, tile_kpos, tile_kseg)

            def out_open_tile(accumulated):
                scores = jnp.where(allowed, tile_scores(query_tile, key_tile, scale), masked_score)
                probabilities = jnp.where(
                    allowed, jnp.exp(scores - log_total[..., None]), 0.0
                ).astype(jnp.bfloat16)
                return accumulated + jnp.einsum(
                    "hgrk,khd->rhgd", probabilities, value_tile, preferred_element_type=jnp.float32
                )

            def out_closed_tile(accumulated):
                return accumulated

            return (lax.cond(jnp.any(allowed), out_open_tile, out_closed_tile, running), None)

        output, _ = lax.scan(
            out_step,
            jnp.zeros(query_tile.shape, jnp.float32),
            (key_tiles, value_tiles, kpos_tiles, kseg_tiles),
        )
        return (output, log_total)

    outputs, log_totals = lax.map(
        one_block,
        (
            query_split(query_heads, query_block),
            query_split(query_pos, query_block),
            query_split(query_seg, query_block),
        ),
    )
    return (outputs.reshape(query_heads.shape), log_totals)


def attention_backward(
    query_heads, key_heads, value_heads, places, attended_grad, attended, log_totals
):
    query_pos, query_seg, key_pos, key_seg = places
    count_of_rows, kv_heads, group_size, head_size = query_heads.shape
    scale = head_size ** (-0.5)
    query_block = min(512, count_of_rows)
    key_tiles, value_tiles, kpos_tiles, kseg_tiles = key_tiling(
        key_heads, value_heads, key_pos, key_seg
    )

    def block_grads(sums, block_item):
        query_tile, grad_tile, output_tile, tile_lse, tile_pos, tile_seg = block_item
        tile_delta = jnp.einsum("rhgd,rhgd->hgr", grad_tile.astype(jnp.float32), output_tile)

        def back_step(query_grad, tile_item):
            key_tile, value_tile, tile_kpos, tile_kseg = tile_item
            allowed = visible(tile_pos, tile_seg, tile_kpos, tile_kseg)

            def back_open_tile(query_grad):
                scores = jnp.where(allowed, tile_scores(query_tile, key_tile, scale), masked_score)
                probabilities = jnp.where(allowed, jnp.exp(scores - tile_lse[..., None]), 0.0)
                prob_grad = jnp.einsum(
                    "rhgd,khd->hgrk", grad_tile, value_tile, preferred_element_type=jnp.float32
                )
                score_grad = (probabilities * (prob_grad - tile_delta[..., None])).astype(
                    jnp.bfloat16
                )
                query_grad = query_grad + scale * jnp.einsum(
                    "hgrk,khd->rhgd", score_grad, key_tile, preferred_element_type=jnp.float32
                )
                key_part = scale * jnp.einsum(
                    "hgrk,rhgd->khd", score_grad, query_tile, preferred_element_type=jnp.float32
                )
                value_part = jnp.einsum(
                    "hgrk,rhgd->khd",
                    probabilities.astype(jnp.bfloat16),
                    grad_tile,
                    preferred_element_type=jnp.float32,
                )
                return (query_grad, key_part, value_part)

            def back_closed_tile(query_grad):
                return (
                    query_grad,
                    jnp.zeros(key_tile.shape, jnp.float32),
                    jnp.zeros(value_tile.shape, jnp.float32),
                )

            query_grad, key_part, value_part = lax.cond(
                jnp.any(allowed), back_open_tile, back_closed_tile, query_grad
            )
            return (query_grad, (key_part, value_part))

        query_grad, (key_parts, value_parts) = lax.scan(
            back_step,
            jnp.zeros(query_tile.shape, jnp.float32),
            (key_tiles, value_tiles, kpos_tiles, kseg_tiles),
        )
        return ((sums[0] + key_parts, sums[1] + value_parts), query_grad)

    initial = (jnp.zeros(key_tiles.shape, jnp.float32), jnp.zeros(value_tiles.shape, jnp.float32))
    block_items = (
        query_split(query_heads, query_block),
        query_split(attended_grad, query_block),
        query_split(attended, query_block),
        log_totals,
        query_split(query_pos, query_block),
        query_split(query_seg, query_block),
    )
    (key_sum, value_sum), query_grads = lax.scan(block_grads, initial, block_items)
    key_rows = key_heads.shape[0]
    return (
        query_grads.reshape(query_heads.shape),
        key_sum.reshape(key_rows, -1),
        value_sum.reshape(key_rows, -1),
    )


def forward_pass(weights, inputs, places, tables, gather_pair):
    (
        attn_gain,
        query_full,
        key_complete,
        value_complete,
        out_full,
        ffn_gain,
        gate_full,
        up_full,
        down_full,
    ) = weights
    cosine_table, sine_table = tables
    count_of_rows = inputs.shape[0]
    normalized_input = rms_scale(inputs, attn_gain.astype(jnp.float32)).astype(jnp.bfloat16)
    query_lin = jnp.dot(normalized_input, query_full, preferred_element_type=jnp.float32)
    key_lin = jnp.dot(normalized_input, key_complete, preferred_element_type=jnp.float32)
    value_lin = jnp.dot(normalized_input, value_complete, preferred_element_type=jnp.float32)
    kv_heads = key_lin.shape[1] // HEAD_WIDTH
    query_rot = rotary_apply(
        query_lin.reshape(count_of_rows, -1, HEAD_WIDTH), cosine_table, sine_table
    ).astype(jnp.bfloat16)
    key_rot = (
        rotary_apply(key_lin.reshape(count_of_rows, kv_heads, HEAD_WIDTH), cosine_table, sine_table)
        .astype(jnp.bfloat16)
        .reshape(count_of_rows, -1)
    )
    value_low = value_lin.astype(jnp.bfloat16)
    keys_all, values_all = gather_pair((key_rot, value_low))
    group_size = query_rot.shape[1] // kv_heads
    query_heads = query_rot.reshape(count_of_rows, kv_heads, group_size, HEAD_WIDTH)
    key_heads = keys_all.reshape(-1, kv_heads, HEAD_WIDTH)
    value_heads = values_all.reshape(-1, kv_heads, HEAD_WIDTH)
    attended, log_totals = attention_forward(query_heads, key_heads, value_heads, places)
    attended_low = attended.reshape(count_of_rows, -1).astype(jnp.bfloat16)
    mixed = inputs + jnp.dot(attended_low, out_full, preferred_element_type=jnp.float32)
    normed_two = rms_scale(mixed, ffn_gain.astype(jnp.float32)).astype(jnp.bfloat16)
    gate = jnp.dot(normed_two, gate_full, preferred_element_type=jnp.float32)
    up_value = jnp.dot(normed_two, up_full, preferred_element_type=jnp.float32)
    hidden = (jax.nn.silu(gate) * up_value).astype(jnp.bfloat16)
    result = mixed + jnp.dot(hidden, down_full, preferred_element_type=jnp.float32)
    return (
        normalized_input,
        query_heads,
        key_heads,
        value_heads,
        attended,
        attended_low,
        log_totals,
        mixed,
        normed_two,
        gate,
        up_value,
        hidden,
        result,
    )


def general_local(
    tokens,
    block_map,
    attention_gain,
    query_weight,
    key_matrix,
    value_matrix,
    output_weight,
    feedforward_gain,
    gate_weight,
    up_weight,
    down_weight,
    out_grad,
):
    shards = (
        attention_gain,
        query_weight,
        key_matrix,
        value_matrix,
        output_weight,
        feedforward_gain,
        gate_weight,
        up_weight,
        down_weight,
    )
    count_of_rows = tokens.shape[1]
    ctx_rank = lax.axis_index("ctx")
    blocks = block_map[0]
    block_rows = count_of_rows // 2
    group_rows = blocks.shape[0] * block_rows
    prompt_rows = group_rows // 2
    natural = (
        blocks[:, None] * block_rows + jnp.arange(block_rows, dtype=jnp.int32)[None, :]
    ).reshape(-1)
    in_prompt = natural < prompt_rows
    key_pos = jnp.where(in_prompt, natural, prompt_rows + (natural - prompt_rows) % CONTINUE_LENGTH)
    key_seg = jnp.where(in_prompt, 0, 1 + (natural - prompt_rows) // CONTINUE_LENGTH)
    query_pos = lax.dynamic_slice_in_dim(key_pos, ctx_rank * count_of_rows, count_of_rows)
    query_seg = lax.dynamic_slice_in_dim(key_seg, ctx_rank * count_of_rows, count_of_rows)
    places = (query_pos, query_seg, key_pos, key_seg)
    cosine_table, sine_table = rope_tables(query_pos, HEAD_WIDTH)
    tables = (cosine_table, sine_table)
    inputs = tokens[0].astype(jnp.float32)
    full_weights = (
        lax.all_gather(shards[0], ("group", "wshard"), axis=0, tiled=True),
        lax.all_gather(shards[1], ("group", "wshard"), axis=0, tiled=True),
        lax.all_gather(shards[2], ("group", "wshard"), axis=0, tiled=True),
        lax.all_gather(shards[3], ("group", "wshard"), axis=0, tiled=True),
        lax.all_gather(shards[4], ("group", "wshard"), axis=0, tiled=True),
        lax.all_gather(shards[5], ("group", "wshard"), axis=0, tiled=True),
        lax.all_gather(shards[6], ("group", "wshard"), axis=0, tiled=True),
        lax.all_gather(shards[7], ("group", "wshard"), axis=0, tiled=True),
        lax.all_gather(shards[8], ("group", "wshard"), axis=0, tiled=True),
    )
    forward = forward_pass(
        full_weights,
        inputs,
        places,
        tables,
        lambda packed: jax.tree.map(
            lambda part, own: part.astype(own.dtype),
            lax.all_gather(as_sent(packed), "ctx", axis=0, tiled=True),
            packed,
        ),
    )
    layer_out = forward[12].astype(jnp.bfloat16)
    back_weights = (
        lax.all_gather(shards[0], ("group", "wshard"), axis=0, tiled=True),
        lax.all_gather(shards[1], ("group", "wshard"), axis=0, tiled=True),
        lax.all_gather(shards[2], ("group", "wshard"), axis=0, tiled=True),
        lax.all_gather(shards[3], ("group", "wshard"), axis=0, tiled=True),
        lax.all_gather(shards[4], ("group", "wshard"), axis=0, tiled=True),
        lax.all_gather(shards[5], ("group", "wshard"), axis=0, tiled=True),
        lax.all_gather(shards[6], ("group", "wshard"), axis=0, tiled=True),
        lax.all_gather(shards[7], ("group", "wshard"), axis=0, tiled=True),
        lax.all_gather(shards[8], ("group", "wshard"), axis=0, tiled=True),
    )
    saved = forward_pass(
        back_weights,
        inputs,
        places,
        tables,
        lambda packed: jax.tree.map(
            lambda part, own: part.astype(own.dtype),
            lax.all_gather(as_sent(packed), "ctx", axis=0, tiled=True),
            packed,
        ),
    )
    (
        normalized_input,
        query_heads,
        key_heads,
        value_heads,
        attended,
        attended_low,
        log_totals,
        mixed,
        normed_two,
        gate,
        up_value,
        hidden,
        result,
    ) = saved
    (
        attn_gain,
        query_full,
        key_complete,
        value_complete,
        out_full,
        ffn_gain,
        gate_full,
        up_full,
        down_full,
    ) = back_weights
    upstream = out_grad[0].astype(jnp.float32)
    ffn_grad = upstream.astype(jnp.bfloat16)
    grad_down = jnp.einsum("rf,rd->fd", hidden, ffn_grad, preferred_element_type=jnp.float32)
    hidden_grad = jnp.einsum("rd,fd->rf", ffn_grad, down_full, preferred_element_type=jnp.float32)
    gate_sigmoid = jax.nn.sigmoid(gate)
    gate_grad = (
        hidden_grad * up_value * gate_sigmoid * (1.0 + gate * (1.0 - gate_sigmoid))
    ).astype(jnp.bfloat16)
    up_grad = (hidden_grad * (gate * gate_sigmoid)).astype(jnp.bfloat16)
    grad_gate = jnp.einsum("rd,rf->df", normed_two, gate_grad, preferred_element_type=jnp.float32)
    grad_up = jnp.einsum("rd,rf->df", normed_two, up_grad, preferred_element_type=jnp.float32)
    normed_two_grad = jnp.einsum(
        "rf,df->rd", gate_grad, gate_full, preferred_element_type=jnp.float32
    ) + jnp.einsum("rf,df->rd", up_grad, up_full, preferred_element_type=jnp.float32)
    grad_ffn_gain, mixed_back = rms_back(mixed, ffn_gain.astype(jnp.float32), normed_two_grad)
    mixed_grad = upstream + mixed_back
    attn_grad = mixed_grad.astype(jnp.bfloat16)
    grad_out = jnp.einsum("rf,rd->fd", attended_low, attn_grad, preferred_element_type=jnp.float32)
    attended_grad = (
        jnp.einsum("rd,fd->rf", attn_grad, out_full, preferred_element_type=jnp.float32)
        .astype(jnp.bfloat16)
        .reshape(attended.shape)
    )
    query_grad, key_grad, value_grad = attention_backward(
        query_heads, key_heads, value_heads, places, attended_grad, attended, log_totals
    )
    key_local, value_local = (
        lax.psum_scatter(
            key_grad.astype(jnp.bfloat16), "ctx", scatter_dimension=0, tiled=True
        ).astype(jnp.float32),
        lax.psum_scatter(
            value_grad.astype(jnp.bfloat16), "ctx", scatter_dimension=0, tiled=True
        ).astype(jnp.float32),
    )
    query_lin_grad = (
        rotary_apply(query_grad.reshape(count_of_rows, -1, HEAD_WIDTH), cosine_table, -sine_table)
        .reshape(count_of_rows, -1)
        .astype(jnp.bfloat16)
    )
    key_lin_grad = (
        rotary_apply(key_local.reshape(count_of_rows, -1, HEAD_WIDTH), cosine_table, -sine_table)
        .reshape(count_of_rows, -1)
        .astype(jnp.bfloat16)
    )
    value_lin_grad = value_local.astype(jnp.bfloat16)
    grad_query = jnp.einsum(
        "rd,rf->df", normalized_input, query_lin_grad, preferred_element_type=jnp.float32
    )
    grad_key = jnp.einsum(
        "rd,rf->df", normalized_input, key_lin_grad, preferred_element_type=jnp.float32
    )
    grad_value = jnp.einsum(
        "rd,rf->df", normalized_input, value_lin_grad, preferred_element_type=jnp.float32
    )
    normed_grad = jnp.einsum(
        "rf,df->rd", query_lin_grad, query_full, preferred_element_type=jnp.float32
    )
    normed_grad = normed_grad + jnp.einsum(
        "rf,df->rd", key_lin_grad, key_complete, preferred_element_type=jnp.float32
    )
    normed_grad = normed_grad + jnp.einsum(
        "rf,df->rd", value_lin_grad, value_complete, preferred_element_type=jnp.float32
    )
    grad_attn_gain, input_back = rms_back(inputs, attn_gain.astype(jnp.float32), normed_grad)
    input_grad = mixed_grad + input_back
    partial_grads = (
        grad_attn_gain,
        grad_query,
        grad_key,
        grad_value,
        grad_out,
        grad_ffn_gain,
        grad_gate,
        grad_up,
        grad_down,
    )
    reduced = (
        lax.psum_scatter(
            partial_grads[0].astype(jnp.bfloat16),
            ("group", "wshard"),
            scatter_dimension=0,
            tiled=True,
        ).astype(jnp.float32),
        lax.psum_scatter(
            partial_grads[1].astype(jnp.bfloat16),
            ("group", "wshard"),
            scatter_dimension=0,
            tiled=True,
        ).astype(jnp.float32),
        lax.psum_scatter(
            partial_grads[2].astype(jnp.bfloat16),
            ("group", "wshard"),
            scatter_dimension=0,
            tiled=True,
        ).astype(jnp.float32),
        lax.psum_scatter(
            partial_grads[3].astype(jnp.bfloat16),
            ("group", "wshard"),
            scatter_dimension=0,
            tiled=True,
        ).astype(jnp.float32),
        lax.psum_scatter(
            partial_grads[4].astype(jnp.bfloat16),
            ("group", "wshard"),
            scatter_dimension=0,
            tiled=True,
        ).astype(jnp.float32),
        lax.psum_scatter(
            partial_grads[5].astype(jnp.bfloat16),
            ("group", "wshard"),
            scatter_dimension=0,
            tiled=True,
        ).astype(jnp.float32),
        lax.psum_scatter(
            partial_grads[6].astype(jnp.bfloat16),
            ("group", "wshard"),
            scatter_dimension=0,
            tiled=True,
        ).astype(jnp.float32),
        lax.psum_scatter(
            partial_grads[7].astype(jnp.bfloat16),
            ("group", "wshard"),
            scatter_dimension=0,
            tiled=True,
        ).astype(jnp.float32),
        lax.psum_scatter(
            partial_grads[8].astype(jnp.bfloat16),
            ("group", "wshard"),
            scatter_dimension=0,
            tiled=True,
        ).astype(jnp.float32),
    )
    summed = (
        lax.psum(reduced[0].astype(jnp.bfloat16), "ctx").astype(jnp.float32),
        lax.psum(reduced[1].astype(jnp.bfloat16), "ctx").astype(jnp.float32),
        lax.psum(reduced[2].astype(jnp.bfloat16), "ctx").astype(jnp.float32),
        lax.psum(reduced[3].astype(jnp.bfloat16), "ctx").astype(jnp.float32),
        lax.psum(reduced[4].astype(jnp.bfloat16), "ctx").astype(jnp.float32),
        lax.psum(reduced[5].astype(jnp.bfloat16), "ctx").astype(jnp.float32),
        lax.psum(reduced[6].astype(jnp.bfloat16), "ctx").astype(jnp.float32),
        lax.psum(reduced[7].astype(jnp.bfloat16), "ctx").astype(jnp.float32),
        lax.psum(reduced[8].astype(jnp.bfloat16), "ctx").astype(jnp.float32),
    )
    gain_attn, gain_ffn = (summed[0], summed[5])
    matrices = (summed[1], summed[2], summed[3], summed[4], summed[6], summed[7], summed[8])
    return (
        layer_out[None],
        input_grad[None],
        gain_attn,
        matrices[0],
        matrices[1],
        matrices[2],
        matrices[3],
        gain_ffn,
        matrices[4],
        matrices[5],
        matrices[6],
    )


SAFE_BOUND = 90.0
OWNERS = ("group", "wshard")
SWAP = [(0, 1), (1, 0)]


def exact_attention(seen, q, k, v, k_other, v_other, kv_heads, prompt_rows):
    rows = q.shape[1]
    heads = q.shape[0] // HEAD_WIDTH
    keys = jnp.concatenate([k_other, k], axis=1).reshape(kv_heads, HEAD_WIDTH, -1)
    values = jnp.concatenate([v_other, v], axis=1).reshape(kv_heads, HEAD_WIDTH, -1)
    at = jnp.arange(rows)
    in_prompt = at < prompt_rows
    piece = jnp.where(in_prompt, -1, (at - prompt_rows) // CONTINUE_LENGTH)
    own = (at[None, :] <= at[:, None]) & (in_prompt[None, :] | (piece[None, :] == piece[:, None]))
    other = jnp.broadcast_to(jnp.where(in_prompt, seen > 0, True)[:, None], (rows, k_other.shape[1]))
    allowed = jnp.concatenate([other, own], axis=1)

    def one_head(head):
        query = lax.dynamic_index_in_dim(q.reshape(heads, HEAD_WIDTH, rows), head, 0, False)
        key = lax.dynamic_index_in_dim(keys, head // (heads // kv_heads), 0, False)
        value = lax.dynamic_index_in_dim(values, head // (heads // kv_heads), 0, False)
        scores = jnp.where(allowed, contract(query, key, 0, 0), masked_score)
        top = jnp.max(scores, axis=1, keepdims=True)
        weights = jnp.exp2(scores - top)
        total = jnp.sum(weights, axis=1, keepdims=True)
        out = contract(value, (weights / total).astype(bf16), 1, 1)
        return out.astype(bf16), (top + jnp.log2(total))[:, 0]

    out, lse = lax.map(one_head, jnp.arange(heads))
    return out.reshape(q.shape), lse.reshape(kv_heads, heads // kv_heads, rows)


def swap(array):
    return lax.ppermute(array, "ctx", SWAP)


def fast_local(
    tokens, block_map, attention_gain, query_weight, key_matrix, value_matrix, output_weight,
    feedforward_gain, gate_weight, up_weight, down_weight, out_grad,
):
    x, dy = tokens[0], out_grad[0]
    rows, width = x.shape
    prompt_rows = rows // 2
    q_rows, kv_rows = query_weight.shape[1], key_matrix.shape[1]
    kv_heads = kv_rows // HEAD_WIDTH
    hidden = gate_weight.shape[1]
    shard_rows = query_weight.shape[0]
    block = lax.dynamic_index_in_dim(block_map[0], 2 * lax.axis_index("ctx"), 0, False)
    seen = (block > 0).astype(jnp.int32)
    prompt_total = block_map.shape[1] // 2 * prompt_rows

    depth = lax.axis_size("group")

    gains = jnp.pad(jnp.stack([attention_gain, feedforward_gain], axis=1), ((0, 0), (0, 126)))
    wide = lax.all_gather(
        jnp.concatenate([output_weight, gate_weight, up_weight], axis=1), OWNERS, axis=0, tiled=True
    )
    wd = lax.all_gather(down_weight, OWNERS, axis=0, tiled=True)
    shard = jnp.concatenate([query_weight, key_matrix, value_matrix, gains], axis=1)
    end = q_rows + 2 * kv_rows
    split = shard.shape[1] // 3 // 128 * 128
    first = gather_all(shard, depth, split).reshape(width, -1)
    gain_pair = first[:, end : end + 2].astype(f32).T
    gain_a, gain_f = gain_pair[0:1], gain_pair[1:2]

    at = jnp.arange(rows, dtype=jnp.int32)
    positions = jnp.where(
        at < prompt_rows, block * prompt_rows + at, prompt_total + (at - prompt_rows) % CONTINUE_LENGTH
    )
    half = HEAD_WIDTH // 2
    frequency = rope_base ** (-(jnp.arange(half, dtype=f32) * 2.0) / HEAD_WIDTH)
    angles = frequency[:, None] * positions.astype(f32)[None, :]
    cos, sin = jnp.cos(angles), jnp.sin(angles)

    q, k, v, h1, norm_q, norm_k = project(x, gain_a, first, cos, sin, q_rows, kv_rows)
    k_other, v_other = swap(k[:, :prompt_rows]), swap(v[:, :prompt_rows])
    acc = own_forward(q, k, v, kv_heads, prompt_rows)
    other_norm = jnp.max(jnp.sum(jnp.square(k_other.astype(f32)).reshape(kv_heads, HEAD_WIDTH, -1), axis=1))
    bound = jnp.max(norm_q) * jnp.maximum(jnp.max(norm_k), other_norm)
    o, lse = lax.cond(
        bound < SAFE_BOUND * SAFE_BOUND,
        lambda: other_forward(seen[None], q, k_other, v_other, acc, kv_heads, prompt_rows),
        lambda: exact_attention(seen, q, k, v, k_other, v_other, kv_heads, prompt_rows),
    )
    layer_out, h2, hid, dgate, dup, dattn, dob, delta, dgain_f = middle(
        x, dy, o, gain_f, wide, wd, kv_heads
    )
    scatter = lambda a: lax.psum_scatter(a, OWNERS, scatter_dimension=0, tiled=True)
    d_down = down_grads(dy, hid)
    d_wide = wide_grads(o, h2, dattn, dgate, dup)
    dob, d_down, d_wide = lax.optimization_barrier((dob, d_down, d_wide))
    d_down, d_wide = scatter(d_down), scatter(d_wide)
    dq_part, dk_other, dv_other = other_backward(
        seen[None], q, dob, lse, delta, k_other, v_other, kv_heads, prompt_rows
    )
    dk_in, dv_in = swap(dk_other), swap(dv_other)
    dq, dk, dv = own_backward(q, dob, lse, delta, k, v, dq_part, kv_heads, prompt_rows)

    def over_ctx(part):
        return part.astype(f32) + swap(part).astype(f32)

    d_down, d_wide, dq = lax.optimization_barrier((d_down, d_wide, dq))
    d_down, d_wide = over_ctx(d_down), over_ctx(d_wide)
    grad_tokens, d_first = finish(
        x, h1, dattn, gain_a, first, dq, dk, dv, dk_in, dv_in, cos, sin, dgain_f
    )
    d_first = reduce_all(d_first.reshape(4 * depth, shard_rows, -1), depth, split)
    return (
        layer_out[None],
        grad_tokens[None],
        d_first[:, end],
        d_first[:, :q_rows],
        d_first[:, q_rows : q_rows + kv_rows],
        d_first[:, q_rows + kv_rows : end],
        d_wide[:, 2 * hidden :],
        d_first[:, end + 1],
        d_wide[:, :hidden],
        d_wide[:, hidden : 2 * hidden],
        d_down,
    )


def local(mesh, tokens, block_map, *rest):
    block_rows = tokens.shape[1] // 2
    whole = (
        mesh.shape["ctx"] == 2
        and mesh.shape["wshard"] == 4
        and block_rows % CONTINUE_LENGTH == 0
        and tokens.shape[0] == 1
    )
    return (fast_local if whole else general_local)(tokens, block_map, *rest)


def solution(mesh):
    return jax.shard_map(
        lambda *args: local(mesh, *args),
        mesh=mesh,
        in_specs=(
            P(("group", "wshard"), "ctx", None),
            P(("group", "wshard"), None),
            P(("group", "wshard")),
            P(("group", "wshard"), None),
            P(("group", "wshard"), None),
            P(("group", "wshard"), None),
            P(("group", "wshard"), None),
            P(("group", "wshard")),
            P(("group", "wshard"), None),
            P(("group", "wshard"), None),
            P(("group", "wshard"), None),
            P(("group", "wshard"), "ctx", None),
        ),
        out_specs=(
            P(("group", "wshard"), "ctx", None),
            P(("group", "wshard"), "ctx", None),
            P(("group", "wshard")),
            P(("group", "wshard"), None),
            P(("group", "wshard"), None),
            P(("group", "wshard"), None),
            P(("group", "wshard"), None),
            P(("group", "wshard")),
            P(("group", "wshard"), None),
            P(("group", "wshard"), None),
            P(("group", "wshard"), None),
        ),
        check_vma=False,
    )
```

```python
import functools
import jax
import jax.numpy as jnp
from jax import lax
from jax.experimental import pallas as pl
from jax.experimental.pallas import tpu as pltpu
from jax.sharding import PartitionSpec as P

f32 = jnp.float32
bf16 = jnp.bfloat16
HEAD_WIDTH = 64
CONTINUE_LENGTH = 512
norm_eps = 1e-05
LOG2E = 1.4426950408889634
LN2 = 0.6931471805599453
MIB = 2**20


def contract(a, b, dim_a, dim_b):
    return lax.dot_general(
        a, b, (((dim_a,), (dim_b,)), ((), ())), preferred_element_type=f32
    )


def resident(shape):
    zeros = (0,) * len(shape)
    return pl.BlockSpec(shape, lambda *_: zeros, pipeline_mode=pl.Buffered(1))


def project_kernel(x_ref, gain_ref, w_ref, cos_ref, sin_ref, q_ref, k_ref, v_ref, kv_ref, nq_ref, nk_ref, *, prompt_steps):
    x = x_ref[...].astype(f32)
    inverse = lax.rsqrt(jnp.mean(x * x, axis=-1, keepdims=True) + norm_eps)
    h = (x * inverse * gain_ref[...]).astype(bf16)
    q_rows, kv_rows = q_ref.shape[0], k_ref.shape[0]
    half = HEAD_WIDTH // 2
    scale = LOG2E * HEAD_WIDTH**-0.5
    cos, sin = cos_ref[...], sin_ref[...]

    def rotated(lin, out_ref, base, cos, sin):
        worst = jnp.zeros((1, lin.shape[1]), f32)
        for head in range(lin.shape[0] // HEAD_WIDTH):
            at = head * HEAD_WIDTH
            a, b = lin[at : at + half], lin[at + half : at + HEAD_WIDTH]
            first = (a * cos - b * sin).astype(bf16)
            second = (b * cos + a * sin).astype(bf16)
            out_ref[base + at : base + at + half] = first
            out_ref[base + at + half : base + at + HEAD_WIDTH] = second
            fa, fb = first.astype(f32), second.astype(f32)
            worst = jnp.maximum(worst, jnp.sum(fa * fa + fb * fb, axis=0, keepdims=True))
        return worst

    ht = h.T
    chunk = kv_rows
    qc, qs = cos * scale, sin * scale
    worst_q = worst_k = None
    for at in range(0, q_rows + 2 * kv_rows, chunk):
        lin = contract(w_ref[:, at : at + chunk], ht, 0, 0)
        if at < q_rows:
            worst = rotated(lin, q_ref, at, qc, qs)
            worst_q = worst if worst_q is None else jnp.maximum(worst_q, worst)
        elif at < q_rows + kv_rows:
            worst = rotated(lin, k_ref, at - q_rows, cos, sin)
            worst_k = worst if worst_k is None else jnp.maximum(worst_k, worst)
        else:
            v_ref[pl.ds(at - q_rows - kv_rows, chunk)] = lin.astype(bf16)
    nq_ref[...] = worst_q
    nk_ref[...] = worst_k

    @pl.when(pl.program_id(0) < prompt_steps)
    def _():
        kv_ref[0] = k_ref[...]
        kv_ref[1] = v_ref[...]


def project(x, gain, w, cos, sin, q_rows, kv_rows, prompt_rows, tile=512):
    rows, width = x.shape
    prompt_steps = prompt_rows // tile
    cols = lambda n: pl.BlockSpec((n, tile), lambda i: (0, i))
    return pl.pallas_call(
        functools.partial(project_kernel, prompt_steps=prompt_steps),
        grid=(rows // tile,),
        in_specs=[
            pl.BlockSpec((tile, width), lambda i: (i, 0)),
            resident(gain.shape),
            resident(w.shape),
            cols(cos.shape[0]),
            cols(cos.shape[0]),
        ],
        out_specs=(
            cols(q_rows),
            cols(kv_rows),
            cols(kv_rows),
            pl.BlockSpec((2, kv_rows, tile), lambda i: (0, 0, jnp.minimum(i, prompt_steps - 1))),
            cols(1),
            cols(1),
        ),
        out_shape=(
            jax.ShapeDtypeStruct((q_rows, rows), bf16),
            jax.ShapeDtypeStruct((kv_rows, rows), bf16),
            jax.ShapeDtypeStruct((kv_rows, rows), bf16),
            jax.ShapeDtypeStruct((2, kv_rows, prompt_rows), bf16),
            jax.ShapeDtypeStruct((1, rows), f32),
            jax.ShapeDtypeStruct((1, rows), f32),
        ),
        compiler_params=pltpu.CompilerParams(vmem_limit_bytes=60 * MIB),
        name="project",
    )(x, gain, w, cos, sin)


ONES = 16
SAFE_BOUND = 80.0
FAR = -1e30


def causal(keys, columns):
    return lax.broadcasted_iota(jnp.int32, (keys, columns), 0) <= lax.broadcasted_iota(
        jnp.int32, (keys, columns), 1
    )


def masked(tile, fill):
    step = tile.shape[0]
    front = jnp.where(causal(step, step), tile[:, :step], fill)
    return front if tile.shape[1] == step else jnp.concatenate([front, tile[:, step:]], axis=1)


def strips(prompt_rows, rows, step):
    tiles = []
    at = 0
    while at < rows:
        end = prompt_rows if at < prompt_rows else at + CONTINUE_LENGTH
        tiles += [(end - key, key, end) for key in range(at, end, step)]
        at = end
    room, laid = [], []
    for width, key, end in sorted(tiles, reverse=True):
        for strip in range(len(room) + 1):
            if strip == len(room):
                room.append(rows - prompt_rows)
            if room[strip] >= width:
                laid.append((key, key, end, strip, rows - prompt_rows - room[strip]))
                room[strip] -= width
                break
    return sorted(laid), len(room) * step


def in_parts(row):
    high = row.astype(bf16)
    rest = row - high.astype(f32)
    middle = rest.astype(bf16)
    low = (rest - middle.astype(f32)).astype(bf16)
    return jnp.concatenate([high, middle, low, jnp.zeros((ONES - 3, row.shape[1]), bf16)], axis=0)


def widened(matrix):
    return jnp.concatenate([matrix, jnp.ones((matrix.shape[0], ONES), bf16)], axis=1)


def head_rows(head):
    return slice(head * HEAD_WIDTH, (head + 1) * HEAD_WIDTH)


def own_forward_kernel(
    q_ref, k_ref, v_ref, nq_ref, nk_ref, acc_ref, top_ref, p_ref, query_ref, keys_ref, values_ref,
    *, group, prompt_rows, step
):
    rows = q_ref.shape[1]
    wide = HEAD_WIDTH + ONES
    tiles, _ = strips(prompt_rows, rows, step)

    keys_ref[...] = widened(k_ref[...].T)
    values_ref[:HEAD_WIDTH] = v_ref[...]
    values_ref[HEAD_WIDTH:] = jnp.ones((ONES, rows), bf16)
    top_ref[...] = jnp.zeros_like(top_ref)
    for head in range(group):
        query_ref[head, :HEAD_WIDTH] = q_ref[head_rows(head)]
        query_ref[head, HEAD_WIDTH:] = jnp.zeros((ONES, rows), bf16)

    @pl.when(jnp.max(nq_ref[...]) * jnp.max(nk_ref[...]) >= SAFE_BOUND * SAFE_BOUND)
    def _():
        for head in range(group):
            top_ref[0, head : head + 1] = jnp.full((1, rows), FAR, f32)
            for key, first, end, _, _ in tiles:
                scores = masked(contract(keys_ref[key : key + step], query_ref[head, :, first:end], 1, 0), FAR)
                top_ref[0, head : head + 1, first:end] = jnp.maximum(
                    top_ref[0, head : head + 1, first:end], jnp.max(scores, axis=0, keepdims=True)
                )
            scores = contract(keys_ref[:prompt_rows], query_ref[head, :, prompt_rows:], 1, 0)
            top_ref[0, head : head + 1, prompt_rows:] = jnp.maximum(
                top_ref[0, head : head + 1, prompt_rows:], jnp.max(scores, axis=0, keepdims=True)
            )
        for head in range(group):
            query_ref[head, HEAD_WIDTH:] = in_parts(-top_ref[0, head : head + 1])

    for head in range(group):
        weights = jnp.exp2(contract(keys_ref[:prompt_rows], query_ref[head, :, prompt_rows:], 1, 0)).astype(bf16)
        p_ref[head, :prompt_rows] = weights
        acc_ref[head * wide : (head + 1) * wide, prompt_rows:] = contract(
            values_ref[:, :prompt_rows], weights, 1, 0
        )
    for key, first, end, strip, column in tiles:
        for head in range(group):
            scores = contract(keys_ref[key : key + step], query_ref[head, :, first:end], 1, 0)
            weights = masked(jnp.exp2(scores), 0.0).astype(bf16)
            row = prompt_rows + strip * step
            p_ref[head, row : row + step, column : column + end - first] = weights
            part = contract(values_ref[:, key : key + step], weights, 1, 0)
            at = slice(head * wide, (head + 1) * wide)
            if key == 0:
                acc_ref[at, first:end] = part
            else:
                acc_ref[at, first:end] += part


def own_forward(q, k, v, norm_q, norm_k, kv_heads, prompt_rows, step=256):
    rows = q.shape[1]
    group = q.shape[0] // HEAD_WIDTH // kv_heads
    wide = HEAD_WIDTH + ONES
    block = lambda n: pl.BlockSpec((n, rows), lambda h: (h, 0))
    _, strip_rows = strips(prompt_rows, rows, step)
    assert strip_rows == prompt_rows
    shape = jax.ShapeDtypeStruct
    return pl.pallas_call(
        functools.partial(own_forward_kernel, group=group, prompt_rows=prompt_rows, step=step),
        grid=(kv_heads,),
        in_specs=[
            block(group * HEAD_WIDTH), block(HEAD_WIDTH), block(HEAD_WIDTH), resident(norm_q.shape), resident(norm_k.shape)
        ],
        out_specs=(
            block(group * wide),
            pl.BlockSpec((1, group, rows), lambda h: (h, 0, 0)),
            pl.BlockSpec((group, 2 * prompt_rows, rows - prompt_rows), lambda h: (h, 0, 0)),
        ),
        scratch_shapes=[
            pltpu.VMEM((group, wide, rows), bf16),
            pltpu.VMEM((rows, wide), bf16),
            pltpu.VMEM((wide, rows), bf16),
        ],
        out_shape=(
            shape((kv_heads * group * wide, rows), f32),
            shape((kv_heads, group, rows), f32),
            shape((kv_heads * group, 2 * prompt_rows, rows - prompt_rows), bf16),
        ),
        compiler_params=pltpu.CompilerParams(vmem_limit_bytes=60 * MIB),
        name="own_forward",
    )(q, k, v, norm_q, norm_k)


def other_forward_kernel(
    seen_ref, q_ref, k_ref, v_ref, nq_ref, acc_ref, top_ref, o_ref, own_ref, far_ref, p_ref, query_ref, keys_ref,
    values_ref, *, group, prompt_rows
):
    rows = q_ref.shape[1]
    wide = HEAD_WIDTH + ONES
    seen = seen_ref[0] > 0
    key = k_ref[0].astype(f32)
    norm_k = jnp.max(jnp.sum(key * key, axis=0, keepdims=True))
    slow = jnp.max(nq_ref[...]) * norm_k >= SAFE_BOUND * SAFE_BOUND
    keys_ref[...] = widened(k_ref[0].T)
    values_ref[:HEAD_WIDTH] = v_ref[0]
    values_ref[HEAD_WIDTH:] = jnp.ones((ONES, keys_ref.shape[0]), bf16)
    for head in range(group):
        query_ref[head, :HEAD_WIDTH] = q_ref[head_rows(head)]
        query_ref[head, HEAD_WIDTH:] = jnp.zeros((ONES, rows), bf16)
    far_ref[...] = jnp.zeros_like(far_ref)

    @pl.when(slow)
    def _():
        for head in range(group):
            for first, end in ((0, prompt_rows), (prompt_rows, rows)):
                scores = contract(keys_ref[...], query_ref[head, :, first:end], 1, 0)
                far_ref[0, head : head + 1, first:end] = jnp.max(scores, axis=0, keepdims=True)
            query_ref[head, HEAD_WIDTH:] = in_parts(-far_ref[0, head : head + 1])

    def finish(first, end, with_other):
        for head in range(group):
            own = acc_ref[head * wide : (head + 1) * wide, first:end]
            own_top = top_ref[0, head : head + 1, first:end]
            if with_other:
                weights = jnp.exp2(contract(keys_ref[...], query_ref[head, :, first:end], 1, 0)).astype(bf16)
                p_ref[head, :, first:end] = weights
                far = contract(values_ref[...], weights, 1, 0)
                far_top = far_ref[0, head : head + 1, first:end]
                top = jnp.maximum(own_top, far_top)
                own_scale, far_scale = jnp.exp2(own_top - top), jnp.exp2(far_top - top)
                total = own * own_scale + far * far_scale
                inverse = 1.0 / total[HEAD_WIDTH : HEAD_WIDTH + 1]
                far_ref[0, head : head + 1, first:end] = far_scale * inverse
                own_ref[0, head : head + 1, first:end] = own_scale * inverse
            else:
                total = own
                inverse = 1.0 / total[HEAD_WIDTH : HEAD_WIDTH + 1]
                far_ref[0, head : head + 1, first:end] = jnp.zeros_like(inverse)
                own_ref[0, head : head + 1, first:end] = inverse
            o_ref[head_rows(head), first:end] = (total[:HEAD_WIDTH] * inverse).astype(bf16)

    finish(prompt_rows, rows, True)

    @pl.when(seen)
    def _():
        finish(0, prompt_rows, True)

    @pl.when(jnp.logical_not(seen))
    def _():
        finish(0, prompt_rows, False)


def half_index(h, j, seen):
    return (h, 0, 1 - j * jnp.minimum(seen[0], 1))


def other_forward(seen, q, kv, norm_q, acc, top, kv_heads, prompt_rows):
    rows = q.shape[1]
    group = q.shape[0] // HEAD_WIDTH // kv_heads
    wide = HEAD_WIDTH + ONES
    keys = kv.shape[2]
    block = lambda n, m: pl.BlockSpec((n, m), lambda h, s: (h, 0))
    row_block = pl.BlockSpec((1, group, rows), lambda h, s: (h, 0, 0))
    shape = jax.ShapeDtypeStruct
    return pl.pallas_call(
        functools.partial(other_forward_kernel, group=group, prompt_rows=prompt_rows),
        grid_spec=pltpu.PrefetchScalarGridSpec(
            num_scalar_prefetch=1,
            grid=(kv_heads,),
            in_specs=[
                block(group * HEAD_WIDTH, rows),
                pl.BlockSpec((1, HEAD_WIDTH, keys), lambda h, s: (0, h, 0)),
                pl.BlockSpec((1, HEAD_WIDTH, keys), lambda h, s: (1, h, 0)),
                resident(norm_q.shape),
                block(group * wide, rows),
                row_block,
            ],
            out_specs=(
                block(group * HEAD_WIDTH, rows),
                row_block,
                row_block,
                pl.BlockSpec((group, keys, rows), lambda h, s: (h, 0, 0)),
            ),
            scratch_shapes=[
                pltpu.VMEM((group, wide, rows), bf16),
                pltpu.VMEM((keys, wide), bf16),
                pltpu.VMEM((wide, keys), bf16),
            ],
        ),
        out_shape=(
            shape(q.shape, bf16),
            shape((kv_heads, group, rows), f32),
            shape((kv_heads, group, rows), f32),
            shape((kv_heads * group, keys, rows), bf16),
        ),
        compiler_params=pltpu.CompilerParams(vmem_limit_bytes=60 * MIB),
        name="other_forward",
    )(seen, q, kv, kv, norm_q, acc, top)


def tile_backward(values, key_rows, weights, query, grad):
    slopes = contract(values, grad, 1, 0)
    slopes = (weights.astype(f32) * slopes).astype(bf16)
    query_grad = contract(key_rows, slopes, 1, 0)
    key_grad = contract(query, slopes, 1, 1)
    value_grad = contract(grad[:HEAD_WIDTH], weights, 1, 1)
    return query_grad, key_grad, value_grad


def fill_grads(g_ref, scale_ref, delta_ref, grad_ref, group):
    for head in range(group):
        scale = scale_ref[0, head : head + 1]
        grad_ref[head, :HEAD_WIDTH] = (g_ref[head_rows(head)].astype(f32) * scale).astype(bf16)
        grad_ref[head, HEAD_WIDTH:] = in_parts(-delta_ref[0, head : head + 1] * scale)


def other_backward_kernel(
    seen_ref, q_ref, g_ref, scale_ref, delta_ref, k_ref, v_ref, p_ref, dq_ref, dkv_ref,
    grad_ref, values_ref, dk_sum, dv_sum, dq_sum, *, group, prompt_rows, step
):
    rows = q_ref.shape[1]
    seen = seen_ref[0] > 0
    stage = pl.program_id(1)

    def part(first, last, fresh):
        for low in range(0, k_ref.shape[2], step):
            span = slice(low, low + step)
            key_sum = value_sum = None
            for head in range(group):
                query_grad, key_grad, value_grad = tile_backward(
                    values_ref[span], k_ref[0, :, span], p_ref[head, span],
                    q_ref[head_rows(head), first:last], grad_ref[head, :, first:last],
                )
                if low == 0:
                    dq_sum[head_rows(head), first:last] = query_grad
                else:
                    dq_sum[head_rows(head), first:last] += query_grad
                key_sum = key_grad if key_sum is None else key_sum + key_grad
                value_sum = value_grad if value_sum is None else value_sum + value_grad
            if fresh:
                dk_sum[:, span] = key_sum
                dv_sum[:, span] = value_sum
            else:
                dk_sum[:, span] += key_sum
                dv_sum[:, span] += value_sum

    @pl.when(stage == 0)
    def _():
        fill_grads(g_ref, scale_ref, delta_ref, grad_ref, group)
        values_ref[...] = widened(v_ref[0].T)
        part(prompt_rows, rows, True)

    @pl.when((stage == 1) & seen)
    def _():
        part(0, prompt_rows, False)

    @pl.when((stage == 1) & jnp.logical_not(seen))
    def _():
        dq_sum[:, :prompt_rows] = jnp.zeros((dq_ref.shape[0], prompt_rows), f32)

    @pl.when(stage == 1)
    def _():
        dq_ref[...] = dq_sum[...].astype(bf16)
        dkv_ref[0] = dk_sum[...].astype(bf16)
        dkv_ref[1] = dv_sum[...].astype(bf16)


def other_backward(seen, q, g, scale, delta, kv, p, kv_heads, prompt_rows, step=256):
    rows = q.shape[1]
    group = q.shape[0] // HEAD_WIDTH // kv_heads
    keys = kv.shape[2]
    block = lambda n, m: pl.BlockSpec((n, m), lambda h, j, s: (h, 0))
    row_block = pl.BlockSpec((1, group, rows), lambda h, j, s: (h, 0, 0))
    wide = group * HEAD_WIDTH
    shape = jax.ShapeDtypeStruct
    return pl.pallas_call(
        functools.partial(other_backward_kernel, group=group, prompt_rows=prompt_rows, step=step),
        grid_spec=pltpu.PrefetchScalarGridSpec(
            num_scalar_prefetch=1,
            grid=(kv_heads, 2),
            in_specs=[
                block(wide, rows), block(wide, rows), row_block, row_block,
                pl.BlockSpec((1, HEAD_WIDTH, keys), lambda h, j, s: (0, h, 0)),
                pl.BlockSpec((1, HEAD_WIDTH, keys), lambda h, j, s: (1, h, 0)),
                pl.BlockSpec((group, keys, prompt_rows), half_index),
            ],
            out_specs=(block(wide, rows), pl.BlockSpec((2, HEAD_WIDTH, keys), lambda h, j, s: (0, h, 0))),
            scratch_shapes=[
                pltpu.VMEM((group, HEAD_WIDTH + ONES, rows), bf16),
                pltpu.VMEM((keys, HEAD_WIDTH + ONES), bf16),
                pltpu.VMEM((HEAD_WIDTH, keys), f32),
                pltpu.VMEM((HEAD_WIDTH, keys), f32),
                pltpu.VMEM((wide, rows), f32),
            ],
        ),
        out_shape=(shape(q.shape, bf16), shape(kv.shape, bf16)),
        compiler_params=pltpu.CompilerParams(vmem_limit_bytes=60 * MIB),
        name="other_backward",
    )(seen, q, g, scale, delta, kv, kv, p)


def own_backward_kernel(
    q_ref, g_ref, scale_ref, delta_ref, k_ref, v_ref, p_ref, dq_in_ref, dq_ref, dk_ref, dv_ref,
    grad_ref, values_ref, dk_sum, dv_sum, dq_sum, *, group, prompt_rows, step
):
    rows = q_ref.shape[1]
    stage = pl.program_id(1)
    tiles, _ = strips(prompt_rows, rows, step)

    def one(key, first, end, place, columns):
        span = slice(key, key + step)
        key_sum = value_sum = None
        for head in range(group):
            query_grad, key_grad, value_grad = tile_backward(
                values_ref[span], k_ref[:, span], p_ref[head, place, columns],
                q_ref[head_rows(head), first:end], grad_ref[head, :, first:end],
            )
            dq_sum[head_rows(head), first:end] += query_grad
            key_sum = key_grad if key_sum is None else key_sum + key_grad
            value_sum = value_grad if value_sum is None else value_sum + value_grad
        dk_sum[:, span] += key_sum
        dv_sum[:, span] += value_sum

    @pl.when(stage == 0)
    def _():
        fill_grads(g_ref, scale_ref, delta_ref, grad_ref, group)
        values_ref[...] = widened(v_ref[...].T)
        dq_sum[...] = dq_in_ref[...].astype(f32)
        dk_sum[...] = jnp.zeros_like(dk_sum)
        dv_sum[...] = jnp.zeros_like(dv_sum)
        for key in range(0, prompt_rows, step):
            one(key, prompt_rows, rows, slice(key, key + step), slice(0, rows - prompt_rows))

    @pl.when(stage == 1)
    def _():
        for key, first, end, strip, column in tiles:
            one(key, first, end, slice(strip * step, (strip + 1) * step), slice(column, column + end - first))
        dq_ref[...] = dq_sum[...].astype(bf16)
        dk_ref[...] = dk_sum[...].astype(bf16)
        dv_ref[...] = dv_sum[...].astype(bf16)


def own_backward(q, g, scale, delta, k, v, p, dq, kv_heads, prompt_rows, step=256):
    rows = q.shape[1]
    group = q.shape[0] // HEAD_WIDTH // kv_heads
    block = lambda n: pl.BlockSpec((n, rows), lambda h, j: (h, 0))
    row_block = pl.BlockSpec((1, group, rows), lambda h, j: (h, 0, 0))
    wide = group * HEAD_WIDTH
    shape = jax.ShapeDtypeStruct
    return pl.pallas_call(
        functools.partial(own_backward_kernel, group=group, prompt_rows=prompt_rows, step=step),
        grid=(kv_heads, 2),
        in_specs=[
            block(wide), block(wide), row_block, row_block, block(HEAD_WIDTH), block(HEAD_WIDTH),
            pl.BlockSpec((group, prompt_rows, rows - prompt_rows), lambda h, j: (h, j, 0)),
            block(wide),
        ],
        out_specs=(block(wide), block(HEAD_WIDTH), block(HEAD_WIDTH)),
        scratch_shapes=[
            pltpu.VMEM((group, HEAD_WIDTH + ONES, rows), bf16),
            pltpu.VMEM((rows, HEAD_WIDTH + ONES), bf16),
            pltpu.VMEM((HEAD_WIDTH, rows), f32),
            pltpu.VMEM((HEAD_WIDTH, rows), f32),
            pltpu.VMEM((wide, rows), f32),
        ],
        out_shape=(shape(q.shape, bf16), shape(k.shape, bf16), shape(v.shape, bf16)),
        compiler_params=pltpu.CompilerParams(vmem_limit_bytes=60 * MIB),
        name="own_backward",
    )(q, g, scale, delta, k, v, p, dq)


def middle_kernel(
    x_ref, dy_ref, o_ref, gain_ref, wide_any, wd_any,
    out_ref, h2_ref, hidden_ref, dgate_ref, dup_ref, dattn_ref, dob_ref, delta_ref, dgain_ref,
    wo_ref, wg_ref, wu_ref, wd_ref, sems, *, chunk
):
    step = pl.program_id(0)
    inner, total = wo_ref.shape[1], wg_ref.shape[1]
    copies = [
        pltpu.make_async_copy(source, target, sems.at[i])
        for i, (source, target) in enumerate(
            (
                (wide_any.at[:, pl.ds(0, inner)], wo_ref),
                (wide_any.at[:, pl.ds(inner, total)], wg_ref),
                (wide_any.at[:, pl.ds(inner + total, total)], wu_ref),
                (wd_any, wd_ref),
            )
        )
    ]

    @pl.when(step == 0)
    def _():
        for copy in copies:
            copy.start()
        dgain_ref[...] = jnp.zeros_like(dgain_ref)
        copies[0].wait()

    ob = o_ref[...]
    x1 = x_ref[...].astype(f32) + contract(ob, wo_ref[...], 0, 0)
    inverse = lax.rsqrt(jnp.mean(x1 * x1, axis=-1, keepdims=True) + norm_eps)
    gain = gain_ref[...]
    h2 = (x1 * inverse * gain).astype(bf16)
    h2_ref[...] = h2
    dy = dy_ref[...]

    @pl.when(step == 0)
    def _():
        for copy in copies[1:]:
            copy.wait()

    result = x1
    dh2 = None
    for low in range(0, wg_ref.shape[1], chunk):
        span = slice(low, low + chunk)
        gate = contract(h2, wg_ref[:, span], 1, 0)
        up = contract(h2, wu_ref[:, span], 1, 0)
        dhidden = contract(dy, wd_ref[span], 1, 1)
        sigma = 0.5 + 0.5 * jnp.tanh(0.5 * gate)
        silu = gate * sigma
        hidden = (silu * up).astype(bf16)
        hidden_ref[:, span] = hidden
        result = result + contract(hidden, wd_ref[span], 1, 0)
        dgate = (dhidden * up * sigma * (1.0 + gate * (1.0 - sigma))).astype(bf16)
        dup = (dhidden * silu).astype(bf16)
        dgate_ref[:, span] = dgate
        dup_ref[:, span] = dup
        part = contract(dgate, wg_ref[:, span], 1, 1) + contract(dup, wu_ref[:, span], 1, 1)
        dh2 = part if dh2 is None else dh2 + part
    out_ref[...] = result.astype(bf16)
    dgain_ref[...] += jnp.sum(dh2 * x1 * inverse, axis=0, keepdims=True)
    u = dh2 * gain
    dx1 = dy.astype(f32) + inverse * u - x1 * (inverse * inverse * inverse) * jnp.mean(
        u * x1, axis=-1, keepdims=True
    )
    dattn = dx1.astype(bf16)
    dattn_ref[...] = dattn
    dob = contract(wo_ref[...], dattn, 1, 1).astype(bf16)
    dob_ref[...] = dob
    product = dob.astype(f32) * ob.astype(f32)
    heads, group = delta_ref.shape[0], delta_ref.shape[1]
    for kv in range(heads):
        for member in range(group):
            at = (kv * group + member) * HEAD_WIDTH
            delta_ref[kv, member : member + 1] = jnp.sum(
                product[at : at + HEAD_WIDTH], axis=0, keepdims=True
            )


def middle(x, dy, o, gain, wide, wd, kv_heads, tile=256, chunk=768):
    rows, width = x.shape
    hidden = wd.shape[0]
    q_rows = o.shape[0]
    group = q_rows // HEAD_WIDTH // kv_heads
    by_row = lambda n: pl.BlockSpec((tile, n), lambda i: (i, 0))
    any_spec = pl.BlockSpec(memory_space=pl.ANY)
    shape = jax.ShapeDtypeStruct
    return pl.pallas_call(
        functools.partial(middle_kernel, chunk=chunk),
        grid=(rows // tile,),
        in_specs=[by_row(width), by_row(width), pl.BlockSpec((q_rows, tile), lambda i: (0, i)),
                  resident(gain.shape)] + [any_spec] * 2,
        out_specs=(
            by_row(width), by_row(width), by_row(hidden), by_row(hidden), by_row(hidden), by_row(width),
            pl.BlockSpec((q_rows, tile), lambda i: (0, i)),
            pl.BlockSpec((kv_heads, group, tile), lambda i: (0, 0, i)),
            pl.BlockSpec((1, width), lambda i: (0, 0)),
        ),
        out_shape=(
            shape((rows, width), bf16), shape((rows, width), bf16), shape((rows, hidden), bf16),
            shape((rows, hidden), bf16), shape((rows, hidden), bf16), shape((rows, width), bf16),
            shape((q_rows, rows), bf16), shape((kv_heads, group, rows), f32), shape((1, width), f32),
        ),
        scratch_shapes=[pltpu.VMEM(s, bf16) for s in ((width, q_rows), (width, hidden), (width, hidden), wd.shape)]
        + [pltpu.SemaphoreType.DMA((4,))],
        compiler_params=pltpu.CompilerParams(vmem_limit_bytes=62 * MIB),
        name="middle",
    )(x, dy, o, gain, wide, wd)


def down_grads_kernel(dy_ref, hidden_ref, down_ref):
    down_ref[...] = contract(hidden_ref[...], dy_ref[...], 0, 0).astype(bf16)


def down_grads(dy, hidden, tile=512):
    rows, width = dy.shape
    total = hidden.shape[1]
    return pl.pallas_call(
        down_grads_kernel,
        grid=(total // tile,),
        in_specs=[resident(dy.shape), pl.BlockSpec((rows, tile), lambda i: (0, i))],
        out_specs=pl.BlockSpec((tile, width), lambda i: (i, 0)),
        out_shape=jax.ShapeDtypeStruct((total, width), bf16),
        compiler_params=pltpu.CompilerParams(vmem_limit_bytes=60 * MIB),
        name="down_grads",
    )(dy, hidden)


def wide_grads_kernel(o_ref, h2_ref, dgate_ref, dup_ref, dattn_ref, out_ref, *, each):
    step = pl.program_id(0)

    @pl.when(step < each)
    def _():
        out_ref[...] = contract(h2_ref[...], dgate_ref[...], 0, 0).astype(bf16)

    @pl.when((step >= each) & (step < 2 * each))
    def _():
        out_ref[...] = contract(h2_ref[...], dup_ref[...], 0, 0).astype(bf16)

    @pl.when(step >= 2 * each)
    def _():
        out_ref[...] = contract(o_ref[...], dattn_ref[...], 1, 0).astype(bf16)


def wide_grads(o, h2, dattn, dgate, dup, tile=512):
    rows, width = h2.shape
    total = dgate.shape[1]
    each = total // tile
    steps = 2 * each + pl.cdiv(width, tile)
    cols = lambda low, count: pl.BlockSpec((rows, tile), lambda i: (0, jnp.clip(i - low, 0, count - 1)))
    return pl.pallas_call(
        functools.partial(wide_grads_kernel, each=each),
        grid=(steps,),
        in_specs=[
            resident(o.shape), resident(h2.shape), cols(0, each), cols(each, each), cols(2 * each, steps - 2 * each)
        ],
        out_specs=pl.BlockSpec((width, tile), lambda i: (0, i)),
        out_shape=jax.ShapeDtypeStruct((width, 2 * total + width), bf16),
        compiler_params=pltpu.CompilerParams(vmem_limit_bytes=60 * MIB),
        name="wide_grads",
    )(o, h2, dgate, dup, dattn)


def finish_kernel(
    x_ref, dattn_ref, gain_ref, w_ref, dq_ref, dk_ref, dv_ref, dkv_in_ref, cos_ref, sin_ref,
    dgain_f_ref, out_ref, dw_ref, acc_ref, dgain_ref, *, prompt_steps
):
    step = pl.program_id(0)

    @pl.when(step == 0)
    def _():
        dgain_ref[...] = jnp.zeros_like(dgain_ref)
        acc_ref[...] = jnp.zeros_like(acc_ref)

    half = HEAD_WIDTH // 2
    cos, sin = cos_ref[...], sin_ref[...]

    def with_received(ref, which):
        return ref[...].astype(f32) + jnp.where(step < prompt_steps, dkv_in_ref[which].astype(f32), 0.0)

    def turned(value, scale):
        c, s = cos * scale, sin * scale
        pieces = []
        for at in range(0, value.shape[0], HEAD_WIDTH):
            a, b = value[at : at + half], value[at + half : at + HEAD_WIDTH]
            pieces += [a * c + b * s, b * c - a * s]
        return jnp.concatenate(pieces, axis=0)

    lin = jnp.concatenate(
        [
            turned(dq_ref[...].astype(f32), HEAD_WIDTH**-0.5),
            turned(with_received(dk_ref, 0), LN2),
            with_received(dv_ref, 1),
        ],
        axis=0,
    ).astype(bf16).T
    inner = lin.shape[1]
    x = x_ref[...].astype(f32)
    inverse = lax.rsqrt(jnp.mean(x * x, axis=-1, keepdims=True) + norm_eps)
    h = (x * inverse * gain_ref[...]).astype(bf16)
    acc_ref[...] += contract(h, lin, 0, 0)
    dh = contract(lin, w_ref[:, :inner], 1, 1)
    dgain_ref[0:1] += jnp.sum(dh * x * inverse, axis=0, keepdims=True)
    u = dh * gain_ref[...]
    out_ref[...] = (
        dattn_ref[...].astype(f32)
        + inverse * u
        - x * (inverse * inverse * inverse) * jnp.mean(u * x, axis=-1, keepdims=True)
    )

    @pl.when(step == pl.num_programs(0) - 1)
    def _():
        dw_ref[:, :inner] = acc_ref[...].astype(bf16)
        dgain_ref[1:2] = dgain_f_ref[...]
        dw_ref[:, inner:] = dgain_ref[...].T.astype(bf16)


def finish(x, dattn, gain, w, dq, dk, dv, dkv_in, cos, sin, dgain_f, tile=256):
    rows, width = x.shape
    by_row = pl.BlockSpec((tile, width), lambda i: (i, 0))
    cols = lambda n: pl.BlockSpec((n, tile), lambda i: (0, i))
    steps = dkv_in.shape[2] // tile
    few = pl.BlockSpec((2, dk.shape[0], tile), lambda i: (0, 0, jnp.minimum(i, steps - 1)))
    shape = jax.ShapeDtypeStruct
    inner = dq.shape[0] + dk.shape[0] + dv.shape[0]
    return pl.pallas_call(
        functools.partial(finish_kernel, prompt_steps=steps),
        grid=(rows // tile,),
        in_specs=[by_row, by_row, resident(gain.shape), resident(w.shape),
                  cols(dq.shape[0]), cols(dk.shape[0]), cols(dv.shape[0]),
                  few,
                  cols(cos.shape[0]), cols(cos.shape[0]), resident(dgain_f.shape)],
        out_specs=(by_row, pl.BlockSpec(w.shape, lambda i: (0, 0))),
        out_shape=(shape((rows, width), f32), shape(w.shape, bf16)),
        scratch_shapes=[pltpu.VMEM((width, inner), f32), pltpu.VMEM((w.shape[1] - inner, width), f32)],
        compiler_params=pltpu.CompilerParams(vmem_limit_bytes=60 * MIB),
        name="finish",
    )(x, dattn, gain, w, dq, dk, dv, dkv_in, cos, sin, dgain_f)


def settle_kernel(first_ref, wide_ref, wide_in_ref, down_ref, down_in_ref, *outs, widths):
    refs = list(outs)
    at = 0
    for width in widths[0]:
        refs.pop(0)[...] = first_ref[:, at : at + width]
        at += width
    gains = first_ref[:, at:].T
    refs.pop(0)[...] = gains[0:1]
    refs.pop(0)[...] = gains[1:2]
    at = 0
    for width in widths[1]:
        span = slice(at, at + width)
        refs.pop(0)[...] = wide_ref[:, span].astype(f32) + wide_in_ref[:, span].astype(f32)
        at += width
    refs.pop(0)[...] = down_ref[...].astype(f32) + down_in_ref[...].astype(f32)


def settle(first, wide, wide_in, down, down_in, first_widths, wide_widths):
    rows = first.shape[0]
    shape = jax.ShapeDtypeStruct
    return pl.pallas_call(
        functools.partial(settle_kernel, widths=(first_widths, wide_widths)),
        out_shape=[shape((rows, n), f32) for n in first_widths]
        + [shape((1, rows), f32)] * 2
        + [shape((rows, n), f32) for n in wide_widths]
        + [shape(down.shape, f32)],
        compiler_params=pltpu.CompilerParams(vmem_limit_bytes=60 * MIB),
        name="settle",
    )(first, wide, wide_in, down, down_in)


MESH_ID = pl.DeviceIdType.MESH


def whereabouts():
    z, y, w = lax.axis_index("group"), lax.axis_index("ctx"), lax.axis_index("wshard")
    return z, y, w // 2, w % 2


def device_at(z, y, x, core):
    return (z, y, x * 2 + core)


def slot_at(z, x, core):
    return z * 4 + x * 2 + core


def greet(partners):
    barrier = pltpu.get_barrier_semaphore()
    for partner in partners:
        pl.semaphore_signal(barrier, inc=1, device_id=partner, device_id_type=MESH_ID)
    pl.semaphore_wait(barrier, len(partners))


def neighbours(depth):
    z, y, x, core = whereabouts()
    along = [device_at((z + d) % depth, y, x, core) for d in range(1, depth)]
    return along, device_at(z, y, 1 - x, core), device_at(z, 1 - y, x, core), device_at(z, y, x, 1 - core)


class Copies:
    def __init__(self, send_sems, recv_sems):
        self.send_sems, self.recv_sems, self.made = send_sems, recv_sems, []

    def make(self, source, target, device):
        at = len(self.made)
        copy = pltpu.make_async_remote_copy(
            src_ref=source,
            dst_ref=target,
            send_sem=self.send_sems.at[at],
            recv_sem=self.recv_sems.at[at],
            device_id=device,
            device_id_type=MESH_ID,
        )
        self.made.append(copy)
        return copy


def gather_kernel(shard_ref, out_ref, send_sems, recv_sems, own_sem, *, depth, split):
    z, y, x, core = whereabouts()
    along, over_x, over_y, over_core = neighbours(depth)
    columns = out_ref.shape[2]
    given = pl.ds(pl.multiple_of(y * (columns - split), 128), split)
    got = pl.ds(pl.multiple_of((1 - y) * (columns - split), 128), split)
    common = pl.ds(split, columns - 2 * split)
    me = slot_at(z, x, core)
    copies = Copies(send_sems, recv_sems)
    view = lambda slot, span: out_ref.at[slot, :, span]

    own = pltpu.make_async_copy(shard_ref, out_ref.at[me], own_sem)
    own.start()
    own.wait()
    greet(along + [over_x, over_y, over_core])

    def send(slot, span, device):
        copy = copies.make(view(slot, span), view(slot, span), device)
        copy.start()
        return copy

    spans = (given, common)
    from_z, from_x, from_y, from_core = {}, {}, {}, []

    def onward(slot, part, d, side):
        if side == 0:
            from_x[d, part] = send(slot, spans[part], over_x)
        if part == 0:
            from_y[d, side] = send(slot, given, over_y)
        from_core.append(send(slot, spans[part], over_core))

    for part in range(2):
        for d in range(1, depth):
            from_z[d, part] = send(me, spans[part], along[d - 1])
        onward(me, part, 0, 0)
    for part in range(2):
        for d in range(1, depth):
            from_z[d, part].wait_recv()
            onward(slot_at((z + depth - d) % depth, x, core), part, d, 0)
    for part in range(2):
        for d in range(depth):
            from_x[d, part].wait_recv()
            onward(slot_at((z + depth - d) % depth, 1 - x, core), part, d, 1)
    for side in range(2):
        for d in range(depth):
            from_y[d, side].wait_recv()
            slot = slot_at((z + depth - d) % depth, x if side == 0 else 1 - x, core)
            from_core.append(send(slot, got, over_core))
    for copy in from_core:
        copy.wait_recv()
    for copy in copies.made:
        copy.wait_send()


def gather_all(shard, depth, split):
    rows, columns = shard.shape
    count = 2 * (depth - 1) + 2 * depth + 2 * depth + 6 * depth
    return pl.pallas_call(
        functools.partial(gather_kernel, depth=depth, split=split),
        in_specs=[pl.BlockSpec(memory_space=pltpu.VMEM)],
        out_specs=pl.BlockSpec(memory_space=pltpu.VMEM),
        out_shape=jax.ShapeDtypeStruct((4 * depth, rows, columns), shard.dtype),
        scratch_shapes=[
            pltpu.SemaphoreType.DMA((count,)),
            pltpu.SemaphoreType.DMA((count,)),
            pltpu.SemaphoreType.DMA,
        ],
        compiler_params=pltpu.CompilerParams(
            collective_id=1, has_side_effects=True, vmem_limit_bytes=60 * MIB
        ),
        name="gather_all",
    )(shard)


def reduce_kernel(
    part_ref, out_ref, core_ref, sum_ref, x_ref, line_ref, z_ref, last_ref, twin_ref, send_sems, recv_sems, *, depth
):
    z, y, x, core = whereabouts()
    along, over_x, over_y, over_core = neighbours(depth)
    copies = Copies(send_sems, recv_sems)
    greet(along + [over_x, over_y, over_core])

    def send(source, target, device):
        copy = copies.make(source, target, device)
        copy.start()
        return copy

    distances = list(range(1, depth)) + [0]
    order = [(d, side) for side in (1, 0) for d in distances]
    place = lambda d, side: ((z + d) % depth, x if side == 0 else 1 - x)
    from_core = []
    for at, (d, side) in enumerate(order):
        to_z, to_x = place(d, side)
        from_core.append(send(part_ref.at[slot_at(to_z, to_x, 1 - core)], core_ref.at[at], over_core))
    from_x = []
    for at, (d, side) in enumerate(order):
        from_core[at].wait_recv()
        to_z, to_x = place(d, side)
        sum_ref[at] = (part_ref[slot_at(to_z, to_x, core)].astype(f32) + core_ref[at].astype(f32)).astype(bf16)
        if side == 1:
            from_x.append(send(sum_ref.at[at], x_ref.at[at], over_x))
    from_z = []
    for at, d in enumerate(distances):
        from_x[at].wait_recv()
        line_ref[at] = (sum_ref[depth + at].astype(f32) + x_ref[at].astype(f32)).astype(bf16)
        if d:
            from_z.append(send(line_ref.at[at], z_ref.at[at], along[d - 1]))
    total = line_ref[depth - 1].astype(f32)
    for at in range(depth - 1):
        from_z[at].wait_recv()
        total = total + z_ref[at].astype(f32)
    last_ref[...] = total.astype(bf16)
    twin = send(last_ref, twin_ref, over_y)
    twin.wait_recv()
    out_ref[...] = total + twin_ref[...].astype(f32)
    for copy in copies.made:
        copy.wait_send()


def reduce_all(parts, depth):
    slots, rows, columns = parts.shape
    count = 2 * depth + depth + depth - 1 + 1
    buffer = lambda *count: pltpu.VMEM(count + (rows, columns), bf16)
    return pl.pallas_call(
        functools.partial(reduce_kernel, depth=depth),
        in_specs=[pl.BlockSpec(memory_space=pltpu.VMEM)],
        out_specs=pl.BlockSpec(memory_space=pltpu.VMEM),
        out_shape=jax.ShapeDtypeStruct((rows, columns), f32),
        scratch_shapes=[
            buffer(2 * depth),
            buffer(2 * depth),
            buffer(depth),
            buffer(depth),
            buffer(depth - 1),
            buffer(),
            buffer(),
            pltpu.SemaphoreType.DMA((count,)),
            pltpu.SemaphoreType.DMA((count,)),
        ],
        compiler_params=pltpu.CompilerParams(
            collective_id=2, has_side_effects=True, vmem_limit_bytes=60 * MIB
        ),
        name="reduce_all",
    )(parts)


rope_base = 10000.0
masked_score = -1e30


def as_sent(array):

    def short(part):
        return part.astype(jnp.bfloat16) if part.dtype == jnp.float32 else part

    return jax.tree.map(short, array)


def rms_scale(value_rows_list, gain):
    return (
        value_rows_list
        * lax.rsqrt(jnp.mean(value_rows_list * value_rows_list, axis=-1, keepdims=True) + norm_eps)
        * gain
    )


def rms_back(value_rows_list, gain, upstream):
    inverse = lax.rsqrt(
        jnp.mean(value_rows_list * value_rows_list, axis=-1, keepdims=True) + norm_eps
    )
    scaled = upstream * gain
    gain_grad = jnp.sum(upstream * value_rows_list * inverse, axis=0)
    values_grad = inverse * scaled - value_rows_list * (inverse * inverse * inverse) * jnp.mean(
        scaled * value_rows_list, axis=-1, keepdims=True
    )
    return (gain_grad, values_grad)


def rope_tables(token_positions, head_size):
    half_size = head_size // 2
    frequency = rope_base ** (-(jnp.arange(half_size, dtype=jnp.float32) * 2.0) / head_size)
    angles = token_positions.astype(jnp.float32)[:, None] * frequency[None, :]
    return (jnp.cos(angles), jnp.sin(angles))


def rotary_apply(value_rows_list, cosine_table, sine_table):
    half_size = value_rows_list.shape[-1] // 2
    leading = value_rows_list[..., :half_size]
    trailing = value_rows_list[..., half_size:]
    cos_rows = cosine_table[:, None, :]
    sin_rows = sine_table[:, None, :]
    return jnp.concatenate(
        [leading * cos_rows - trailing * sin_rows, trailing * cos_rows + leading * sin_rows],
        axis=-1,
    )


def visible(query_pos, query_seg, key_pos, key_seg):
    same_doc = (key_seg[None, :] == query_seg[:, None]) | (key_seg[None, :] == 0)
    return same_doc & (key_pos[None, :] <= query_pos[:, None])


def tile_scores(query_tile, key_tile, scale):
    return (
        jnp.einsum("rhgd,khd->hgrk", query_tile, key_tile, preferred_element_type=jnp.float32)
        * scale
    )


def key_tiling(key_heads, value_heads, key_pos, key_seg):
    key_block = min(256, key_heads.shape[0])
    tile_count = key_heads.shape[0] // key_block
    return (
        key_heads.reshape(tile_count, key_block, key_heads.shape[1], key_heads.shape[2]),
        value_heads.reshape(tile_count, key_block, value_heads.shape[1], value_heads.shape[2]),
        key_pos.reshape(tile_count, key_block),
        key_seg.reshape(tile_count, key_block),
    )


def query_split(value_rows_list, query_block):
    return value_rows_list.reshape(
        (value_rows_list.shape[0] // query_block, query_block) + value_rows_list.shape[1:]
    )


def attention_forward(query_heads, key_heads, value_heads, places):
    query_pos, query_seg, key_pos, key_seg = places
    count_of_rows, kv_heads, group_size, head_size = query_heads.shape
    scale = head_size ** (-0.5)
    query_block = min(512, count_of_rows)
    key_tiles, value_tiles, kpos_tiles, kseg_tiles = key_tiling(
        key_heads, value_heads, key_pos, key_seg
    )

    def one_block(block_item):
        query_tile, tile_pos, tile_seg = block_item
        state_shape = (kv_heads, group_size, query_tile.shape[0])

        def lse_step(running, tile_item):
            key_tile, tile_kpos, tile_kseg = tile_item
            allowed = visible(tile_pos, tile_seg, tile_kpos, tile_kseg)

            def lse_open_tile(state):
                row_top, row_total = state
                scores = jnp.where(allowed, tile_scores(query_tile, key_tile, scale), masked_score)
                new_top = jnp.maximum(row_top, jnp.max(scores, axis=-1))
                weights = jnp.where(allowed, jnp.exp(scores - new_top[..., None]), 0.0)
                return (new_top, row_total * jnp.exp(row_top - new_top) + jnp.sum(weights, axis=-1))

            def lse_closed_tile(state):
                return state

            return (lax.cond(jnp.any(allowed), lse_open_tile, lse_closed_tile, running), None)

        initial = (
            jnp.full(state_shape, masked_score, jnp.float32),
            jnp.zeros(state_shape, jnp.float32),
        )
        (row_top, row_total), _ = lax.scan(lse_step, initial, (key_tiles, kpos_tiles, kseg_tiles))
        log_total = row_top + jnp.log(row_total)

        def out_step(running, tile_item):
            key_tile, value_tile, tile_kpos, tile_kseg = tile_item
            allowed = visible(tile_pos, tile_seg, tile_kpos, tile_kseg)

            def out_open_tile(accumulated):
                scores = jnp.where(allowed, tile_scores(query_tile, key_tile, scale), masked_score)
                probabilities = jnp.where(
                    allowed, jnp.exp(scores - log_total[..., None]), 0.0
                ).astype(jnp.bfloat16)
                return accumulated + jnp.einsum(
                    "hgrk,khd->rhgd", probabilities, value_tile, preferred_element_type=jnp.float32
                )

            def out_closed_tile(accumulated):
                return accumulated

            return (lax.cond(jnp.any(allowed), out_open_tile, out_closed_tile, running), None)

        output, _ = lax.scan(
            out_step,
            jnp.zeros(query_tile.shape, jnp.float32),
            (key_tiles, value_tiles, kpos_tiles, kseg_tiles),
        )
        return (output, log_total)

    outputs, log_totals = lax.map(
        one_block,
        (
            query_split(query_heads, query_block),
            query_split(query_pos, query_block),
            query_split(query_seg, query_block),
        ),
    )
    return (outputs.reshape(query_heads.shape), log_totals)


def attention_backward(
    query_heads, key_heads, value_heads, places, attended_grad, attended, log_totals
):
    query_pos, query_seg, key_pos, key_seg = places
    count_of_rows, kv_heads, group_size, head_size = query_heads.shape
    scale = head_size ** (-0.5)
    query_block = min(512, count_of_rows)
    key_tiles, value_tiles, kpos_tiles, kseg_tiles = key_tiling(
        key_heads, value_heads, key_pos, key_seg
    )

    def block_grads(sums, block_item):
        query_tile, grad_tile, output_tile, tile_lse, tile_pos, tile_seg = block_item
        tile_delta = jnp.einsum("rhgd,rhgd->hgr", grad_tile.astype(jnp.float32), output_tile)

        def back_step(query_grad, tile_item):
            key_tile, value_tile, tile_kpos, tile_kseg = tile_item
            allowed = visible(tile_pos, tile_seg, tile_kpos, tile_kseg)

            def back_open_tile(query_grad):
                scores = jnp.where(allowed, tile_scores(query_tile, key_tile, scale), masked_score)
                probabilities = jnp.where(allowed, jnp.exp(scores - tile_lse[..., None]), 0.0)
                prob_grad = jnp.einsum(
                    "rhgd,khd->hgrk", grad_tile, value_tile, preferred_element_type=jnp.float32
                )
                score_grad = (probabilities * (prob_grad - tile_delta[..., None])).astype(
                    jnp.bfloat16
                )
                query_grad = query_grad + scale * jnp.einsum(
                    "hgrk,khd->rhgd", score_grad, key_tile, preferred_element_type=jnp.float32
                )
                key_part = scale * jnp.einsum(
                    "hgrk,rhgd->khd", score_grad, query_tile, preferred_element_type=jnp.float32
                )
                value_part = jnp.einsum(
                    "hgrk,rhgd->khd",
                    probabilities.astype(jnp.bfloat16),
                    grad_tile,
                    preferred_element_type=jnp.float32,
                )
                return (query_grad, key_part, value_part)

            def back_closed_tile(query_grad):
                return (
                    query_grad,
                    jnp.zeros(key_tile.shape, jnp.float32),
                    jnp.zeros(value_tile.shape, jnp.float32),
                )

            query_grad, key_part, value_part = lax.cond(
                jnp.any(allowed), back_open_tile, back_closed_tile, query_grad
            )
            return (query_grad, (key_part, value_part))

        query_grad, (key_parts, value_parts) = lax.scan(
            back_step,
            jnp.zeros(query_tile.shape, jnp.float32),
            (key_tiles, value_tiles, kpos_tiles, kseg_tiles),
        )
        return ((sums[0] + key_parts, sums[1] + value_parts), query_grad)

    initial = (jnp.zeros(key_tiles.shape, jnp.float32), jnp.zeros(value_tiles.shape, jnp.float32))
    block_items = (
        query_split(query_heads, query_block),
        query_split(attended_grad, query_block),
        query_split(attended, query_block),
        log_totals,
        query_split(query_pos, query_block),
        query_split(query_seg, query_block),
    )
    (key_sum, value_sum), query_grads = lax.scan(block_grads, initial, block_items)
    key_rows = key_heads.shape[0]
    return (
        query_grads.reshape(query_heads.shape),
        key_sum.reshape(key_rows, -1),
        value_sum.reshape(key_rows, -1),
    )


def forward_pass(weights, inputs, places, tables, gather_pair):
    (
        attn_gain,
        query_full,
        key_complete,
        value_complete,
        out_full,
        ffn_gain,
        gate_full,
        up_full,
        down_full,
    ) = weights
    cosine_table, sine_table = tables
    count_of_rows = inputs.shape[0]
    normalized_input = rms_scale(inputs, attn_gain.astype(jnp.float32)).astype(jnp.bfloat16)
    query_lin = jnp.dot(normalized_input, query_full, preferred_element_type=jnp.float32)
    key_lin = jnp.dot(normalized_input, key_complete, preferred_element_type=jnp.float32)
    value_lin = jnp.dot(normalized_input, value_complete, preferred_element_type=jnp.float32)
    kv_heads = key_lin.shape[1] // HEAD_WIDTH
    query_rot = rotary_apply(
        query_lin.reshape(count_of_rows, -1, HEAD_WIDTH), cosine_table, sine_table
    ).astype(jnp.bfloat16)
    key_rot = (
        rotary_apply(key_lin.reshape(count_of_rows, kv_heads, HEAD_WIDTH), cosine_table, sine_table)
        .astype(jnp.bfloat16)
        .reshape(count_of_rows, -1)
    )
    value_low = value_lin.astype(jnp.bfloat16)
    keys_all, values_all = gather_pair((key_rot, value_low))
    group_size = query_rot.shape[1] // kv_heads
    query_heads = query_rot.reshape(count_of_rows, kv_heads, group_size, HEAD_WIDTH)
    key_heads = keys_all.reshape(-1, kv_heads, HEAD_WIDTH)
    value_heads = values_all.reshape(-1, kv_heads, HEAD_WIDTH)
    attended, log_totals = attention_forward(query_heads, key_heads, value_heads, places)
    attended_low = attended.reshape(count_of_rows, -1).astype(jnp.bfloat16)
    mixed = inputs + jnp.dot(attended_low, out_full, preferred_element_type=jnp.float32)
    normed_two = rms_scale(mixed, ffn_gain.astype(jnp.float32)).astype(jnp.bfloat16)
    gate = jnp.dot(normed_two, gate_full, preferred_element_type=jnp.float32)
    up_value = jnp.dot(normed_two, up_full, preferred_element_type=jnp.float32)
    hidden = (jax.nn.silu(gate) * up_value).astype(jnp.bfloat16)
    result = mixed + jnp.dot(hidden, down_full, preferred_element_type=jnp.float32)
    return (
        normalized_input,
        query_heads,
        key_heads,
        value_heads,
        attended,
        attended_low,
        log_totals,
        mixed,
        normed_two,
        gate,
        up_value,
        hidden,
        result,
    )


def general_local(
    tokens,
    block_map,
    attention_gain,
    query_weight,
    key_matrix,
    value_matrix,
    output_weight,
    feedforward_gain,
    gate_weight,
    up_weight,
    down_weight,
    out_grad,
):
    shards = (
        attention_gain,
        query_weight,
        key_matrix,
        value_matrix,
        output_weight,
        feedforward_gain,
        gate_weight,
        up_weight,
        down_weight,
    )
    count_of_rows = tokens.shape[1]
    ctx_rank = lax.axis_index("ctx")
    blocks = block_map[0]
    block_rows = count_of_rows // 2
    group_rows = blocks.shape[0] * block_rows
    prompt_rows = group_rows // 2
    natural = (
        blocks[:, None] * block_rows + jnp.arange(block_rows, dtype=jnp.int32)[None, :]
    ).reshape(-1)
    in_prompt = natural < prompt_rows
    key_pos = jnp.where(in_prompt, natural, prompt_rows + (natural - prompt_rows) % CONTINUE_LENGTH)
    key_seg = jnp.where(in_prompt, 0, 1 + (natural - prompt_rows) // CONTINUE_LENGTH)
    query_pos = lax.dynamic_slice_in_dim(key_pos, ctx_rank * count_of_rows, count_of_rows)
    query_seg = lax.dynamic_slice_in_dim(key_seg, ctx_rank * count_of_rows, count_of_rows)
    places = (query_pos, query_seg, key_pos, key_seg)
    cosine_table, sine_table = rope_tables(query_pos, HEAD_WIDTH)
    tables = (cosine_table, sine_table)
    inputs = tokens[0].astype(jnp.float32)
    full_weights = (
        lax.all_gather(shards[0], ("group", "wshard"), axis=0, tiled=True),
        lax.all_gather(shards[1], ("group", "wshard"), axis=0, tiled=True),
        lax.all_gather(shards[2], ("group", "wshard"), axis=0, tiled=True),
        lax.all_gather(shards[3], ("group", "wshard"), axis=0, tiled=True),
        lax.all_gather(shards[4], ("group", "wshard"), axis=0, tiled=True),
        lax.all_gather(shards[5], ("group", "wshard"), axis=0, tiled=True),
        lax.all_gather(shards[6], ("group", "wshard"), axis=0, tiled=True),
        lax.all_gather(shards[7], ("group", "wshard"), axis=0, tiled=True),
        lax.all_gather(shards[8], ("group", "wshard"), axis=0, tiled=True),
    )
    forward = forward_pass(
        full_weights,
        inputs,
        places,
        tables,
        lambda packed: jax.tree.map(
            lambda part, own: part.astype(own.dtype),
            lax.all_gather(as_sent(packed), "ctx", axis=0, tiled=True),
            packed,
        ),
    )
    layer_out = forward[12].astype(jnp.bfloat16)
    back_weights = (
        lax.all_gather(shards[0], ("group", "wshard"), axis=0, tiled=True),
        lax.all_gather(shards[1], ("group", "wshard"), axis=0, tiled=True),
        lax.all_gather(shards[2], ("group", "wshard"), axis=0, tiled=True),
        lax.all_gather(shards[3], ("group", "wshard"), axis=0, tiled=True),
        lax.all_gather(shards[4], ("group", "wshard"), axis=0, tiled=True),
        lax.all_gather(shards[5], ("group", "wshard"), axis=0, tiled=True),
        lax.all_gather(shards[6], ("group", "wshard"), axis=0, tiled=True),
        lax.all_gather(shards[7], ("group", "wshard"), axis=0, tiled=True),
        lax.all_gather(shards[8], ("group", "wshard"), axis=0, tiled=True),
    )
    saved = forward_pass(
        back_weights,
        inputs,
        places,
        tables,
        lambda packed: jax.tree.map(
            lambda part, own: part.astype(own.dtype),
            lax.all_gather(as_sent(packed), "ctx", axis=0, tiled=True),
            packed,
        ),
    )
    (
        normalized_input,
        query_heads,
        key_heads,
        value_heads,
        attended,
        attended_low,
        log_totals,
        mixed,
        normed_two,
        gate,
        up_value,
        hidden,
        result,
    ) = saved
    (
        attn_gain,
        query_full,
        key_complete,
        value_complete,
        out_full,
        ffn_gain,
        gate_full,
        up_full,
        down_full,
    ) = back_weights
    upstream = out_grad[0].astype(jnp.float32)
    ffn_grad = upstream.astype(jnp.bfloat16)
    grad_down = jnp.einsum("rf,rd->fd", hidden, ffn_grad, preferred_element_type=jnp.float32)
    hidden_grad = jnp.einsum("rd,fd->rf", ffn_grad, down_full, preferred_element_type=jnp.float32)
    gate_sigmoid = jax.nn.sigmoid(gate)
    gate_grad = (
        hidden_grad * up_value * gate_sigmoid * (1.0 + gate * (1.0 - gate_sigmoid))
    ).astype(jnp.bfloat16)
    up_grad = (hidden_grad * (gate * gate_sigmoid)).astype(jnp.bfloat16)
    grad_gate = jnp.einsum("rd,rf->df", normed_two, gate_grad, preferred_element_type=jnp.float32)
    grad_up = jnp.einsum("rd,rf->df", normed_two, up_grad, preferred_element_type=jnp.float32)
    normed_two_grad = jnp.einsum(
        "rf,df->rd", gate_grad, gate_full, preferred_element_type=jnp.float32
    ) + jnp.einsum("rf,df->rd", up_grad, up_full, preferred_element_type=jnp.float32)
    grad_ffn_gain, mixed_back = rms_back(mixed, ffn_gain.astype(jnp.float32), normed_two_grad)
    mixed_grad = upstream + mixed_back
    attn_grad = mixed_grad.astype(jnp.bfloat16)
    grad_out = jnp.einsum("rf,rd->fd", attended_low, attn_grad, preferred_element_type=jnp.float32)
    attended_grad = (
        jnp.einsum("rd,fd->rf", attn_grad, out_full, preferred_element_type=jnp.float32)
        .astype(jnp.bfloat16)
        .reshape(attended.shape)
    )
    query_grad, key_grad, value_grad = attention_backward(
        query_heads, key_heads, value_heads, places, attended_grad, attended, log_totals
    )
    key_local, value_local = (
        lax.psum_scatter(
            key_grad.astype(jnp.bfloat16), "ctx", scatter_dimension=0, tiled=True
        ).astype(jnp.float32),
        lax.psum_scatter(
            value_grad.astype(jnp.bfloat16), "ctx", scatter_dimension=0, tiled=True
        ).astype(jnp.float32),
    )
    query_lin_grad = (
        rotary_apply(query_grad.reshape(count_of_rows, -1, HEAD_WIDTH), cosine_table, -sine_table)
        .reshape(count_of_rows, -1)
        .astype(jnp.bfloat16)
    )
    key_lin_grad = (
        rotary_apply(key_local.reshape(count_of_rows, -1, HEAD_WIDTH), cosine_table, -sine_table)
        .reshape(count_of_rows, -1)
        .astype(jnp.bfloat16)
    )
    value_lin_grad = value_local.astype(jnp.bfloat16)
    grad_query = jnp.einsum(
        "rd,rf->df", normalized_input, query_lin_grad, preferred_element_type=jnp.float32
    )
    grad_key = jnp.einsum(
        "rd,rf->df", normalized_input, key_lin_grad, preferred_element_type=jnp.float32
    )
    grad_value = jnp.einsum(
        "rd,rf->df", normalized_input, value_lin_grad, preferred_element_type=jnp.float32
    )
    normed_grad = jnp.einsum(
        "rf,df->rd", query_lin_grad, query_full, preferred_element_type=jnp.float32
    )
    normed_grad = normed_grad + jnp.einsum(
        "rf,df->rd", key_lin_grad, key_complete, preferred_element_type=jnp.float32
    )
    normed_grad = normed_grad + jnp.einsum(
        "rf,df->rd", value_lin_grad, value_complete, preferred_element_type=jnp.float32
    )
    grad_attn_gain, input_back = rms_back(inputs, attn_gain.astype(jnp.float32), normed_grad)
    input_grad = mixed_grad + input_back
    partial_grads = (
        grad_attn_gain,
        grad_query,
        grad_key,
        grad_value,
        grad_out,
        grad_ffn_gain,
        grad_gate,
        grad_up,
        grad_down,
    )
    reduced = (
        lax.psum_scatter(
            partial_grads[0].astype(jnp.bfloat16),
            ("group", "wshard"),
            scatter_dimension=0,
            tiled=True,
        ).astype(jnp.float32),
        lax.psum_scatter(
            partial_grads[1].astype(jnp.bfloat16),
            ("group", "wshard"),
            scatter_dimension=0,
            tiled=True,
        ).astype(jnp.float32),
        lax.psum_scatter(
            partial_grads[2].astype(jnp.bfloat16),
            ("group", "wshard"),
            scatter_dimension=0,
            tiled=True,
        ).astype(jnp.float32),
        lax.psum_scatter(
            partial_grads[3].astype(jnp.bfloat16),
            ("group", "wshard"),
            scatter_dimension=0,
            tiled=True,
        ).astype(jnp.float32),
        lax.psum_scatter(
            partial_grads[4].astype(jnp.bfloat16),
            ("group", "wshard"),
            scatter_dimension=0,
            tiled=True,
        ).astype(jnp.float32),
        lax.psum_scatter(
            partial_grads[5].astype(jnp.bfloat16),
            ("group", "wshard"),
            scatter_dimension=0,
            tiled=True,
        ).astype(jnp.float32),
        lax.psum_scatter(
            partial_grads[6].astype(jnp.bfloat16),
            ("group", "wshard"),
            scatter_dimension=0,
            tiled=True,
        ).astype(jnp.float32),
        lax.psum_scatter(
            partial_grads[7].astype(jnp.bfloat16),
            ("group", "wshard"),
            scatter_dimension=0,
            tiled=True,
        ).astype(jnp.float32),
        lax.psum_scatter(
            partial_grads[8].astype(jnp.bfloat16),
            ("group", "wshard"),
            scatter_dimension=0,
            tiled=True,
        ).astype(jnp.float32),
    )
    summed = (
        lax.psum(reduced[0].astype(jnp.bfloat16), "ctx").astype(jnp.float32),
        lax.psum(reduced[1].astype(jnp.bfloat16), "ctx").astype(jnp.float32),
        lax.psum(reduced[2].astype(jnp.bfloat16), "ctx").astype(jnp.float32),
        lax.psum(reduced[3].astype(jnp.bfloat16), "ctx").astype(jnp.float32),
        lax.psum(reduced[4].astype(jnp.bfloat16), "ctx").astype(jnp.float32),
        lax.psum(reduced[5].astype(jnp.bfloat16), "ctx").astype(jnp.float32),
        lax.psum(reduced[6].astype(jnp.bfloat16), "ctx").astype(jnp.float32),
        lax.psum(reduced[7].astype(jnp.bfloat16), "ctx").astype(jnp.float32),
        lax.psum(reduced[8].astype(jnp.bfloat16), "ctx").astype(jnp.float32),
    )
    gain_attn, gain_ffn = (summed[0], summed[5])
    matrices = (summed[1], summed[2], summed[3], summed[4], summed[6], summed[7], summed[8])
    return (
        layer_out[None],
        input_grad[None],
        gain_attn,
        matrices[0],
        matrices[1],
        matrices[2],
        matrices[3],
        gain_ffn,
        matrices[4],
        matrices[5],
        matrices[6],
    )


OWNERS = ("group", "wshard")
SWAP = [(0, 1), (1, 0)]


def swap(array):
    return lax.ppermute(array, "ctx", SWAP)


def fast_local(
    tokens, block_map, attention_gain, query_weight, key_matrix, value_matrix, output_weight,
    feedforward_gain, gate_weight, up_weight, down_weight, out_grad,
):
    x, dy = tokens[0], out_grad[0]
    rows, width = x.shape
    prompt_rows = rows // 2
    q_rows, kv_rows = query_weight.shape[1], key_matrix.shape[1]
    kv_heads = kv_rows // HEAD_WIDTH
    hidden = gate_weight.shape[1]
    shard_rows = query_weight.shape[0]
    block = lax.dynamic_index_in_dim(block_map[0], 2 * lax.axis_index("ctx"), 0, False)
    seen = (block > 0).astype(jnp.int32)
    prompt_total = block_map.shape[1] // 2 * prompt_rows

    depth = lax.axis_size("group")

    gains = jnp.pad(jnp.stack([attention_gain, feedforward_gain], axis=1), ((0, 0), (0, 126)))
    wide = lax.all_gather(
        jnp.concatenate([output_weight, gate_weight, up_weight], axis=1), OWNERS, axis=0, tiled=True
    )
    wd = lax.all_gather(down_weight, OWNERS, axis=0, tiled=True)
    shard = jnp.concatenate([query_weight, key_matrix, value_matrix, gains], axis=1)
    end = q_rows + 2 * kv_rows
    split = shard.shape[1] // 3 // 128 * 128
    first = gather_all(shard, depth, split).reshape(width, -1)
    gain_pair = first[:, end : end + 2].astype(f32).T
    gain_a, gain_f = gain_pair[0:1], gain_pair[1:2]

    at = jnp.arange(rows, dtype=jnp.int32)
    positions = jnp.where(
        at < prompt_rows, block * prompt_rows + at, prompt_total + (at - prompt_rows) % CONTINUE_LENGTH
    )
    half = HEAD_WIDTH // 2
    frequency = rope_base ** (-(jnp.arange(half, dtype=f32) * 2.0) / HEAD_WIDTH)
    angles = frequency[:, None] * positions.astype(f32)[None, :]
    cos, sin = jnp.cos(angles), jnp.sin(angles)

    q, k, v, kv, norm_q, norm_k = project(x, gain_a, first, cos, sin, q_rows, kv_rows, prompt_rows)
    kv_other = swap(kv)
    acc, top, p_own = own_forward(q, k, v, norm_q, norm_k, kv_heads, prompt_rows)
    o, own_scale, far_scale, p_far = other_forward(seen[None], q, kv_other, norm_q, acc, top, kv_heads, prompt_rows)
    layer_out, h2, hid, dgate, dup, dattn, dob, delta, dgain_f = middle(x, dy, o, gain_f, wide, wd, kv_heads)
    scatter = lambda a: lax.psum_scatter(a, OWNERS, scatter_dimension=0, tiled=True)
    d_down = down_grads(dy, hid)
    h2, d_down = lax.optimization_barrier((h2, d_down))
    d_down = scatter(d_down)
    d_wide = wide_grads(o, h2, dattn, dgate, dup)
    dob, d_wide = lax.optimization_barrier((dob, d_wide))
    d_wide = scatter(d_wide)
    dq, dkv_far = other_backward(seen[None], q, dob, far_scale, delta, kv_other, p_far, kv_heads, prompt_rows)
    dkv_in = swap(dkv_far)
    d_down, dkv_in = lax.optimization_barrier((d_down, dkv_in))
    d_down_in = swap(d_down)
    dq, dk, dv = own_backward(q, dob, own_scale, delta, k, v, p_own, dq, kv_heads, prompt_rows)
    grad_tokens, d_first = finish(x, dattn, gain_a, first, dq, dk, dv, dkv_in, cos, sin, dgain_f)
    d_first, d_wide = lax.optimization_barrier((d_first, d_wide))
    d_wide_in = swap(d_wide)
    d_first = reduce_all(d_first.reshape(4 * depth, shard_rows, -1), depth)
    d_q, d_k, d_v, d_gain_a, d_gain_f, d_gate, d_up, d_out, d_down = settle(
        d_first, d_wide, d_wide_in, d_down, d_down_in, (q_rows, kv_rows, kv_rows), (hidden, hidden, q_rows)
    )
    return (
        layer_out[None],
        grad_tokens[None],
        d_gain_a[0],
        d_q,
        d_k,
        d_v,
        d_out,
        d_gain_f[0],
        d_gate,
        d_up,
        d_down,
    )


def local(mesh, tokens, block_map, *rest):
    block_rows = tokens.shape[1] // 2
    whole = (
        mesh.shape["ctx"] == 2
        and mesh.shape["wshard"] == 4
        and block_rows % CONTINUE_LENGTH == 0
        and tokens.shape[0] == 1
    )
    return (fast_local if whole else general_local)(tokens, block_map, *rest)


def solution(mesh):
    return jax.shard_map(
        lambda *args: local(mesh, *args),
        mesh=mesh,
        in_specs=(
            P(("group", "wshard"), "ctx", None),
            P(("group", "wshard"), None),
            P(("group", "wshard")),
            P(("group", "wshard"), None),
            P(("group", "wshard"), None),
            P(("group", "wshard"), None),
            P(("group", "wshard"), None),
            P(("group", "wshard")),
            P(("group", "wshard"), None),
            P(("group", "wshard"), None),
            P(("group", "wshard"), None),
            P(("group", "wshard"), "ctx", None),
        ),
        out_specs=(
            P(("group", "wshard"), "ctx", None),
            P(("group", "wshard"), "ctx", None),
            P(("group", "wshard")),
            P(("group", "wshard"), None),
            P(("group", "wshard"), None),
            P(("group", "wshard"), None),
            P(("group", "wshard"), None),
            P(("group", "wshard")),
            P(("group", "wshard"), None),
            P(("group", "wshard"), None),
            P(("group", "wshard"), None),
        ),
        check_vma=False,
    )
```

```python
import functools
import jax
import jax.numpy as jnp
from jax import lax
from jax.experimental import pallas as pl
from jax.experimental.pallas import tpu as pltpu
from jax.sharding import PartitionSpec as P

f32 = jnp.float32
bf16 = jnp.bfloat16
HEAD_WIDTH = 64
CONTINUE_LENGTH = 512
norm_eps = 1e-05
LOG2E = 1.4426950408889634
LN2 = 0.6931471805599453
MIB = 2**20


def contract(a, b, dim_a, dim_b):
    return lax.dot_general(
        a, b, (((dim_a,), (dim_b,)), ((), ())), preferred_element_type=f32
    )


def resident(shape):
    zeros = (0,) * len(shape)
    return pl.BlockSpec(shape, lambda *_: zeros, pipeline_mode=pl.Buffered(1))


def project_kernel(
    x_ref, w_ref, cos_ref, sin_ref, q_ref, k_ref, v_ref, kv_ref, nq_ref, nk_ref, gains_ref, *, prompt_steps
):
    @pl.when(pl.program_id(0) == 0)
    def _():
        gains_ref[...] = w_ref[:, w_ref.shape[1] - 128 :].astype(f32).T[: gains_ref.shape[0]]

    x = x_ref[...].astype(f32)
    inverse = lax.rsqrt(jnp.mean(x * x, axis=-1, keepdims=True) + norm_eps)
    h = (x * inverse * gains_ref[0:1]).astype(bf16)
    q_rows, kv_rows = q_ref.shape[0], k_ref.shape[0]
    half = HEAD_WIDTH // 2
    scale = LOG2E * HEAD_WIDTH**-0.5
    cos, sin = cos_ref[...], sin_ref[...]

    def rotated(lin, out_ref, base, cos, sin):
        worst = jnp.zeros((1, lin.shape[1]), f32)
        for head in range(lin.shape[0] // HEAD_WIDTH):
            at = head * HEAD_WIDTH
            a, b = lin[at : at + half], lin[at + half : at + HEAD_WIDTH]
            first = (a * cos - b * sin).astype(bf16)
            second = (b * cos + a * sin).astype(bf16)
            out_ref[base + at : base + at + half] = first
            out_ref[base + at + half : base + at + HEAD_WIDTH] = second
            fa, fb = first.astype(f32), second.astype(f32)
            worst = jnp.maximum(worst, jnp.sum(fa * fa + fb * fb, axis=0, keepdims=True))
        return worst

    ht = h.T
    chunk = kv_rows
    qc, qs = cos * scale, sin * scale
    worst_q = worst_k = None
    for at in range(0, q_rows + 2 * kv_rows, chunk):
        lin = contract(w_ref[:, at : at + chunk], ht, 0, 0)
        if at < q_rows:
            worst = rotated(lin, q_ref, at, qc, qs)
            worst_q = worst if worst_q is None else jnp.maximum(worst_q, worst)
        elif at < q_rows + kv_rows:
            worst = rotated(lin, k_ref, at - q_rows, cos, sin)
            worst_k = worst if worst_k is None else jnp.maximum(worst_k, worst)
        else:
            v_ref[pl.ds(at - q_rows - kv_rows, chunk)] = lin.astype(bf16)
    nq_ref[...] = worst_q
    nk_ref[...] = worst_k

    @pl.when(pl.program_id(0) < prompt_steps)
    def _():
        kv_ref[0] = k_ref[...]
        kv_ref[1] = v_ref[...]


def project(x, w, cos, sin, q_rows, kv_rows, prompt_rows, tile=512):
    rows, width = x.shape
    prompt_steps = prompt_rows // tile
    cols = lambda n: pl.BlockSpec((n, tile), lambda i: (0, i))
    return pl.pallas_call(
        functools.partial(project_kernel, prompt_steps=prompt_steps),
        grid=(rows // tile,),
        in_specs=[
            pl.BlockSpec((tile, width), lambda i: (i, 0)),
            resident(w.shape),
            cols(cos.shape[0]),
            cols(cos.shape[0]),
        ],
        out_specs=(
            cols(q_rows),
            cols(kv_rows),
            cols(kv_rows),
            pl.BlockSpec((2, kv_rows, tile), lambda i: (0, 0, jnp.minimum(i, prompt_steps - 1))),
            cols(1),
            cols(1),
            pl.BlockSpec((8, width), lambda i: (0, 0)),
        ),
        out_shape=(
            jax.ShapeDtypeStruct((q_rows, rows), bf16),
            jax.ShapeDtypeStruct((kv_rows, rows), bf16),
            jax.ShapeDtypeStruct((kv_rows, rows), bf16),
            jax.ShapeDtypeStruct((2, kv_rows, prompt_rows), bf16),
            jax.ShapeDtypeStruct((1, rows), f32),
            jax.ShapeDtypeStruct((1, rows), f32),
            jax.ShapeDtypeStruct((8, width), f32),
        ),
        compiler_params=pltpu.CompilerParams(vmem_limit_bytes=60 * MIB),
        name="project",
    )(x, w, cos, sin)


ONES = 16
SAFE_BOUND = 80.0
FAR = -1e30


def causal(keys, columns):
    return lax.broadcasted_iota(jnp.int32, (keys, columns), 0) <= lax.broadcasted_iota(
        jnp.int32, (keys, columns), 1
    )


def masked(tile, fill):
    step = tile.shape[0]
    front = jnp.where(causal(step, step), tile[:, :step], fill)
    return front if tile.shape[1] == step else jnp.concatenate([front, tile[:, step:]], axis=1)


def strips(prompt_rows, rows, step):
    tiles = []
    at = 0
    while at < rows:
        end = prompt_rows if at < prompt_rows else at + CONTINUE_LENGTH
        tiles += [(end - key, key, end) for key in range(at, end, step)]
        at = end
    room, laid = [], []
    for width, key, end in sorted(tiles, reverse=True):
        for strip in range(len(room) + 1):
            if strip == len(room):
                room.append(rows - prompt_rows)
            if room[strip] >= width:
                laid.append((key, key, end, strip, rows - prompt_rows - room[strip]))
                room[strip] -= width
                break
    return sorted(laid), len(room) * step


def in_parts(row):
    high = row.astype(bf16)
    rest = row - high.astype(f32)
    middle = rest.astype(bf16)
    low = (rest - middle.astype(f32)).astype(bf16)
    return jnp.concatenate([high, middle, low, jnp.zeros((ONES - 3, row.shape[1]), bf16)], axis=0)


def widened(matrix):
    return jnp.concatenate([matrix, jnp.ones((matrix.shape[0], ONES), bf16)], axis=1)


def head_rows(head):
    return slice(head * HEAD_WIDTH, (head + 1) * HEAD_WIDTH)


def own_forward_kernel(
    q_ref, k_ref, v_ref, nq_ref, nk_ref, acc_ref, top_ref, p_ref, query_ref, keys_ref, values_ref,
    *, group, prompt_rows, step
):
    rows = q_ref.shape[1]
    wide = HEAD_WIDTH + ONES
    tiles, _ = strips(prompt_rows, rows, step)

    keys_ref[...] = widened(k_ref[...].T)
    values_ref[:HEAD_WIDTH] = v_ref[...]
    values_ref[HEAD_WIDTH:] = jnp.ones((ONES, rows), bf16)
    top_ref[...] = jnp.zeros_like(top_ref)
    for head in range(group):
        query_ref[head, :HEAD_WIDTH] = q_ref[head_rows(head)]
        query_ref[head, HEAD_WIDTH:] = jnp.zeros((ONES, rows), bf16)

    @pl.when(jnp.max(nq_ref[...]) * jnp.max(nk_ref[...]) >= SAFE_BOUND * SAFE_BOUND)
    def _():
        for head in range(group):
            top_ref[0, head : head + 1] = jnp.full((1, rows), FAR, f32)
            for key, first, end, _, _ in tiles:
                scores = masked(contract(keys_ref[key : key + step], query_ref[head, :, first:end], 1, 0), FAR)
                top_ref[0, head : head + 1, first:end] = jnp.maximum(
                    top_ref[0, head : head + 1, first:end], jnp.max(scores, axis=0, keepdims=True)
                )
            scores = contract(keys_ref[:prompt_rows], query_ref[head, :, prompt_rows:], 1, 0)
            top_ref[0, head : head + 1, prompt_rows:] = jnp.maximum(
                top_ref[0, head : head + 1, prompt_rows:], jnp.max(scores, axis=0, keepdims=True)
            )
        for head in range(group):
            query_ref[head, HEAD_WIDTH:] = in_parts(-top_ref[0, head : head + 1])

    for head in range(group):
        weights = jnp.exp2(contract(keys_ref[:prompt_rows], query_ref[head, :, prompt_rows:], 1, 0)).astype(bf16)
        p_ref[head, :prompt_rows] = weights
        acc_ref[head * wide : (head + 1) * wide, prompt_rows:] = contract(
            values_ref[:, :prompt_rows], weights, 1, 0
        )
    for key, first, end, strip, column in tiles:
        for head in range(group):
            scores = contract(keys_ref[key : key + step], query_ref[head, :, first:end], 1, 0)
            weights = masked(jnp.exp2(scores), 0.0).astype(bf16)
            row = prompt_rows + strip * step
            p_ref[head, row : row + step, column : column + end - first] = weights
            part = contract(values_ref[:, key : key + step], weights, 1, 0)
            at = slice(head * wide, (head + 1) * wide)
            if key == 0:
                acc_ref[at, first:end] = part
            else:
                acc_ref[at, first:end] += part


def own_forward(q, k, v, norm_q, norm_k, kv_heads, prompt_rows, step=256):
    rows = q.shape[1]
    group = q.shape[0] // HEAD_WIDTH // kv_heads
    wide = HEAD_WIDTH + ONES
    block = lambda n: pl.BlockSpec((n, rows), lambda h: (h, 0))
    _, strip_rows = strips(prompt_rows, rows, step)
    assert strip_rows == prompt_rows
    shape = jax.ShapeDtypeStruct
    return pl.pallas_call(
        functools.partial(own_forward_kernel, group=group, prompt_rows=prompt_rows, step=step),
        grid=(kv_heads,),
        in_specs=[
            block(group * HEAD_WIDTH), block(HEAD_WIDTH), block(HEAD_WIDTH), resident(norm_q.shape), resident(norm_k.shape)
        ],
        out_specs=(
            block(group * wide),
            pl.BlockSpec((1, group, rows), lambda h: (h, 0, 0)),
            pl.BlockSpec((group, 2 * prompt_rows, rows - prompt_rows), lambda h: (h, 0, 0)),
        ),
        scratch_shapes=[
            pltpu.VMEM((group, wide, rows), bf16),
            pltpu.VMEM((rows, wide), bf16),
            pltpu.VMEM((wide, rows), bf16),
        ],
        out_shape=(
            shape((kv_heads * group * wide, rows), f32),
            shape((kv_heads, group, rows), f32),
            shape((kv_heads * group, 2 * prompt_rows, rows - prompt_rows), bf16),
        ),
        compiler_params=pltpu.CompilerParams(vmem_limit_bytes=60 * MIB),
        name="own_forward",
    )(q, k, v, norm_q, norm_k)


def other_forward_kernel(
    seen_ref, q_ref, k_ref, v_ref, nq_ref, acc_ref, top_ref, o_ref, own_ref, far_ref, p_ref, query_ref, keys_ref,
    values_ref, *, group, prompt_rows
):
    rows = q_ref.shape[1]
    wide = HEAD_WIDTH + ONES
    seen = seen_ref[0] > 0
    key = k_ref[0].astype(f32)
    norm_k = jnp.max(jnp.sum(key * key, axis=0, keepdims=True))
    slow = jnp.max(nq_ref[...]) * norm_k >= SAFE_BOUND * SAFE_BOUND
    keys_ref[...] = widened(k_ref[0].T)
    values_ref[:HEAD_WIDTH] = v_ref[0]
    values_ref[HEAD_WIDTH:] = jnp.ones((ONES, keys_ref.shape[0]), bf16)
    for head in range(group):
        query_ref[head, :HEAD_WIDTH] = q_ref[head_rows(head)]
        query_ref[head, HEAD_WIDTH:] = jnp.zeros((ONES, rows), bf16)
    far_ref[...] = jnp.zeros_like(far_ref)

    @pl.when(slow)
    def _():
        for head in range(group):
            for first, end in ((0, prompt_rows), (prompt_rows, rows)):
                scores = contract(keys_ref[...], query_ref[head, :, first:end], 1, 0)
                far_ref[0, head : head + 1, first:end] = jnp.max(scores, axis=0, keepdims=True)
            query_ref[head, HEAD_WIDTH:] = in_parts(-far_ref[0, head : head + 1])

    def finish(first, end, with_other):
        for head in range(group):
            own = acc_ref[head * wide : (head + 1) * wide, first:end]
            own_top = top_ref[0, head : head + 1, first:end]
            if with_other:
                weights = jnp.exp2(contract(keys_ref[...], query_ref[head, :, first:end], 1, 0)).astype(bf16)
                p_ref[head, :, first:end] = weights
                far = contract(values_ref[...], weights, 1, 0)
                far_top = far_ref[0, head : head + 1, first:end]
                top = jnp.maximum(own_top, far_top)
                own_scale, far_scale = jnp.exp2(own_top - top), jnp.exp2(far_top - top)
                total = own * own_scale + far * far_scale
                inverse = 1.0 / total[HEAD_WIDTH : HEAD_WIDTH + 1]
                far_ref[0, head : head + 1, first:end] = far_scale * inverse
                own_ref[0, head : head + 1, first:end] = own_scale * inverse
            else:
                total = own
                inverse = 1.0 / total[HEAD_WIDTH : HEAD_WIDTH + 1]
                far_ref[0, head : head + 1, first:end] = jnp.zeros_like(inverse)
                own_ref[0, head : head + 1, first:end] = inverse
            o_ref[head_rows(head), first:end] = (total[:HEAD_WIDTH] * inverse).astype(bf16)

    finish(prompt_rows, rows, True)

    @pl.when(seen)
    def _():
        finish(0, prompt_rows, True)

    @pl.when(jnp.logical_not(seen))
    def _():
        finish(0, prompt_rows, False)


def half_index(h, j, seen):
    return (h, 0, 1 - j * jnp.minimum(seen[0], 1))


def other_forward(seen, q, kv, norm_q, acc, top, kv_heads, prompt_rows):
    rows = q.shape[1]
    group = q.shape[0] // HEAD_WIDTH // kv_heads
    wide = HEAD_WIDTH + ONES
    keys = kv.shape[2]
    block = lambda n, m: pl.BlockSpec((n, m), lambda h, s: (h, 0))
    row_block = pl.BlockSpec((1, group, rows), lambda h, s: (h, 0, 0))
    shape = jax.ShapeDtypeStruct
    return pl.pallas_call(
        functools.partial(other_forward_kernel, group=group, prompt_rows=prompt_rows),
        grid_spec=pltpu.PrefetchScalarGridSpec(
            num_scalar_prefetch=1,
            grid=(kv_heads,),
            in_specs=[
                block(group * HEAD_WIDTH, rows),
                pl.BlockSpec((1, HEAD_WIDTH, keys), lambda h, s: (0, h, 0)),
                pl.BlockSpec((1, HEAD_WIDTH, keys), lambda h, s: (1, h, 0)),
                resident(norm_q.shape),
                block(group * wide, rows),
                row_block,
            ],
            out_specs=(
                block(group * HEAD_WIDTH, rows),
                row_block,
                row_block,
                pl.BlockSpec((group, keys, rows), lambda h, s: (h, 0, 0)),
            ),
            scratch_shapes=[
                pltpu.VMEM((group, wide, rows), bf16),
                pltpu.VMEM((keys, wide), bf16),
                pltpu.VMEM((wide, keys), bf16),
            ],
        ),
        out_shape=(
            shape(q.shape, bf16),
            shape((kv_heads, group, rows), f32),
            shape((kv_heads, group, rows), f32),
            shape((kv_heads * group, keys, rows), bf16),
        ),
        compiler_params=pltpu.CompilerParams(vmem_limit_bytes=60 * MIB),
        name="other_forward",
    )(seen, q, kv, kv, norm_q, acc, top)


def tile_backward(values, key_rows, weights, query, grad):
    slopes = contract(values, grad, 1, 0)
    slopes = (weights.astype(f32) * slopes).astype(bf16)
    query_grad = contract(key_rows, slopes, 1, 0)
    key_grad = contract(query, slopes, 1, 1)
    value_grad = contract(grad[:HEAD_WIDTH], weights, 1, 1)
    return query_grad, key_grad, value_grad


def fill_grads(g_ref, scale_ref, delta_ref, grad_ref, group):
    for head in range(group):
        scale = scale_ref[0, head : head + 1]
        grad_ref[head, :HEAD_WIDTH] = (g_ref[head_rows(head)].astype(f32) * scale).astype(bf16)
        grad_ref[head, HEAD_WIDTH:] = in_parts(-delta_ref[0, head : head + 1] * scale)


def other_backward_kernel(
    seen_ref, q_ref, g_ref, scale_ref, delta_ref, k_ref, v_ref, p_ref, dq_ref, dkv_ref,
    grad_ref, values_ref, dk_sum, dv_sum, dq_sum, *, group, prompt_rows, step
):
    rows = q_ref.shape[1]
    seen = seen_ref[0] > 0
    stage = pl.program_id(1)

    def part(first, last, fresh):
        for low in range(0, k_ref.shape[2], step):
            span = slice(low, low + step)
            key_sum = value_sum = None
            for head in range(group):
                query_grad, key_grad, value_grad = tile_backward(
                    values_ref[span], k_ref[0, :, span], p_ref[head, span],
                    q_ref[head_rows(head), first:last], grad_ref[head, :, first:last],
                )
                if low == 0:
                    dq_sum[head_rows(head), first:last] = query_grad
                else:
                    dq_sum[head_rows(head), first:last] += query_grad
                key_sum = key_grad if key_sum is None else key_sum + key_grad
                value_sum = value_grad if value_sum is None else value_sum + value_grad
            if fresh:
                dk_sum[:, span] = key_sum
                dv_sum[:, span] = value_sum
            else:
                dk_sum[:, span] += key_sum
                dv_sum[:, span] += value_sum

    @pl.when(stage == 0)
    def _():
        fill_grads(g_ref, scale_ref, delta_ref, grad_ref, group)
        values_ref[...] = widened(v_ref[0].T)
        part(prompt_rows, rows, True)

    @pl.when((stage == 1) & seen)
    def _():
        part(0, prompt_rows, False)

    @pl.when((stage == 1) & jnp.logical_not(seen))
    def _():
        dq_sum[:, :prompt_rows] = jnp.zeros((dq_ref.shape[0], prompt_rows), f32)

    @pl.when(stage == 1)
    def _():
        dq_ref[...] = dq_sum[...].astype(bf16)
        dkv_ref[0] = dk_sum[...].astype(bf16)
        dkv_ref[1] = dv_sum[...].astype(bf16)


def other_backward(seen, q, g, scale, delta, kv, p, kv_heads, prompt_rows, step=256):
    rows = q.shape[1]
    group = q.shape[0] // HEAD_WIDTH // kv_heads
    keys = kv.shape[2]
    block = lambda n, m: pl.BlockSpec((n, m), lambda h, j, s: (h, 0))
    row_block = pl.BlockSpec((1, group, rows), lambda h, j, s: (h, 0, 0))
    wide = group * HEAD_WIDTH
    shape = jax.ShapeDtypeStruct
    return pl.pallas_call(
        functools.partial(other_backward_kernel, group=group, prompt_rows=prompt_rows, step=step),
        grid_spec=pltpu.PrefetchScalarGridSpec(
            num_scalar_prefetch=1,
            grid=(kv_heads, 2),
            in_specs=[
                block(wide, rows), block(wide, rows), row_block, row_block,
                pl.BlockSpec((1, HEAD_WIDTH, keys), lambda h, j, s: (0, h, 0)),
                pl.BlockSpec((1, HEAD_WIDTH, keys), lambda h, j, s: (1, h, 0)),
                pl.BlockSpec((group, keys, prompt_rows), half_index),
            ],
            out_specs=(block(wide, rows), pl.BlockSpec((2, HEAD_WIDTH, keys), lambda h, j, s: (0, h, 0))),
            scratch_shapes=[
                pltpu.VMEM((group, HEAD_WIDTH + ONES, rows), bf16),
                pltpu.VMEM((keys, HEAD_WIDTH + ONES), bf16),
                pltpu.VMEM((HEAD_WIDTH, keys), f32),
                pltpu.VMEM((HEAD_WIDTH, keys), f32),
                pltpu.VMEM((wide, rows), f32),
            ],
        ),
        out_shape=(shape(q.shape, bf16), shape(kv.shape, bf16)),
        compiler_params=pltpu.CompilerParams(vmem_limit_bytes=60 * MIB),
        name="other_backward",
    )(seen, q, g, scale, delta, kv, kv, p)


def own_backward_kernel(
    q_ref, g_ref, scale_ref, delta_ref, k_ref, v_ref, p_ref, dq_in_ref, dq_ref, dk_ref, dv_ref,
    grad_ref, values_ref, dk_sum, dv_sum, dq_sum, *, group, prompt_rows, step
):
    rows = q_ref.shape[1]
    stage = pl.program_id(1)
    tiles, _ = strips(prompt_rows, rows, step)

    def one(key, first, end, place, columns):
        span = slice(key, key + step)
        key_sum = value_sum = None
        for head in range(group):
            query_grad, key_grad, value_grad = tile_backward(
                values_ref[span], k_ref[:, span], p_ref[head, place, columns],
                q_ref[head_rows(head), first:end], grad_ref[head, :, first:end],
            )
            dq_sum[head_rows(head), first:end] += query_grad
            key_sum = key_grad if key_sum is None else key_sum + key_grad
            value_sum = value_grad if value_sum is None else value_sum + value_grad
        dk_sum[:, span] += key_sum
        dv_sum[:, span] += value_sum

    @pl.when(stage == 0)
    def _():
        fill_grads(g_ref, scale_ref, delta_ref, grad_ref, group)
        values_ref[...] = widened(v_ref[...].T)
        dq_sum[...] = dq_in_ref[...].astype(f32)
        dk_sum[...] = jnp.zeros_like(dk_sum)
        dv_sum[...] = jnp.zeros_like(dv_sum)
        for key in range(0, prompt_rows, step):
            one(key, prompt_rows, rows, slice(key, key + step), slice(0, rows - prompt_rows))

    @pl.when(stage == 1)
    def _():
        for key, first, end, strip, column in tiles:
            one(key, first, end, slice(strip * step, (strip + 1) * step), slice(column, column + end - first))
        dq_ref[...] = dq_sum[...].astype(bf16)
        dk_ref[...] = dk_sum[...].astype(bf16)
        dv_ref[...] = dv_sum[...].astype(bf16)


def own_backward(q, g, scale, delta, k, v, p, dq, kv_heads, prompt_rows, step=256):
    rows = q.shape[1]
    group = q.shape[0] // HEAD_WIDTH // kv_heads
    block = lambda n: pl.BlockSpec((n, rows), lambda h, j: (h, 0))
    row_block = pl.BlockSpec((1, group, rows), lambda h, j: (h, 0, 0))
    wide = group * HEAD_WIDTH
    shape = jax.ShapeDtypeStruct
    return pl.pallas_call(
        functools.partial(own_backward_kernel, group=group, prompt_rows=prompt_rows, step=step),
        grid=(kv_heads, 2),
        in_specs=[
            block(wide), block(wide), row_block, row_block, block(HEAD_WIDTH), block(HEAD_WIDTH),
            pl.BlockSpec((group, prompt_rows, rows - prompt_rows), lambda h, j: (h, j, 0)),
            block(wide),
        ],
        out_specs=(block(wide), block(HEAD_WIDTH), block(HEAD_WIDTH)),
        scratch_shapes=[
            pltpu.VMEM((group, HEAD_WIDTH + ONES, rows), bf16),
            pltpu.VMEM((rows, HEAD_WIDTH + ONES), bf16),
            pltpu.VMEM((HEAD_WIDTH, rows), f32),
            pltpu.VMEM((HEAD_WIDTH, rows), f32),
            pltpu.VMEM((wide, rows), f32),
        ],
        out_shape=(shape(q.shape, bf16), shape(k.shape, bf16), shape(v.shape, bf16)),
        compiler_params=pltpu.CompilerParams(vmem_limit_bytes=60 * MIB),
        name="own_backward",
    )(q, g, scale, delta, k, v, p, dq)


def middle_kernel(
    x_ref, dy_ref, o_ref, gain_ref, wide_any, wd_any,
    out_ref, h2_ref, hidden_ref, dgate_ref, dup_ref, dattn_ref, dob_ref, delta_ref,
    wo_ref, wg_ref, wu_ref, wd_ref, sems, *, chunk
):
    step = pl.program_id(0)
    inner, total = wo_ref.shape[1], wg_ref.shape[1]
    copies = [
        pltpu.make_async_copy(source, target, sems.at[i])
        for i, (source, target) in enumerate(
            (
                (wide_any.at[:, pl.ds(0, inner)], wo_ref),
                (wide_any.at[:, pl.ds(inner, total)], wg_ref),
                (wide_any.at[:, pl.ds(inner + total, total)], wu_ref),
                (wd_any, wd_ref),
            )
        )
    ]

    @pl.when(step == 0)
    def _():
        for copy in copies:
            copy.start()
        copies[0].wait()

    ob = o_ref[...]
    x1 = x_ref[...].astype(f32) + contract(ob, wo_ref[...], 0, 0)
    inverse = lax.rsqrt(jnp.mean(x1 * x1, axis=-1, keepdims=True) + norm_eps)
    gain = gain_ref[1:2]
    h2 = (x1 * inverse * gain).astype(bf16)
    h2_ref[...] = h2
    dy = dy_ref[...]

    @pl.when(step == 0)
    def _():
        for copy in copies[1:]:
            copy.wait()

    result = x1
    dh2 = None
    for low in range(0, wg_ref.shape[1], chunk):
        span = slice(low, low + chunk)
        gate = contract(h2, wg_ref[:, span], 1, 0)
        up = contract(h2, wu_ref[:, span], 1, 0)
        dhidden = contract(dy, wd_ref[span], 1, 1)
        sigma = 0.5 + 0.5 * jnp.tanh(0.5 * gate)
        silu = gate * sigma
        hidden = (silu * up).astype(bf16)
        hidden_ref[:, span] = hidden
        result = result + contract(hidden, wd_ref[span], 1, 0)
        dgate = (dhidden * up * sigma * (1.0 + gate * (1.0 - sigma))).astype(bf16)
        dup = (dhidden * silu).astype(bf16)
        dgate_ref[:, span] = dgate
        dup_ref[:, span] = dup
        part = contract(dgate, wg_ref[:, span], 1, 1) + contract(dup, wu_ref[:, span], 1, 1)
        dh2 = part if dh2 is None else dh2 + part
    out_ref[...] = result.astype(bf16)
    u = dh2 * gain
    dx1 = dy.astype(f32) + inverse * u - x1 * (inverse * inverse * inverse) * jnp.mean(
        u * x1, axis=-1, keepdims=True
    )
    dattn = dx1.astype(bf16)
    dattn_ref[...] = dattn
    dob = contract(wo_ref[...], dattn, 1, 1).astype(bf16)
    dob_ref[...] = dob
    product = dob.astype(f32) * ob.astype(f32)
    heads, group = delta_ref.shape[0], delta_ref.shape[1]
    for kv in range(heads):
        for member in range(group):
            at = (kv * group + member) * HEAD_WIDTH
            delta_ref[kv, member : member + 1] = jnp.sum(
                product[at : at + HEAD_WIDTH], axis=0, keepdims=True
            )


def middle(x, dy, o, gain, wide, wd, kv_heads, tile=256, chunk=768):
    rows, width = x.shape
    hidden = wd.shape[0]
    q_rows = o.shape[0]
    group = q_rows // HEAD_WIDTH // kv_heads
    by_row = lambda n: pl.BlockSpec((tile, n), lambda i: (i, 0))
    any_spec = pl.BlockSpec(memory_space=pl.ANY)
    shape = jax.ShapeDtypeStruct
    return pl.pallas_call(
        functools.partial(middle_kernel, chunk=chunk),
        grid=(rows // tile,),
        in_specs=[by_row(width), by_row(width), pl.BlockSpec((q_rows, tile), lambda i: (0, i)),
                  resident(gain.shape)] + [any_spec] * 2,
        out_specs=(
            by_row(width), by_row(width), by_row(hidden), by_row(hidden), by_row(hidden), by_row(width),
            pl.BlockSpec((q_rows, tile), lambda i: (0, i)),
            pl.BlockSpec((kv_heads, group, tile), lambda i: (0, 0, i)),
        ),
        out_shape=(
            shape((rows, width), bf16), shape((rows, width), bf16), shape((rows, hidden), bf16),
            shape((rows, hidden), bf16), shape((rows, hidden), bf16), shape((rows, width), bf16),
            shape((q_rows, rows), bf16), shape((kv_heads, group, rows), f32),
        ),
        scratch_shapes=[pltpu.VMEM(s, bf16) for s in ((width, q_rows), (width, hidden), (width, hidden), wd.shape)]
        + [pltpu.SemaphoreType.DMA((4,))],
        compiler_params=pltpu.CompilerParams(vmem_limit_bytes=62 * MIB),
        name="middle",
    )(x, dy, o, gain, wide, wd)


def down_grads_kernel(dy_ref, hidden_ref, down_ref):
    down_ref[...] = contract(hidden_ref[...], dy_ref[...], 0, 0).astype(bf16)


def down_grads(dy, hidden, tile=512):
    rows, width = dy.shape
    total = hidden.shape[1]
    return pl.pallas_call(
        down_grads_kernel,
        grid=(total // tile,),
        in_specs=[resident(dy.shape), pl.BlockSpec((rows, tile), lambda i: (0, i))],
        out_specs=pl.BlockSpec((tile, width), lambda i: (i, 0)),
        out_shape=jax.ShapeDtypeStruct((total, width), bf16),
        compiler_params=pltpu.CompilerParams(vmem_limit_bytes=60 * MIB),
        name="down_grads",
    )(dy, hidden)


def wide_grads_kernel(o_ref, h2_ref, dgate_ref, dup_ref, dattn_ref, out_ref, *, each):
    step = pl.program_id(0)

    @pl.when(step < each)
    def _():
        out_ref[...] = contract(h2_ref[...], dgate_ref[...], 0, 0).astype(bf16)

    @pl.when((step >= each) & (step < 2 * each))
    def _():
        out_ref[...] = contract(h2_ref[...], dup_ref[...], 0, 0).astype(bf16)

    @pl.when(step >= 2 * each)
    def _():
        out_ref[...] = contract(o_ref[...], dattn_ref[...], 1, 0).astype(bf16)


def wide_grads(o, h2, dattn, dgate, dup, tile=512):
    rows, width = h2.shape
    total = dgate.shape[1]
    each = total // tile
    steps = 2 * each + pl.cdiv(width, tile)
    cols = lambda low, count: pl.BlockSpec((rows, tile), lambda i: (0, jnp.clip(i - low, 0, count - 1)))
    return pl.pallas_call(
        functools.partial(wide_grads_kernel, each=each),
        grid=(steps,),
        in_specs=[
            resident(o.shape), resident(h2.shape), cols(0, each), cols(each, each), cols(2 * each, steps - 2 * each)
        ],
        out_specs=pl.BlockSpec((width, tile), lambda i: (0, i)),
        out_shape=jax.ShapeDtypeStruct((width, 2 * total + width), bf16),
        compiler_params=pltpu.CompilerParams(vmem_limit_bytes=60 * MIB),
        name="wide_grads",
    )(o, h2, dgate, dup, dattn)


def last_grads_kernel(
    x_ref, gain_ref, dq_ref, dk_ref, dv_ref, dkv_in_ref, cos_ref, sin_ref, lin_ref, dw_ref, acc_ref, *, prompt_steps
):
    step = pl.program_id(0)
    half = HEAD_WIDTH // 2
    cos, sin = cos_ref[...], sin_ref[...]

    def with_received(ref, which):
        return ref[...].astype(f32) + jnp.where(step < prompt_steps, dkv_in_ref[which].astype(f32), 0.0)

    def turned(value, scale):
        c, s = cos * scale, sin * scale
        pieces = []
        for at in range(0, value.shape[0], HEAD_WIDTH):
            a, b = value[at : at + half], value[at + half : at + HEAD_WIDTH]
            pieces += [a * c + b * s, b * c - a * s]
        return jnp.concatenate(pieces, axis=0)

    lin = jnp.concatenate(
        [
            turned(dq_ref[...].astype(f32), HEAD_WIDTH**-0.5),
            turned(with_received(dk_ref, 0), LN2),
            with_received(dv_ref, 1),
        ],
        axis=0,
    ).astype(bf16).T
    lin_ref[...] = lin
    x = x_ref[...].astype(f32)
    inverse = lax.rsqrt(jnp.mean(x * x, axis=-1, keepdims=True) + norm_eps)
    h = (x * inverse * gain_ref[0:1]).astype(bf16)
    part = contract(h, lin, 0, 0)

    @pl.when(step == 0)
    def _():
        acc_ref[...] = part

    @pl.when(step > 0)
    def _():
        acc_ref[...] += part

    @pl.when(step == pl.num_programs(0) - 1)
    def _():
        dw_ref[...] = acc_ref[...].astype(bf16)


def last_grads(x, gains, dq, dk, dv, dkv_in, cos, sin, tile=512):
    rows, width = x.shape
    cols = lambda n: pl.BlockSpec((n, tile), lambda i: (0, i))
    steps = dkv_in.shape[2] // tile
    few = pl.BlockSpec((2, dk.shape[0], tile), lambda i: (0, 0, jnp.minimum(i, steps - 1)))
    shape = jax.ShapeDtypeStruct
    inner = dq.shape[0] + dk.shape[0] + dv.shape[0]
    return pl.pallas_call(
        functools.partial(last_grads_kernel, prompt_steps=steps),
        grid=(rows // tile,),
        in_specs=[pl.BlockSpec((tile, width), lambda i: (i, 0)), resident(gains.shape),
                  cols(dq.shape[0]), cols(dk.shape[0]), cols(dv.shape[0]), few,
                  cols(cos.shape[0]), cols(cos.shape[0])],
        out_specs=(pl.BlockSpec((tile, inner), lambda i: (i, 0)), pl.BlockSpec((width, inner), lambda i: (0, 0))),
        out_shape=(shape((rows, inner), bf16), shape((width, inner), bf16)),
        scratch_shapes=[pltpu.VMEM((width, inner), f32)],
        compiler_params=pltpu.CompilerParams(vmem_limit_bytes=60 * MIB),
        name="last_grads",
    )(x, gains, dq, dk, dv, dkv_in, cos, sin)


def settle_kernel(first_ref, wide_ref, wide_in_ref, down_ref, down_in_ref, gains_ref, wa_ref, wb_ref, wc_ref, wg_ref, wu_ref, *outs):
    da, db, dc, dgate, dup, dout, ddown, gain_a, gain_f = outs
    gains = gains_ref[...].astype(f32)

    def spread(total, which):
        return jnp.broadcast_to(total / gains[:, which : which + 1], gains.shape).T[0:1]

    total = None
    at = 0
    for out, weight in ((da, wa_ref), (db, wb_ref), (dc, wc_ref)):
        value = first_ref[:, at : at + out.shape[1]]
        out[...] = value
        part = jnp.sum(value * weight[...].astype(f32), axis=1, keepdims=True)
        total = part if total is None else total + part
        at += out.shape[1]
    gain_a[...] = spread(total, 0)
    total = None
    at = 0
    for out, weight in ((dgate, wg_ref), (dup, wu_ref), (dout, None)):
        span = slice(at, at + out.shape[1])
        value = wide_ref[:, span].astype(f32) + wide_in_ref[:, span].astype(f32)
        out[...] = value
        if weight is not None:
            part = jnp.sum(value * weight[...].astype(f32), axis=1, keepdims=True)
            total = part if total is None else total + part
        at += out.shape[1]
    gain_f[...] = spread(total, 1)
    ddown[...] = down_ref[...].astype(f32) + down_in_ref[...].astype(f32)


def settle(first, wide, wide_in, down, down_in, gains, wa, wb, wc, wo, wg, wu):
    rows = first.shape[0]
    shape = jax.ShapeDtypeStruct
    return pl.pallas_call(
        settle_kernel,
        out_shape=[shape(w.shape, f32) for w in (wa, wb, wc, wg, wu, wo, down)] + [shape((1, rows), f32)] * 2,
        compiler_params=pltpu.CompilerParams(vmem_limit_bytes=60 * MIB),
        name="settle",
    )(first, wide, wide_in, down, down_in, gains, wa, wb, wc, wg, wu)


MESH_ID = pl.DeviceIdType.MESH


def whereabouts():
    z, y, w = lax.axis_index("group"), lax.axis_index("ctx"), lax.axis_index("wshard")
    return z, y, w // 2, w % 2


def device_at(z, y, x, core):
    return (z, y, x * 2 + core)


def slot_at(z, x, core):
    return z * 4 + x * 2 + core


def greet(partners):
    barrier = pltpu.get_barrier_semaphore()
    for partner in partners:
        pl.semaphore_signal(barrier, inc=1, device_id=partner, device_id_type=MESH_ID)
    pl.semaphore_wait(barrier, len(partners))


def neighbours(depth):
    z, y, x, core = whereabouts()
    along = [device_at((z + d) % depth, y, x, core) for d in range(1, depth)]
    return along, device_at(z, y, 1 - x, core), device_at(z, 1 - y, x, core), device_at(z, y, x, 1 - core)


class Copies:
    def __init__(self, send_sems, recv_sems):
        self.send_sems, self.recv_sems, self.made = send_sems, recv_sems, []

    def make(self, source, target, device):
        at = len(self.made)
        copy = pltpu.make_async_remote_copy(
            src_ref=source,
            dst_ref=target,
            send_sem=self.send_sems.at[at],
            recv_sem=self.recv_sems.at[at],
            device_id=device,
            device_id_type=MESH_ID,
        )
        self.made.append(copy)
        return copy


def gather_kernel(*refs, depth, split):
    *shards, wo_ref, wg_ref, wu_ref, out_ref, wide_ref, send_sems, recv_sems, own_sems = refs
    z, y, x, core = whereabouts()
    along, over_x, over_y, over_core = neighbours(depth)
    columns = out_ref.shape[2]
    given = pl.ds(pl.multiple_of(y * (columns - split), 128), split)
    got = pl.ds(pl.multiple_of((1 - y) * (columns - split), 128), split)
    common = pl.ds(split, columns - 2 * split)
    me = slot_at(z, x, core)
    copies = Copies(send_sems, recv_sems)
    view = lambda slot, span: out_ref.at[slot, :, span]

    def side_by_side(sources, target, first_sem):
        at = 0
        placed = []
        for index, source in enumerate(sources):
            width = source.shape[1]
            copy = pltpu.make_async_copy(source, target.at[:, pl.ds(at, width)], own_sems.at[first_sem + index])
            copy.start()
            placed.append(copy)
            at += width
        return placed

    own = side_by_side(shards, out_ref.at[me], 0)
    wide = side_by_side((wo_ref, wg_ref, wu_ref), wide_ref, len(shards))
    greet(along + [over_x, over_y, over_core])
    for copy in own:
        copy.wait()

    def send(slot, span, device):
        copy = copies.make(view(slot, span), view(slot, span), device)
        copy.start()
        return copy

    spans = (given, common)
    from_z, from_x, from_y, from_core = {}, {}, {}, []

    def onward(slot, part, d, side):
        if side == 0:
            from_x[d, part] = send(slot, spans[part], over_x)
        if part == 0:
            from_y[d, side] = send(slot, given, over_y)
        from_core.append(send(slot, spans[part], over_core))

    for part in range(2):
        for d in range(1, depth):
            from_z[d, part] = send(me, spans[part], along[d - 1])
        from_x[0, part] = send(me, spans[part], over_x)
    from_core.append(send(me, slice(None), over_core))
    for part in range(2):
        for d in range(1, depth):
            from_z[d, part].wait_recv()
            onward(slot_at((z + depth - d) % depth, x, core), part, d, 0)
    for part in range(2):
        for d in range(depth):
            from_x[d, part].wait_recv()
            onward(slot_at((z + depth - d) % depth, 1 - x, core), part, d, 1)
    for side in range(2):
        for d in range(1 - side, depth):
            from_y[d, side].wait_recv()
            slot = slot_at((z + depth - d) % depth, x if side == 0 else 1 - x, core)
            from_core.append(send(slot, got, over_core))
    for copy in from_core:
        copy.wait_recv()
    for copy in copies.made:
        copy.wait_send()
    for copy in wide:
        copy.wait()


def gather_all(shards, wide, depth, split):
    rows = shards[0].shape[0]
    columns = sum(shard.shape[1] for shard in shards)
    count = 2 * (depth - 1) + 2 * depth + 2 * depth - 1 + 3 * (2 * depth - 1) + 1
    return pl.pallas_call(
        functools.partial(gather_kernel, depth=depth, split=split),
        in_specs=[pl.BlockSpec(memory_space=pl.ANY)] * (len(shards) + len(wide)),
        out_specs=(pl.BlockSpec(memory_space=pltpu.VMEM), pl.BlockSpec(memory_space=pl.ANY)),
        out_shape=(
            jax.ShapeDtypeStruct((4 * depth, rows, columns), bf16),
            jax.ShapeDtypeStruct((rows, sum(shard.shape[1] for shard in wide)), bf16),
        ),
        scratch_shapes=[
            pltpu.SemaphoreType.DMA((count,)),
            pltpu.SemaphoreType.DMA((count,)),
            pltpu.SemaphoreType.DMA((len(shards) + len(wide),)),
        ],
        compiler_params=pltpu.CompilerParams(
            collective_id=1, has_side_effects=True, vmem_limit_bytes=60 * MIB
        ),
        name="gather_all",
    )(*shards, *wide)


def reduce_kernel(
    part_ref, lin_ref, w_ref, gain_ref, x_ref, dattn_ref, out_ref, tokens_ref,
    core_ref, sum_ref, over_ref, line_ref, z_ref, last_ref, twin_ref, send_sems, recv_sems, *, depth
):
    step = pl.program_id(0)
    steps = pl.num_programs(0)
    z, y, x, core = whereabouts()
    along, over_x, over_y, over_core = neighbours(depth)

    distances = list(range(1, depth)) + [0]
    order = [(d, side) for side in (1, 0) for d in distances]
    place = lambda d, side: ((z + d) % depth, x if side == 0 else 1 - x)

    def remote(source, target, device, at):
        return pltpu.make_async_remote_copy(
            src_ref=source,
            dst_ref=target,
            send_sem=send_sems.at[at],
            recv_sem=recv_sems.at[at],
            device_id=device,
            device_id_type=MESH_ID,
        )

    def to_core(at):
        to_z, to_x = place(*order[at])
        return remote(part_ref.at[slot_at(to_z, to_x, 1 - core)], core_ref.at[at], over_core, at)

    def to_x(at):
        return remote(sum_ref.at[at], over_ref.at[at], over_x, 2 * depth + at)

    def to_z(at):
        return remote(line_ref.at[at], z_ref.at[at], along[distances[at] - 1], 3 * depth + at)

    def to_y():
        return remote(last_ref, twin_ref, over_y, 4 * depth - 1)

    def core_sums(at):
        to_core(at).wait_recv()
        own_z, own_x = place(*order[at])
        sum_ref[at] = (part_ref[slot_at(own_z, own_x, core)].astype(f32) + core_ref[at].astype(f32)).astype(bf16)

    @pl.when(step == 0)
    def _():
        greet(along + [over_x, over_y, over_core])
        for at in range(2 * depth):
            to_core(at).start()

    @pl.when(step == 1)
    def _():
        for at in range(depth):
            core_sums(at)
            to_x(at).start()

    @pl.when(step == 2)
    def _():
        for at in range(depth, 2 * depth):
            core_sums(at)

    for at in range(depth):

        @pl.when(step == jnp.minimum(3 + at, steps - 1))
        def _():
            to_x(at).wait_recv()
            line_ref[at] = (sum_ref[depth + at].astype(f32) + over_ref[at].astype(f32)).astype(bf16)
            if distances[at]:
                to_z(at).start()

    lin = lin_ref[...]
    dh = contract(lin, w_ref[:, : lin.shape[1]], 1, 1)
    tokens = x_ref[...].astype(f32)
    inverse = lax.rsqrt(jnp.mean(tokens * tokens, axis=-1, keepdims=True) + norm_eps)
    u = dh * gain_ref[0:1]
    tokens_ref[...] = (
        dattn_ref[...].astype(f32)
        + inverse * u
        - tokens * (inverse * inverse * inverse) * jnp.mean(u * tokens, axis=-1, keepdims=True)
    )

    @pl.when(step == steps - 1)
    def _():
        total = line_ref[depth - 1].astype(f32)
        for at in range(depth - 1):
            to_z(at).wait_recv()
            total = total + z_ref[at].astype(f32)
        last_ref[...] = total.astype(bf16)
        to_y().start()
        to_y().wait_recv()
        out_ref[...] = total + twin_ref[...].astype(f32)
        for at in range(2 * depth):
            to_core(at).wait_send()
        for at in range(depth):
            to_x(at).wait_send()
        for at in range(depth - 1):
            to_z(at).wait_send()
        to_y().wait_send()


def reduce_all(parts, lin, w, gains, x, dattn, depth, tile=256):
    slots, rows, columns = parts.shape
    count, width = x.shape
    sems = 4 * depth
    buffer = lambda *count: pltpu.VMEM(count + (rows, columns), bf16)
    by_row = lambda n: pl.BlockSpec((tile, n), lambda i: (i, 0))
    return pl.pallas_call(
        functools.partial(reduce_kernel, depth=depth),
        grid=(count // tile,),
        in_specs=[
            resident(parts.shape), by_row(lin.shape[1]), resident(w.shape), resident(gains.shape),
            by_row(width), by_row(width),
        ],
        out_specs=(pl.BlockSpec((rows, columns), lambda i: (0, 0)), by_row(width)),
        out_shape=(jax.ShapeDtypeStruct((rows, columns), f32), jax.ShapeDtypeStruct((count, width), f32)),
        scratch_shapes=[
            buffer(2 * depth),
            buffer(2 * depth),
            buffer(depth),
            buffer(depth),
            buffer(depth - 1),
            buffer(),
            buffer(),
            pltpu.SemaphoreType.DMA((sems,)),
            pltpu.SemaphoreType.DMA((sems,)),
        ],
        compiler_params=pltpu.CompilerParams(
            collective_id=2, has_side_effects=True, vmem_limit_bytes=60 * MIB
        ),
        name="reduce_all",
    )(parts, lin, w, gains, x, dattn)


rope_base = 10000.0
masked_score = -1e30


def as_sent(array):

    def short(part):
        return part.astype(jnp.bfloat16) if part.dtype == jnp.float32 else part

    return jax.tree.map(short, array)


def rms_scale(value_rows_list, gain):
    return (
        value_rows_list
        * lax.rsqrt(jnp.mean(value_rows_list * value_rows_list, axis=-1, keepdims=True) + norm_eps)
        * gain
    )


def rms_back(value_rows_list, gain, upstream):
    inverse = lax.rsqrt(
        jnp.mean(value_rows_list * value_rows_list, axis=-1, keepdims=True) + norm_eps
    )
    scaled = upstream * gain
    gain_grad = jnp.sum(upstream * value_rows_list * inverse, axis=0)
    values_grad = inverse * scaled - value_rows_list * (inverse * inverse * inverse) * jnp.mean(
        scaled * value_rows_list, axis=-1, keepdims=True
    )
    return (gain_grad, values_grad)


def rope_tables(token_positions, head_size):
    half_size = head_size // 2
    frequency = rope_base ** (-(jnp.arange(half_size, dtype=jnp.float32) * 2.0) / head_size)
    angles = token_positions.astype(jnp.float32)[:, None] * frequency[None, :]
    return (jnp.cos(angles), jnp.sin(angles))


def rotary_apply(value_rows_list, cosine_table, sine_table):
    half_size = value_rows_list.shape[-1] // 2
    leading = value_rows_list[..., :half_size]
    trailing = value_rows_list[..., half_size:]
    cos_rows = cosine_table[:, None, :]
    sin_rows = sine_table[:, None, :]
    return jnp.concatenate(
        [leading * cos_rows - trailing * sin_rows, trailing * cos_rows + leading * sin_rows],
        axis=-1,
    )


def visible(query_pos, query_seg, key_pos, key_seg):
    same_doc = (key_seg[None, :] == query_seg[:, None]) | (key_seg[None, :] == 0)
    return same_doc & (key_pos[None, :] <= query_pos[:, None])


def tile_scores(query_tile, key_tile, scale):
    return (
        jnp.einsum("rhgd,khd->hgrk", query_tile, key_tile, preferred_element_type=jnp.float32)
        * scale
    )


def key_tiling(key_heads, value_heads, key_pos, key_seg):
    key_block = min(256, key_heads.shape[0])
    tile_count = key_heads.shape[0] // key_block
    return (
        key_heads.reshape(tile_count, key_block, key_heads.shape[1], key_heads.shape[2]),
        value_heads.reshape(tile_count, key_block, value_heads.shape[1], value_heads.shape[2]),
        key_pos.reshape(tile_count, key_block),
        key_seg.reshape(tile_count, key_block),
    )


def query_split(value_rows_list, query_block):
    return value_rows_list.reshape(
        (value_rows_list.shape[0] // query_block, query_block) + value_rows_list.shape[1:]
    )


def attention_forward(query_heads, key_heads, value_heads, places):
    query_pos, query_seg, key_pos, key_seg = places
    count_of_rows, kv_heads, group_size, head_size = query_heads.shape
    scale = head_size ** (-0.5)
    query_block = min(512, count_of_rows)
    key_tiles, value_tiles, kpos_tiles, kseg_tiles = key_tiling(
        key_heads, value_heads, key_pos, key_seg
    )

    def one_block(block_item):
        query_tile, tile_pos, tile_seg = block_item
        state_shape = (kv_heads, group_size, query_tile.shape[0])

        def lse_step(running, tile_item):
            key_tile, tile_kpos, tile_kseg = tile_item
            allowed = visible(tile_pos, tile_seg, tile_kpos, tile_kseg)

            def lse_open_tile(state):
                row_top, row_total = state
                scores = jnp.where(allowed, tile_scores(query_tile, key_tile, scale), masked_score)
                new_top = jnp.maximum(row_top, jnp.max(scores, axis=-1))
                weights = jnp.where(allowed, jnp.exp(scores - new_top[..., None]), 0.0)
                return (new_top, row_total * jnp.exp(row_top - new_top) + jnp.sum(weights, axis=-1))

            def lse_closed_tile(state):
                return state

            return (lax.cond(jnp.any(allowed), lse_open_tile, lse_closed_tile, running), None)

        initial = (
            jnp.full(state_shape, masked_score, jnp.float32),
            jnp.zeros(state_shape, jnp.float32),
        )
        (row_top, row_total), _ = lax.scan(lse_step, initial, (key_tiles, kpos_tiles, kseg_tiles))
        log_total = row_top + jnp.log(row_total)

        def out_step(running, tile_item):
            key_tile, value_tile, tile_kpos, tile_kseg = tile_item
            allowed = visible(tile_pos, tile_seg, tile_kpos, tile_kseg)

            def out_open_tile(accumulated):
                scores = jnp.where(allowed, tile_scores(query_tile, key_tile, scale), masked_score)
                probabilities = jnp.where(
                    allowed, jnp.exp(scores - log_total[..., None]), 0.0
                ).astype(jnp.bfloat16)
                return accumulated + jnp.einsum(
                    "hgrk,khd->rhgd", probabilities, value_tile, preferred_element_type=jnp.float32
                )

            def out_closed_tile(accumulated):
                return accumulated

            return (lax.cond(jnp.any(allowed), out_open_tile, out_closed_tile, running), None)

        output, _ = lax.scan(
            out_step,
            jnp.zeros(query_tile.shape, jnp.float32),
            (key_tiles, value_tiles, kpos_tiles, kseg_tiles),
        )
        return (output, log_total)

    outputs, log_totals = lax.map(
        one_block,
        (
            query_split(query_heads, query_block),
            query_split(query_pos, query_block),
            query_split(query_seg, query_block),
        ),
    )
    return (outputs.reshape(query_heads.shape), log_totals)


def attention_backward(
    query_heads, key_heads, value_heads, places, attended_grad, attended, log_totals
):
    query_pos, query_seg, key_pos, key_seg = places
    count_of_rows, kv_heads, group_size, head_size = query_heads.shape
    scale = head_size ** (-0.5)
    query_block = min(512, count_of_rows)
    key_tiles, value_tiles, kpos_tiles, kseg_tiles = key_tiling(
        key_heads, value_heads, key_pos, key_seg
    )

    def block_grads(sums, block_item):
        query_tile, grad_tile, output_tile, tile_lse, tile_pos, tile_seg = block_item
        tile_delta = jnp.einsum("rhgd,rhgd->hgr", grad_tile.astype(jnp.float32), output_tile)

        def back_step(query_grad, tile_item):
            key_tile, value_tile, tile_kpos, tile_kseg = tile_item
            allowed = visible(tile_pos, tile_seg, tile_kpos, tile_kseg)

            def back_open_tile(query_grad):
                scores = jnp.where(allowed, tile_scores(query_tile, key_tile, scale), masked_score)
                probabilities = jnp.where(allowed, jnp.exp(scores - tile_lse[..., None]), 0.0)
                prob_grad = jnp.einsum(
                    "rhgd,khd->hgrk", grad_tile, value_tile, preferred_element_type=jnp.float32
                )
                score_grad = (probabilities * (prob_grad - tile_delta[..., None])).astype(
                    jnp.bfloat16
                )
                query_grad = query_grad + scale * jnp.einsum(
                    "hgrk,khd->rhgd", score_grad, key_tile, preferred_element_type=jnp.float32
                )
                key_part = scale * jnp.einsum(
                    "hgrk,rhgd->khd", score_grad, query_tile, preferred_element_type=jnp.float32
                )
                value_part = jnp.einsum(
                    "hgrk,rhgd->khd",
                    probabilities.astype(jnp.bfloat16),
                    grad_tile,
                    preferred_element_type=jnp.float32,
                )
                return (query_grad, key_part, value_part)

            def back_closed_tile(query_grad):
                return (
                    query_grad,
                    jnp.zeros(key_tile.shape, jnp.float32),
                    jnp.zeros(value_tile.shape, jnp.float32),
                )

            query_grad, key_part, value_part = lax.cond(
                jnp.any(allowed), back_open_tile, back_closed_tile, query_grad
            )
            return (query_grad, (key_part, value_part))

        query_grad, (key_parts, value_parts) = lax.scan(
            back_step,
            jnp.zeros(query_tile.shape, jnp.float32),
            (key_tiles, value_tiles, kpos_tiles, kseg_tiles),
        )
        return ((sums[0] + key_parts, sums[1] + value_parts), query_grad)

    initial = (jnp.zeros(key_tiles.shape, jnp.float32), jnp.zeros(value_tiles.shape, jnp.float32))
    block_items = (
        query_split(query_heads, query_block),
        query_split(attended_grad, query_block),
        query_split(attended, query_block),
        log_totals,
        query_split(query_pos, query_block),
        query_split(query_seg, query_block),
    )
    (key_sum, value_sum), query_grads = lax.scan(block_grads, initial, block_items)
    key_rows = key_heads.shape[0]
    return (
        query_grads.reshape(query_heads.shape),
        key_sum.reshape(key_rows, -1),
        value_sum.reshape(key_rows, -1),
    )


def forward_pass(weights, inputs, places, tables, gather_pair):
    (
        attn_gain,
        query_full,
        key_complete,
        value_complete,
        out_full,
        ffn_gain,
        gate_full,
        up_full,
        down_full,
    ) = weights
    cosine_table, sine_table = tables
    count_of_rows = inputs.shape[0]
    normalized_input = rms_scale(inputs, attn_gain.astype(jnp.float32)).astype(jnp.bfloat16)
    query_lin = jnp.dot(normalized_input, query_full, preferred_element_type=jnp.float32)
    key_lin = jnp.dot(normalized_input, key_complete, preferred_element_type=jnp.float32)
    value_lin = jnp.dot(normalized_input, value_complete, preferred_element_type=jnp.float32)
    kv_heads = key_lin.shape[1] // HEAD_WIDTH
    query_rot = rotary_apply(
        query_lin.reshape(count_of_rows, -1, HEAD_WIDTH), cosine_table, sine_table
    ).astype(jnp.bfloat16)
    key_rot = (
        rotary_apply(key_lin.reshape(count_of_rows, kv_heads, HEAD_WIDTH), cosine_table, sine_table)
        .astype(jnp.bfloat16)
        .reshape(count_of_rows, -1)
    )
    value_low = value_lin.astype(jnp.bfloat16)
    keys_all, values_all = gather_pair((key_rot, value_low))
    group_size = query_rot.shape[1] // kv_heads
    query_heads = query_rot.reshape(count_of_rows, kv_heads, group_size, HEAD_WIDTH)
    key_heads = keys_all.reshape(-1, kv_heads, HEAD_WIDTH)
    value_heads = values_all.reshape(-1, kv_heads, HEAD_WIDTH)
    attended, log_totals = attention_forward(query_heads, key_heads, value_heads, places)
    attended_low = attended.reshape(count_of_rows, -1).astype(jnp.bfloat16)
    mixed = inputs + jnp.dot(attended_low, out_full, preferred_element_type=jnp.float32)
    normed_two = rms_scale(mixed, ffn_gain.astype(jnp.float32)).astype(jnp.bfloat16)
    gate = jnp.dot(normed_two, gate_full, preferred_element_type=jnp.float32)
    up_value = jnp.dot(normed_two, up_full, preferred_element_type=jnp.float32)
    hidden = (jax.nn.silu(gate) * up_value).astype(jnp.bfloat16)
    result = mixed + jnp.dot(hidden, down_full, preferred_element_type=jnp.float32)
    return (
        normalized_input,
        query_heads,
        key_heads,
        value_heads,
        attended,
        attended_low,
        log_totals,
        mixed,
        normed_two,
        gate,
        up_value,
        hidden,
        result,
    )


def general_local(
    tokens,
    block_map,
    attention_gain,
    query_weight,
    key_matrix,
    value_matrix,
    output_weight,
    feedforward_gain,
    gate_weight,
    up_weight,
    down_weight,
    out_grad,
):
    shards = (
        attention_gain,
        query_weight,
        key_matrix,
        value_matrix,
        output_weight,
        feedforward_gain,
        gate_weight,
        up_weight,
        down_weight,
    )
    count_of_rows = tokens.shape[1]
    ctx_rank = lax.axis_index("ctx")
    blocks = block_map[0]
    block_rows = count_of_rows // 2
    group_rows = blocks.shape[0] * block_rows
    prompt_rows = group_rows // 2
    natural = (
        blocks[:, None] * block_rows + jnp.arange(block_rows, dtype=jnp.int32)[None, :]
    ).reshape(-1)
    in_prompt = natural < prompt_rows
    key_pos = jnp.where(in_prompt, natural, prompt_rows + (natural - prompt_rows) % CONTINUE_LENGTH)
    key_seg = jnp.where(in_prompt, 0, 1 + (natural - prompt_rows) // CONTINUE_LENGTH)
    query_pos = lax.dynamic_slice_in_dim(key_pos, ctx_rank * count_of_rows, count_of_rows)
    query_seg = lax.dynamic_slice_in_dim(key_seg, ctx_rank * count_of_rows, count_of_rows)
    places = (query_pos, query_seg, key_pos, key_seg)
    cosine_table, sine_table = rope_tables(query_pos, HEAD_WIDTH)
    tables = (cosine_table, sine_table)
    inputs = tokens[0].astype(jnp.float32)
    full_weights = (
        lax.all_gather(shards[0], ("group", "wshard"), axis=0, tiled=True),
        lax.all_gather(shards[1], ("group", "wshard"), axis=0, tiled=True),
        lax.all_gather(shards[2], ("group", "wshard"), axis=0, tiled=True),
        lax.all_gather(shards[3], ("group", "wshard"), axis=0, tiled=True),
        lax.all_gather(shards[4], ("group", "wshard"), axis=0, tiled=True),
        lax.all_gather(shards[5], ("group", "wshard"), axis=0, tiled=True),
        lax.all_gather(shards[6], ("group", "wshard"), axis=0, tiled=True),
        lax.all_gather(shards[7], ("group", "wshard"), axis=0, tiled=True),
        lax.all_gather(shards[8], ("group", "wshard"), axis=0, tiled=True),
    )
    forward = forward_pass(
        full_weights,
        inputs,
        places,
        tables,
        lambda packed: jax.tree.map(
            lambda part, own: part.astype(own.dtype),
            lax.all_gather(as_sent(packed), "ctx", axis=0, tiled=True),
            packed,
        ),
    )
    layer_out = forward[12].astype(jnp.bfloat16)
    back_weights = (
        lax.all_gather(shards[0], ("group", "wshard"), axis=0, tiled=True),
        lax.all_gather(shards[1], ("group", "wshard"), axis=0, tiled=True),
        lax.all_gather(shards[2], ("group", "wshard"), axis=0, tiled=True),
        lax.all_gather(shards[3], ("group", "wshard"), axis=0, tiled=True),
        lax.all_gather(shards[4], ("group", "wshard"), axis=0, tiled=True),
        lax.all_gather(shards[5], ("group", "wshard"), axis=0, tiled=True),
        lax.all_gather(shards[6], ("group", "wshard"), axis=0, tiled=True),
        lax.all_gather(shards[7], ("group", "wshard"), axis=0, tiled=True),
        lax.all_gather(shards[8], ("group", "wshard"), axis=0, tiled=True),
    )
    saved = forward_pass(
        back_weights,
        inputs,
        places,
        tables,
        lambda packed: jax.tree.map(
            lambda part, own: part.astype(own.dtype),
            lax.all_gather(as_sent(packed), "ctx", axis=0, tiled=True),
            packed,
        ),
    )
    (
        normalized_input,
        query_heads,
        key_heads,
        value_heads,
        attended,
        attended_low,
        log_totals,
        mixed,
        normed_two,
        gate,
        up_value,
        hidden,
        result,
    ) = saved
    (
        attn_gain,
        query_full,
        key_complete,
        value_complete,
        out_full,
        ffn_gain,
        gate_full,
        up_full,
        down_full,
    ) = back_weights
    upstream = out_grad[0].astype(jnp.float32)
    ffn_grad = upstream.astype(jnp.bfloat16)
    grad_down = jnp.einsum("rf,rd->fd", hidden, ffn_grad, preferred_element_type=jnp.float32)
    hidden_grad = jnp.einsum("rd,fd->rf", ffn_grad, down_full, preferred_element_type=jnp.float32)
    gate_sigmoid = jax.nn.sigmoid(gate)
    gate_grad = (
        hidden_grad * up_value * gate_sigmoid * (1.0 + gate * (1.0 - gate_sigmoid))
    ).astype(jnp.bfloat16)
    up_grad = (hidden_grad * (gate * gate_sigmoid)).astype(jnp.bfloat16)
    grad_gate = jnp.einsum("rd,rf->df", normed_two, gate_grad, preferred_element_type=jnp.float32)
    grad_up = jnp.einsum("rd,rf->df", normed_two, up_grad, preferred_element_type=jnp.float32)
    normed_two_grad = jnp.einsum(
        "rf,df->rd", gate_grad, gate_full, preferred_element_type=jnp.float32
    ) + jnp.einsum("rf,df->rd", up_grad, up_full, preferred_element_type=jnp.float32)
    grad_ffn_gain, mixed_back = rms_back(mixed, ffn_gain.astype(jnp.float32), normed_two_grad)
    mixed_grad = upstream + mixed_back
    attn_grad = mixed_grad.astype(jnp.bfloat16)
    grad_out = jnp.einsum("rf,rd->fd", attended_low, attn_grad, preferred_element_type=jnp.float32)
    attended_grad = (
        jnp.einsum("rd,fd->rf", attn_grad, out_full, preferred_element_type=jnp.float32)
        .astype(jnp.bfloat16)
        .reshape(attended.shape)
    )
    query_grad, key_grad, value_grad = attention_backward(
        query_heads, key_heads, value_heads, places, attended_grad, attended, log_totals
    )
    key_local, value_local = (
        lax.psum_scatter(
            key_grad.astype(jnp.bfloat16), "ctx", scatter_dimension=0, tiled=True
        ).astype(jnp.float32),
        lax.psum_scatter(
            value_grad.astype(jnp.bfloat16), "ctx", scatter_dimension=0, tiled=True
        ).astype(jnp.float32),
    )
    query_lin_grad = (
        rotary_apply(query_grad.reshape(count_of_rows, -1, HEAD_WIDTH), cosine_table, -sine_table)
        .reshape(count_of_rows, -1)
        .astype(jnp.bfloat16)
    )
    key_lin_grad = (
        rotary_apply(key_local.reshape(count_of_rows, -1, HEAD_WIDTH), cosine_table, -sine_table)
        .reshape(count_of_rows, -1)
        .astype(jnp.bfloat16)
    )
    value_lin_grad = value_local.astype(jnp.bfloat16)
    grad_query = jnp.einsum(
        "rd,rf->df", normalized_input, query_lin_grad, preferred_element_type=jnp.float32
    )
    grad_key = jnp.einsum(
        "rd,rf->df", normalized_input, key_lin_grad, preferred_element_type=jnp.float32
    )
    grad_value = jnp.einsum(
        "rd,rf->df", normalized_input, value_lin_grad, preferred_element_type=jnp.float32
    )
    normed_grad = jnp.einsum(
        "rf,df->rd", query_lin_grad, query_full, preferred_element_type=jnp.float32
    )
    normed_grad = normed_grad + jnp.einsum(
        "rf,df->rd", key_lin_grad, key_complete, preferred_element_type=jnp.float32
    )
    normed_grad = normed_grad + jnp.einsum(
        "rf,df->rd", value_lin_grad, value_complete, preferred_element_type=jnp.float32
    )
    grad_attn_gain, input_back = rms_back(inputs, attn_gain.astype(jnp.float32), normed_grad)
    input_grad = mixed_grad + input_back
    partial_grads = (
        grad_attn_gain,
        grad_query,
        grad_key,
        grad_value,
        grad_out,
        grad_ffn_gain,
        grad_gate,
        grad_up,
        grad_down,
    )
    reduced = (
        lax.psum_scatter(
            partial_grads[0].astype(jnp.bfloat16),
            ("group", "wshard"),
            scatter_dimension=0,
            tiled=True,
        ).astype(jnp.float32),
        lax.psum_scatter(
            partial_grads[1].astype(jnp.bfloat16),
            ("group", "wshard"),
            scatter_dimension=0,
            tiled=True,
        ).astype(jnp.float32),
        lax.psum_scatter(
            partial_grads[2].astype(jnp.bfloat16),
            ("group", "wshard"),
            scatter_dimension=0,
            tiled=True,
        ).astype(jnp.float32),
        lax.psum_scatter(
            partial_grads[3].astype(jnp.bfloat16),
            ("group", "wshard"),
            scatter_dimension=0,
            tiled=True,
        ).astype(jnp.float32),
        lax.psum_scatter(
            partial_grads[4].astype(jnp.bfloat16),
            ("group", "wshard"),
            scatter_dimension=0,
            tiled=True,
        ).astype(jnp.float32),
        lax.psum_scatter(
            partial_grads[5].astype(jnp.bfloat16),
            ("group", "wshard"),
            scatter_dimension=0,
            tiled=True,
        ).astype(jnp.float32),
        lax.psum_scatter(
            partial_grads[6].astype(jnp.bfloat16),
            ("group", "wshard"),
            scatter_dimension=0,
            tiled=True,
        ).astype(jnp.float32),
        lax.psum_scatter(
            partial_grads[7].astype(jnp.bfloat16),
            ("group", "wshard"),
            scatter_dimension=0,
            tiled=True,
        ).astype(jnp.float32),
        lax.psum_scatter(
            partial_grads[8].astype(jnp.bfloat16),
            ("group", "wshard"),
            scatter_dimension=0,
            tiled=True,
        ).astype(jnp.float32),
    )
    summed = (
        lax.psum(reduced[0].astype(jnp.bfloat16), "ctx").astype(jnp.float32),
        lax.psum(reduced[1].astype(jnp.bfloat16), "ctx").astype(jnp.float32),
        lax.psum(reduced[2].astype(jnp.bfloat16), "ctx").astype(jnp.float32),
        lax.psum(reduced[3].astype(jnp.bfloat16), "ctx").astype(jnp.float32),
        lax.psum(reduced[4].astype(jnp.bfloat16), "ctx").astype(jnp.float32),
        lax.psum(reduced[5].astype(jnp.bfloat16), "ctx").astype(jnp.float32),
        lax.psum(reduced[6].astype(jnp.bfloat16), "ctx").astype(jnp.float32),
        lax.psum(reduced[7].astype(jnp.bfloat16), "ctx").astype(jnp.float32),
        lax.psum(reduced[8].astype(jnp.bfloat16), "ctx").astype(jnp.float32),
    )
    gain_attn, gain_ffn = (summed[0], summed[5])
    matrices = (summed[1], summed[2], summed[3], summed[4], summed[6], summed[7], summed[8])
    return (
        layer_out[None],
        input_grad[None],
        gain_attn,
        matrices[0],
        matrices[1],
        matrices[2],
        matrices[3],
        gain_ffn,
        matrices[4],
        matrices[5],
        matrices[6],
    )


OWNERS = ("group", "wshard")
SWAP = [(0, 1), (1, 0)]


def swap(array):
    return lax.ppermute(array, "ctx", SWAP)


def fast_local(
    tokens, block_map, attention_gain, query_weight, key_matrix, value_matrix, output_weight,
    feedforward_gain, gate_weight, up_weight, down_weight, out_grad,
):
    x, dy = tokens[0], out_grad[0]
    rows, width = x.shape
    prompt_rows = rows // 2
    q_rows, kv_rows = query_weight.shape[1], key_matrix.shape[1]
    kv_heads = kv_rows // HEAD_WIDTH
    hidden = gate_weight.shape[1]
    shard_rows = query_weight.shape[0]
    block = lax.dynamic_index_in_dim(block_map[0], 2 * lax.axis_index("ctx"), 0, False)
    seen = (block > 0).astype(jnp.int32)
    prompt_total = block_map.shape[1] // 2 * prompt_rows

    depth = lax.axis_size("group")

    gain_columns = jnp.pad(jnp.stack([attention_gain, feedforward_gain], axis=1), ((0, 0), (0, 126)))
    shards = (query_weight, key_matrix, value_matrix, gain_columns)
    split = sum(shard.shape[1] for shard in shards) // 3 // 128 * 128
    wd = lax.all_gather(down_weight, OWNERS, axis=0, tiled=True)
    first, wide = gather_all(shards, (output_weight, gate_weight, up_weight), depth, split)
    first = first.reshape(width, -1)
    wide = lax.all_gather(wide, OWNERS, axis=0, tiled=True)

    at = jnp.arange(rows, dtype=jnp.int32)
    positions = jnp.where(
        at < prompt_rows, block * prompt_rows + at, prompt_total + (at - prompt_rows) % CONTINUE_LENGTH
    )
    half = HEAD_WIDTH // 2
    frequency = rope_base ** (-(jnp.arange(half, dtype=f32) * 2.0) / HEAD_WIDTH)
    angles = frequency[:, None] * positions.astype(f32)[None, :]
    cos, sin = jnp.cos(angles), jnp.sin(angles)

    q, k, v, kv, norm_q, norm_k, gains = project(x, first, cos, sin, q_rows, kv_rows, prompt_rows)
    kv_other = swap(kv)
    acc, top, p_own = own_forward(q, k, v, norm_q, norm_k, kv_heads, prompt_rows)
    o, own_scale, far_scale, p_far = other_forward(seen[None], q, kv_other, norm_q, acc, top, kv_heads, prompt_rows)
    layer_out, h2, hid, dgate, dup, dattn, dob, delta = middle(x, dy, o, gains, wide, wd, kv_heads)
    scatter = lambda a: lax.psum_scatter(a, OWNERS, scatter_dimension=0, tiled=True)
    d_down = down_grads(dy, hid)
    h2, d_down = lax.optimization_barrier((h2, d_down))
    d_down = scatter(d_down)
    d_wide = wide_grads(o, h2, dattn, dgate, dup)
    dob, d_wide = lax.optimization_barrier((dob, d_wide))
    d_wide = scatter(d_wide)
    dq, dkv_far = other_backward(seen[None], q, dob, far_scale, delta, kv_other, p_far, kv_heads, prompt_rows)
    dkv_in = swap(dkv_far)
    d_down, dkv_in = lax.optimization_barrier((d_down, dkv_in))
    d_down_in = swap(d_down)
    dq, dk, dv = own_backward(q, dob, own_scale, delta, k, v, p_own, dq, kv_heads, prompt_rows)
    lin, d_first = last_grads(x, gains, dq, dk, dv, dkv_in, cos, sin)
    d_first, d_wide = lax.optimization_barrier((d_first, d_wide))
    d_wide_in = swap(d_wide)
    d_first, grad_tokens = reduce_all(d_first.reshape(4 * depth, shard_rows, -1), lin, first, gains, x, dattn, depth)
    d_q, d_k, d_v, d_gate, d_up, d_out, d_down, d_gain_a, d_gain_f = settle(
        d_first, d_wide, d_wide_in, d_down, d_down_in, gain_columns,
        query_weight, key_matrix, value_matrix, output_weight, gate_weight, up_weight,
    )
    return (
        layer_out[None],
        grad_tokens[None],
        d_gain_a[0],
        d_q,
        d_k,
        d_v,
        d_out,
        d_gain_f[0],
        d_gate,
        d_up,
        d_down,
    )


def local(mesh, tokens, block_map, *rest):
    block_rows = tokens.shape[1] // 2
    whole = (
        mesh.shape["ctx"] == 2
        and mesh.shape["wshard"] == 4
        and block_rows % CONTINUE_LENGTH == 0
        and tokens.shape[0] == 1
    )
    return (fast_local if whole else general_local)(tokens, block_map, *rest)


def solution(mesh):
    return jax.shard_map(
        lambda *args: local(mesh, *args),
        mesh=mesh,
        in_specs=(
            P(("group", "wshard"), "ctx", None),
            P(("group", "wshard"), None),
            P(("group", "wshard")),
            P(("group", "wshard"), None),
            P(("group", "wshard"), None),
            P(("group", "wshard"), None),
            P(("group", "wshard"), None),
            P(("group", "wshard")),
            P(("group", "wshard"), None),
            P(("group", "wshard"), None),
            P(("group", "wshard"), None),
            P(("group", "wshard"), "ctx", None),
        ),
        out_specs=(
            P(("group", "wshard"), "ctx", None),
            P(("group", "wshard"), "ctx", None),
            P(("group", "wshard")),
            P(("group", "wshard"), None),
            P(("group", "wshard"), None),
            P(("group", "wshard"), None),
            P(("group", "wshard"), None),
            P(("group", "wshard")),
            P(("group", "wshard"), None),
            P(("group", "wshard"), None),
            P(("group", "wshard"), None),
        ),
        check_vma=False,
    )
```

```python
import functools

import jax
import jax.numpy as jnp
import numpy as np
from jax import lax
from jax.experimental import pallas as pl
from jax.experimental.pallas import tpu as pltpu
from jax.sharding import PartitionSpec as P

f32 = jnp.float32
bf16 = jnp.bfloat16
HEAD_WIDTH = 64
CONTINUE_LENGTH = 512
norm_eps = 1e-05
LOG2E = 1.4426950408889634
LN2 = 0.6931471805599453
MIB = 2**20


def contract(a, b, dim_a, dim_b):
    return lax.dot_general(
        a, b, (((dim_a,), (dim_b,)), ((), ())), preferred_element_type=f32
    )


def resident(shape):
    zeros = (0,) * len(shape)
    return pl.BlockSpec(shape, lambda *_: zeros, pipeline_mode=pl.Buffered(1))


def project_kernel(
    x_ref, w_ref, cos_ref, sin_ref, q_ref, k_ref, v_ref, kv_ref, nq_ref, nk_ref, gains_ref, *, prompt_steps
):
    @pl.when(pl.program_id(0) == 0)
    def _():
        gains_ref[...] = w_ref[:, w_ref.shape[1] - 128 :].astype(f32).T[: gains_ref.shape[0]]

    x = x_ref[...].astype(f32)
    inverse = lax.rsqrt(jnp.mean(x * x, axis=-1, keepdims=True) + norm_eps)
    h = (x * inverse * gains_ref[0:1]).astype(bf16)
    q_rows, kv_rows = q_ref.shape[0], k_ref.shape[0]
    half = HEAD_WIDTH // 2
    scale = LOG2E * HEAD_WIDTH**-0.5
    cos, sin = cos_ref[...], sin_ref[...]

    def rotated(lin, out_ref, base, cos, sin):
        worst = jnp.zeros((1, lin.shape[1]), f32)
        for head in range(lin.shape[0] // HEAD_WIDTH):
            at = head * HEAD_WIDTH
            a, b = lin[at : at + half], lin[at + half : at + HEAD_WIDTH]
            first = (a * cos - b * sin).astype(bf16)
            second = (b * cos + a * sin).astype(bf16)
            out_ref[base + at : base + at + half] = first
            out_ref[base + at + half : base + at + HEAD_WIDTH] = second
            fa, fb = first.astype(f32), second.astype(f32)
            worst = jnp.maximum(worst, jnp.sum(fa * fa + fb * fb, axis=0, keepdims=True))
        return worst

    ht = h.T
    chunk = kv_rows
    qc, qs = cos * scale, sin * scale
    worst_q = worst_k = None
    for at in range(0, q_rows + 2 * kv_rows, chunk):
        lin = contract(w_ref[:, at : at + chunk], ht, 0, 0)
        if at < q_rows:
            worst = rotated(lin, q_ref, at, qc, qs)
            worst_q = worst if worst_q is None else jnp.maximum(worst_q, worst)
        elif at < q_rows + kv_rows:
            worst = rotated(lin, k_ref, at - q_rows, cos, sin)
            worst_k = worst if worst_k is None else jnp.maximum(worst_k, worst)
        else:
            v_ref[pl.ds(at - q_rows - kv_rows, chunk)] = lin.astype(bf16)
    nq_ref[...] = worst_q
    nk_ref[...] = worst_k

    @pl.when(pl.program_id(0) < prompt_steps)
    def _():
        kv_ref[0] = k_ref[...]
        kv_ref[1] = v_ref[...]


def project(x, w, cos, sin, q_rows, kv_rows, prompt_rows, tile=512):
    rows, width = x.shape
    prompt_steps = prompt_rows // tile
    cols = lambda n: pl.BlockSpec((n, tile), lambda i: (0, i))
    return pl.pallas_call(
        functools.partial(project_kernel, prompt_steps=prompt_steps),
        grid=(rows // tile,),
        in_specs=[
            pl.BlockSpec((tile, width), lambda i: (i, 0)),
            resident(w.shape),
            cols(cos.shape[0]),
            cols(cos.shape[0]),
        ],
        out_specs=(
            cols(q_rows),
            cols(kv_rows),
            cols(kv_rows),
            pl.BlockSpec((2, kv_rows, tile), lambda i: (0, 0, jnp.minimum(i, prompt_steps - 1))),
            cols(1),
            cols(1),
            pl.BlockSpec((8, width), lambda i: (0, 0)),
        ),
        out_shape=(
            jax.ShapeDtypeStruct((q_rows, rows), bf16),
            jax.ShapeDtypeStruct((kv_rows, rows), bf16),
            jax.ShapeDtypeStruct((kv_rows, rows), bf16),
            jax.ShapeDtypeStruct((2, kv_rows, prompt_rows), bf16),
            jax.ShapeDtypeStruct((1, rows), f32),
            jax.ShapeDtypeStruct((1, rows), f32),
            jax.ShapeDtypeStruct((8, width), f32),
        ),
        compiler_params=pltpu.CompilerParams(vmem_limit_bytes=60 * MIB),
        name="project",
    )(x, w, cos, sin)


ONES = 16
SAFE_BOUND = 80.0
FAR = -1e30


def causal(keys, columns):
    return lax.broadcasted_iota(jnp.int32, (keys, columns), 0) <= lax.broadcasted_iota(
        jnp.int32, (keys, columns), 1
    )


def masked(tile, fill):
    step = tile.shape[0]
    front = jnp.where(causal(step, step), tile[:, :step], fill)
    return front if tile.shape[1] == step else jnp.concatenate([front, tile[:, step:]], axis=1)


def strips(prompt_rows, rows, step):
    tiles = []
    at = 0
    while at < rows:
        end = prompt_rows if at < prompt_rows else at + CONTINUE_LENGTH
        tiles += [(end - key, key, end) for key in range(at, end, step)]
        at = end
    room, laid = [], []
    for width, key, end in sorted(tiles, reverse=True):
        for strip in range(len(room) + 1):
            if strip == len(room):
                room.append(rows - prompt_rows)
            if room[strip] >= width:
                laid.append((key, key, end, strip, rows - prompt_rows - room[strip]))
                room[strip] -= width
                break
    return sorted(laid), len(room) * step


def in_parts(row):
    high = row.astype(bf16)
    rest = row - high.astype(f32)
    middle = rest.astype(bf16)
    low = (rest - middle.astype(f32)).astype(bf16)
    return jnp.concatenate([high, middle, low, jnp.zeros((ONES - 3, row.shape[1]), bf16)], axis=0)


def widened(matrix):
    return jnp.concatenate([matrix, jnp.ones((matrix.shape[0], ONES), bf16)], axis=1)


def head_rows(head):
    return slice(head * HEAD_WIDTH, (head + 1) * HEAD_WIDTH)


def own_forward_kernel(
    q_ref, k_ref, v_ref, nq_ref, nk_ref, acc_ref, top_ref, p_ref, query_ref, keys_ref, values_ref,
    *, group, prompt_rows, step
):
    rows = q_ref.shape[1]
    wide = HEAD_WIDTH + ONES
    tiles, _ = strips(prompt_rows, rows, step)

    keys_ref[...] = widened(k_ref[...].T)
    values_ref[:HEAD_WIDTH] = v_ref[...]
    values_ref[HEAD_WIDTH:] = jnp.ones((ONES, rows), bf16)
    top_ref[...] = jnp.zeros_like(top_ref)
    for head in range(group):
        query_ref[head, :HEAD_WIDTH] = q_ref[head_rows(head)]
        query_ref[head, HEAD_WIDTH:] = jnp.zeros((ONES, rows), bf16)

    @pl.when(jnp.max(nq_ref[...]) * jnp.max(nk_ref[...]) >= SAFE_BOUND * SAFE_BOUND)
    def _():
        for head in range(group):
            top_ref[0, head : head + 1] = jnp.full((1, rows), FAR, f32)
            for key, first, end, _, _ in tiles:
                scores = masked(contract(keys_ref[key : key + step], query_ref[head, :, first:end], 1, 0), FAR)
                top_ref[0, head : head + 1, first:end] = jnp.maximum(
                    top_ref[0, head : head + 1, first:end], jnp.max(scores, axis=0, keepdims=True)
                )
            scores = contract(keys_ref[:prompt_rows], query_ref[head, :, prompt_rows:], 1, 0)
            top_ref[0, head : head + 1, prompt_rows:] = jnp.maximum(
                top_ref[0, head : head + 1, prompt_rows:], jnp.max(scores, axis=0, keepdims=True)
            )
        for head in range(group):
            query_ref[head, HEAD_WIDTH:] = in_parts(-top_ref[0, head : head + 1])

    for head in range(group):
        weights = jnp.exp2(contract(keys_ref[:prompt_rows], query_ref[head, :, prompt_rows:], 1, 0)).astype(bf16)
        p_ref[head, :prompt_rows] = weights
        acc_ref[head * wide : (head + 1) * wide, prompt_rows:] = contract(
            values_ref[:, :prompt_rows], weights, 1, 0
        )
    for key, first, end, strip, column in tiles:
        for head in range(group):
            scores = contract(keys_ref[key : key + step], query_ref[head, :, first:end], 1, 0)
            weights = masked(jnp.exp2(scores), 0.0).astype(bf16)
            row = prompt_rows + strip * step
            p_ref[head, row : row + step, column : column + end - first] = weights
            part = contract(values_ref[:, key : key + step], weights, 1, 0)
            at = slice(head * wide, (head + 1) * wide)
            if key == 0:
                acc_ref[at, first:end] = part
            else:
                acc_ref[at, first:end] += part


def own_forward(q, k, v, norm_q, norm_k, kv_heads, prompt_rows, step=256):
    rows = q.shape[1]
    group = q.shape[0] // HEAD_WIDTH // kv_heads
    wide = HEAD_WIDTH + ONES
    block = lambda n: pl.BlockSpec((n, rows), lambda h: (h, 0))
    _, strip_rows = strips(prompt_rows, rows, step)
    assert strip_rows == prompt_rows
    shape = jax.ShapeDtypeStruct
    return pl.pallas_call(
        functools.partial(own_forward_kernel, group=group, prompt_rows=prompt_rows, step=step),
        grid=(kv_heads,),
        in_specs=[
            block(group * HEAD_WIDTH), block(HEAD_WIDTH), block(HEAD_WIDTH), resident(norm_q.shape), resident(norm_k.shape)
        ],
        out_specs=(
            block(group * wide),
            pl.BlockSpec((1, group, rows), lambda h: (h, 0, 0)),
            pl.BlockSpec((group, 2 * prompt_rows, rows - prompt_rows), lambda h: (h, 0, 0)),
        ),
        scratch_shapes=[
            pltpu.VMEM((group, wide, rows), bf16),
            pltpu.VMEM((rows, wide), bf16),
            pltpu.VMEM((wide, rows), bf16),
        ],
        out_shape=(
            shape((kv_heads * group * wide, rows), f32),
            shape((kv_heads, group, rows), f32),
            shape((kv_heads * group, 2 * prompt_rows, rows - prompt_rows), bf16),
        ),
        compiler_params=pltpu.CompilerParams(vmem_limit_bytes=60 * MIB),
        name="own_forward",
    )(q, k, v, norm_q, norm_k)


def other_forward_kernel(
    seen_ref, q_ref, k_ref, v_ref, nq_ref, acc_ref, top_ref, o_ref, own_ref, far_ref, p_ref, query_ref, keys_ref,
    values_ref, *, group, prompt_rows
):
    rows = q_ref.shape[1]
    wide = HEAD_WIDTH + ONES
    seen = seen_ref[0] > 0
    key = k_ref[0].astype(f32)
    norm_k = jnp.max(jnp.sum(key * key, axis=0, keepdims=True))
    slow = jnp.max(nq_ref[...]) * norm_k >= SAFE_BOUND * SAFE_BOUND
    keys_ref[...] = widened(k_ref[0].T)
    values_ref[:HEAD_WIDTH] = v_ref[0]
    values_ref[HEAD_WIDTH:] = jnp.ones((ONES, keys_ref.shape[0]), bf16)
    for head in range(group):
        query_ref[head, :HEAD_WIDTH] = q_ref[head_rows(head)]
        query_ref[head, HEAD_WIDTH:] = jnp.zeros((ONES, rows), bf16)
    far_ref[...] = jnp.zeros_like(far_ref)

    @pl.when(slow)
    def _():
        for head in range(group):
            for first, end in ((0, prompt_rows), (prompt_rows, rows)):
                scores = contract(keys_ref[...], query_ref[head, :, first:end], 1, 0)
                far_ref[0, head : head + 1, first:end] = jnp.max(scores, axis=0, keepdims=True)
            query_ref[head, HEAD_WIDTH:] = in_parts(-far_ref[0, head : head + 1])

    def finish(first, end, with_other):
        for head in range(group):
            own = acc_ref[head * wide : (head + 1) * wide, first:end]
            own_top = top_ref[0, head : head + 1, first:end]
            if with_other:
                weights = jnp.exp2(contract(keys_ref[...], query_ref[head, :, first:end], 1, 0)).astype(bf16)
                p_ref[head, :, first:end] = weights
                far = contract(values_ref[...], weights, 1, 0)
                far_top = far_ref[0, head : head + 1, first:end]
                top = jnp.maximum(own_top, far_top)
                own_scale, far_scale = jnp.exp2(own_top - top), jnp.exp2(far_top - top)
                total = own * own_scale + far * far_scale
                inverse = 1.0 / total[HEAD_WIDTH : HEAD_WIDTH + 1]
                far_ref[0, head : head + 1, first:end] = far_scale * inverse
                own_ref[0, head : head + 1, first:end] = own_scale * inverse
            else:
                total = own
                inverse = 1.0 / total[HEAD_WIDTH : HEAD_WIDTH + 1]
                far_ref[0, head : head + 1, first:end] = jnp.zeros_like(inverse)
                own_ref[0, head : head + 1, first:end] = inverse
            o_ref[head_rows(head), first:end] = (total[:HEAD_WIDTH] * inverse).astype(bf16)

    finish(prompt_rows, rows, True)

    @pl.when(seen)
    def _():
        finish(0, prompt_rows, True)

    @pl.when(jnp.logical_not(seen))
    def _():
        finish(0, prompt_rows, False)


def half_index(h, j, seen):
    return (h, 0, 1 - j * jnp.minimum(seen[0], 1))


def other_forward(seen, q, kv, norm_q, acc, top, kv_heads, prompt_rows):
    rows = q.shape[1]
    group = q.shape[0] // HEAD_WIDTH // kv_heads
    wide = HEAD_WIDTH + ONES
    keys = kv.shape[2]
    block = lambda n, m: pl.BlockSpec((n, m), lambda h, s: (h, 0))
    row_block = pl.BlockSpec((1, group, rows), lambda h, s: (h, 0, 0))
    shape = jax.ShapeDtypeStruct
    return pl.pallas_call(
        functools.partial(other_forward_kernel, group=group, prompt_rows=prompt_rows),
        grid_spec=pltpu.PrefetchScalarGridSpec(
            num_scalar_prefetch=1,
            grid=(kv_heads,),
            in_specs=[
                block(group * HEAD_WIDTH, rows),
                pl.BlockSpec((1, HEAD_WIDTH, keys), lambda h, s: (0, h, 0)),
                pl.BlockSpec((1, HEAD_WIDTH, keys), lambda h, s: (1, h, 0)),
                resident(norm_q.shape),
                block(group * wide, rows),
                row_block,
            ],
            out_specs=(
                block(group * HEAD_WIDTH, rows),
                row_block,
                row_block,
                pl.BlockSpec((group, keys, rows), lambda h, s: (h, 0, 0)),
            ),
            scratch_shapes=[
                pltpu.VMEM((group, wide, rows), bf16),
                pltpu.VMEM((keys, wide), bf16),
                pltpu.VMEM((wide, keys), bf16),
            ],
        ),
        out_shape=(
            shape(q.shape, bf16),
            shape((kv_heads, group, rows), f32),
            shape((kv_heads, group, rows), f32),
            shape((kv_heads * group, keys, rows), bf16),
        ),
        compiler_params=pltpu.CompilerParams(vmem_limit_bytes=60 * MIB),
        name="other_forward",
    )(seen, q, kv, kv, norm_q, acc, top)


def tile_backward(values, key_rows, weights, query, grad):
    slopes = contract(values, grad, 1, 0)
    slopes = (weights.astype(f32) * slopes).astype(bf16)
    query_grad = contract(key_rows, slopes, 1, 0)
    key_grad = contract(query, slopes, 1, 1)
    value_grad = contract(grad[:HEAD_WIDTH], weights, 1, 1)
    return query_grad, key_grad, value_grad


def fill_grads(g_ref, scale_ref, delta_ref, grad_ref, group):
    for head in range(group):
        scale = scale_ref[0, head : head + 1]
        grad_ref[head, :HEAD_WIDTH] = (g_ref[head_rows(head)].astype(f32) * scale).astype(bf16)
        grad_ref[head, HEAD_WIDTH:] = in_parts(-delta_ref[0, head : head + 1] * scale)


def other_backward_kernel(
    seen_ref, q_ref, g_ref, scale_ref, delta_ref, k_ref, v_ref, p_ref, dq_ref, dkv_ref,
    grad_ref, values_ref, dk_sum, dv_sum, dq_sum, *, group, prompt_rows, step
):
    rows = q_ref.shape[1]
    seen = seen_ref[0] > 0
    stage = pl.program_id(1)

    def part(first, last, fresh):
        for low in range(0, k_ref.shape[2], step):
            span = slice(low, low + step)
            key_sum = value_sum = None
            for head in range(group):
                query_grad, key_grad, value_grad = tile_backward(
                    values_ref[span], k_ref[0, :, span], p_ref[head, span],
                    q_ref[head_rows(head), first:last], grad_ref[head, :, first:last],
                )
                if low == 0:
                    dq_sum[head_rows(head), first:last] = query_grad
                else:
                    dq_sum[head_rows(head), first:last] += query_grad
                key_sum = key_grad if key_sum is None else key_sum + key_grad
                value_sum = value_grad if value_sum is None else value_sum + value_grad
            if fresh:
                dk_sum[:, span] = key_sum
                dv_sum[:, span] = value_sum
            else:
                dk_sum[:, span] += key_sum
                dv_sum[:, span] += value_sum

    @pl.when(stage == 0)
    def _():
        fill_grads(g_ref, scale_ref, delta_ref, grad_ref, group)
        values_ref[...] = widened(v_ref[0].T)
        part(prompt_rows, rows, True)

    @pl.when((stage == 1) & seen)
    def _():
        part(0, prompt_rows, False)

    @pl.when((stage == 1) & jnp.logical_not(seen))
    def _():
        dq_sum[:, :prompt_rows] = jnp.zeros((dq_ref.shape[0], prompt_rows), f32)

    @pl.when(stage == 1)
    def _():
        dq_ref[...] = dq_sum[...].astype(bf16)
        dkv_ref[0] = dk_sum[...].astype(bf16)
        dkv_ref[1] = dv_sum[...].astype(bf16)


def other_backward(seen, q, g, scale, delta, kv, p, kv_heads, prompt_rows, step=256):
    rows = q.shape[1]
    group = q.shape[0] // HEAD_WIDTH // kv_heads
    keys = kv.shape[2]
    block = lambda n, m: pl.BlockSpec((n, m), lambda h, j, s: (h, 0))
    row_block = pl.BlockSpec((1, group, rows), lambda h, j, s: (h, 0, 0))
    wide = group * HEAD_WIDTH
    shape = jax.ShapeDtypeStruct
    return pl.pallas_call(
        functools.partial(other_backward_kernel, group=group, prompt_rows=prompt_rows, step=step),
        grid_spec=pltpu.PrefetchScalarGridSpec(
            num_scalar_prefetch=1,
            grid=(kv_heads, 2),
            in_specs=[
                block(wide, rows), block(wide, rows), row_block, row_block,
                pl.BlockSpec((1, HEAD_WIDTH, keys), lambda h, j, s: (0, h, 0)),
                pl.BlockSpec((1, HEAD_WIDTH, keys), lambda h, j, s: (1, h, 0)),
                pl.BlockSpec((group, keys, prompt_rows), half_index),
            ],
            out_specs=(block(wide, rows), pl.BlockSpec((2, HEAD_WIDTH, keys), lambda h, j, s: (0, h, 0))),
            scratch_shapes=[
                pltpu.VMEM((group, HEAD_WIDTH + ONES, rows), bf16),
                pltpu.VMEM((keys, HEAD_WIDTH + ONES), bf16),
                pltpu.VMEM((HEAD_WIDTH, keys), f32),
                pltpu.VMEM((HEAD_WIDTH, keys), f32),
                pltpu.VMEM((wide, rows), f32),
            ],
        ),
        out_shape=(shape(q.shape, bf16), shape(kv.shape, bf16)),
        compiler_params=pltpu.CompilerParams(vmem_limit_bytes=60 * MIB),
        name="other_backward",
    )(seen, q, g, scale, delta, kv, kv, p)


def own_backward_kernel(
    q_ref, g_ref, scale_ref, delta_ref, k_ref, v_ref, p_ref, dq_in_ref, dq_ref, dk_ref, dv_ref,
    grad_ref, values_ref, dk_sum, dv_sum, dq_sum, *, group, prompt_rows, step
):
    rows = q_ref.shape[1]
    stage = pl.program_id(1)
    tiles, _ = strips(prompt_rows, rows, step)

    def one(key, first, end, place, columns):
        span = slice(key, key + step)
        key_sum = value_sum = None
        for head in range(group):
            query_grad, key_grad, value_grad = tile_backward(
                values_ref[span], k_ref[:, span], p_ref[head, place, columns],
                q_ref[head_rows(head), first:end], grad_ref[head, :, first:end],
            )
            dq_sum[head_rows(head), first:end] += query_grad
            key_sum = key_grad if key_sum is None else key_sum + key_grad
            value_sum = value_grad if value_sum is None else value_sum + value_grad
        dk_sum[:, span] += key_sum
        dv_sum[:, span] += value_sum

    @pl.when(stage == 0)
    def _():
        fill_grads(g_ref, scale_ref, delta_ref, grad_ref, group)
        values_ref[...] = widened(v_ref[...].T)
        dq_sum[...] = dq_in_ref[...].astype(f32)
        dk_sum[...] = jnp.zeros_like(dk_sum)
        dv_sum[...] = jnp.zeros_like(dv_sum)
        for key in range(0, prompt_rows, step):
            one(key, prompt_rows, rows, slice(key, key + step), slice(0, rows - prompt_rows))

    @pl.when(stage == 1)
    def _():
        for key, first, end, strip, column in tiles:
            one(key, first, end, slice(strip * step, (strip + 1) * step), slice(column, column + end - first))
        dq_ref[...] = dq_sum[...].astype(bf16)
        dk_ref[...] = dk_sum[...].astype(bf16)
        dv_ref[...] = dv_sum[...].astype(bf16)


def own_backward(q, g, scale, delta, k, v, p, dq, kv_heads, prompt_rows, step=256):
    rows = q.shape[1]
    group = q.shape[0] // HEAD_WIDTH // kv_heads
    block = lambda n: pl.BlockSpec((n, rows), lambda h, j: (h, 0))
    row_block = pl.BlockSpec((1, group, rows), lambda h, j: (h, 0, 0))
    wide = group * HEAD_WIDTH
    shape = jax.ShapeDtypeStruct
    return pl.pallas_call(
        functools.partial(own_backward_kernel, group=group, prompt_rows=prompt_rows, step=step),
        grid=(kv_heads, 2),
        in_specs=[
            block(wide), block(wide), row_block, row_block, block(HEAD_WIDTH), block(HEAD_WIDTH),
            pl.BlockSpec((group, prompt_rows, rows - prompt_rows), lambda h, j: (h, j, 0)),
            block(wide),
        ],
        out_specs=(block(wide), block(HEAD_WIDTH), block(HEAD_WIDTH)),
        scratch_shapes=[
            pltpu.VMEM((group, HEAD_WIDTH + ONES, rows), bf16),
            pltpu.VMEM((rows, HEAD_WIDTH + ONES), bf16),
            pltpu.VMEM((HEAD_WIDTH, rows), f32),
            pltpu.VMEM((HEAD_WIDTH, rows), f32),
            pltpu.VMEM((wide, rows), f32),
        ],
        out_shape=(shape(q.shape, bf16), shape(k.shape, bf16), shape(v.shape, bf16)),
        compiler_params=pltpu.CompilerParams(vmem_limit_bytes=60 * MIB),
        name="own_backward",
    )(q, g, scale, delta, k, v, p, dq)


def middle_kernel(
    x_ref, dy_ref, o_ref, gain_ref, wide_any, wd_any,
    out_ref, h2_ref, hidden_ref, dgate_ref, dup_ref, dattn_ref, dob_ref, delta_ref,
    wo_ref, wg_ref, wu_ref, wd_ref, sems, *, chunk
):
    step = pl.program_id(0)
    inner, total = wo_ref.shape[1], wg_ref.shape[1]
    lows = list(range(0, total, chunk))

    def loads(index):
        low = lows[index]
        span = pl.ds(low, chunk)
        places = (
            (wide_any.at[:, pl.ds(inner + low, chunk)], wg_ref.at[:, span]),
            (wide_any.at[:, pl.ds(inner + total + low, chunk)], wu_ref.at[:, span]),
            (wd_any.at[span], wd_ref.at[span]),
        )
        return [
            pltpu.make_async_copy(source, target, sems.at[1 + 3 * index + i])
            for i, (source, target) in enumerate(places)
        ]

    def rows(loading):
        if loading:
            first = pltpu.make_async_copy(wide_any.at[:, pl.ds(0, inner)], wo_ref, sems.at[0])
            first.start()
            for index in range(len(lows)):
                for copy in loads(index):
                    copy.start()
            first.wait()
        ob = o_ref[...]
        x1 = x_ref[...].astype(f32) + contract(ob, wo_ref[...], 0, 0)
        inverse = lax.rsqrt(jnp.mean(x1 * x1, axis=-1, keepdims=True) + norm_eps)
        gain = gain_ref[1:2]
        h2 = (x1 * inverse * gain).astype(bf16)
        h2_ref[...] = h2
        dy = dy_ref[...]
        result = x1
        dh2 = None
        for index, low in enumerate(lows):
            if loading:
                for copy in loads(index):
                    copy.wait()
            span = slice(low, low + chunk)
            gate = contract(h2, wg_ref[:, span], 1, 0)
            up = contract(h2, wu_ref[:, span], 1, 0)
            dhidden = contract(dy, wd_ref[span], 1, 1)
            sigma = 0.5 + 0.5 * jnp.tanh(0.5 * gate)
            silu = gate * sigma
            hidden = (silu * up).astype(bf16)
            hidden_ref[:, span] = hidden
            result = result + contract(hidden, wd_ref[span], 1, 0)
            dgate = (dhidden * up * (sigma + silu * (1.0 - sigma))).astype(bf16)
            dup = (dhidden * silu).astype(bf16)
            dgate_ref[:, span] = dgate
            dup_ref[:, span] = dup
            part = contract(dgate, wg_ref[:, span], 1, 1) + contract(dup, wu_ref[:, span], 1, 1)
            dh2 = part if dh2 is None else dh2 + part
        out_ref[...] = result.astype(bf16)
        u = dh2 * gain
        dx1 = dy.astype(f32) + inverse * u - x1 * (inverse * inverse * inverse) * jnp.mean(
            u * x1, axis=-1, keepdims=True
        )
        dattn = dx1.astype(bf16)
        dattn_ref[...] = dattn
        dob = contract(wo_ref[...], dattn, 1, 1).astype(bf16)
        dob_ref[...] = dob
        product = dob.astype(f32) * ob.astype(f32)
        heads, group = delta_ref.shape[0], delta_ref.shape[1]
        for kv in range(heads):
            for member in range(group):
                at = (kv * group + member) * HEAD_WIDTH
                delta_ref[kv, member : member + 1] = jnp.sum(
                    product[at : at + HEAD_WIDTH], axis=0, keepdims=True
                )

    @pl.when(step == 0)
    def _():
        rows(True)

    @pl.when(step > 0)
    def _():
        rows(False)


def middle(x, dy, o, gain, wide, wd, kv_heads, tile=256, chunk=768):
    rows, width = x.shape
    hidden = wd.shape[0]
    q_rows = o.shape[0]
    group = q_rows // HEAD_WIDTH // kv_heads
    by_row = lambda n: pl.BlockSpec((tile, n), lambda i: (i, 0))
    any_spec = pl.BlockSpec(memory_space=pl.ANY)
    shape = jax.ShapeDtypeStruct
    return pl.pallas_call(
        functools.partial(middle_kernel, chunk=chunk),
        grid=(rows // tile,),
        in_specs=[by_row(width), by_row(width), pl.BlockSpec((q_rows, tile), lambda i: (0, i)),
                  resident(gain.shape)] + [any_spec] * 2,
        out_specs=(
            by_row(width), by_row(width), by_row(hidden), by_row(hidden), by_row(hidden), by_row(width),
            pl.BlockSpec((q_rows, tile), lambda i: (0, i)),
            pl.BlockSpec((kv_heads, group, tile), lambda i: (0, 0, i)),
        ),
        out_shape=(
            shape((rows, width), bf16), shape((rows, width), bf16), shape((rows, hidden), bf16),
            shape((rows, hidden), bf16), shape((rows, hidden), bf16), shape((rows, width), bf16),
            shape((q_rows, rows), bf16), shape((kv_heads, group, rows), f32),
        ),
        scratch_shapes=[pltpu.VMEM(s, bf16) for s in ((width, q_rows), (width, hidden), (width, hidden), wd.shape)]
        + [pltpu.SemaphoreType.DMA((1 + 3 * (hidden // chunk),))],
        compiler_params=pltpu.CompilerParams(vmem_limit_bytes=62 * MIB),
        name="middle",
    )(x, dy, o, gain, wide, wd)


def down_grads_kernel(dy_ref, hidden_ref, down_ref):
    down_ref[...] = contract(hidden_ref[...], dy_ref[...], 0, 0).astype(bf16)


def down_grads(dy, hidden, tile=512):
    rows, width = dy.shape
    total = hidden.shape[1]
    return pl.pallas_call(
        down_grads_kernel,
        grid=(total // tile,),
        in_specs=[resident(dy.shape), pl.BlockSpec((rows, tile), lambda i: (0, i))],
        out_specs=pl.BlockSpec((tile, width), lambda i: (i, 0)),
        out_shape=jax.ShapeDtypeStruct((total, width), bf16),
        compiler_params=pltpu.CompilerParams(vmem_limit_bytes=60 * MIB),
        name="down_grads",
    )(dy, hidden)


def wide_grads_kernel(o_any, h2_ref, dgate_ref, dup_ref, dattn_ref, out_ref, o_ref, sem, *, each):
    step = pl.program_id(0)
    copy = pltpu.make_async_copy(o_any, o_ref, sem)
    tile = out_ref.shape[1]
    rest = o_ref.shape[0] % tile

    @pl.when(step == 0)
    def _():
        copy.start()

    @pl.when(step < each)
    def _():
        out_ref[...] = contract(h2_ref[...], dgate_ref[...], 0, 0).astype(bf16)

    @pl.when((step >= each) & (step < 2 * each))
    def _():
        out_ref[...] = contract(h2_ref[...], dup_ref[...], 0, 0).astype(bf16)

    @pl.when(step == 2 * each)
    def _():
        copy.wait()

    last = pl.num_programs(0) - 1

    @pl.when((step >= 2 * each) & (step < last))
    def _():
        out_ref[...] = contract(o_ref[...], dattn_ref[...], 1, 0).astype(bf16)

    @pl.when(step == last)
    def _():
        width = rest or tile
        out_ref[:, :width] = contract(o_ref[...], dattn_ref[:, :width], 1, 0).astype(bf16)


def wide_grads(o, h2, dattn, dgate, dup, tile=512):
    rows, width = h2.shape
    total = dgate.shape[1]
    each = total // tile
    steps = 2 * each + pl.cdiv(width, tile)
    cols = lambda low, count: pl.BlockSpec((rows, tile), lambda i: (0, jnp.clip(i - low, 0, count - 1)))
    return pl.pallas_call(
        functools.partial(wide_grads_kernel, each=each),
        grid=(steps,),
        in_specs=[
            pl.BlockSpec(memory_space=pl.ANY), resident(h2.shape),
            cols(0, each), cols(each, each), cols(2 * each, steps - 2 * each),
        ],
        out_specs=pl.BlockSpec((width, tile), lambda i: (0, i)),
        out_shape=jax.ShapeDtypeStruct((width, 2 * total + width), bf16),
        scratch_shapes=[pltpu.VMEM(o.shape, bf16), pltpu.SemaphoreType.DMA],
        compiler_params=pltpu.CompilerParams(vmem_limit_bytes=60 * MIB),
        name="wide_grads",
    )(o, h2, dgate, dup, dattn)


def last_grads_kernel(
    x_ref, gain_ref, dq_ref, dk_ref, dv_ref, dkv_in_ref, cos_ref, sin_ref, lin_ref, dw_ref, acc_ref, *, prompt_steps
):
    step = pl.program_id(0)
    half = HEAD_WIDTH // 2
    cos, sin = cos_ref[...], sin_ref[...]

    def with_received(ref, which):
        return ref[...].astype(f32) + jnp.where(step < prompt_steps, dkv_in_ref[which].astype(f32), 0.0)

    def turned(value, scale):
        c, s = cos * scale, sin * scale
        pieces = []
        for at in range(0, value.shape[0], HEAD_WIDTH):
            a, b = value[at : at + half], value[at + half : at + HEAD_WIDTH]
            pieces += [a * c + b * s, b * c - a * s]
        return jnp.concatenate(pieces, axis=0)

    lin = jnp.concatenate(
        [
            turned(dq_ref[...].astype(f32), HEAD_WIDTH**-0.5),
            turned(with_received(dk_ref, 0), LN2),
            with_received(dv_ref, 1),
        ],
        axis=0,
    ).astype(bf16).T
    lin_ref[...] = lin
    x = x_ref[...].astype(f32)
    inverse = lax.rsqrt(jnp.mean(x * x, axis=-1, keepdims=True) + norm_eps)
    h = (x * inverse * gain_ref[0:1]).astype(bf16)
    part = contract(h, lin, 0, 0)

    @pl.when(step == 0)
    def _():
        acc_ref[...] = part

    @pl.when(step > 0)
    def _():
        acc_ref[...] += part

    @pl.when(step == pl.num_programs(0) - 1)
    def _():
        dw_ref[...] = acc_ref[...].astype(bf16)


def last_grads(x, gains, dq, dk, dv, dkv_in, cos, sin, tile=512):
    rows, width = x.shape
    cols = lambda n: pl.BlockSpec((n, tile), lambda i: (0, i))
    steps = dkv_in.shape[2] // tile
    few = pl.BlockSpec((2, dk.shape[0], tile), lambda i: (0, 0, jnp.minimum(i, steps - 1)))
    shape = jax.ShapeDtypeStruct
    inner = dq.shape[0] + dk.shape[0] + dv.shape[0]
    return pl.pallas_call(
        functools.partial(last_grads_kernel, prompt_steps=steps),
        grid=(rows // tile,),
        in_specs=[pl.BlockSpec((tile, width), lambda i: (i, 0)), resident(gains.shape),
                  cols(dq.shape[0]), cols(dk.shape[0]), cols(dv.shape[0]), few,
                  cols(cos.shape[0]), cols(cos.shape[0])],
        out_specs=(pl.BlockSpec((tile, inner), lambda i: (i, 0)), pl.BlockSpec((width, inner), lambda i: (0, 0))),
        out_shape=(shape((rows, inner), bf16), shape((width, inner), bf16)),
        scratch_shapes=[pltpu.VMEM((width, inner), f32)],
        compiler_params=pltpu.CompilerParams(vmem_limit_bytes=60 * MIB),
        name="last_grads",
    )(x, gains, dq, dk, dv, dkv_in, cos, sin)


def settle_kernel(
    low_ref, first_ref, wide_ref, wide_in_ref, down_ref, down_in_ref, gains_ref, wa_ref, wb_ref, wc_ref, wg_ref, wu_ref,
    tokens_ref, *outs
):
    tokens_ref[...] = low_ref[...].astype(f32)

    @pl.when(pl.program_id(0) == 0)
    def _():
        settle_weights(
            first_ref, wide_ref, wide_in_ref, down_ref, down_in_ref, gains_ref, wa_ref, wb_ref, wc_ref, wg_ref, wu_ref, *outs
        )


def settle_weights(
    first_ref, wide_ref, wide_in_ref, down_ref, down_in_ref, gains_ref, wa_ref, wb_ref, wc_ref, wg_ref, wu_ref, *outs
):
    da, db, dc, dgate, dup, dout, ddown, gain_a, gain_f = outs
    gains = gains_ref[...].astype(f32)

    def spread(total, which):
        return jnp.broadcast_to(total / gains[:, which : which + 1], gains.shape).T[0:1]

    total = None
    at = 0
    for out, weight in ((da, wa_ref), (db, wb_ref), (dc, wc_ref)):
        value = first_ref[:, at : at + out.shape[1]]
        out[...] = value
        part = jnp.sum(value * weight[...].astype(f32), axis=1, keepdims=True)
        total = part if total is None else total + part
        at += out.shape[1]
    gain_a[...] = spread(total, 0)
    total = None
    at = 0
    for out, weight in ((dgate, wg_ref), (dup, wu_ref), (dout, None)):
        span = slice(at, at + out.shape[1])
        value = wide_ref[:, span].astype(f32) + wide_in_ref[:, span].astype(f32)
        out[...] = value
        if weight is not None:
            part = jnp.sum(value * weight[...].astype(f32), axis=1, keepdims=True)
            total = part if total is None else total + part
        at += out.shape[1]
    gain_f[...] = spread(total, 1)
    ddown[...] = down_ref[...].astype(f32) + down_in_ref[...].astype(f32)


def settle(low, first, wide, wide_in, down, down_in, gains, wa, wb, wc, wo, wg, wu):
    rows = first.shape[0]
    count, width = low.shape
    tile = count // 2
    shape = jax.ShapeDtypeStruct
    by_row = pl.BlockSpec((tile, width), lambda i: (i, 0))
    given = (first, wide, wide_in, down, down_in, gains, wa, wb, wc, wg, wu)
    whole = [shape(w.shape, f32) for w in (wa, wb, wc, wg, wu, wo, down)] + [shape((1, rows), f32)] * 2
    return pl.pallas_call(
        settle_kernel,
        grid=(count // tile,),
        in_specs=[by_row] + [resident(array.shape) for array in given],
        out_specs=[by_row] + [pl.BlockSpec(array.shape, lambda i: (0, 0)) for array in whole],
        out_shape=[shape(low.shape, f32)] + whole,
        compiler_params=pltpu.CompilerParams(vmem_limit_bytes=60 * MIB),
        name="settle",
    )(low, *given)


MESH_ID = pl.DeviceIdType.MESH


def whereabouts():
    z, y, w = lax.axis_index("group"), lax.axis_index("ctx"), lax.axis_index("wshard")
    return z, y, w // 2, w % 2


def device_at(z, y, x, core):
    return (z, y, x * 2 + core)


def slot_at(z, x, core):
    return z * 4 + x * 2 + core


def greet(partners):
    barrier = pltpu.get_barrier_semaphore()
    for partner in partners:
        pl.semaphore_signal(barrier, inc=1, device_id=partner, device_id_type=MESH_ID)
    pl.semaphore_wait(barrier, len(partners))


def neighbours(depth):
    z, y, x, core = whereabouts()
    along = [device_at((z + d) % depth, y, x, core) for d in range(1, depth)]
    return along, device_at(z, y, 1 - x, core), device_at(z, 1 - y, x, core), device_at(z, y, x, 1 - core)


class Copies:
    def __init__(self, send_sems, recv_sems):
        self.send_sems, self.recv_sems, self.made = send_sems, recv_sems, []

    def make(self, source, target, device):
        at = len(self.made)
        copy = pltpu.make_async_remote_copy(
            src_ref=source,
            dst_ref=target,
            send_sem=self.send_sems.at[at],
            recv_sem=self.recv_sems.at[at],
            device_id=device,
            device_id_type=MESH_ID,
        )
        self.made.append(copy)
        return copy


def gather_kernel(*refs, depth, split):
    *shards, wo_ref, wg_ref, wu_ref, out_ref, wide_ref, send_sems, recv_sems, own_sems = refs
    z, y, x, core = whereabouts()
    along, over_x, over_y, over_core = neighbours(depth)
    columns = out_ref.shape[2]
    given = pl.ds(pl.multiple_of(y * (columns - split), 128), split)
    got = pl.ds(pl.multiple_of((1 - y) * (columns - split), 128), split)
    common = pl.ds(split, columns - 2 * split)
    me = slot_at(z, x, core)
    copies = Copies(send_sems, recv_sems)
    view = lambda slot, span: out_ref.at[slot, :, span]

    def side_by_side(sources, target, first_sem):
        at = 0
        placed = []
        for index, source in enumerate(sources):
            width = source.shape[1]
            copy = pltpu.make_async_copy(source, target.at[:, pl.ds(at, width)], own_sems.at[first_sem + index])
            copy.start()
            placed.append(copy)
            at += width
        return placed

    own = side_by_side(shards, out_ref.at[me], 0)
    wide = side_by_side((wo_ref, wg_ref, wu_ref), wide_ref, len(shards))
    greet(along + [over_x, over_y, over_core])
    for copy in own:
        copy.wait()

    def send(slot, span, device):
        copy = copies.make(view(slot, span), view(slot, span), device)
        copy.start()
        return copy

    spans = (given, common)
    from_z, from_x, from_y, from_core = {}, {}, {}, []

    def onward(slot, part, d, side):
        if side == 0:
            from_x[d, part] = send(slot, spans[part], over_x)
        if part == 0:
            from_y[d, side] = send(slot, given, over_y)
        from_core.append(send(slot, spans[part], over_core))

    for part in range(2):
        for d in range(1, depth):
            from_z[d, part] = send(me, spans[part], along[d - 1])
        from_x[0, part] = send(me, spans[part], over_x)
    from_core.append(send(me, slice(None), over_core))
    for part in range(2):
        for d in range(1, depth):
            from_z[d, part].wait_recv()
            onward(slot_at((z + depth - d) % depth, x, core), part, d, 0)
    for part in range(2):
        for d in range(depth):
            from_x[d, part].wait_recv()
            onward(slot_at((z + depth - d) % depth, 1 - x, core), part, d, 1)
    for side in range(2):
        for d in range(1 - side, depth):
            from_y[d, side].wait_recv()
            slot = slot_at((z + depth - d) % depth, x if side == 0 else 1 - x, core)
            from_core.append(send(slot, got, over_core))
    for copy in from_core:
        copy.wait_recv()
    for copy in copies.made:
        copy.wait_send()
    for copy in wide:
        copy.wait()


def gather_all(shards, wide, depth, split):
    rows = shards[0].shape[0]
    columns = sum(shard.shape[1] for shard in shards)
    count = 2 * (depth - 1) + 2 * depth + 2 * depth - 1 + 3 * (2 * depth - 1) + 1
    return pl.pallas_call(
        functools.partial(gather_kernel, depth=depth, split=split),
        in_specs=[pl.BlockSpec(memory_space=pl.ANY)] * (len(shards) + len(wide)),
        out_specs=(pl.BlockSpec(memory_space=pltpu.VMEM), pl.BlockSpec(memory_space=pl.ANY)),
        out_shape=(
            jax.ShapeDtypeStruct((4 * depth, rows, columns), bf16),
            jax.ShapeDtypeStruct((rows, sum(shard.shape[1] for shard in wide)), bf16),
        ),
        scratch_shapes=[
            pltpu.SemaphoreType.DMA((count,)),
            pltpu.SemaphoreType.DMA((count,)),
            pltpu.SemaphoreType.DMA((len(shards) + len(wide),)),
        ],
        compiler_params=pltpu.CompilerParams(
            collective_id=1, has_side_effects=True, vmem_limit_bytes=60 * MIB
        ),
        name="gather_all",
    )(*shards, *wide)


def reduce_kernel(
    part_ref, lin_ref, w_ref, gain_ref, x_ref, dattn_ref, out_ref, tokens_ref,
    core_ref, sum_ref, over_ref, line_ref, z_ref, last_ref, twin_ref, send_sems, recv_sems, *, depth
):
    step = pl.program_id(0)
    steps = pl.num_programs(0)
    z, y, x, core = whereabouts()
    along, over_x, over_y, over_core = neighbours(depth)

    distances = list(range(1, depth)) + [0]
    order = [(d, side) for side in (1, 0) for d in distances]
    place = lambda d, side: ((z + d) % depth, x if side == 0 else 1 - x)

    def remote(source, target, device, at):
        return pltpu.make_async_remote_copy(
            src_ref=source,
            dst_ref=target,
            send_sem=send_sems.at[at],
            recv_sem=recv_sems.at[at],
            device_id=device,
            device_id_type=MESH_ID,
        )

    def to_core(at):
        to_z, to_x = place(*order[at])
        return remote(part_ref.at[slot_at(to_z, to_x, 1 - core)], core_ref.at[at], over_core, at)

    def to_x(at):
        return remote(sum_ref.at[at], over_ref.at[at], over_x, 2 * depth + at)

    def to_z(at):
        return remote(line_ref.at[at], z_ref.at[at], along[distances[at] - 1], 3 * depth + at)

    def to_y():
        return remote(last_ref, twin_ref, over_y, 4 * depth - 1)

    def core_sums(at):
        to_core(at).wait_recv()
        own_z, own_x = place(*order[at])
        sum_ref[at] = (part_ref[slot_at(own_z, own_x, core)].astype(f32) + core_ref[at].astype(f32)).astype(bf16)

    @pl.when(step == 0)
    def _():
        greet(along + [over_x, over_y, over_core])
        for at in range(2 * depth):
            to_core(at).start()

    @pl.when(step == 1)
    def _():
        for at in range(depth):
            core_sums(at)
            to_x(at).start()

    @pl.when(step == 2)
    def _():
        for at in range(depth, 2 * depth):
            core_sums(at)

    for at in range(depth):

        @pl.when(step == jnp.minimum(3 + at, steps - 1))
        def _():
            to_x(at).wait_recv()
            line_ref[at] = (sum_ref[depth + at].astype(f32) + over_ref[at].astype(f32)).astype(bf16)
            if distances[at]:
                to_z(at).start()

    lin = lin_ref[...]
    dh = contract(lin, w_ref[:, : lin.shape[1]], 1, 1)
    tokens = x_ref[...].astype(f32)
    inverse = lax.rsqrt(jnp.mean(tokens * tokens, axis=-1, keepdims=True) + norm_eps)
    u = dh * gain_ref[0:1]
    tokens_ref[...] = (
        dattn_ref[...].astype(f32)
        + inverse * u
        - tokens * (inverse * inverse * inverse) * jnp.mean(u * tokens, axis=-1, keepdims=True)
    ).astype(bf16)

    @pl.when(step == steps - 1)
    def _():
        total = line_ref[depth - 1].astype(f32)
        for at in range(depth - 1):
            to_z(at).wait_recv()
            total = total + z_ref[at].astype(f32)
        last_ref[...] = total.astype(bf16)
        to_y().start()
        to_y().wait_recv()
        out_ref[...] = total + twin_ref[...].astype(f32)
        for at in range(2 * depth):
            to_core(at).wait_send()
        for at in range(depth):
            to_x(at).wait_send()
        for at in range(depth - 1):
            to_z(at).wait_send()
        to_y().wait_send()


def reduce_all(parts, lin, w, gains, x, dattn, depth, tile=256):
    slots, rows, columns = parts.shape
    count, width = x.shape
    sems = 4 * depth
    buffer = lambda *count: pltpu.VMEM(count + (rows, columns), bf16)
    by_row = lambda n: pl.BlockSpec((tile, n), lambda i: (i, 0))
    return pl.pallas_call(
        functools.partial(reduce_kernel, depth=depth),
        grid=(count // tile,),
        in_specs=[
            resident(parts.shape), by_row(lin.shape[1]), resident(w.shape), resident(gains.shape),
            by_row(width), by_row(width),
        ],
        out_specs=(pl.BlockSpec((rows, columns), lambda i: (0, 0)), by_row(width)),
        out_shape=(jax.ShapeDtypeStruct((rows, columns), f32), jax.ShapeDtypeStruct((count, width), bf16)),
        scratch_shapes=[
            buffer(2 * depth),
            buffer(2 * depth),
            buffer(depth),
            buffer(depth),
            buffer(depth - 1),
            buffer(),
            buffer(),
            pltpu.SemaphoreType.DMA((sems,)),
            pltpu.SemaphoreType.DMA((sems,)),
        ],
        compiler_params=pltpu.CompilerParams(
            collective_id=2, has_side_effects=True, vmem_limit_bytes=60 * MIB
        ),
        name="reduce_all",
    )(parts, lin, w, gains, x, dattn)


rope_base = 10000.0
masked_score = -1e30


def as_sent(array):

    def short(part):
        return part.astype(jnp.bfloat16) if part.dtype == jnp.float32 else part

    return jax.tree.map(short, array)


def rms_scale(value_rows_list, gain):
    return (
        value_rows_list
        * lax.rsqrt(jnp.mean(value_rows_list * value_rows_list, axis=-1, keepdims=True) + norm_eps)
        * gain
    )


def rms_back(value_rows_list, gain, upstream):
    inverse = lax.rsqrt(
        jnp.mean(value_rows_list * value_rows_list, axis=-1, keepdims=True) + norm_eps
    )
    scaled = upstream * gain
    gain_grad = jnp.sum(upstream * value_rows_list * inverse, axis=0)
    values_grad = inverse * scaled - value_rows_list * (inverse * inverse * inverse) * jnp.mean(
        scaled * value_rows_list, axis=-1, keepdims=True
    )
    return (gain_grad, values_grad)


def rope_tables(token_positions, head_size):
    half_size = head_size // 2
    frequency = rope_base ** (-(jnp.arange(half_size, dtype=jnp.float32) * 2.0) / head_size)
    angles = token_positions.astype(jnp.float32)[:, None] * frequency[None, :]
    return (jnp.cos(angles), jnp.sin(angles))


def rotary_apply(value_rows_list, cosine_table, sine_table):
    half_size = value_rows_list.shape[-1] // 2
    leading = value_rows_list[..., :half_size]
    trailing = value_rows_list[..., half_size:]
    cos_rows = cosine_table[:, None, :]
    sin_rows = sine_table[:, None, :]
    return jnp.concatenate(
        [leading * cos_rows - trailing * sin_rows, trailing * cos_rows + leading * sin_rows],
        axis=-1,
    )


def visible(query_pos, query_seg, key_pos, key_seg):
    same_doc = (key_seg[None, :] == query_seg[:, None]) | (key_seg[None, :] == 0)
    return same_doc & (key_pos[None, :] <= query_pos[:, None])


def tile_scores(query_tile, key_tile, scale):
    return (
        jnp.einsum("rhgd,khd->hgrk", query_tile, key_tile, preferred_element_type=jnp.float32)
        * scale
    )


def key_tiling(key_heads, value_heads, key_pos, key_seg):
    key_block = min(256, key_heads.shape[0])
    tile_count = key_heads.shape[0] // key_block
    return (
        key_heads.reshape(tile_count, key_block, key_heads.shape[1], key_heads.shape[2]),
        value_heads.reshape(tile_count, key_block, value_heads.shape[1], value_heads.shape[2]),
        key_pos.reshape(tile_count, key_block),
        key_seg.reshape(tile_count, key_block),
    )


def query_split(value_rows_list, query_block):
    return value_rows_list.reshape(
        (value_rows_list.shape[0] // query_block, query_block) + value_rows_list.shape[1:]
    )


def attention_forward(query_heads, key_heads, value_heads, places):
    query_pos, query_seg, key_pos, key_seg = places
    count_of_rows, kv_heads, group_size, head_size = query_heads.shape
    scale = head_size ** (-0.5)
    query_block = min(512, count_of_rows)
    key_tiles, value_tiles, kpos_tiles, kseg_tiles = key_tiling(
        key_heads, value_heads, key_pos, key_seg
    )

    def one_block(block_item):
        query_tile, tile_pos, tile_seg = block_item
        state_shape = (kv_heads, group_size, query_tile.shape[0])

        def lse_step(running, tile_item):
            key_tile, tile_kpos, tile_kseg = tile_item
            allowed = visible(tile_pos, tile_seg, tile_kpos, tile_kseg)

            def lse_open_tile(state):
                row_top, row_total = state
                scores = jnp.where(allowed, tile_scores(query_tile, key_tile, scale), masked_score)
                new_top = jnp.maximum(row_top, jnp.max(scores, axis=-1))
                weights = jnp.where(allowed, jnp.exp(scores - new_top[..., None]), 0.0)
                return (new_top, row_total * jnp.exp(row_top - new_top) + jnp.sum(weights, axis=-1))

            def lse_closed_tile(state):
                return state

            return (lax.cond(jnp.any(allowed), lse_open_tile, lse_closed_tile, running), None)

        initial = (
            jnp.full(state_shape, masked_score, jnp.float32),
            jnp.zeros(state_shape, jnp.float32),
        )
        (row_top, row_total), _ = lax.scan(lse_step, initial, (key_tiles, kpos_tiles, kseg_tiles))
        log_total = row_top + jnp.log(row_total)

        def out_step(running, tile_item):
            key_tile, value_tile, tile_kpos, tile_kseg = tile_item
            allowed = visible(tile_pos, tile_seg, tile_kpos, tile_kseg)

            def out_open_tile(accumulated):
                scores = jnp.where(allowed, tile_scores(query_tile, key_tile, scale), masked_score)
                probabilities = jnp.where(
                    allowed, jnp.exp(scores - log_total[..., None]), 0.0
                ).astype(jnp.bfloat16)
                return accumulated + jnp.einsum(
                    "hgrk,khd->rhgd", probabilities, value_tile, preferred_element_type=jnp.float32
                )

            def out_closed_tile(accumulated):
                return accumulated

            return (lax.cond(jnp.any(allowed), out_open_tile, out_closed_tile, running), None)

        output, _ = lax.scan(
            out_step,
            jnp.zeros(query_tile.shape, jnp.float32),
            (key_tiles, value_tiles, kpos_tiles, kseg_tiles),
        )
        return (output, log_total)

    outputs, log_totals = lax.map(
        one_block,
        (
            query_split(query_heads, query_block),
            query_split(query_pos, query_block),
            query_split(query_seg, query_block),
        ),
    )
    return (outputs.reshape(query_heads.shape), log_totals)


def attention_backward(
    query_heads, key_heads, value_heads, places, attended_grad, attended, log_totals
):
    query_pos, query_seg, key_pos, key_seg = places
    count_of_rows, kv_heads, group_size, head_size = query_heads.shape
    scale = head_size ** (-0.5)
    query_block = min(512, count_of_rows)
    key_tiles, value_tiles, kpos_tiles, kseg_tiles = key_tiling(
        key_heads, value_heads, key_pos, key_seg
    )

    def block_grads(sums, block_item):
        query_tile, grad_tile, output_tile, tile_lse, tile_pos, tile_seg = block_item
        tile_delta = jnp.einsum("rhgd,rhgd->hgr", grad_tile.astype(jnp.float32), output_tile)

        def back_step(query_grad, tile_item):
            key_tile, value_tile, tile_kpos, tile_kseg = tile_item
            allowed = visible(tile_pos, tile_seg, tile_kpos, tile_kseg)

            def back_open_tile(query_grad):
                scores = jnp.where(allowed, tile_scores(query_tile, key_tile, scale), masked_score)
                probabilities = jnp.where(allowed, jnp.exp(scores - tile_lse[..., None]), 0.0)
                prob_grad = jnp.einsum(
                    "rhgd,khd->hgrk", grad_tile, value_tile, preferred_element_type=jnp.float32
                )
                score_grad = (probabilities * (prob_grad - tile_delta[..., None])).astype(
                    jnp.bfloat16
                )
                query_grad = query_grad + scale * jnp.einsum(
                    "hgrk,khd->rhgd", score_grad, key_tile, preferred_element_type=jnp.float32
                )
                key_part = scale * jnp.einsum(
                    "hgrk,rhgd->khd", score_grad, query_tile, preferred_element_type=jnp.float32
                )
                value_part = jnp.einsum(
                    "hgrk,rhgd->khd",
                    probabilities.astype(jnp.bfloat16),
                    grad_tile,
                    preferred_element_type=jnp.float32,
                )
                return (query_grad, key_part, value_part)

            def back_closed_tile(query_grad):
                return (
                    query_grad,
                    jnp.zeros(key_tile.shape, jnp.float32),
                    jnp.zeros(value_tile.shape, jnp.float32),
                )

            query_grad, key_part, value_part = lax.cond(
                jnp.any(allowed), back_open_tile, back_closed_tile, query_grad
            )
            return (query_grad, (key_part, value_part))

        query_grad, (key_parts, value_parts) = lax.scan(
            back_step,
            jnp.zeros(query_tile.shape, jnp.float32),
            (key_tiles, value_tiles, kpos_tiles, kseg_tiles),
        )
        return ((sums[0] + key_parts, sums[1] + value_parts), query_grad)

    initial = (jnp.zeros(key_tiles.shape, jnp.float32), jnp.zeros(value_tiles.shape, jnp.float32))
    block_items = (
        query_split(query_heads, query_block),
        query_split(attended_grad, query_block),
        query_split(attended, query_block),
        log_totals,
        query_split(query_pos, query_block),
        query_split(query_seg, query_block),
    )
    (key_sum, value_sum), query_grads = lax.scan(block_grads, initial, block_items)
    key_rows = key_heads.shape[0]
    return (
        query_grads.reshape(query_heads.shape),
        key_sum.reshape(key_rows, -1),
        value_sum.reshape(key_rows, -1),
    )


def forward_pass(weights, inputs, places, tables, gather_pair):
    (
        attn_gain,
        query_full,
        key_complete,
        value_complete,
        out_full,
        ffn_gain,
        gate_full,
        up_full,
        down_full,
    ) = weights
    cosine_table, sine_table = tables
    count_of_rows = inputs.shape[0]
    normalized_input = rms_scale(inputs, attn_gain.astype(jnp.float32)).astype(jnp.bfloat16)
    query_lin = jnp.dot(normalized_input, query_full, preferred_element_type=jnp.float32)
    key_lin = jnp.dot(normalized_input, key_complete, preferred_element_type=jnp.float32)
    value_lin = jnp.dot(normalized_input, value_complete, preferred_element_type=jnp.float32)
    kv_heads = key_lin.shape[1] // HEAD_WIDTH
    query_rot = rotary_apply(
        query_lin.reshape(count_of_rows, -1, HEAD_WIDTH), cosine_table, sine_table
    ).astype(jnp.bfloat16)
    key_rot = (
        rotary_apply(key_lin.reshape(count_of_rows, kv_heads, HEAD_WIDTH), cosine_table, sine_table)
        .astype(jnp.bfloat16)
        .reshape(count_of_rows, -1)
    )
    value_low = value_lin.astype(jnp.bfloat16)
    keys_all, values_all = gather_pair((key_rot, value_low))
    group_size = query_rot.shape[1] // kv_heads
    query_heads = query_rot.reshape(count_of_rows, kv_heads, group_size, HEAD_WIDTH)
    key_heads = keys_all.reshape(-1, kv_heads, HEAD_WIDTH)
    value_heads = values_all.reshape(-1, kv_heads, HEAD_WIDTH)
    attended, log_totals = attention_forward(query_heads, key_heads, value_heads, places)
    attended_low = attended.reshape(count_of_rows, -1).astype(jnp.bfloat16)
    mixed = inputs + jnp.dot(attended_low, out_full, preferred_element_type=jnp.float32)
    normed_two = rms_scale(mixed, ffn_gain.astype(jnp.float32)).astype(jnp.bfloat16)
    gate = jnp.dot(normed_two, gate_full, preferred_element_type=jnp.float32)
    up_value = jnp.dot(normed_two, up_full, preferred_element_type=jnp.float32)
    hidden = (jax.nn.silu(gate) * up_value).astype(jnp.bfloat16)
    result = mixed + jnp.dot(hidden, down_full, preferred_element_type=jnp.float32)
    return (
        normalized_input,
        query_heads,
        key_heads,
        value_heads,
        attended,
        attended_low,
        log_totals,
        mixed,
        normed_two,
        gate,
        up_value,
        hidden,
        result,
    )


def general_local(
    tokens,
    block_map,
    attention_gain,
    query_weight,
    key_matrix,
    value_matrix,
    output_weight,
    feedforward_gain,
    gate_weight,
    up_weight,
    down_weight,
    out_grad,
):
    shards = (
        attention_gain,
        query_weight,
        key_matrix,
        value_matrix,
        output_weight,
        feedforward_gain,
        gate_weight,
        up_weight,
        down_weight,
    )
    count_of_rows = tokens.shape[1]
    ctx_rank = lax.axis_index("ctx")
    blocks = block_map[0]
    block_rows = count_of_rows // 2
    group_rows = blocks.shape[0] * block_rows
    prompt_rows = group_rows // 2
    natural = (
        blocks[:, None] * block_rows + jnp.arange(block_rows, dtype=jnp.int32)[None, :]
    ).reshape(-1)
    in_prompt = natural < prompt_rows
    key_pos = jnp.where(in_prompt, natural, prompt_rows + (natural - prompt_rows) % CONTINUE_LENGTH)
    key_seg = jnp.where(in_prompt, 0, 1 + (natural - prompt_rows) // CONTINUE_LENGTH)
    query_pos = lax.dynamic_slice_in_dim(key_pos, ctx_rank * count_of_rows, count_of_rows)
    query_seg = lax.dynamic_slice_in_dim(key_seg, ctx_rank * count_of_rows, count_of_rows)
    places = (query_pos, query_seg, key_pos, key_seg)
    cosine_table, sine_table = rope_tables(query_pos, HEAD_WIDTH)
    tables = (cosine_table, sine_table)
    inputs = tokens[0].astype(jnp.float32)
    full_weights = (
        lax.all_gather(shards[0], ("group", "wshard"), axis=0, tiled=True),
        lax.all_gather(shards[1], ("group", "wshard"), axis=0, tiled=True),
        lax.all_gather(shards[2], ("group", "wshard"), axis=0, tiled=True),
        lax.all_gather(shards[3], ("group", "wshard"), axis=0, tiled=True),
        lax.all_gather(shards[4], ("group", "wshard"), axis=0, tiled=True),
        lax.all_gather(shards[5], ("group", "wshard"), axis=0, tiled=True),
        lax.all_gather(shards[6], ("group", "wshard"), axis=0, tiled=True),
        lax.all_gather(shards[7], ("group", "wshard"), axis=0, tiled=True),
        lax.all_gather(shards[8], ("group", "wshard"), axis=0, tiled=True),
    )
    forward = forward_pass(
        full_weights,
        inputs,
        places,
        tables,
        lambda packed: jax.tree.map(
            lambda part, own: part.astype(own.dtype),
            lax.all_gather(as_sent(packed), "ctx", axis=0, tiled=True),
            packed,
        ),
    )
    layer_out = forward[12].astype(jnp.bfloat16)
    back_weights = (
        lax.all_gather(shards[0], ("group", "wshard"), axis=0, tiled=True),
        lax.all_gather(shards[1], ("group", "wshard"), axis=0, tiled=True),
        lax.all_gather(shards[2], ("group", "wshard"), axis=0, tiled=True),
        lax.all_gather(shards[3], ("group", "wshard"), axis=0, tiled=True),
        lax.all_gather(shards[4], ("group", "wshard"), axis=0, tiled=True),
        lax.all_gather(shards[5], ("group", "wshard"), axis=0, tiled=True),
        lax.all_gather(shards[6], ("group", "wshard"), axis=0, tiled=True),
        lax.all_gather(shards[7], ("group", "wshard"), axis=0, tiled=True),
        lax.all_gather(shards[8], ("group", "wshard"), axis=0, tiled=True),
    )
    saved = forward_pass(
        back_weights,
        inputs,
        places,
        tables,
        lambda packed: jax.tree.map(
            lambda part, own: part.astype(own.dtype),
            lax.all_gather(as_sent(packed), "ctx", axis=0, tiled=True),
            packed,
        ),
    )
    (
        normalized_input,
        query_heads,
        key_heads,
        value_heads,
        attended,
        attended_low,
        log_totals,
        mixed,
        normed_two,
        gate,
        up_value,
        hidden,
        result,
    ) = saved
    (
        attn_gain,
        query_full,
        key_complete,
        value_complete,
        out_full,
        ffn_gain,
        gate_full,
        up_full,
        down_full,
    ) = back_weights
    upstream = out_grad[0].astype(jnp.float32)
    ffn_grad = upstream.astype(jnp.bfloat16)
    grad_down = jnp.einsum("rf,rd->fd", hidden, ffn_grad, preferred_element_type=jnp.float32)
    hidden_grad = jnp.einsum("rd,fd->rf", ffn_grad, down_full, preferred_element_type=jnp.float32)
    gate_sigmoid = jax.nn.sigmoid(gate)
    gate_grad = (
        hidden_grad * up_value * gate_sigmoid * (1.0 + gate * (1.0 - gate_sigmoid))
    ).astype(jnp.bfloat16)
    up_grad = (hidden_grad * (gate * gate_sigmoid)).astype(jnp.bfloat16)
    grad_gate = jnp.einsum("rd,rf->df", normed_two, gate_grad, preferred_element_type=jnp.float32)
    grad_up = jnp.einsum("rd,rf->df", normed_two, up_grad, preferred_element_type=jnp.float32)
    normed_two_grad = jnp.einsum(
        "rf,df->rd", gate_grad, gate_full, preferred_element_type=jnp.float32
    ) + jnp.einsum("rf,df->rd", up_grad, up_full, preferred_element_type=jnp.float32)
    grad_ffn_gain, mixed_back = rms_back(mixed, ffn_gain.astype(jnp.float32), normed_two_grad)
    mixed_grad = upstream + mixed_back
    attn_grad = mixed_grad.astype(jnp.bfloat16)
    grad_out = jnp.einsum("rf,rd->fd", attended_low, attn_grad, preferred_element_type=jnp.float32)
    attended_grad = (
        jnp.einsum("rd,fd->rf", attn_grad, out_full, preferred_element_type=jnp.float32)
        .astype(jnp.bfloat16)
        .reshape(attended.shape)
    )
    query_grad, key_grad, value_grad = attention_backward(
        query_heads, key_heads, value_heads, places, attended_grad, attended, log_totals
    )
    key_local, value_local = (
        lax.psum_scatter(
            key_grad.astype(jnp.bfloat16), "ctx", scatter_dimension=0, tiled=True
        ).astype(jnp.float32),
        lax.psum_scatter(
            value_grad.astype(jnp.bfloat16), "ctx", scatter_dimension=0, tiled=True
        ).astype(jnp.float32),
    )
    query_lin_grad = (
        rotary_apply(query_grad.reshape(count_of_rows, -1, HEAD_WIDTH), cosine_table, -sine_table)
        .reshape(count_of_rows, -1)
        .astype(jnp.bfloat16)
    )
    key_lin_grad = (
        rotary_apply(key_local.reshape(count_of_rows, -1, HEAD_WIDTH), cosine_table, -sine_table)
        .reshape(count_of_rows, -1)
        .astype(jnp.bfloat16)
    )
    value_lin_grad = value_local.astype(jnp.bfloat16)
    grad_query = jnp.einsum(
        "rd,rf->df", normalized_input, query_lin_grad, preferred_element_type=jnp.float32
    )
    grad_key = jnp.einsum(
        "rd,rf->df", normalized_input, key_lin_grad, preferred_element_type=jnp.float32
    )
    grad_value = jnp.einsum(
        "rd,rf->df", normalized_input, value_lin_grad, preferred_element_type=jnp.float32
    )
    normed_grad = jnp.einsum(
        "rf,df->rd", query_lin_grad, query_full, preferred_element_type=jnp.float32
    )
    normed_grad = normed_grad + jnp.einsum(
        "rf,df->rd", key_lin_grad, key_complete, preferred_element_type=jnp.float32
    )
    normed_grad = normed_grad + jnp.einsum(
        "rf,df->rd", value_lin_grad, value_complete, preferred_element_type=jnp.float32
    )
    grad_attn_gain, input_back = rms_back(inputs, attn_gain.astype(jnp.float32), normed_grad)
    input_grad = mixed_grad + input_back
    partial_grads = (
        grad_attn_gain,
        grad_query,
        grad_key,
        grad_value,
        grad_out,
        grad_ffn_gain,
        grad_gate,
        grad_up,
        grad_down,
    )
    reduced = (
        lax.psum_scatter(
            partial_grads[0].astype(jnp.bfloat16),
            ("group", "wshard"),
            scatter_dimension=0,
            tiled=True,
        ).astype(jnp.float32),
        lax.psum_scatter(
            partial_grads[1].astype(jnp.bfloat16),
            ("group", "wshard"),
            scatter_dimension=0,
            tiled=True,
        ).astype(jnp.float32),
        lax.psum_scatter(
            partial_grads[2].astype(jnp.bfloat16),
            ("group", "wshard"),
            scatter_dimension=0,
            tiled=True,
        ).astype(jnp.float32),
        lax.psum_scatter(
            partial_grads[3].astype(jnp.bfloat16),
            ("group", "wshard"),
            scatter_dimension=0,
            tiled=True,
        ).astype(jnp.float32),
        lax.psum_scatter(
            partial_grads[4].astype(jnp.bfloat16),
            ("group", "wshard"),
            scatter_dimension=0,
            tiled=True,
        ).astype(jnp.float32),
        lax.psum_scatter(
            partial_grads[5].astype(jnp.bfloat16),
            ("group", "wshard"),
            scatter_dimension=0,
            tiled=True,
        ).astype(jnp.float32),
        lax.psum_scatter(
            partial_grads[6].astype(jnp.bfloat16),
            ("group", "wshard"),
            scatter_dimension=0,
            tiled=True,
        ).astype(jnp.float32),
        lax.psum_scatter(
            partial_grads[7].astype(jnp.bfloat16),
            ("group", "wshard"),
            scatter_dimension=0,
            tiled=True,
        ).astype(jnp.float32),
        lax.psum_scatter(
            partial_grads[8].astype(jnp.bfloat16),
            ("group", "wshard"),
            scatter_dimension=0,
            tiled=True,
        ).astype(jnp.float32),
    )
    summed = (
        lax.psum(reduced[0].astype(jnp.bfloat16), "ctx").astype(jnp.float32),
        lax.psum(reduced[1].astype(jnp.bfloat16), "ctx").astype(jnp.float32),
        lax.psum(reduced[2].astype(jnp.bfloat16), "ctx").astype(jnp.float32),
        lax.psum(reduced[3].astype(jnp.bfloat16), "ctx").astype(jnp.float32),
        lax.psum(reduced[4].astype(jnp.bfloat16), "ctx").astype(jnp.float32),
        lax.psum(reduced[5].astype(jnp.bfloat16), "ctx").astype(jnp.float32),
        lax.psum(reduced[6].astype(jnp.bfloat16), "ctx").astype(jnp.float32),
        lax.psum(reduced[7].astype(jnp.bfloat16), "ctx").astype(jnp.float32),
        lax.psum(reduced[8].astype(jnp.bfloat16), "ctx").astype(jnp.float32),
    )
    gain_attn, gain_ffn = (summed[0], summed[5])
    matrices = (summed[1], summed[2], summed[3], summed[4], summed[6], summed[7], summed[8])
    return (
        layer_out[None],
        input_grad[None],
        gain_attn,
        matrices[0],
        matrices[1],
        matrices[2],
        matrices[3],
        gain_ffn,
        matrices[4],
        matrices[5],
        matrices[6],
    )


OWNERS = ("group", "wshard")
SWAP = [(0, 1), (1, 0)]


def swap(array):
    return lax.ppermute(array, "ctx", SWAP)


def fast_local(
    tokens, block_map, attention_gain, query_weight, key_matrix, value_matrix, output_weight,
    feedforward_gain, gate_weight, up_weight, down_weight, out_grad,
):
    x, dy = tokens[0], out_grad[0]
    rows, width = x.shape
    prompt_rows = rows // 2
    q_rows, kv_rows = query_weight.shape[1], key_matrix.shape[1]
    kv_heads = kv_rows // HEAD_WIDTH
    hidden = gate_weight.shape[1]
    shard_rows = query_weight.shape[0]
    block = lax.dynamic_index_in_dim(block_map[0], 2 * lax.axis_index("ctx"), 0, False)
    seen = (block > 0).astype(jnp.int32)
    prompt_total = block_map.shape[1] // 2 * prompt_rows

    depth = lax.axis_size("group")

    gain_columns = jnp.pad(jnp.stack([attention_gain, feedforward_gain], axis=1), ((0, 0), (0, 126)))
    shards = (query_weight, key_matrix, value_matrix, gain_columns)
    split = sum(shard.shape[1] for shard in shards) // 3 // 128 * 128
    wd = lax.all_gather(down_weight, OWNERS, axis=0, tiled=True)
    first, wide = gather_all(shards, (output_weight, gate_weight, up_weight), depth, split)
    first = first.reshape(width, -1)
    wide = lax.all_gather(wide, OWNERS, axis=0, tiled=True)

    at = jnp.arange(rows, dtype=jnp.int32)
    positions = jnp.where(
        at < prompt_rows, block * prompt_rows + at, prompt_total + (at - prompt_rows) % CONTINUE_LENGTH
    )
    half = HEAD_WIDTH // 2
    frequency = (rope_base ** (-(np.arange(half) * 2.0) / HEAD_WIDTH)).astype(np.float32)
    angles = frequency[:, None] * positions.astype(f32)[None, :]
    cos, sin = jnp.cos(angles), jnp.sin(angles)

    q, k, v, kv, norm_q, norm_k, gains = project(x, first, cos, sin, q_rows, kv_rows, prompt_rows)
    kv_other = swap(kv)
    acc, top, p_own = own_forward(q, k, v, norm_q, norm_k, kv_heads, prompt_rows)
    o, own_scale, far_scale, p_far = other_forward(seen[None], q, kv_other, norm_q, acc, top, kv_heads, prompt_rows)
    layer_out, h2, hid, dgate, dup, dattn, dob, delta = middle(x, dy, o, gains, wide, wd, kv_heads)
    scatter = lambda a: lax.psum_scatter(a, OWNERS, scatter_dimension=0, tiled=True)
    d_down = down_grads(dy, hid)
    h2, d_down = lax.optimization_barrier((h2, d_down))
    d_down = scatter(d_down)
    d_wide = wide_grads(o, h2, dattn, dgate, dup)
    dob, d_wide = lax.optimization_barrier((dob, d_wide))
    d_wide = scatter(d_wide)
    dq, dkv_far = other_backward(seen[None], q, dob, far_scale, delta, kv_other, p_far, kv_heads, prompt_rows)
    dkv_in = swap(dkv_far)
    d_down, dkv_in = lax.optimization_barrier((d_down, dkv_in))
    d_down_in = swap(d_down)
    dq, dk, dv = own_backward(q, dob, own_scale, delta, k, v, p_own, dq, kv_heads, prompt_rows)
    lin, d_first = last_grads(x, gains, dq, dk, dv, dkv_in, cos, sin)
    d_first, d_wide = lax.optimization_barrier((d_first, d_wide))
    d_wide_in = swap(d_wide)
    d_first, low_tokens = reduce_all(d_first.reshape(4 * depth, shard_rows, -1), lin, first, gains, x, dattn, depth)
    grad_tokens, d_q, d_k, d_v, d_gate, d_up, d_out, d_down, d_gain_a, d_gain_f = settle(
        low_tokens, d_first, d_wide, d_wide_in, d_down, d_down_in, gain_columns,
        query_weight, key_matrix, value_matrix, output_weight, gate_weight, up_weight,
    )
    return (
        layer_out[None],
        grad_tokens[None],
        d_gain_a[0],
        d_q,
        d_k,
        d_v,
        d_out,
        d_gain_f[0],
        d_gate,
        d_up,
        d_down,
    )


def local(mesh, tokens, block_map, *rest):
    block_rows = tokens.shape[1] // 2
    whole = (
        mesh.shape["ctx"] == 2
        and mesh.shape["wshard"] == 4
        and block_rows % CONTINUE_LENGTH == 0
        and tokens.shape[0] == 1
    )
    return (fast_local if whole else general_local)(tokens, block_map, *rest)


def solution(mesh):
    return jax.shard_map(
        lambda *args: local(mesh, *args),
        mesh=mesh,
        in_specs=(
            P(("group", "wshard"), "ctx", None),
            P(("group", "wshard"), None),
            P(("group", "wshard")),
            P(("group", "wshard"), None),
            P(("group", "wshard"), None),
            P(("group", "wshard"), None),
            P(("group", "wshard"), None),
            P(("group", "wshard")),
            P(("group", "wshard"), None),
            P(("group", "wshard"), None),
            P(("group", "wshard"), None),
            P(("group", "wshard"), "ctx", None),
        ),
        out_specs=(
            P(("group", "wshard"), "ctx", None),
            P(("group", "wshard"), "ctx", None),
            P(("group", "wshard")),
            P(("group", "wshard"), None),
            P(("group", "wshard"), None),
            P(("group", "wshard"), None),
            P(("group", "wshard"), None),
            P(("group", "wshard")),
            P(("group", "wshard"), None),
            P(("group", "wshard"), None),
            P(("group", "wshard"), None),
        ),
        check_vma=False,
    )
```

```python
import functools

import jax
import jax.numpy as jnp
import numpy as np
from jax import lax
from jax.experimental import pallas as pl
from jax.experimental.pallas import tpu as pltpu
from jax.sharding import PartitionSpec as P

f32 = jnp.float32
bf16 = jnp.bfloat16
HEAD_WIDTH = 64
CONTINUE_LENGTH = 512
norm_eps = 1e-05
LOG2E = 1.4426950408889634
LN2 = 0.6931471805599453
MIB = 2**20


def contract(a, b, dim_a, dim_b):
    return lax.dot_general(
        a, b, (((dim_a,), (dim_b,)), ((), ())), preferred_element_type=f32
    )


def resident(shape):
    zeros = (0,) * len(shape)
    return pl.BlockSpec(shape, lambda *_: zeros, pipeline_mode=pl.Buffered(1))


def project_kernel(
    x_ref, w_ref, cos_ref, sin_ref, q_ref, k_ref, v_ref, kv_ref, nq_ref, nk_ref, gains_ref, *, prompt_steps
):
    @pl.when(pl.program_id(0) == 0)
    def _():
        gains_ref[...] = w_ref[:, w_ref.shape[1] - 128 :].astype(f32).T[: gains_ref.shape[0]]

    x = x_ref[...].astype(f32)
    inverse = lax.rsqrt(jnp.mean(x * x, axis=-1, keepdims=True) + norm_eps)
    h = (x * inverse * gains_ref[0:1]).astype(bf16)
    q_rows, kv_rows = q_ref.shape[0], k_ref.shape[0]
    half = HEAD_WIDTH // 2
    scale = LOG2E * HEAD_WIDTH**-0.5
    cos, sin = cos_ref[...], sin_ref[...]

    def rotated(lin, out_ref, base, cos, sin):
        worst = jnp.zeros((1, lin.shape[1]), f32)
        for head in range(lin.shape[0] // HEAD_WIDTH):
            at = head * HEAD_WIDTH
            a, b = lin[at : at + half], lin[at + half : at + HEAD_WIDTH]
            first = (a * cos - b * sin).astype(bf16)
            second = (b * cos + a * sin).astype(bf16)
            out_ref[base + at : base + at + half] = first
            out_ref[base + at + half : base + at + HEAD_WIDTH] = second
            fa, fb = first.astype(f32), second.astype(f32)
            worst = jnp.maximum(worst, jnp.sum(fa * fa + fb * fb, axis=0, keepdims=True))
        return worst

    ht = h.T
    chunk = kv_rows
    qc, qs = cos * scale, sin * scale
    worst_q = worst_k = None
    for at in range(0, q_rows + 2 * kv_rows, chunk):
        lin = contract(w_ref[:, at : at + chunk], ht, 0, 0)
        if at < q_rows:
            worst = rotated(lin, q_ref, at, qc, qs)
            worst_q = worst if worst_q is None else jnp.maximum(worst_q, worst)
        elif at < q_rows + kv_rows:
            worst = rotated(lin, k_ref, at - q_rows, cos, sin)
            worst_k = worst if worst_k is None else jnp.maximum(worst_k, worst)
        else:
            v_ref[pl.ds(at - q_rows - kv_rows, chunk)] = lin.astype(bf16)
    nq_ref[...] = worst_q
    nk_ref[...] = worst_k

    @pl.when(pl.program_id(0) < prompt_steps)
    def _():
        kv_ref[0] = k_ref[...]
        kv_ref[1] = v_ref[...]


def project(x, w, cos, sin, q_rows, kv_rows, prompt_rows, tile=512):
    rows, width = x.shape
    prompt_steps = prompt_rows // tile
    cols = lambda n: pl.BlockSpec((n, tile), lambda i: (0, i))
    return pl.pallas_call(
        functools.partial(project_kernel, prompt_steps=prompt_steps),
        grid=(rows // tile,),
        in_specs=[
            pl.BlockSpec((tile, width), lambda i: (i, 0)),
            resident(w.shape),
            cols(cos.shape[0]),
            cols(cos.shape[0]),
        ],
        out_specs=(
            cols(q_rows),
            cols(kv_rows),
            cols(kv_rows),
            pl.BlockSpec((2, kv_rows, tile), lambda i: (0, 0, jnp.minimum(i, prompt_steps - 1))),
            cols(1),
            cols(1),
            pl.BlockSpec((8, width), lambda i: (0, 0)),
        ),
        out_shape=(
            jax.ShapeDtypeStruct((q_rows, rows), bf16),
            jax.ShapeDtypeStruct((kv_rows, rows), bf16),
            jax.ShapeDtypeStruct((kv_rows, rows), bf16),
            jax.ShapeDtypeStruct((2, kv_rows, prompt_rows), bf16),
            jax.ShapeDtypeStruct((1, rows), f32),
            jax.ShapeDtypeStruct((1, rows), f32),
            jax.ShapeDtypeStruct((8, width), f32),
        ),
        compiler_params=pltpu.CompilerParams(vmem_limit_bytes=60 * MIB),
        name="project",
    )(x, w, cos, sin)


ONES = 16
SAFE_BOUND = 80.0
FAR = -1e30


def causal(keys, columns):
    return lax.broadcasted_iota(jnp.int32, (keys, columns), 0) <= lax.broadcasted_iota(
        jnp.int32, (keys, columns), 1
    )


def masked(tile, fill):
    step = tile.shape[0]
    front = jnp.where(causal(step, step), tile[:, :step], fill)
    return front if tile.shape[1] == step else jnp.concatenate([front, tile[:, step:]], axis=1)


def strips(prompt_rows, rows, step):
    tiles = []
    at = 0
    while at < rows:
        end = prompt_rows if at < prompt_rows else at + CONTINUE_LENGTH
        tiles += [(end - key, key, end) for key in range(at, end, step)]
        at = end
    room, laid = [], []
    for width, key, end in sorted(tiles, reverse=True):
        for strip in range(len(room) + 1):
            if strip == len(room):
                room.append(rows - prompt_rows)
            if room[strip] >= width:
                laid.append((key, key, end, strip, rows - prompt_rows - room[strip]))
                room[strip] -= width
                break
    return sorted(laid), len(room) * step


def in_parts(row):
    high = row.astype(bf16)
    rest = row - high.astype(f32)
    middle = rest.astype(bf16)
    low = (rest - middle.astype(f32)).astype(bf16)
    return jnp.concatenate([high, middle, low, jnp.zeros((ONES - 3, row.shape[1]), bf16)], axis=0)


def widened(matrix):
    return jnp.concatenate([matrix, jnp.ones((matrix.shape[0], ONES), bf16)], axis=1)


def head_rows(head):
    return slice(head * HEAD_WIDTH, (head + 1) * HEAD_WIDTH)


def own_forward_kernel(
    q_ref, k_ref, v_ref, nq_ref, nk_ref, acc_ref, top_ref, p_ref, query_ref, keys_ref, values_ref,
    *, group, prompt_rows, step
):
    rows = q_ref.shape[1]
    wide = HEAD_WIDTH + ONES
    tiles, _ = strips(prompt_rows, rows, step)

    keys_ref[...] = widened(k_ref[...].T)
    values_ref[:HEAD_WIDTH] = v_ref[...]
    values_ref[HEAD_WIDTH:] = jnp.ones((ONES, rows), bf16)
    top_ref[...] = jnp.zeros_like(top_ref)
    for head in range(group):
        query_ref[head, :HEAD_WIDTH] = q_ref[head_rows(head)]
        query_ref[head, HEAD_WIDTH:] = jnp.zeros((ONES, rows), bf16)

    @pl.when(jnp.max(nq_ref[...]) * jnp.max(nk_ref[...]) >= SAFE_BOUND * SAFE_BOUND)
    def _():
        for head in range(group):
            top_ref[0, head : head + 1] = jnp.full((1, rows), FAR, f32)
            for key, first, end, _, _ in tiles:
                scores = masked(contract(keys_ref[key : key + step], query_ref[head, :, first:end], 1, 0), FAR)
                top_ref[0, head : head + 1, first:end] = jnp.maximum(
                    top_ref[0, head : head + 1, first:end], jnp.max(scores, axis=0, keepdims=True)
                )
            scores = contract(keys_ref[:prompt_rows], query_ref[head, :, prompt_rows:], 1, 0)
            top_ref[0, head : head + 1, prompt_rows:] = jnp.maximum(
                top_ref[0, head : head + 1, prompt_rows:], jnp.max(scores, axis=0, keepdims=True)
            )
        for head in range(group):
            query_ref[head, HEAD_WIDTH:] = in_parts(-top_ref[0, head : head + 1])

    for head in range(group):
        weights = jnp.exp2(contract(keys_ref[:prompt_rows], query_ref[head, :, prompt_rows:], 1, 0)).astype(bf16)
        p_ref[head, :prompt_rows] = weights
        acc_ref[head * wide : (head + 1) * wide, prompt_rows:] = contract(
            values_ref[:, :prompt_rows], weights, 1, 0
        )
    for key, first, end, strip, column in tiles:
        for head in range(group):
            scores = contract(keys_ref[key : key + step], query_ref[head, :, first:end], 1, 0)
            weights = masked(jnp.exp2(scores), 0.0).astype(bf16)
            row = prompt_rows + strip * step
            p_ref[head, row : row + step, column : column + end - first] = weights
            part = contract(values_ref[:, key : key + step], weights, 1, 0)
            at = slice(head * wide, (head + 1) * wide)
            if key == 0:
                acc_ref[at, first:end] = part
            else:
                acc_ref[at, first:end] += part


def own_forward(q, k, v, norm_q, norm_k, kv_heads, prompt_rows, step=256):
    rows = q.shape[1]
    group = q.shape[0] // HEAD_WIDTH // kv_heads
    wide = HEAD_WIDTH + ONES
    block = lambda n: pl.BlockSpec((n, rows), lambda h: (h, 0))
    _, strip_rows = strips(prompt_rows, rows, step)
    assert strip_rows == prompt_rows
    shape = jax.ShapeDtypeStruct
    return pl.pallas_call(
        functools.partial(own_forward_kernel, group=group, prompt_rows=prompt_rows, step=step),
        grid=(kv_heads,),
        in_specs=[
            block(group * HEAD_WIDTH), block(HEAD_WIDTH), block(HEAD_WIDTH), resident(norm_q.shape), resident(norm_k.shape)
        ],
        out_specs=(
            block(group * wide),
            pl.BlockSpec((1, group, rows), lambda h: (h, 0, 0)),
            pl.BlockSpec((group, 2 * prompt_rows, rows - prompt_rows), lambda h: (h, 0, 0)),
        ),
        scratch_shapes=[
            pltpu.VMEM((group, wide, rows), bf16),
            pltpu.VMEM((rows, wide), bf16),
            pltpu.VMEM((wide, rows), bf16),
        ],
        out_shape=(
            shape((kv_heads * group * wide, rows), f32),
            shape((kv_heads, group, rows), f32),
            shape((kv_heads * group, 2 * prompt_rows, rows - prompt_rows), bf16),
        ),
        compiler_params=pltpu.CompilerParams(vmem_limit_bytes=60 * MIB),
        name="own_forward",
    )(q, k, v, norm_q, norm_k)


def other_forward_kernel(
    seen_ref, q_ref, k_ref, v_ref, nq_ref, acc_ref, top_ref, o_ref, own_ref, far_ref, p_ref, query_ref, keys_ref,
    values_ref, *, group, prompt_rows
):
    rows = q_ref.shape[1]
    wide = HEAD_WIDTH + ONES
    seen = seen_ref[0] > 0
    key = k_ref[0].astype(f32)
    norm_k = jnp.max(jnp.sum(key * key, axis=0, keepdims=True))
    slow = jnp.max(nq_ref[...]) * norm_k >= SAFE_BOUND * SAFE_BOUND
    keys_ref[...] = widened(k_ref[0].T)
    values_ref[:HEAD_WIDTH] = v_ref[0]
    values_ref[HEAD_WIDTH:] = jnp.ones((ONES, keys_ref.shape[0]), bf16)
    for head in range(group):
        query_ref[head, :HEAD_WIDTH] = q_ref[head_rows(head)]
        query_ref[head, HEAD_WIDTH:] = jnp.zeros((ONES, rows), bf16)
    far_ref[...] = jnp.zeros_like(far_ref)

    @pl.when(slow)
    def _():
        for head in range(group):
            for first, end in ((0, prompt_rows), (prompt_rows, rows)):
                scores = contract(keys_ref[...], query_ref[head, :, first:end], 1, 0)
                far_ref[0, head : head + 1, first:end] = jnp.max(scores, axis=0, keepdims=True)
            query_ref[head, HEAD_WIDTH:] = in_parts(-far_ref[0, head : head + 1])

    def finish(first, end, with_other):
        for head in range(group):
            own = acc_ref[head * wide : (head + 1) * wide, first:end]
            own_top = top_ref[0, head : head + 1, first:end]
            if with_other:
                weights = jnp.exp2(contract(keys_ref[...], query_ref[head, :, first:end], 1, 0)).astype(bf16)
                p_ref[head, :, first:end] = weights
                far = contract(values_ref[...], weights, 1, 0)
                far_top = far_ref[0, head : head + 1, first:end]
                top = jnp.maximum(own_top, far_top)
                own_scale, far_scale = jnp.exp2(own_top - top), jnp.exp2(far_top - top)
                total = own * own_scale + far * far_scale
                inverse = 1.0 / total[HEAD_WIDTH : HEAD_WIDTH + 1]
                far_ref[0, head : head + 1, first:end] = far_scale * inverse
                own_ref[0, head : head + 1, first:end] = own_scale * inverse
            else:
                total = own
                inverse = 1.0 / total[HEAD_WIDTH : HEAD_WIDTH + 1]
                far_ref[0, head : head + 1, first:end] = jnp.zeros_like(inverse)
                own_ref[0, head : head + 1, first:end] = inverse
            o_ref[head_rows(head), first:end] = (total[:HEAD_WIDTH] * inverse).astype(bf16)

    finish(prompt_rows, rows, True)

    @pl.when(seen)
    def _():
        finish(0, prompt_rows, True)

    @pl.when(jnp.logical_not(seen))
    def _():
        finish(0, prompt_rows, False)


def half_index(h, j, seen):
    return (h, 0, 1 - j * jnp.minimum(seen[0], 1))


def other_forward(seen, q, kv, norm_q, acc, top, kv_heads, prompt_rows):
    rows = q.shape[1]
    group = q.shape[0] // HEAD_WIDTH // kv_heads
    wide = HEAD_WIDTH + ONES
    keys = kv.shape[2]
    block = lambda n, m: pl.BlockSpec((n, m), lambda h, s: (h, 0))
    row_block = pl.BlockSpec((1, group, rows), lambda h, s: (h, 0, 0))
    shape = jax.ShapeDtypeStruct
    return pl.pallas_call(
        functools.partial(other_forward_kernel, group=group, prompt_rows=prompt_rows),
        grid_spec=pltpu.PrefetchScalarGridSpec(
            num_scalar_prefetch=1,
            grid=(kv_heads,),
            in_specs=[
                block(group * HEAD_WIDTH, rows),
                pl.BlockSpec((1, HEAD_WIDTH, keys), lambda h, s: (0, h, 0)),
                pl.BlockSpec((1, HEAD_WIDTH, keys), lambda h, s: (1, h, 0)),
                resident(norm_q.shape),
                block(group * wide, rows),
                row_block,
            ],
            out_specs=(
                block(group * HEAD_WIDTH, rows),
                row_block,
                row_block,
                pl.BlockSpec((group, keys, rows), lambda h, s: (h, 0, 0)),
            ),
            scratch_shapes=[
                pltpu.VMEM((group, wide, rows), bf16),
                pltpu.VMEM((keys, wide), bf16),
                pltpu.VMEM((wide, keys), bf16),
            ],
        ),
        out_shape=(
            shape(q.shape, bf16),
            shape((kv_heads, group, rows), f32),
            shape((kv_heads, group, rows), f32),
            shape((kv_heads * group, keys, rows), bf16),
        ),
        compiler_params=pltpu.CompilerParams(vmem_limit_bytes=60 * MIB),
        name="other_forward",
    )(seen, q, kv, kv, norm_q, acc, top)


def tile_backward(values, key_rows, weights, query, grad):
    slopes = contract(values, grad, 1, 0)
    slopes = (weights.astype(f32) * slopes).astype(bf16)
    query_grad = contract(key_rows, slopes, 1, 0)
    key_grad = contract(query, slopes, 1, 1)
    value_grad = contract(grad[:HEAD_WIDTH], weights, 1, 1)
    return query_grad, key_grad, value_grad


def fill_grads(g_ref, scale_ref, delta_ref, grad_ref, group):
    for head in range(group):
        scale = scale_ref[0, head : head + 1]
        grad_ref[head, :HEAD_WIDTH] = (g_ref[head_rows(head)].astype(f32) * scale).astype(bf16)
        grad_ref[head, HEAD_WIDTH:] = in_parts(-delta_ref[0, head : head + 1] * scale)


def other_backward_kernel(
    seen_ref, q_ref, g_ref, scale_ref, delta_ref, k_ref, v_ref, p_ref, dq_ref, dkv_ref,
    grad_ref, values_ref, dk_sum, dv_sum, dq_sum, *, group, prompt_rows, step
):
    rows = q_ref.shape[1]
    seen = seen_ref[0] > 0
    stage = pl.program_id(1)

    def part(first, last, fresh):
        for low in range(0, k_ref.shape[2], step):
            span = slice(low, low + step)
            key_sum = value_sum = None
            for head in range(group):
                query_grad, key_grad, value_grad = tile_backward(
                    values_ref[span], k_ref[0, :, span], p_ref[head, span],
                    q_ref[head_rows(head), first:last], grad_ref[head, :, first:last],
                )
                if low == 0:
                    dq_sum[head_rows(head), first:last] = query_grad
                else:
                    dq_sum[head_rows(head), first:last] += query_grad
                key_sum = key_grad if key_sum is None else key_sum + key_grad
                value_sum = value_grad if value_sum is None else value_sum + value_grad
            if fresh:
                dk_sum[:, span] = key_sum
                dv_sum[:, span] = value_sum
            else:
                dk_sum[:, span] += key_sum
                dv_sum[:, span] += value_sum

    @pl.when(stage == 0)
    def _():
        fill_grads(g_ref, scale_ref, delta_ref, grad_ref, group)
        values_ref[...] = widened(v_ref[0].T)
        part(prompt_rows, rows, True)

    @pl.when((stage == 1) & seen)
    def _():
        part(0, prompt_rows, False)

    @pl.when((stage == 1) & jnp.logical_not(seen))
    def _():
        dq_sum[:, :prompt_rows] = jnp.zeros((dq_ref.shape[0], prompt_rows), f32)

    @pl.when(stage == 1)
    def _():
        dq_ref[...] = dq_sum[...].astype(bf16)
        dkv_ref[0] = dk_sum[...].astype(bf16)
        dkv_ref[1] = dv_sum[...].astype(bf16)


def other_backward(seen, q, g, scale, delta, kv, p, kv_heads, prompt_rows, step=256):
    rows = q.shape[1]
    group = q.shape[0] // HEAD_WIDTH // kv_heads
    keys = kv.shape[2]
    block = lambda n, m: pl.BlockSpec((n, m), lambda h, j, s: (h, 0))
    row_block = pl.BlockSpec((1, group, rows), lambda h, j, s: (h, 0, 0))
    wide = group * HEAD_WIDTH
    shape = jax.ShapeDtypeStruct
    return pl.pallas_call(
        functools.partial(other_backward_kernel, group=group, prompt_rows=prompt_rows, step=step),
        grid_spec=pltpu.PrefetchScalarGridSpec(
            num_scalar_prefetch=1,
            grid=(kv_heads, 2),
            in_specs=[
                block(wide, rows), block(wide, rows), row_block, row_block,
                pl.BlockSpec((1, HEAD_WIDTH, keys), lambda h, j, s: (0, h, 0)),
                pl.BlockSpec((1, HEAD_WIDTH, keys), lambda h, j, s: (1, h, 0)),
                pl.BlockSpec((group, keys, prompt_rows), half_index),
            ],
            out_specs=(block(wide, rows), pl.BlockSpec((2, HEAD_WIDTH, keys), lambda h, j, s: (0, h, 0))),
            scratch_shapes=[
                pltpu.VMEM((group, HEAD_WIDTH + ONES, rows), bf16),
                pltpu.VMEM((keys, HEAD_WIDTH + ONES), bf16),
                pltpu.VMEM((HEAD_WIDTH, keys), f32),
                pltpu.VMEM((HEAD_WIDTH, keys), f32),
                pltpu.VMEM((wide, rows), f32),
            ],
        ),
        out_shape=(shape(q.shape, bf16), shape(kv.shape, bf16)),
        compiler_params=pltpu.CompilerParams(vmem_limit_bytes=60 * MIB),
        name="other_backward",
    )(seen, q, g, scale, delta, kv, kv, p)


def own_backward_kernel(
    q_ref, g_ref, scale_ref, delta_ref, k_ref, v_ref, p_ref, dq_in_ref, dq_ref, dk_ref, dv_ref,
    grad_ref, values_ref, dk_sum, dv_sum, dq_sum, *, group, prompt_rows, step
):
    rows = q_ref.shape[1]
    stage = pl.program_id(1)
    tiles, _ = strips(prompt_rows, rows, step)

    def one(key, first, end, place, columns):
        span = slice(key, key + step)
        key_sum = value_sum = None
        for head in range(group):
            query_grad, key_grad, value_grad = tile_backward(
                values_ref[span], k_ref[:, span], p_ref[head, place, columns],
                q_ref[head_rows(head), first:end], grad_ref[head, :, first:end],
            )
            dq_sum[head_rows(head), first:end] += query_grad
            key_sum = key_grad if key_sum is None else key_sum + key_grad
            value_sum = value_grad if value_sum is None else value_sum + value_grad
        dk_sum[:, span] += key_sum
        dv_sum[:, span] += value_sum

    @pl.when(stage == 0)
    def _():
        fill_grads(g_ref, scale_ref, delta_ref, grad_ref, group)
        values_ref[...] = widened(v_ref[...].T)
        dq_sum[...] = dq_in_ref[...].astype(f32)
        dk_sum[...] = jnp.zeros_like(dk_sum)
        dv_sum[...] = jnp.zeros_like(dv_sum)
        for key in range(0, prompt_rows, step):
            one(key, prompt_rows, rows, slice(key, key + step), slice(0, rows - prompt_rows))

    @pl.when(stage == 1)
    def _():
        for key, first, end, strip, column in tiles:
            one(key, first, end, slice(strip * step, (strip + 1) * step), slice(column, column + end - first))
        dq_ref[...] = dq_sum[...].astype(bf16)
        dk_ref[...] = dk_sum[...].astype(bf16)
        dv_ref[...] = dv_sum[...].astype(bf16)


def own_backward(q, g, scale, delta, k, v, p, dq, kv_heads, prompt_rows, step=256):
    rows = q.shape[1]
    group = q.shape[0] // HEAD_WIDTH // kv_heads
    block = lambda n: pl.BlockSpec((n, rows), lambda h, j: (h, 0))
    row_block = pl.BlockSpec((1, group, rows), lambda h, j: (h, 0, 0))
    wide = group * HEAD_WIDTH
    shape = jax.ShapeDtypeStruct
    return pl.pallas_call(
        functools.partial(own_backward_kernel, group=group, prompt_rows=prompt_rows, step=step),
        grid=(kv_heads, 2),
        in_specs=[
            block(wide), block(wide), row_block, row_block, block(HEAD_WIDTH), block(HEAD_WIDTH),
            pl.BlockSpec((group, prompt_rows, rows - prompt_rows), lambda h, j: (h, j, 0)),
            block(wide),
        ],
        out_specs=(block(wide), block(HEAD_WIDTH), block(HEAD_WIDTH)),
        scratch_shapes=[
            pltpu.VMEM((group, HEAD_WIDTH + ONES, rows), bf16),
            pltpu.VMEM((rows, HEAD_WIDTH + ONES), bf16),
            pltpu.VMEM((HEAD_WIDTH, rows), f32),
            pltpu.VMEM((HEAD_WIDTH, rows), f32),
            pltpu.VMEM((wide, rows), f32),
        ],
        out_shape=(shape(q.shape, bf16), shape(k.shape, bf16), shape(v.shape, bf16)),
        compiler_params=pltpu.CompilerParams(vmem_limit_bytes=60 * MIB),
        name="own_backward",
    )(q, g, scale, delta, k, v, p, dq)


def middle_kernel(
    x_ref, dy_ref, o_ref, gain_ref, wide_any, wd_any,
    out_ref, h2_ref, hidden_ref, dgate_ref, dup_ref, dattn_ref, dob_ref, delta_ref,
    wo_ref, wg_ref, wu_ref, wd_ref, sems, *, chunk
):
    step = pl.program_id(0)
    inner, total = wo_ref.shape[1], wg_ref.shape[1]
    lows = list(range(0, total, chunk))

    def loads(index):
        low = lows[index]
        span = pl.ds(low, chunk)
        places = (
            (wide_any.at[:, pl.ds(inner + low, chunk)], wg_ref.at[:, span]),
            (wide_any.at[:, pl.ds(inner + total + low, chunk)], wu_ref.at[:, span]),
            (wd_any.at[span], wd_ref.at[span]),
        )
        return [
            pltpu.make_async_copy(source, target, sems.at[1 + 3 * index + i])
            for i, (source, target) in enumerate(places)
        ]

    def rows(loading):
        if loading:
            first = pltpu.make_async_copy(wide_any.at[:, pl.ds(0, inner)], wo_ref, sems.at[0])
            first.start()
            for index in range(len(lows)):
                for copy in loads(index):
                    copy.start()
            first.wait()
        ob = o_ref[...]
        x1 = x_ref[...].astype(f32) + contract(ob, wo_ref[...], 0, 0)
        inverse = lax.rsqrt(jnp.mean(x1 * x1, axis=-1, keepdims=True) + norm_eps)
        gain = gain_ref[1:2]
        h2 = (x1 * inverse * gain).astype(bf16)
        h2_ref[...] = h2
        dy = dy_ref[...]
        result = x1
        dh2 = None
        for index, low in enumerate(lows):
            if loading:
                for copy in loads(index):
                    copy.wait()
            span = slice(low, low + chunk)
            gate = contract(h2, wg_ref[:, span], 1, 0)
            up = contract(h2, wu_ref[:, span], 1, 0)
            dhidden = contract(dy, wd_ref[span], 1, 1)
            sigma = 0.5 + 0.5 * jnp.tanh(0.5 * gate)
            silu = gate * sigma
            hidden = (silu * up).astype(bf16)
            hidden_ref[:, span] = hidden
            result = result + contract(hidden, wd_ref[span], 1, 0)
            dgate = (dhidden * up * (sigma + silu * (1.0 - sigma))).astype(bf16)
            dup = (dhidden * silu).astype(bf16)
            dgate_ref[:, span] = dgate
            dup_ref[:, span] = dup
            part = contract(dgate, wg_ref[:, span], 1, 1) + contract(dup, wu_ref[:, span], 1, 1)
            dh2 = part if dh2 is None else dh2 + part
        out_ref[...] = result.astype(bf16)
        u = dh2 * gain
        dx1 = dy.astype(f32) + inverse * u - x1 * (inverse * inverse * inverse) * jnp.mean(
            u * x1, axis=-1, keepdims=True
        )
        dattn = dx1.astype(bf16)
        dattn_ref[...] = dattn
        dob = contract(wo_ref[...], dattn, 1, 1).astype(bf16)
        dob_ref[...] = dob
        product = dob.astype(f32) * ob.astype(f32)
        heads, group = delta_ref.shape[0], delta_ref.shape[1]
        for kv in range(heads):
            for member in range(group):
                at = (kv * group + member) * HEAD_WIDTH
                delta_ref[kv, member : member + 1] = jnp.sum(
                    product[at : at + HEAD_WIDTH], axis=0, keepdims=True
                )

    @pl.when(step == 0)
    def _():
        rows(True)

    @pl.when(step > 0)
    def _():
        rows(False)


def middle(x, dy, o, gain, wide, wd, kv_heads, tile=256, chunk=768):
    rows, width = x.shape
    hidden = wd.shape[0]
    q_rows = o.shape[0]
    group = q_rows // HEAD_WIDTH // kv_heads
    by_row = lambda n: pl.BlockSpec((tile, n), lambda i: (i, 0))
    any_spec = pl.BlockSpec(memory_space=pl.ANY)
    shape = jax.ShapeDtypeStruct
    return pl.pallas_call(
        functools.partial(middle_kernel, chunk=chunk),
        grid=(rows // tile,),
        in_specs=[by_row(width), by_row(width), pl.BlockSpec((q_rows, tile), lambda i: (0, i)),
                  resident(gain.shape)] + [any_spec] * 2,
        out_specs=(
            by_row(width), by_row(width), by_row(hidden), by_row(hidden), by_row(hidden), by_row(width),
            pl.BlockSpec((q_rows, tile), lambda i: (0, i)),
            pl.BlockSpec((kv_heads, group, tile), lambda i: (0, 0, i)),
        ),
        out_shape=(
            shape((rows, width), bf16), shape((rows, width), bf16), shape((rows, hidden), bf16),
            shape((rows, hidden), bf16), shape((rows, hidden), bf16), shape((rows, width), bf16),
            shape((q_rows, rows), bf16), shape((kv_heads, group, rows), f32),
        ),
        scratch_shapes=[pltpu.VMEM(s, bf16) for s in ((width, q_rows), (width, hidden), (width, hidden), wd.shape)]
        + [pltpu.SemaphoreType.DMA((1 + 3 * (hidden // chunk),))],
        compiler_params=pltpu.CompilerParams(vmem_limit_bytes=62 * MIB),
        name="middle",
    )(x, dy, o, gain, wide, wd)


def down_grads_kernel(dy_ref, hidden_ref, down_ref):
    down_ref[...] = contract(hidden_ref[...], dy_ref[...], 0, 0).astype(bf16)


def down_grads(dy, hidden, tile=512):
    rows, width = dy.shape
    total = hidden.shape[1]
    return pl.pallas_call(
        down_grads_kernel,
        grid=(total // tile,),
        in_specs=[resident(dy.shape), pl.BlockSpec((rows, tile), lambda i: (0, i))],
        out_specs=pl.BlockSpec((tile, width), lambda i: (i, 0)),
        out_shape=jax.ShapeDtypeStruct((total, width), bf16),
        compiler_params=pltpu.CompilerParams(vmem_limit_bytes=60 * MIB),
        name="down_grads",
    )(dy, hidden)


def wide_grads_kernel(o_any, h2_ref, dgate_ref, dup_ref, dattn_ref, out_ref, o_ref, sem, *, each):
    step = pl.program_id(0)
    copy = pltpu.make_async_copy(o_any, o_ref, sem)
    tile = out_ref.shape[1]
    rest = o_ref.shape[0] % tile

    @pl.when(step == 0)
    def _():
        copy.start()

    @pl.when(step < each)
    def _():
        out_ref[...] = contract(h2_ref[...], dgate_ref[...], 0, 0).astype(bf16)

    @pl.when((step >= each) & (step < 2 * each))
    def _():
        out_ref[...] = contract(h2_ref[...], dup_ref[...], 0, 0).astype(bf16)

    @pl.when(step == 2 * each)
    def _():
        copy.wait()

    last = pl.num_programs(0) - 1

    @pl.when((step >= 2 * each) & (step < last))
    def _():
        out_ref[...] = contract(o_ref[...], dattn_ref[...], 1, 0).astype(bf16)

    @pl.when(step == last)
    def _():
        width = rest or tile
        out_ref[:, :width] = contract(o_ref[...], dattn_ref[:, :width], 1, 0).astype(bf16)


def wide_grads(o, h2, dattn, dgate, dup, tile=512):
    rows, width = h2.shape
    total = dgate.shape[1]
    each = total // tile
    steps = 2 * each + pl.cdiv(width, tile)
    cols = lambda low, count: pl.BlockSpec((rows, tile), lambda i: (0, jnp.clip(i - low, 0, count - 1)))
    return pl.pallas_call(
        functools.partial(wide_grads_kernel, each=each),
        grid=(steps,),
        in_specs=[
            pl.BlockSpec(memory_space=pl.ANY), resident(h2.shape),
            cols(0, each), cols(each, each), cols(2 * each, steps - 2 * each),
        ],
        out_specs=pl.BlockSpec((width, tile), lambda i: (0, i)),
        out_shape=jax.ShapeDtypeStruct((width, 2 * total + width), bf16),
        scratch_shapes=[pltpu.VMEM(o.shape, bf16), pltpu.SemaphoreType.DMA],
        compiler_params=pltpu.CompilerParams(vmem_limit_bytes=60 * MIB),
        name="wide_grads",
    )(o, h2, dgate, dup, dattn)


def last_grads_kernel(
    x_ref, gain_ref, dq_ref, dk_ref, dv_ref, dkv_in_ref, cos_ref, sin_ref, lin_ref, dw_ref, acc_ref, *, prompt_steps
):
    step = pl.program_id(0)
    half = HEAD_WIDTH // 2
    cos, sin = cos_ref[...], sin_ref[...]

    def with_received(ref, which):
        return ref[...].astype(f32) + jnp.where(step < prompt_steps, dkv_in_ref[which].astype(f32), 0.0)

    def turned(value, scale):
        c, s = cos * scale, sin * scale
        pieces = []
        for at in range(0, value.shape[0], HEAD_WIDTH):
            a, b = value[at : at + half], value[at + half : at + HEAD_WIDTH]
            pieces += [a * c + b * s, b * c - a * s]
        return jnp.concatenate(pieces, axis=0)

    lin = jnp.concatenate(
        [
            turned(dq_ref[...].astype(f32), HEAD_WIDTH**-0.5),
            turned(with_received(dk_ref, 0), LN2),
            with_received(dv_ref, 1),
        ],
        axis=0,
    ).astype(bf16).T
    lin_ref[...] = lin
    x = x_ref[...].astype(f32)
    inverse = lax.rsqrt(jnp.mean(x * x, axis=-1, keepdims=True) + norm_eps)
    h = (x * inverse * gain_ref[0:1]).astype(bf16)
    part = contract(h, lin, 0, 0)

    @pl.when(step == 0)
    def _():
        acc_ref[...] = part

    @pl.when(step > 0)
    def _():
        acc_ref[...] += part

    @pl.when(step == pl.num_programs(0) - 1)
    def _():
        dw_ref[...] = acc_ref[...].astype(bf16)


def last_grads(x, gains, dq, dk, dv, dkv_in, cos, sin, tile=512):
    rows, width = x.shape
    cols = lambda n: pl.BlockSpec((n, tile), lambda i: (0, i))
    steps = dkv_in.shape[2] // tile
    few = pl.BlockSpec((2, dk.shape[0], tile), lambda i: (0, 0, jnp.minimum(i, steps - 1)))
    shape = jax.ShapeDtypeStruct
    inner = dq.shape[0] + dk.shape[0] + dv.shape[0]
    return pl.pallas_call(
        functools.partial(last_grads_kernel, prompt_steps=steps),
        grid=(rows // tile,),
        in_specs=[pl.BlockSpec((tile, width), lambda i: (i, 0)), resident(gains.shape),
                  cols(dq.shape[0]), cols(dk.shape[0]), cols(dv.shape[0]), few,
                  cols(cos.shape[0]), cols(cos.shape[0])],
        out_specs=(pl.BlockSpec((tile, inner), lambda i: (i, 0)), pl.BlockSpec((width, inner), lambda i: (0, 0))),
        out_shape=(shape((rows, inner), bf16), shape((width, inner), bf16)),
        scratch_shapes=[pltpu.VMEM((width, inner), f32)],
        compiler_params=pltpu.CompilerParams(vmem_limit_bytes=60 * MIB),
        name="last_grads",
    )(x, gains, dq, dk, dv, dkv_in, cos, sin)


def settle_kernel(
    low_ref, first_ref, wide_ref, wide_in_ref, down_ref, down_in_ref, gains_ref, wa_ref, wb_ref, wc_ref, wg_ref, wu_ref,
    tokens_ref, *outs
):
    tokens_ref[...] = low_ref[...].astype(f32)

    @pl.when(pl.program_id(0) == 0)
    def _():
        settle_weights(
            first_ref, wide_ref, wide_in_ref, down_ref, down_in_ref, gains_ref, wa_ref, wb_ref, wc_ref, wg_ref, wu_ref, *outs
        )


def settle_weights(
    first_ref, wide_ref, wide_in_ref, down_ref, down_in_ref, gains_ref, wa_ref, wb_ref, wc_ref, wg_ref, wu_ref, *outs
):
    da, db, dc, dgate, dup, dout, ddown, gain_a, gain_f = outs
    gains = gains_ref[...].astype(f32)

    def spread(total, which):
        return jnp.broadcast_to(total / gains[:, which : which + 1], gains.shape).T[0:1]

    total = None
    at = 0
    for out, weight in ((da, wa_ref), (db, wb_ref), (dc, wc_ref)):
        value = first_ref[:, at : at + out.shape[1]]
        out[...] = value
        part = jnp.sum(value * weight[...].astype(f32), axis=1, keepdims=True)
        total = part if total is None else total + part
        at += out.shape[1]
    gain_a[...] = spread(total, 0)
    total = None
    at = 0
    for out, weight in ((dgate, wg_ref), (dup, wu_ref), (dout, None)):
        span = slice(at, at + out.shape[1])
        value = wide_ref[:, span].astype(f32) + wide_in_ref[:, span].astype(f32)
        out[...] = value
        if weight is not None:
            part = jnp.sum(value * weight[...].astype(f32), axis=1, keepdims=True)
            total = part if total is None else total + part
        at += out.shape[1]
    gain_f[...] = spread(total, 1)
    ddown[...] = down_ref[...].astype(f32) + down_in_ref[...].astype(f32)


def settle(low, first, wide, wide_in, down, down_in, gains, wa, wb, wc, wo, wg, wu):
    rows = first.shape[0]
    count, width = low.shape
    tile = count // 2
    shape = jax.ShapeDtypeStruct
    by_row = pl.BlockSpec((tile, width), lambda i: (i, 0))
    given = (first, wide, wide_in, down, down_in, gains, wa, wb, wc, wg, wu)
    whole = [shape(w.shape, f32) for w in (wa, wb, wc, wg, wu, wo, down)] + [shape((1, rows), f32)] * 2
    return pl.pallas_call(
        settle_kernel,
        grid=(count // tile,),
        in_specs=[by_row] + [resident(array.shape) for array in given],
        out_specs=[by_row] + [pl.BlockSpec(array.shape, lambda i: (0, 0)) for array in whole],
        out_shape=[shape(low.shape, f32)] + whole,
        compiler_params=pltpu.CompilerParams(vmem_limit_bytes=60 * MIB),
        name="settle",
    )(low, *given)


MESH_ID = pl.DeviceIdType.MESH


def whereabouts():
    z, y, w = lax.axis_index("group"), lax.axis_index("ctx"), lax.axis_index("wshard")
    return z, y, w // 2, w % 2


def device_at(z, y, x, core):
    return (z, y, x * 2 + core)


def slot_at(z, x, core):
    return z * 4 + x * 2 + core


def greet(partners):
    barrier = pltpu.get_barrier_semaphore()
    for partner in partners:
        pl.semaphore_signal(barrier, inc=1, device_id=partner, device_id_type=MESH_ID)
    pl.semaphore_wait(barrier, len(partners))


def neighbours(depth):
    z, y, x, core = whereabouts()
    along = [device_at((z + d) % depth, y, x, core) for d in range(1, depth)]
    return along, device_at(z, y, 1 - x, core), device_at(z, 1 - y, x, core), device_at(z, y, x, 1 - core)


class Copies:
    def __init__(self, send_sems, recv_sems):
        self.send_sems, self.recv_sems, self.made = send_sems, recv_sems, []

    def make(self, source, target, device):
        at = len(self.made)
        copy = pltpu.make_async_remote_copy(
            src_ref=source,
            dst_ref=target,
            send_sem=self.send_sems.at[at],
            recv_sem=self.recv_sems.at[at],
            device_id=device,
            device_id_type=MESH_ID,
        )
        self.made.append(copy)
        return copy


def gather_kernel(*refs, depth, split):
    *shards, wo_ref, wg_ref, wu_ref, out_ref, wide_ref, send_sems, recv_sems, own_sems = refs
    z, y, x, core = whereabouts()
    along, over_x, over_y, over_core = neighbours(depth)
    columns = out_ref.shape[2]
    given = pl.ds(pl.multiple_of(y * (columns - split), 128), split)
    got = pl.ds(pl.multiple_of((1 - y) * (columns - split), 128), split)
    common = pl.ds(split, columns - 2 * split)
    me = slot_at(z, x, core)
    copies = Copies(send_sems, recv_sems)
    view = lambda slot, span: out_ref.at[slot, :, span]

    def side_by_side(sources, target, first_sem):
        at = 0
        placed = []
        for index, source in enumerate(sources):
            width = source.shape[1]
            copy = pltpu.make_async_copy(source, target.at[:, pl.ds(at, width)], own_sems.at[first_sem + index])
            copy.start()
            placed.append(copy)
            at += width
        return placed

    own = side_by_side(shards, out_ref.at[me], 0)
    wide = side_by_side((wo_ref, wg_ref, wu_ref), wide_ref, len(shards))
    greet(along + [over_x, over_y, over_core])
    for copy in own:
        copy.wait()

    def send(slot, span, device):
        copy = copies.make(view(slot, span), view(slot, span), device)
        copy.start()
        return copy

    spans = (given, common)
    from_z, from_x, from_y, from_core = {}, {}, {}, []

    def onward(slot, part, d, side):
        if side == 0:
            from_x[d, part] = send(slot, spans[part], over_x)
        if part == 0:
            from_y[d, side] = send(slot, given, over_y)
        from_core.append(send(slot, spans[part], over_core))

    for part in range(2):
        for d in range(1, depth):
            from_z[d, part] = send(me, spans[part], along[d - 1])
        from_x[0, part] = send(me, spans[part], over_x)
    from_core.append(send(me, slice(None), over_core))
    for part in range(2):
        for d in range(1, depth):
            from_z[d, part].wait_recv()
            onward(slot_at((z + depth - d) % depth, x, core), part, d, 0)
    for part in range(2):
        for d in range(depth):
            from_x[d, part].wait_recv()
            onward(slot_at((z + depth - d) % depth, 1 - x, core), part, d, 1)
    for side in range(2):
        for d in range(1 - side, depth):
            from_y[d, side].wait_recv()
            slot = slot_at((z + depth - d) % depth, x if side == 0 else 1 - x, core)
            from_core.append(send(slot, got, over_core))
    for copy in from_core:
        copy.wait_recv()
    for copy in copies.made:
        copy.wait_send()
    for copy in wide:
        copy.wait()


def gather_all(shards, wide, depth, split):
    rows = shards[0].shape[0]
    columns = sum(shard.shape[1] for shard in shards)
    count = 2 * (depth - 1) + 2 * depth + 2 * depth - 1 + 3 * (2 * depth - 1) + 1
    return pl.pallas_call(
        functools.partial(gather_kernel, depth=depth, split=split),
        in_specs=[pl.BlockSpec(memory_space=pl.ANY)] * (len(shards) + len(wide)),
        out_specs=(pl.BlockSpec(memory_space=pltpu.VMEM), pl.BlockSpec(memory_space=pl.ANY)),
        out_shape=(
            jax.ShapeDtypeStruct((4 * depth, rows, columns), bf16),
            jax.ShapeDtypeStruct((rows, sum(shard.shape[1] for shard in wide)), bf16),
        ),
        scratch_shapes=[
            pltpu.SemaphoreType.DMA((count,)),
            pltpu.SemaphoreType.DMA((count,)),
            pltpu.SemaphoreType.DMA((len(shards) + len(wide),)),
        ],
        compiler_params=pltpu.CompilerParams(
            collective_id=1, has_side_effects=True, vmem_limit_bytes=60 * MIB
        ),
        name="gather_all",
    )(*shards, *wide)


def reduce_kernel(
    part_any, lin_ref, w_any, gain_ref, x_ref, dattn_ref, out_ref, tokens_ref,
    mine_ref, w_ref, core_ref, sum_ref, over_ref, line_ref, z_ref, last_ref, twin_ref, send_sems, recv_sems, local_sems,
    *, depth
):
    step = pl.program_id(0)
    steps = pl.num_programs(0)
    z, y, x, core = whereabouts()
    along, over_x, over_y, over_core = neighbours(depth)

    distances = list(range(1, depth)) + [0]
    order = [(d, side) for side in (1, 0) for d in distances]
    place = lambda d, side: ((z + d) % depth, x if side == 0 else 1 - x)

    def remote(source, target, device, at):
        return pltpu.make_async_remote_copy(
            src_ref=source,
            dst_ref=target,
            send_sem=send_sems.at[at],
            recv_sem=recv_sems.at[at],
            device_id=device,
            device_id_type=MESH_ID,
        )

    def to_core(at):
        to_z, to_x = place(*order[at])
        return remote(part_any.at[slot_at(to_z, to_x, 1 - core)], core_ref.at[at], over_core, at)

    def own(at):
        own_z, own_x = place(*order[at])
        return pltpu.make_async_copy(part_any.at[slot_at(own_z, own_x, core)], mine_ref.at[at], local_sems.at[at])

    def weights():
        return pltpu.make_async_copy(w_any.at[:, pl.ds(0, w_ref.shape[1])], w_ref, local_sems.at[2 * depth])

    def to_x(at):
        return remote(sum_ref.at[at], over_ref.at[at], over_x, 2 * depth + at)

    def to_z(at):
        return remote(line_ref.at[at], z_ref.at[at], along[distances[at] - 1], 3 * depth + at)

    def to_y():
        return remote(last_ref, twin_ref, over_y, 4 * depth - 1)

    def core_sums(at):
        own(at).wait()
        to_core(at).wait_recv()
        sum_ref[at] = (mine_ref[at].astype(f32) + core_ref[at].astype(f32)).astype(bf16)

    @pl.when(step == 0)
    def _():
        greet(along + [over_x, over_y, over_core])
        for at in range(2 * depth):
            to_core(at).start()
        for at in range(2 * depth):
            own(at).start()
        weights().start()
        weights().wait()

    @pl.when(step == 1)
    def _():
        for at in range(depth):
            core_sums(at)
            to_x(at).start()

    @pl.when(step == 2)
    def _():
        for at in range(depth, 2 * depth):
            core_sums(at)

    for at in range(depth):

        @pl.when(step == jnp.minimum(3 + at, steps - 1))
        def _():
            to_x(at).wait_recv()
            line_ref[at] = (sum_ref[depth + at].astype(f32) + over_ref[at].astype(f32)).astype(bf16)
            if distances[at]:
                to_z(at).start()

    lin = lin_ref[...]
    dh = contract(lin, w_ref[...], 1, 1)
    tokens = x_ref[...].astype(f32)
    inverse = lax.rsqrt(jnp.mean(tokens * tokens, axis=-1, keepdims=True) + norm_eps)
    u = dh * gain_ref[0:1]
    tokens_ref[...] = (
        dattn_ref[...].astype(f32)
        + inverse * u
        - tokens * (inverse * inverse * inverse) * jnp.mean(u * tokens, axis=-1, keepdims=True)
    ).astype(bf16)

    @pl.when(step == steps - 1)
    def _():
        total = line_ref[depth - 1].astype(f32)
        for at in range(depth - 1):
            to_z(at).wait_recv()
            total = total + z_ref[at].astype(f32)
        last_ref[...] = total.astype(bf16)
        to_y().start()
        to_y().wait_recv()
        out_ref[...] = total + twin_ref[...].astype(f32)
        for at in range(2 * depth):
            to_core(at).wait_send()
        for at in range(depth):
            to_x(at).wait_send()
        for at in range(depth - 1):
            to_z(at).wait_send()
        to_y().wait_send()


def reduce_all(parts, lin, w, gains, x, dattn, depth, tile=256):
    slots, rows, columns = parts.shape
    count, width = x.shape
    sems = 4 * depth
    buffer = lambda *count: pltpu.VMEM(count + (rows, columns), bf16)
    by_row = lambda n: pl.BlockSpec((tile, n), lambda i: (i, 0))
    return pl.pallas_call(
        functools.partial(reduce_kernel, depth=depth),
        grid=(count // tile,),
        in_specs=[
            pl.BlockSpec(memory_space=pl.ANY), by_row(lin.shape[1]), pl.BlockSpec(memory_space=pl.ANY),
            resident(gains.shape),
            by_row(width), by_row(width),
        ],
        out_specs=(pl.BlockSpec((rows, columns), lambda i: (0, 0)), by_row(width)),
        out_shape=(jax.ShapeDtypeStruct((rows, columns), f32), jax.ShapeDtypeStruct((count, width), bf16)),
        scratch_shapes=[
            buffer(2 * depth),
            pltpu.VMEM((width, columns), bf16),
            buffer(2 * depth),
            buffer(2 * depth),
            buffer(depth),
            buffer(depth),
            buffer(depth - 1),
            buffer(),
            buffer(),
            pltpu.SemaphoreType.DMA((sems,)),
            pltpu.SemaphoreType.DMA((sems,)),
            pltpu.SemaphoreType.DMA((2 * depth + 1,)),
        ],
        compiler_params=pltpu.CompilerParams(
            collective_id=2, has_side_effects=True, vmem_limit_bytes=60 * MIB
        ),
        name="reduce_all",
    )(parts, lin, w, gains, x, dattn)


rope_base = 10000.0
masked_score = -1e30


def as_sent(array):

    def short(part):
        return part.astype(jnp.bfloat16) if part.dtype == jnp.float32 else part

    return jax.tree.map(short, array)


def rms_scale(value_rows_list, gain):
    return (
        value_rows_list
        * lax.rsqrt(jnp.mean(value_rows_list * value_rows_list, axis=-1, keepdims=True) + norm_eps)
        * gain
    )


def rms_back(value_rows_list, gain, upstream):
    inverse = lax.rsqrt(
        jnp.mean(value_rows_list * value_rows_list, axis=-1, keepdims=True) + norm_eps
    )
    scaled = upstream * gain
    gain_grad = jnp.sum(upstream * value_rows_list * inverse, axis=0)
    values_grad = inverse * scaled - value_rows_list * (inverse * inverse * inverse) * jnp.mean(
        scaled * value_rows_list, axis=-1, keepdims=True
    )
    return (gain_grad, values_grad)


def rope_tables(token_positions, head_size):
    half_size = head_size // 2
    frequency = rope_base ** (-(jnp.arange(half_size, dtype=jnp.float32) * 2.0) / head_size)
    angles = token_positions.astype(jnp.float32)[:, None] * frequency[None, :]
    return (jnp.cos(angles), jnp.sin(angles))


def rotary_apply(value_rows_list, cosine_table, sine_table):
    half_size = value_rows_list.shape[-1] // 2
    leading = value_rows_list[..., :half_size]
    trailing = value_rows_list[..., half_size:]
    cos_rows = cosine_table[:, None, :]
    sin_rows = sine_table[:, None, :]
    return jnp.concatenate(
        [leading * cos_rows - trailing * sin_rows, trailing * cos_rows + leading * sin_rows],
        axis=-1,
    )


def visible(query_pos, query_seg, key_pos, key_seg):
    same_doc = (key_seg[None, :] == query_seg[:, None]) | (key_seg[None, :] == 0)
    return same_doc & (key_pos[None, :] <= query_pos[:, None])


def tile_scores(query_tile, key_tile, scale):
    return (
        jnp.einsum("rhgd,khd->hgrk", query_tile, key_tile, preferred_element_type=jnp.float32)
        * scale
    )


def key_tiling(key_heads, value_heads, key_pos, key_seg):
    key_block = min(256, key_heads.shape[0])
    tile_count = key_heads.shape[0] // key_block
    return (
        key_heads.reshape(tile_count, key_block, key_heads.shape[1], key_heads.shape[2]),
        value_heads.reshape(tile_count, key_block, value_heads.shape[1], value_heads.shape[2]),
        key_pos.reshape(tile_count, key_block),
        key_seg.reshape(tile_count, key_block),
    )


def query_split(value_rows_list, query_block):
    return value_rows_list.reshape(
        (value_rows_list.shape[0] // query_block, query_block) + value_rows_list.shape[1:]
    )


def attention_forward(query_heads, key_heads, value_heads, places):
    query_pos, query_seg, key_pos, key_seg = places
    count_of_rows, kv_heads, group_size, head_size = query_heads.shape
    scale = head_size ** (-0.5)
    query_block = min(512, count_of_rows)
    key_tiles, value_tiles, kpos_tiles, kseg_tiles = key_tiling(
        key_heads, value_heads, key_pos, key_seg
    )

    def one_block(block_item):
        query_tile, tile_pos, tile_seg = block_item
        state_shape = (kv_heads, group_size, query_tile.shape[0])

        def lse_step(running, tile_item):
            key_tile, tile_kpos, tile_kseg = tile_item
            allowed = visible(tile_pos, tile_seg, tile_kpos, tile_kseg)

            def lse_open_tile(state):
                row_top, row_total = state
                scores = jnp.where(allowed, tile_scores(query_tile, key_tile, scale), masked_score)
                new_top = jnp.maximum(row_top, jnp.max(scores, axis=-1))
                weights = jnp.where(allowed, jnp.exp(scores - new_top[..., None]), 0.0)
                return (new_top, row_total * jnp.exp(row_top - new_top) + jnp.sum(weights, axis=-1))

            def lse_closed_tile(state):
                return state

            return (lax.cond(jnp.any(allowed), lse_open_tile, lse_closed_tile, running), None)

        initial = (
            jnp.full(state_shape, masked_score, jnp.float32),
            jnp.zeros(state_shape, jnp.float32),
        )
        (row_top, row_total), _ = lax.scan(lse_step, initial, (key_tiles, kpos_tiles, kseg_tiles))
        log_total = row_top + jnp.log(row_total)

        def out_step(running, tile_item):
            key_tile, value_tile, tile_kpos, tile_kseg = tile_item
            allowed = visible(tile_pos, tile_seg, tile_kpos, tile_kseg)

            def out_open_tile(accumulated):
                scores = jnp.where(allowed, tile_scores(query_tile, key_tile, scale), masked_score)
                probabilities = jnp.where(
                    allowed, jnp.exp(scores - log_total[..., None]), 0.0
                ).astype(jnp.bfloat16)
                return accumulated + jnp.einsum(
                    "hgrk,khd->rhgd", probabilities, value_tile, preferred_element_type=jnp.float32
                )

            def out_closed_tile(accumulated):
                return accumulated

            return (lax.cond(jnp.any(allowed), out_open_tile, out_closed_tile, running), None)

        output, _ = lax.scan(
            out_step,
            jnp.zeros(query_tile.shape, jnp.float32),
            (key_tiles, value_tiles, kpos_tiles, kseg_tiles),
        )
        return (output, log_total)

    outputs, log_totals = lax.map(
        one_block,
        (
            query_split(query_heads, query_block),
            query_split(query_pos, query_block),
            query_split(query_seg, query_block),
        ),
    )
    return (outputs.reshape(query_heads.shape), log_totals)


def attention_backward(
    query_heads, key_heads, value_heads, places, attended_grad, attended, log_totals
):
    query_pos, query_seg, key_pos, key_seg = places
    count_of_rows, kv_heads, group_size, head_size = query_heads.shape
    scale = head_size ** (-0.5)
    query_block = min(512, count_of_rows)
    key_tiles, value_tiles, kpos_tiles, kseg_tiles = key_tiling(
        key_heads, value_heads, key_pos, key_seg
    )

    def block_grads(sums, block_item):
        query_tile, grad_tile, output_tile, tile_lse, tile_pos, tile_seg = block_item
        tile_delta = jnp.einsum("rhgd,rhgd->hgr", grad_tile.astype(jnp.float32), output_tile)

        def back_step(query_grad, tile_item):
            key_tile, value_tile, tile_kpos, tile_kseg = tile_item
            allowed = visible(tile_pos, tile_seg, tile_kpos, tile_kseg)

            def back_open_tile(query_grad):
                scores = jnp.where(allowed, tile_scores(query_tile, key_tile, scale), masked_score)
                probabilities = jnp.where(allowed, jnp.exp(scores - tile_lse[..., None]), 0.0)
                prob_grad = jnp.einsum(
                    "rhgd,khd->hgrk", grad_tile, value_tile, preferred_element_type=jnp.float32
                )
                score_grad = (probabilities * (prob_grad - tile_delta[..., None])).astype(
                    jnp.bfloat16
                )
                query_grad = query_grad + scale * jnp.einsum(
                    "hgrk,khd->rhgd", score_grad, key_tile, preferred_element_type=jnp.float32
                )
                key_part = scale * jnp.einsum(
                    "hgrk,rhgd->khd", score_grad, query_tile, preferred_element_type=jnp.float32
                )
                value_part = jnp.einsum(
                    "hgrk,rhgd->khd",
                    probabilities.astype(jnp.bfloat16),
                    grad_tile,
                    preferred_element_type=jnp.float32,
                )
                return (query_grad, key_part, value_part)

            def back_closed_tile(query_grad):
                return (
                    query_grad,
                    jnp.zeros(key_tile.shape, jnp.float32),
                    jnp.zeros(value_tile.shape, jnp.float32),
                )

            query_grad, key_part, value_part = lax.cond(
                jnp.any(allowed), back_open_tile, back_closed_tile, query_grad
            )
            return (query_grad, (key_part, value_part))

        query_grad, (key_parts, value_parts) = lax.scan(
            back_step,
            jnp.zeros(query_tile.shape, jnp.float32),
            (key_tiles, value_tiles, kpos_tiles, kseg_tiles),
        )
        return ((sums[0] + key_parts, sums[1] + value_parts), query_grad)

    initial = (jnp.zeros(key_tiles.shape, jnp.float32), jnp.zeros(value_tiles.shape, jnp.float32))
    block_items = (
        query_split(query_heads, query_block),
        query_split(attended_grad, query_block),
        query_split(attended, query_block),
        log_totals,
        query_split(query_pos, query_block),
        query_split(query_seg, query_block),
    )
    (key_sum, value_sum), query_grads = lax.scan(block_grads, initial, block_items)
    key_rows = key_heads.shape[0]
    return (
        query_grads.reshape(query_heads.shape),
        key_sum.reshape(key_rows, -1),
        value_sum.reshape(key_rows, -1),
    )


def forward_pass(weights, inputs, places, tables, gather_pair):
    (
        attn_gain,
        query_full,
        key_complete,
        value_complete,
        out_full,
        ffn_gain,
        gate_full,
        up_full,
        down_full,
    ) = weights
    cosine_table, sine_table = tables
    count_of_rows = inputs.shape[0]
    normalized_input = rms_scale(inputs, attn_gain.astype(jnp.float32)).astype(jnp.bfloat16)
    query_lin = jnp.dot(normalized_input, query_full, preferred_element_type=jnp.float32)
    key_lin = jnp.dot(normalized_input, key_complete, preferred_element_type=jnp.float32)
    value_lin = jnp.dot(normalized_input, value_complete, preferred_element_type=jnp.float32)
    kv_heads = key_lin.shape[1] // HEAD_WIDTH
    query_rot = rotary_apply(
        query_lin.reshape(count_of_rows, -1, HEAD_WIDTH), cosine_table, sine_table
    ).astype(jnp.bfloat16)
    key_rot = (
        rotary_apply(key_lin.reshape(count_of_rows, kv_heads, HEAD_WIDTH), cosine_table, sine_table)
        .astype(jnp.bfloat16)
        .reshape(count_of_rows, -1)
    )
    value_low = value_lin.astype(jnp.bfloat16)
    keys_all, values_all = gather_pair((key_rot, value_low))
    group_size = query_rot.shape[1] // kv_heads
    query_heads = query_rot.reshape(count_of_rows, kv_heads, group_size, HEAD_WIDTH)
    key_heads = keys_all.reshape(-1, kv_heads, HEAD_WIDTH)
    value_heads = values_all.reshape(-1, kv_heads, HEAD_WIDTH)
    attended, log_totals = attention_forward(query_heads, key_heads, value_heads, places)
    attended_low = attended.reshape(count_of_rows, -1).astype(jnp.bfloat16)
    mixed = inputs + jnp.dot(attended_low, out_full, preferred_element_type=jnp.float32)
    normed_two = rms_scale(mixed, ffn_gain.astype(jnp.float32)).astype(jnp.bfloat16)
    gate = jnp.dot(normed_two, gate_full, preferred_element_type=jnp.float32)
    up_value = jnp.dot(normed_two, up_full, preferred_element_type=jnp.float32)
    hidden = (jax.nn.silu(gate) * up_value).astype(jnp.bfloat16)
    result = mixed + jnp.dot(hidden, down_full, preferred_element_type=jnp.float32)
    return (
        normalized_input,
        query_heads,
        key_heads,
        value_heads,
        attended,
        attended_low,
        log_totals,
        mixed,
        normed_two,
        gate,
        up_value,
        hidden,
        result,
    )


def general_local(
    tokens,
    block_map,
    attention_gain,
    query_weight,
    key_matrix,
    value_matrix,
    output_weight,
    feedforward_gain,
    gate_weight,
    up_weight,
    down_weight,
    out_grad,
):
    shards = (
        attention_gain,
        query_weight,
        key_matrix,
        value_matrix,
        output_weight,
        feedforward_gain,
        gate_weight,
        up_weight,
        down_weight,
    )
    count_of_rows = tokens.shape[1]
    ctx_rank = lax.axis_index("ctx")
    blocks = block_map[0]
    block_rows = count_of_rows // 2
    group_rows = blocks.shape[0] * block_rows
    prompt_rows = group_rows // 2
    natural = (
        blocks[:, None] * block_rows + jnp.arange(block_rows, dtype=jnp.int32)[None, :]
    ).reshape(-1)
    in_prompt = natural < prompt_rows
    key_pos = jnp.where(in_prompt, natural, prompt_rows + (natural - prompt_rows) % CONTINUE_LENGTH)
    key_seg = jnp.where(in_prompt, 0, 1 + (natural - prompt_rows) // CONTINUE_LENGTH)
    query_pos = lax.dynamic_slice_in_dim(key_pos, ctx_rank * count_of_rows, count_of_rows)
    query_seg = lax.dynamic_slice_in_dim(key_seg, ctx_rank * count_of_rows, count_of_rows)
    places = (query_pos, query_seg, key_pos, key_seg)
    cosine_table, sine_table = rope_tables(query_pos, HEAD_WIDTH)
    tables = (cosine_table, sine_table)
    inputs = tokens[0].astype(jnp.float32)
    full_weights = (
        lax.all_gather(shards[0], ("group", "wshard"), axis=0, tiled=True),
        lax.all_gather(shards[1], ("group", "wshard"), axis=0, tiled=True),
        lax.all_gather(shards[2], ("group", "wshard"), axis=0, tiled=True),
        lax.all_gather(shards[3], ("group", "wshard"), axis=0, tiled=True),
        lax.all_gather(shards[4], ("group", "wshard"), axis=0, tiled=True),
        lax.all_gather(shards[5], ("group", "wshard"), axis=0, tiled=True),
        lax.all_gather(shards[6], ("group", "wshard"), axis=0, tiled=True),
        lax.all_gather(shards[7], ("group", "wshard"), axis=0, tiled=True),
        lax.all_gather(shards[8], ("group", "wshard"), axis=0, tiled=True),
    )
    forward = forward_pass(
        full_weights,
        inputs,
        places,
        tables,
        lambda packed: jax.tree.map(
            lambda part, own: part.astype(own.dtype),
            lax.all_gather(as_sent(packed), "ctx", axis=0, tiled=True),
            packed,
        ),
    )
    layer_out = forward[12].astype(jnp.bfloat16)
    back_weights = (
        lax.all_gather(shards[0], ("group", "wshard"), axis=0, tiled=True),
        lax.all_gather(shards[1], ("group", "wshard"), axis=0, tiled=True),
        lax.all_gather(shards[2], ("group", "wshard"), axis=0, tiled=True),
        lax.all_gather(shards[3], ("group", "wshard"), axis=0, tiled=True),
        lax.all_gather(shards[4], ("group", "wshard"), axis=0, tiled=True),
        lax.all_gather(shards[5], ("group", "wshard"), axis=0, tiled=True),
        lax.all_gather(shards[6], ("group", "wshard"), axis=0, tiled=True),
        lax.all_gather(shards[7], ("group", "wshard"), axis=0, tiled=True),
        lax.all_gather(shards[8], ("group", "wshard"), axis=0, tiled=True),
    )
    saved = forward_pass(
        back_weights,
        inputs,
        places,
        tables,
        lambda packed: jax.tree.map(
            lambda part, own: part.astype(own.dtype),
            lax.all_gather(as_sent(packed), "ctx", axis=0, tiled=True),
            packed,
        ),
    )
    (
        normalized_input,
        query_heads,
        key_heads,
        value_heads,
        attended,
        attended_low,
        log_totals,
        mixed,
        normed_two,
        gate,
        up_value,
        hidden,
        result,
    ) = saved
    (
        attn_gain,
        query_full,
        key_complete,
        value_complete,
        out_full,
        ffn_gain,
        gate_full,
        up_full,
        down_full,
    ) = back_weights
    upstream = out_grad[0].astype(jnp.float32)
    ffn_grad = upstream.astype(jnp.bfloat16)
    grad_down = jnp.einsum("rf,rd->fd", hidden, ffn_grad, preferred_element_type=jnp.float32)
    hidden_grad = jnp.einsum("rd,fd->rf", ffn_grad, down_full, preferred_element_type=jnp.float32)
    gate_sigmoid = jax.nn.sigmoid(gate)
    gate_grad = (
        hidden_grad * up_value * gate_sigmoid * (1.0 + gate * (1.0 - gate_sigmoid))
    ).astype(jnp.bfloat16)
    up_grad = (hidden_grad * (gate * gate_sigmoid)).astype(jnp.bfloat16)
    grad_gate = jnp.einsum("rd,rf->df", normed_two, gate_grad, preferred_element_type=jnp.float32)
    grad_up = jnp.einsum("rd,rf->df", normed_two, up_grad, preferred_element_type=jnp.float32)
    normed_two_grad = jnp.einsum(
        "rf,df->rd", gate_grad, gate_full, preferred_element_type=jnp.float32
    ) + jnp.einsum("rf,df->rd", up_grad, up_full, preferred_element_type=jnp.float32)
    grad_ffn_gain, mixed_back = rms_back(mixed, ffn_gain.astype(jnp.float32), normed_two_grad)
    mixed_grad = upstream + mixed_back
    attn_grad = mixed_grad.astype(jnp.bfloat16)
    grad_out = jnp.einsum("rf,rd->fd", attended_low, attn_grad, preferred_element_type=jnp.float32)
    attended_grad = (
        jnp.einsum("rd,fd->rf", attn_grad, out_full, preferred_element_type=jnp.float32)
        .astype(jnp.bfloat16)
        .reshape(attended.shape)
    )
    query_grad, key_grad, value_grad = attention_backward(
        query_heads, key_heads, value_heads, places, attended_grad, attended, log_totals
    )
    key_local, value_local = (
        lax.psum_scatter(
            key_grad.astype(jnp.bfloat16), "ctx", scatter_dimension=0, tiled=True
        ).astype(jnp.float32),
        lax.psum_scatter(
            value_grad.astype(jnp.bfloat16), "ctx", scatter_dimension=0, tiled=True
        ).astype(jnp.float32),
    )
    query_lin_grad = (
        rotary_apply(query_grad.reshape(count_of_rows, -1, HEAD_WIDTH), cosine_table, -sine_table)
        .reshape(count_of_rows, -1)
        .astype(jnp.bfloat16)
    )
    key_lin_grad = (
        rotary_apply(key_local.reshape(count_of_rows, -1, HEAD_WIDTH), cosine_table, -sine_table)
        .reshape(count_of_rows, -1)
        .astype(jnp.bfloat16)
    )
    value_lin_grad = value_local.astype(jnp.bfloat16)
    grad_query = jnp.einsum(
        "rd,rf->df", normalized_input, query_lin_grad, preferred_element_type=jnp.float32
    )
    grad_key = jnp.einsum(
        "rd,rf->df", normalized_input, key_lin_grad, preferred_element_type=jnp.float32
    )
    grad_value = jnp.einsum(
        "rd,rf->df", normalized_input, value_lin_grad, preferred_element_type=jnp.float32
    )
    normed_grad = jnp.einsum(
        "rf,df->rd", query_lin_grad, query_full, preferred_element_type=jnp.float32
    )
    normed_grad = normed_grad + jnp.einsum(
        "rf,df->rd", key_lin_grad, key_complete, preferred_element_type=jnp.float32
    )
    normed_grad = normed_grad + jnp.einsum(
        "rf,df->rd", value_lin_grad, value_complete, preferred_element_type=jnp.float32
    )
    grad_attn_gain, input_back = rms_back(inputs, attn_gain.astype(jnp.float32), normed_grad)
    input_grad = mixed_grad + input_back
    partial_grads = (
        grad_attn_gain,
        grad_query,
        grad_key,
        grad_value,
        grad_out,
        grad_ffn_gain,
        grad_gate,
        grad_up,
        grad_down,
    )
    reduced = (
        lax.psum_scatter(
            partial_grads[0].astype(jnp.bfloat16),
            ("group", "wshard"),
            scatter_dimension=0,
            tiled=True,
        ).astype(jnp.float32),
        lax.psum_scatter(
            partial_grads[1].astype(jnp.bfloat16),
            ("group", "wshard"),
            scatter_dimension=0,
            tiled=True,
        ).astype(jnp.float32),
        lax.psum_scatter(
            partial_grads[2].astype(jnp.bfloat16),
            ("group", "wshard"),
            scatter_dimension=0,
            tiled=True,
        ).astype(jnp.float32),
        lax.psum_scatter(
            partial_grads[3].astype(jnp.bfloat16),
            ("group", "wshard"),
            scatter_dimension=0,
            tiled=True,
        ).astype(jnp.float32),
        lax.psum_scatter(
            partial_grads[4].astype(jnp.bfloat16),
            ("group", "wshard"),
            scatter_dimension=0,
            tiled=True,
        ).astype(jnp.float32),
        lax.psum_scatter(
            partial_grads[5].astype(jnp.bfloat16),
            ("group", "wshard"),
            scatter_dimension=0,
            tiled=True,
        ).astype(jnp.float32),
        lax.psum_scatter(
            partial_grads[6].astype(jnp.bfloat16),
            ("group", "wshard"),
            scatter_dimension=0,
            tiled=True,
        ).astype(jnp.float32),
        lax.psum_scatter(
            partial_grads[7].astype(jnp.bfloat16),
            ("group", "wshard"),
            scatter_dimension=0,
            tiled=True,
        ).astype(jnp.float32),
        lax.psum_scatter(
            partial_grads[8].astype(jnp.bfloat16),
            ("group", "wshard"),
            scatter_dimension=0,
            tiled=True,
        ).astype(jnp.float32),
    )
    summed = (
        lax.psum(reduced[0].astype(jnp.bfloat16), "ctx").astype(jnp.float32),
        lax.psum(reduced[1].astype(jnp.bfloat16), "ctx").astype(jnp.float32),
        lax.psum(reduced[2].astype(jnp.bfloat16), "ctx").astype(jnp.float32),
        lax.psum(reduced[3].astype(jnp.bfloat16), "ctx").astype(jnp.float32),
        lax.psum(reduced[4].astype(jnp.bfloat16), "ctx").astype(jnp.float32),
        lax.psum(reduced[5].astype(jnp.bfloat16), "ctx").astype(jnp.float32),
        lax.psum(reduced[6].astype(jnp.bfloat16), "ctx").astype(jnp.float32),
        lax.psum(reduced[7].astype(jnp.bfloat16), "ctx").astype(jnp.float32),
        lax.psum(reduced[8].astype(jnp.bfloat16), "ctx").astype(jnp.float32),
    )
    gain_attn, gain_ffn = (summed[0], summed[5])
    matrices = (summed[1], summed[2], summed[3], summed[4], summed[6], summed[7], summed[8])
    return (
        layer_out[None],
        input_grad[None],
        gain_attn,
        matrices[0],
        matrices[1],
        matrices[2],
        matrices[3],
        gain_ffn,
        matrices[4],
        matrices[5],
        matrices[6],
    )


OWNERS = ("group", "wshard")
SWAP = [(0, 1), (1, 0)]


def swap(array):
    return lax.ppermute(array, "ctx", SWAP)


def fast_local(
    tokens, block_map, attention_gain, query_weight, key_matrix, value_matrix, output_weight,
    feedforward_gain, gate_weight, up_weight, down_weight, out_grad,
):
    x, dy = tokens[0], out_grad[0]
    rows, width = x.shape
    prompt_rows = rows // 2
    q_rows, kv_rows = query_weight.shape[1], key_matrix.shape[1]
    kv_heads = kv_rows // HEAD_WIDTH
    hidden = gate_weight.shape[1]
    shard_rows = query_weight.shape[0]
    block = lax.dynamic_index_in_dim(block_map[0], 2 * lax.axis_index("ctx"), 0, False)
    seen = (block > 0).astype(jnp.int32)
    prompt_total = block_map.shape[1] // 2 * prompt_rows

    depth = lax.axis_size("group")

    gain_columns = jnp.pad(jnp.stack([attention_gain, feedforward_gain], axis=1), ((0, 0), (0, 126)))
    shards = (query_weight, key_matrix, value_matrix, gain_columns)
    split = sum(shard.shape[1] for shard in shards) // 3 // 128 * 128
    wd = lax.all_gather(down_weight, OWNERS, axis=0, tiled=True)
    first, wide = gather_all(shards, (output_weight, gate_weight, up_weight), depth, split)
    first = first.reshape(width, -1)
    wide = lax.all_gather(wide, OWNERS, axis=0, tiled=True)

    at = jnp.arange(rows, dtype=jnp.int32)
    positions = jnp.where(
        at < prompt_rows, block * prompt_rows + at, prompt_total + (at - prompt_rows) % CONTINUE_LENGTH
    )
    half = HEAD_WIDTH // 2
    frequency = (rope_base ** (-(np.arange(half) * 2.0) / HEAD_WIDTH)).astype(np.float32)
    angles = frequency[:, None] * positions.astype(f32)[None, :]
    cos, sin = jnp.cos(angles), jnp.sin(angles)

    q, k, v, kv, norm_q, norm_k, gains = project(x, first, cos, sin, q_rows, kv_rows, prompt_rows)
    kv_other = swap(kv)
    acc, top, p_own = own_forward(q, k, v, norm_q, norm_k, kv_heads, prompt_rows)
    o, own_scale, far_scale, p_far = other_forward(seen[None], q, kv_other, norm_q, acc, top, kv_heads, prompt_rows)
    layer_out, h2, hid, dgate, dup, dattn, dob, delta = middle(x, dy, o, gains, wide, wd, kv_heads)
    scatter = lambda a: lax.psum_scatter(a, OWNERS, scatter_dimension=0, tiled=True)
    d_down = down_grads(dy, hid)
    h2, d_down = lax.optimization_barrier((h2, d_down))
    d_down = scatter(d_down)
    d_wide = wide_grads(o, h2, dattn, dgate, dup)
    dob, d_wide = lax.optimization_barrier((dob, d_wide))
    d_wide = scatter(d_wide)
    dq, dkv_far = other_backward(seen[None], q, dob, far_scale, delta, kv_other, p_far, kv_heads, prompt_rows)
    dkv_in = swap(dkv_far)
    d_down, dkv_in = lax.optimization_barrier((d_down, dkv_in))
    d_down_in = swap(d_down)
    dq, dk, dv = own_backward(q, dob, own_scale, delta, k, v, p_own, dq, kv_heads, prompt_rows)
    lin, d_first = last_grads(x, gains, dq, dk, dv, dkv_in, cos, sin)
    d_first, d_wide = lax.optimization_barrier((d_first, d_wide))
    d_wide_in = swap(d_wide)
    d_first, low_tokens = reduce_all(d_first.reshape(4 * depth, shard_rows, -1), lin, first, gains, x, dattn, depth)
    grad_tokens, d_q, d_k, d_v, d_gate, d_up, d_out, d_down, d_gain_a, d_gain_f = settle(
        low_tokens, d_first, d_wide, d_wide_in, d_down, d_down_in, gain_columns,
        query_weight, key_matrix, value_matrix, output_weight, gate_weight, up_weight,
    )
    return (
        layer_out[None],
        grad_tokens[None],
        d_gain_a[0],
        d_q,
        d_k,
        d_v,
        d_out,
        d_gain_f[0],
        d_gate,
        d_up,
        d_down,
    )


def local(mesh, tokens, block_map, *rest):
    block_rows = tokens.shape[1] // 2
    whole = (
        mesh.shape["ctx"] == 2
        and mesh.shape["wshard"] == 4
        and block_rows % CONTINUE_LENGTH == 0
        and tokens.shape[0] == 1
    )
    return (fast_local if whole else general_local)(tokens, block_map, *rest)


def solution(mesh):
    return jax.shard_map(
        lambda *args: local(mesh, *args),
        mesh=mesh,
        in_specs=(
            P(("group", "wshard"), "ctx", None),
            P(("group", "wshard"), None),
            P(("group", "wshard")),
            P(("group", "wshard"), None),
            P(("group", "wshard"), None),
            P(("group", "wshard"), None),
            P(("group", "wshard"), None),
            P(("group", "wshard")),
            P(("group", "wshard"), None),
            P(("group", "wshard"), None),
            P(("group", "wshard"), None),
            P(("group", "wshard"), "ctx", None),
        ),
        out_specs=(
            P(("group", "wshard"), "ctx", None),
            P(("group", "wshard"), "ctx", None),
            P(("group", "wshard")),
            P(("group", "wshard"), None),
            P(("group", "wshard"), None),
            P(("group", "wshard"), None),
            P(("group", "wshard"), None),
            P(("group", "wshard")),
            P(("group", "wshard"), None),
            P(("group", "wshard"), None),
            P(("group", "wshard"), None),
        ),
        check_vma=False,
    )
```
